32 devices in a mesh: wide: 16 (over z, y, core), narrow: 2 (over x).
Axes of the slice: x: 2, y: 2, z: 4, core: 2. Of those that a mesh axis runs over, the one named last changes fastest.
Arguments:
- tokens_in: bfloat16 [32768, 512], P(('wide', 'narrow')), may hold values from -6 to 6
- ln1_gain: float32 [512], replicated, may hold values from 0.1 to 1.9
- ln1_bias: float32 [512], replicated, may hold values from -4 to 4
- w_qkv: bfloat16 [512, 1536], replicated, may hold values from -0.25 to 0.25
- w_out: bfloat16 [512, 512], replicated, may hold values from -0.75 to 0.75
- ln2_gain: float32 [512], replicated, may hold values from 0.1 to 1.9
- ln2_bias: float32 [512], replicated, may hold values from -4 to 4
- w_up: bfloat16 [512, 2048], P(None, 'narrow'), may hold values from -0.25 to 0.25
- b_up: bfloat16 [2048], P('narrow'), may hold values from -4 to 4
- w_down: bfloat16 [2048, 512], P('narrow'), may hold values from -0.1875 to 0.1875
- b_down: float32 [512], replicated, may hold values from -4 to 4
- segment_ids: int32 [256, 128], P(('wide', 'narrow')), may hold values from 0 to 2, as said below
- step_ids: int32 [256, 128], P(('wide', 'narrow')), may hold values from 0 to 20, as said below
- pad_mask: int32 [256, 128], P(('wide', 'narrow')), may hold values from 0 to 1, as said below
- cotangent: bfloat16 [32768, 512], P(('wide', 'narrow')), may hold values from -6 to 6
Outputs:
- block_out: bfloat16 [32768, 512], P(('wide', 'narrow'))
- grad_tokens: float32 [32768, 512], P(('wide', 'narrow'))
- grad_ln1_gain: float32 [512], replicated
- grad_ln1_bias: float32 [512], replicated
- grad_w_qkv: float32 [512, 1536], replicated
- grad_w_out: float32 [512, 512], replicated
- grad_ln2_gain: float32 [512], replicated
- grad_ln2_bias: float32 [512], replicated
- grad_w_up: float32 [512, 2048], P(None, 'narrow')
- grad_b_up: float32 [2048], P('narrow')
- grad_w_down: float32 [2048, 512], P('narrow')
- grad_b_down: float32 [512], replicated
The draws below stay inside these ranges and needn't reach their ends.
Inputs may be any that keep to these rules, and one draw needn't show every extreme that they name: `segment_ids`: fragment numbers never fall along a row; padding slots carry the number of the row's last fragment. `step_ids`: step numbers never fall within a fragment; padding slots carry 0. `pad_mask`: padding slots stand at the end of a row.
All inputs are finite; a program needn't handle non-finite values.
Results may differ from the reference program's by a relative error of at most 0.019.
Values may be sent and summed in bfloat16 or wider, within the bound.
No kernel may reach another device: no remote copies, remote signals or barrier semaphores. Data moves between devices by JAX's collectives and lax.ppermute only.
A program may use at most 192 MiB of HBM per device.

```python
import math
import jax
import jax.numpy as jnp
from jax import lax

D = 512
HEADS = 8
HEAD = 64
FF = 2048
SLOTS = 128
ROWS = 256
TOKENS = 32768


def fragment_layout(key):
    key_len, key_cnt, key_one, key_two = jax.random.split(key, 4)
    used_steps = jax.random.randint(key_len, (ROWS,), 15, 22).astype(jnp.int32)
    used_steps = used_steps.at[0].set(21)
    pieces = jax.random.randint(key_cnt, (ROWS,), 1, 4).astype(jnp.int32)
    pieces = pieces.at[0].set(1).at[1].set(3)
    first_cut = jax.random.randint(key_one, (ROWS,), 1, 7).astype(jnp.int32)
    second_cut = first_cut + jax.random.randint(key_two, (ROWS,), 1, 7).astype(jnp.int32)
    slot_grid = jnp.arange(SLOTS, dtype=jnp.int32)
    step_grid = jnp.minimum(slot_grid // 6, 20)[None, :]
    pad_flags = (slot_grid[None, :] >= 6 * used_steps[:, None]).astype(jnp.int32)
    past_one = ((step_grid >= first_cut[:, None]) & (pieces[:, None] >= 2)).astype(jnp.int32)
    past_two = ((step_grid >= second_cut[:, None]) & (pieces[:, None] >= 3)).astype(jnp.int32)
    frag_ids = past_one + past_two
    frag_start = past_one * first_cut[:, None] + past_two * (second_cut - first_cut)[:, None]
    local_steps = (step_grid - frag_start) * (1 - pad_flags)
    return (frag_ids, local_steps, pad_flags)


def draw_segment_ids(key, part):
    frag_ids, local_steps, pad_flags = fragment_layout(key)
    return frag_ids


def draw_step_ids(key, part):
    frag_ids, local_steps, pad_flags = fragment_layout(key)
    return local_steps


def draw_pad_mask(key, part):
    frag_ids, local_steps, pad_flags = fragment_layout(key)
    return pad_flags


def block_scale(key, extent, cuts, least, largest):
    gain = 1.0
    for axis_at, parts in cuts:
        heights = jax.random.uniform(jax.random.fold_in(jax.random.fold_in(key, 6), axis_at), (parts,), jnp.float32, least / len(cuts), largest / len(cuts))
        gain = gain * jnp.repeat(jnp.exp(heights), extent[axis_at] // parts).reshape((-1,) + (1,) * (len(extent) - 1 - axis_at))
    return gain


def normal_values(own_key, extent, scale, reach, shards=(), kind=jnp.bfloat16):
    level = block_scale(own_key, extent, shards, -0.22, 0.18) if shards else 1.0
    values = jax.random.normal(own_key, extent, jnp.float32) * scale * level
    return jnp.minimum(jnp.maximum(values, -reach), reach).astype(kind)


def setup_inputs(seed: int = 0) -> dict:
    key_of = jax.random.split(jax.random.key(seed), 16)
    return {
        "tokens_in": normal_values(key_of[0], (TOKENS, D), 1.0, 6.0, ((0, 32),)),
        "ln1_gain": jnp.clip(1.0 + 0.18 * jax.random.normal(key_of[1], (D,), jnp.float32), 0.1, 1.9),
        "ln1_bias": normal_values(key_of[2], (D,), 0.3, 4.0, (), jnp.float32),
        "w_qkv": normal_values(key_of[3], (D, 3 * D), D ** -0.5, 0.25),
        "w_out": normal_values(key_of[4], (D, D), (D // 8) ** -0.5, 0.75),
        "ln2_gain": jnp.clip(1.0 + 0.18 * jax.random.normal(key_of[5], (D,), jnp.float32), 0.1, 1.9),
        "ln2_bias": normal_values(key_of[6], (D,), 0.3, 4.0, (), jnp.float32),
        "w_up": normal_values(key_of[7], (D, FF), D ** -0.5, 0.25, ((1, 2),)),
        "b_up": normal_values(key_of[8], (FF,), 0.5, 4.0, ((0, 2),)),
        "w_down": normal_values(key_of[9], (FF, D), (FF // 2) ** -0.5, 0.1875, ((0, 2),)),
        "b_down": normal_values(key_of[10], (D,), 0.3, 4.0, (), jnp.float32),
        "segment_ids": draw_segment_ids(jax.random.fold_in(key_of[15], 71), 0),
        "step_ids": draw_step_ids(jax.random.fold_in(key_of[15], 71), 0),
        "pad_mask": draw_pad_mask(jax.random.fold_in(key_of[15], 71), 0),
        "cotangent": normal_values(key_of[14], (TOKENS, D), 1.0, 6.0, ((0, 32),)),
    }


@jax.custom_vjp
def low(v):
    return lax.optimization_barrier(v.astype(jnp.bfloat16)).astype(jnp.float32)

@jax.custom_vjp
def low_back(v):
    return v

def low_keep(v):
    return (low(v), None)

def low_pass(kept, grad):
    return (grad,)

def back_keep(v):
    return (v, None)

def back_low(kept, grad):
    return (low(grad),)
low.defvjp(low_keep, low_pass)
low_back.defvjp(back_keep, back_low)
NORM_EPS = 1e-05

def high_dot(left_mat, right_mat):
    return jnp.dot(left_mat, right_mat, precision=lax.Precision.HIGHEST)

def norm_rows(inputs, gain_vec, shift_vec):
    row_mean = lax.optimization_barrier(jnp.mean(inputs, axis=-1, keepdims=True))
    centered = inputs - row_mean
    variance = lax.optimization_barrier(jnp.mean(centered * centered, axis=-1, keepdims=True))
    return centered * lax.rsqrt(variance + NORM_EPS) * gain_vec + shift_vec

def visible_keys(frag_ids, step_nums, pad_flags):
    same_frag = frag_ids[:, :, None] == frag_ids[:, None, :]
    earlier = step_nums[:, None, :] <= step_nums[:, :, None]
    live_keys = (pad_flags == 0)[:, None, :]
    itself = jnp.eye(frag_ids.shape[1], dtype=bool)[None]
    return same_frag & earlier & live_keys | itself

def attend_block(queries, key_rows, value_rows, frag_ids, step_nums, pad_flags):
    visible = visible_keys(frag_ids, step_nums, pad_flags)[:, None]
    scores = jnp.einsum('rqhd,rkhd->rhqk', queries, key_rows, precision=lax.Precision.HIGHEST) * HEAD ** (-0.5)
    scores = jnp.where(visible, low_back(scores), -1e+30)
    row_top = lax.optimization_barrier(jnp.max(scores, axis=-1, keepdims=True))
    weight = jnp.exp(scores - row_top)
    probs = low(weight / lax.optimization_barrier(jnp.sum(weight, axis=-1, keepdims=True)))
    return jnp.einsum('rhqk,rkhd->rqhd', probs, value_rows, precision=lax.Precision.HIGHEST)

def layer(inputs, ln1_gain, ln1_bias, w_qkv, w_out, ln2_gain, ln2_bias, w_up, b_up, w_down, b_down, segment_ids, step_ids, pad_mask):
    group_rows = math.gcd(ROWS, 32)
    blocks = ROWS // group_rows
    block_shape = (blocks, group_rows, SLOTS, HEADS, HEAD)
    normed = low(norm_rows(inputs, ln1_gain, ln1_bias))
    qkv = high_dot(normed, w_qkv)
    queries = low_back(low(qkv[:, :D])).reshape(block_shape)
    key_rows = low_back(low(qkv[:, D:2 * D])).reshape(block_shape)
    value_rows = low_back(low(qkv[:, 2 * D:])).reshape(block_shape)
    frag_blocks = segment_ids.reshape(blocks, group_rows, SLOTS)
    step_blocks = step_ids.reshape(blocks, group_rows, SLOTS)
    pad_blocks = pad_mask.reshape(blocks, group_rows, SLOTS)
    head_mixed = lax.map(jax.checkpoint(lambda block: attend_block(*block)), (queries, key_rows, value_rows, frag_blocks, step_blocks, pad_blocks))
    head_mixed = low_back(low(head_mixed.reshape(TOKENS, D)))
    residual = inputs + low_back(high_dot(head_mixed, w_out))
    second = low(norm_rows(residual, ln2_gain, ln2_bias))
    pre_act = low_back(high_dot(second, w_up) + b_up)
    hidden = low(jax.nn.gelu(pre_act, approximate=False))
    return residual + low_back(high_dot(hidden, w_down) + b_down)

def reference(tokens_in, ln1_gain, ln1_bias, w_qkv, w_out, ln2_gain, ln2_bias, w_up, b_up, w_down, b_down, segment_ids, step_ids, pad_mask, cotangent):
    floats = tuple((member.astype(jnp.float32) for member in (tokens_in, ln1_gain, ln1_bias, w_qkv, w_out, ln2_gain, ln2_bias, w_up, b_up, w_down, b_down)))

    def forward(*weights_in):
        return layer(*weights_in, segment_ids, step_ids, pad_mask)
    result, pullback = jax.vjp(forward, *floats)
    gradients = pullback(cotangent.astype(jnp.float32))
    return (result.astype(jnp.bfloat16), gradients[0], gradients[1], gradients[2], gradients[3], gradients[4], gradients[5], gradients[6], gradients[7], gradients[8], gradients[9], gradients[10])
```

```python
import functools

import jax
import jax.numpy as jnp
import numpy as np
from jax import lax
from jax.experimental import pallas as pl
from jax.experimental.pallas import tpu as pltpu
from jax.sharding import PartitionSpec as P

HEAD = 64
PAIR = 2 * HEAD
NORM_EPS = 1e-05
BF = jnp.bfloat16
F32 = jnp.float32
AXES = ("wide", "narrow")
TILE = 16
TOKS = 256
VMEM_LIMIT = 50 * 1024 * 1024


def mm(a, b):
    return lax.dot_general(a, b, (((1,), (0,)), ((), ())), preferred_element_type=F32)


def mm_nt(a, b):
    return lax.dot_general(a, b, (((1,), (1,)), ((), ())), preferred_element_type=F32)


def mm_tn(a, b):
    return lax.dot_general(a, b, (((0,), (0,)), ((), ())), preferred_element_type=F32)


def whole(*shape):
    return pl.BlockSpec(shape, lambda *_: (0,) * len(shape))


def rows_of(width, toks=TOKS):
    return pl.BlockSpec((toks, width), lambda i, *_: (i, 0))


def call(kernel, name, grid, in_specs, out_specs, out_shape, scratch, info, args):
    return pl.pallas_call(
        kernel,
        grid_spec=pltpu.PrefetchScalarGridSpec(
            num_scalar_prefetch=1, grid=grid, in_specs=in_specs, out_specs=out_specs, scratch_shapes=scratch
        ),
        out_shape=out_shape,
        compiler_params=pltpu.CompilerParams(vmem_limit_bytes=VMEM_LIMIT),
        name=name,
    )(info, *args)


def unit_parts(rows):
    mean = jnp.mean(rows, axis=-1, keepdims=True)
    centered = rows - mean
    inv = lax.rsqrt(jnp.mean(centered * centered, axis=-1, keepdims=True) + NORM_EPS)
    return centered * inv, inv


def norm_back(incoming, unit, inv, gain):
    scaled = incoming * gain
    return inv * (
        scaled
        - jnp.mean(scaled, axis=-1, keepdims=True)
        - unit * jnp.mean(scaled * unit, axis=-1, keepdims=True)
    )


def gelu_pair(x):
    cdf = 0.5 * (1.0 + lax.erf(x * 0.7071067811865476))
    return x * cdf, cdf + x * jnp.exp(-0.5 * x * x) * 0.3989422804014327


def by_head(block):
    lane = lax.broadcasted_iota(jnp.int32, block.shape, 1)
    zero = jnp.zeros_like(block)
    first = lane < HEAD
    return jnp.concatenate([jnp.where(first, block, zero), jnp.where(first, zero, block)], axis=0)


def places(order, blocks):
    bits = blocks.bit_length() - 1
    table = []
    for place in range(blocks):
        owner = 0
        for step in range(bits):
            if place >> (bits - 1 - step) & 1:
                owner ^= order[step]
        table.append(owner)
    return table


def block_at(place, tables, core, own):
    first, second = tables[0][place], tables[1][place]
    if first == second:
        return own ^ first
    return own ^ jnp.where(core == 0, first, second)


def permuted(dst_ref, acc_ref, tables, core, own):
    blocks = len(tables[0])
    size = acc_ref.shape[0] // blocks
    for place in range(blocks):
        block = block_at(place, tables, core, own)
        rows = pl.ds(pl.multiple_of(block * size, size), size)
        dst_ref[place * size : (place + 1) * size, :] = acc_ref[rows, :].astype(dst_ref.dtype)


def attend_kernel(
    info_ref, tok_ref, g1_ref, c1_ref, wqkv_ref, wout_ref, g2_ref, c2_ref, seg_ref, step_ref, pad_ref,
    qkv_ref, prob_ref, mixed_ref, res_ref, second_ref,
):
    slots = seg_ref.shape[1]
    toks, width = tok_ref.shape
    rows = toks // slots
    at = pl.program_id(0)
    tokens = tok_ref[...].astype(F32)
    unit, _ = unit_parts(tokens)
    normed = (unit * g1_ref[...] + c1_ref[...]).astype(BF)
    qkv_ref[...] = mm(normed, wqkv_ref[...]).astype(BF)
    q_id = lax.broadcasted_iota(jnp.int32, (slots, slots), 0)
    k_id = lax.broadcasted_iota(jnp.int32, (slots, slots), 1)
    eye = q_id == k_id
    for r in range(rows):
        here = pl.ds(at * rows + r, 1)
        seg = jnp.broadcast_to(seg_ref[here, :].astype(F32), (slots, slots))
        step = jnp.broadcast_to(step_ref[here, :].astype(F32), (slots, slots))
        live = jnp.broadcast_to(pad_ref[here, :], (slots, slots)) == 0
        visible = ((seg == seg.T) & (step <= step.T) & live) | eye
        span = slice(r * slots, (r + 1) * slots)
        for p in range(width // PAIR):
            cols = slice(p * PAIR, (p + 1) * PAIR)
            q = qkv_ref[span, p * PAIR : (p + 1) * PAIR]
            k = qkv_ref[span, width + p * PAIR : width + (p + 1) * PAIR]
            v = qkv_ref[span, 2 * width + p * PAIR : 2 * width + (p + 1) * PAIR]
            scores = mm_nt(q, by_head(k * HEAD ** (-0.5)))
            halves = []
            for half in (scores[:, :slots], scores[:, slots:]):
                half = jnp.where(visible, half, -1e30)
                weight = jnp.exp(half - jnp.max(half, axis=-1, keepdims=True))
                total = jnp.sum(weight, axis=-1, keepdims=True)
                halves.append((weight * (1.0 / total)).astype(BF))
            prob = jnp.concatenate(halves, axis=1)
            prob_ref[r, p] = prob
            mixed_ref[span, cols] = mm(prob, by_head(v)).astype(BF)
    residual = tokens + mm(mixed_ref[...], wout_ref[...])
    res_ref[...] = residual
    unit, _ = unit_parts(residual)
    second_ref[...] = (unit * g2_ref[...] + c2_ref[...]).astype(BF)


def attend(info, tokens, g1, c1, wqkv, wout, g2, c2, seg, step, pad):
    n, width = tokens.shape
    rows, slots = seg.shape
    per, pairs = TOKS // slots, width // PAIR
    return call(
        attend_kernel,
        "attend",
        (n // TOKS,),
        [rows_of(width), whole(1, width), whole(1, width), whole(*wqkv.shape), whole(*wout.shape)]
        + [whole(1, width)] * 2
        + [whole(rows, slots)] * 3,
        [
            rows_of(3 * width),
            pl.BlockSpec((per, pairs, slots, 2 * slots), lambda i, *_: (i, 0, 0, 0)),
            rows_of(width),
            rows_of(width),
            rows_of(width),
        ],
        [
            jax.ShapeDtypeStruct((n, 3 * width), BF),
            jax.ShapeDtypeStruct((rows, pairs, slots, 2 * slots), BF),
            jax.ShapeDtypeStruct((n, width), BF),
            jax.ShapeDtypeStruct((n, width), F32),
            jax.ShapeDtypeStruct((n, width), BF),
        ],
        [],
        info,
        (tokens, g1, c1, wqkv, wout, g2, c2, seg, step, pad),
    )


def ffn_block(sec, sec_t, dy, dy_t, up, bias, down, acc_ref, bacc_ref, out, dsec):
    units = up.shape[1]
    pre = mm(sec, up) + bias
    hid, slope = gelu_pair(pre)
    hid = hid.astype(BF)
    dpre = (mm_nt(dy, down) * slope).astype(BF)
    acc_ref[:, :units] += mm(sec_t, dpre)
    acc_ref[:, units:] += mm(dy_t, hid)
    bacc_ref[...] += jnp.sum(dpre.astype(F32), axis=0, keepdims=True)
    o = mm(hid, down)
    d = mm_nt(dpre, up)
    return (o if out is None else out + o), (d if dsec is None else dsec + d)


def ffn_own_kernel(tables, info_ref, sec_ref, dy_ref, *refs):
    ups, biases, downs = refs[:2], refs[2:4], refs[4:6]
    out_ref, dsec_ref = refs[6:8]
    grads, bgrads, accs, baccs = refs[8:10], refs[10:12], refs[12:14], refs[14:16]
    at, last = pl.program_id(0), pl.num_programs(0) - 1

    @pl.when(at == 0)
    def _():
        for ref in accs + baccs:
            ref[...] = jnp.zeros_like(ref)

    sec, dy = sec_ref[...], dy_ref[...]
    sec_t, dy_t = sec.T, dy.T
    out = dsec = None
    for i in range(2):
        out, dsec = ffn_block(
            sec, sec_t, dy, dy_t, ups[i][...], biases[i][...].astype(F32), downs[i][...], accs[i], baccs[i], out, dsec
        )
    out_ref[...] = out
    dsec_ref[...] = dsec

    @pl.when(at == last)
    def _():
        core, own = info_ref[0], info_ref[1]
        for i in range(2):
            permuted(grads[i], accs[i], tables, core ^ i, own)
            bgrads[i][...] = baccs[i][...]


def ffn_own(info, tables, second, dy, up, bias, down):
    n, width = second.shape
    units = up.shape[1] // 2
    chunk = lambda i: (lambda t, info: (0, info[0] ^ i))
    return call(
        functools.partial(ffn_own_kernel, tables),
        "ffn_own",
        (n // TOKS,),
        [rows_of(width), rows_of(width)]
        + [pl.BlockSpec((width, units), chunk(i)) for i in range(2)]
        + [pl.BlockSpec((1, units), chunk(i)) for i in range(2)]
        + [pl.BlockSpec((units, width), lambda t, info, i=i: (info[0] ^ i, 0)) for i in range(2)],
        [rows_of(width)] * 2 + [whole(width, 2 * units)] * 2 + [whole(1, units)] * 2,
        [jax.ShapeDtypeStruct((n, width), F32)] * 2
        + [jax.ShapeDtypeStruct((width, 2 * units), BF)] * 2
        + [jax.ShapeDtypeStruct((1, units), F32)] * 2,
        [pltpu.VMEM((width, 2 * units), F32)] * 2 + [pltpu.VMEM((1, units), F32)] * 2,
        info,
        (second, dy, up, up, bias, bias, down, down),
    )


def ffn_rest_kernel(
    tables, count, info_ref, sec_ref, dy_ref, out_part_ref, dsec_part_ref, res_ref, mixed_ref, bdown_ref, g2_ref, wout_ref, *refs
):
    ups, downs = refs[:count], refs[count : 2 * count]
    block_ref, gres_ref, gmix_ref, vec_ref, dwout_ref = refs[2 * count : 2 * count + 5]
    rest = refs[2 * count + 5 :]
    grads, bgrads = rest[:count], rest[count : 2 * count]
    accs, baccs = rest[2 * count : 3 * count], rest[3 * count : 4 * count]
    wacc_ref = rest[4 * count]
    at, last = pl.program_id(0), pl.num_programs(0) - 1
    width = sec_ref.shape[1]

    @pl.when(at == 0)
    def _():
        for ref in accs + baccs + (wacc_ref, vec_ref):
            ref[...] = jnp.zeros_like(ref)

    sec, dy = sec_ref[...], dy_ref[...]
    sec_t, dy_t = sec.T, dy.T
    out, dsec = out_part_ref[...], dsec_part_ref[...]
    for i in range(count):
        bias = ups[i][width : width + TILE, :].astype(F32)[:1]
        out, dsec = ffn_block(sec, sec_t, dy, dy_t, ups[i][:width, :], bias, downs[i][...], accs[i], baccs[i], out, dsec)
    residual = res_ref[...]
    block_ref[...] = (residual + (out + bdown_ref[...])).astype(BF)
    dy32 = dy.astype(F32)
    unit, inv = unit_parts(residual)
    vec_ref[0:1, :] += jnp.sum(dsec * unit, axis=0, keepdims=True)
    vec_ref[1:2, :] += jnp.sum(dsec, axis=0, keepdims=True)
    vec_ref[2:3, :] += jnp.sum(dy32, axis=0, keepdims=True)
    gres = dy32 + norm_back(dsec, unit, inv, g2_ref[...])
    gres_ref[...] = gres
    branch = gres.astype(BF)
    gmix_ref[...] = mm_nt(branch, wout_ref[...]).astype(BF)
    wacc_ref[...] += mm_tn(mixed_ref[...], branch)

    @pl.when(at == last)
    def _():
        core, own = info_ref[0], info_ref[1]
        for i in range(count):
            permuted(grads[i], accs[i], tables, core ^ (i % 2), own)
            bgrads[i][...] = baccs[i][...]
        dwout_ref[...] = wacc_ref[...]


def ffn_rest(info, tables, second, dy, out_part, dsec_part, residual, mixed, bdown, g2, wout, chunks):
    n, width = second.shape
    count = len(chunks)
    units = chunks[0][0].shape[1]
    return call(
        functools.partial(ffn_rest_kernel, tables, count),
        "ffn_rest",
        (n // TOKS,),
        [rows_of(width)] * 6
        + [whole(1, width)] * 2
        + [whole(width, width)]
        + [whole(width + TILE, units)] * count
        + [whole(units, width)] * count,
        [rows_of(width)] * 3
        + [whole(8, width), whole(width, width)]
        + [whole(width, 2 * units)] * count
        + [whole(1, units)] * count,
        [
            jax.ShapeDtypeStruct((n, width), BF),
            jax.ShapeDtypeStruct((n, width), F32),
            jax.ShapeDtypeStruct((n, width), BF),
            jax.ShapeDtypeStruct((8, width), F32),
            jax.ShapeDtypeStruct((width, width), F32),
        ]
        + [jax.ShapeDtypeStruct((width, 2 * units), BF)] * count
        + [jax.ShapeDtypeStruct((1, units), F32)] * count,
        [pltpu.VMEM((width, 2 * units), F32)] * count
        + [pltpu.VMEM((1, units), F32)] * count
        + [pltpu.VMEM((width, width), F32)],
        info,
        (second, dy, out_part, dsec_part, residual, mixed, bdown, g2, wout)
        + tuple(c[0] for c in chunks)
        + tuple(c[1] for c in chunks),
    )


def attend_back_kernel(
    tables, info_ref, qkv_ref, prob_ref, gmix_ref, tok_ref, g1_ref, c1_ref, dwout_ref, grad_ref, dw_keep_ref, dw_send_ref,
    dqkv_ref, acc_ref,
):
    at, last = pl.program_id(0), pl.num_programs(0) - 1
    toks, width = tok_ref.shape
    rows, pairs, slots, _ = prob_ref.shape

    @pl.when(at == 0)
    def _():
        acc_ref[:, : 3 * width] = jnp.zeros((width, 3 * width), F32)
        acc_ref[:, 3 * width :] = dwout_ref[...]

    scale = HEAD ** (-0.5)
    for r in range(rows):
        span = slice(r * slots, (r + 1) * slots)
        for p in range(pairs):
            cols = slice(p * PAIR, (p + 1) * PAIR)
            kcols = slice(width + p * PAIR, width + (p + 1) * PAIR)
            vcols = slice(2 * width + p * PAIR, 2 * width + (p + 1) * PAIR)
            q = qkv_ref[span, cols]
            k = qkv_ref[span, kcols]
            v = qkv_ref[span, vcols]
            g = gmix_ref[span, cols]
            prob = prob_ref[r, p]
            dprob = mm_nt(g, by_head(v))
            p32 = prob.astype(F32)
            prod = p32 * dprob
            first = jnp.sum(prod[:, :slots], axis=-1, keepdims=True)
            second = jnp.sum(prod[:, slots:], axis=-1, keepdims=True)
            ds_a = (p32[:, :slots] * (dprob[:, :slots] - first)).astype(BF)
            ds_b = (p32[:, slots:] * (dprob[:, slots:] - second)).astype(BF)
            dqkv_ref[span, cols] = mm(jnp.concatenate([ds_a, ds_b], axis=1), by_head(k * scale)).astype(BF)
            dqkv_ref[span, kcols] = mm_tn(jnp.concatenate([ds_a, ds_b], axis=0), by_head(q * scale)).astype(BF)
            dqkv_ref[span, vcols] = mm_tn(
                jnp.concatenate([prob[:, :slots], prob[:, slots:]], axis=0), by_head(g)
            ).astype(BF)
    unit, _ = unit_parts(tok_ref[...].astype(F32))
    normed = (unit * g1_ref[...] + c1_ref[...]).astype(BF)
    acc_ref[:, : 3 * width] += mm_tn(normed, dqkv_ref[...])
    grad_ref[...] = dqkv_ref[...]

    @pl.when(at == last)
    def _():
        core, own = info_ref[0], info_ref[2]
        half = width // 2
        size = width // len(tables[0])
        for place in range(len(tables[0])):
            dst = dw_keep_ref if place * size < half else dw_send_ref
            block = block_at(place, tables, core, own)
            rows_at = pl.ds(pl.multiple_of(block * size, size), size)
            to = place * size % half
            dst[to : to + size, :] = acc_ref[rows_at, :].astype(BF)


def attend_back(info, tables, qkv, prob, gmix, tokens, g1, c1, dwout):
    n, width = tokens.shape
    rows, pairs, slots, _ = prob.shape
    per = TOKS // slots
    return call(
        functools.partial(attend_back_kernel, tables),
        "attend_back",
        (n // TOKS,),
        [
            rows_of(3 * width),
            pl.BlockSpec((per, pairs, slots, 2 * slots), lambda i, *_: (i, 0, 0, 0)),
            rows_of(width),
            rows_of(width),
            whole(1, width),
            whole(1, width),
            whole(width, width),
        ],
        [rows_of(3 * width)] + [whole(width // 2, 4 * width)] * 2,
        [jax.ShapeDtypeStruct((n, 3 * width), BF)] + [jax.ShapeDtypeStruct((width // 2, 4 * width), BF)] * 2,
        [pltpu.VMEM((TOKS, 3 * width), BF), pltpu.VMEM((width, 4 * width), F32)],
        info,
        (qkv, prob, gmix, tokens, g1, c1, dwout),
    )


def first_back_kernel(info_ref, dqkv_ref, wqkv_ref, tok_ref, gres_ref, g1_ref, vec_in_ref, out_ref, vec_ref):
    @pl.when(pl.program_id(0) == 0)
    def _():
        vec_ref[...] = vec_in_ref[...]

    dnormed = mm_nt(dqkv_ref[...], wqkv_ref[...])
    unit, inv = unit_parts(tok_ref[...].astype(F32))
    vec_ref[3:4, :] += jnp.sum(dnormed * unit, axis=0, keepdims=True)
    vec_ref[4:5, :] += jnp.sum(dnormed, axis=0, keepdims=True)
    out_ref[...] = gres_ref[...] + norm_back(dnormed, unit, inv, g1_ref[...])


def first_back(info, dqkv, wqkv, tokens, gres, g1, vec):
    n, width = tokens.shape
    return call(
        first_back_kernel,
        "first_back",
        (n // TOKS,),
        [rows_of(3 * width), whole(*wqkv.shape), rows_of(width), rows_of(width), whole(1, width), whole(*vec.shape)],
        [rows_of(width), whole(*vec.shape)],
        [jax.ShapeDtypeStruct((n, width), F32), jax.ShapeDtypeStruct(vec.shape, F32)],
        [],
        info,
        (dqkv, wqkv, tokens, gres, g1, vec),
    )


def ffn_end_kernel(tables, info_ref, keep_ref, other_ref, up_ref, down_ref, full_ref):
    core, own = info_ref[0], info_ref[1]
    units = up_ref.shape[1]
    blocks = len(tables[0])
    size = keep_ref.shape[0] // blocks

    def lay(src_ref, whose):
        for place in range(blocks):
            block = block_at(place, tables, whose, own)
            rows = pl.ds(pl.multiple_of(block * size, size), size)
            part = src_ref[place * size : (place + 1) * size, :].astype(F32)
            up_ref[rows, :] = part[:, :units]
            full_ref[rows, :] = part[:, units:]
        down_ref[...] = full_ref[...].T

    @pl.when(pl.program_id(0) == 0)
    def _():
        lay(keep_ref, core)

    @pl.when(pl.program_id(0) == 1)
    def _():
        lay(other_ref, core ^ 1)


def ffn_end(info, tables, keep, other):
    width, double = keep.shape
    units = double // 2
    return call(
        functools.partial(ffn_end_kernel, tables),
        "ffn_end",
        (2,),
        [whole(width, double)] * 2,
        [
            pl.BlockSpec((width, units), lambda i, info: (0, info[0] ^ i)),
            pl.BlockSpec((units, width), lambda i, info: (info[0] ^ i, 0)),
        ],
        [jax.ShapeDtypeStruct((width, double), F32), jax.ShapeDtypeStruct((double, width), F32)],
        [pltpu.VMEM((width, units), F32)],
        info,
        (keep, other),
    )


def attend_end_kernel(tables, info_ref, keep_ref, other_ref, qkv_ref, out_ref):
    core, own = info_ref[0], info_ref[2]
    width = out_ref.shape[1]
    blocks = len(tables[0])
    size = out_ref.shape[0] // blocks
    half = out_ref.shape[0] // 2
    for place in range(blocks):
        src = keep_ref if place * size < half else other_ref
        at = place * size % half
        block = block_at(place, tables, core, own)
        rows = pl.ds(pl.multiple_of(block * size, size), size)
        part = src[at : at + size, :].astype(F32)
        qkv_ref[rows, :] = part[:, : 3 * width]
        out_ref[rows, :] = part[:, 3 * width :]


def attend_end(info, tables, keep, other):
    rows, width = 2 * keep.shape[0], keep.shape[1] // 4
    return call(
        functools.partial(attend_end_kernel, tables),
        "attend_end",
        (1,),
        [whole(*keep.shape)] * 2,
        [whole(rows, 3 * width), whole(rows, width)],
        [jax.ShapeDtypeStruct((rows, 3 * width), F32), jax.ShapeDtypeStruct((rows, width), F32)],
        [],
        info,
        (keep, other),
    )


def local(
    wide, narrow, tokens_in, ln1_gain, ln1_bias, w_qkv, w_out, ln2_gain, ln2_bias, w_up, b_up, w_down, b_down, segment_ids,
    step_ids, pad_mask, cotangent,
):
    width = tokens_in.shape[1]
    units = w_up.shape[1] // 2
    core_mask = narrow
    narrow_masks = [1 << b for b in range(narrow.bit_length() - 1)]
    wide_masks = [narrow << b for b in range(1, wide.bit_length() - 1)]

    def swap(value, first, second=None):
        masks = (first, first if second is None else second)
        pairs = [(i, i ^ masks[i // narrow & 1]) for i in range(wide * narrow)]
        return lax.ppermute(value, AXES, pairs)

    def add(a, b):
        return (a.astype(F32) + b.astype(F32)).astype(a.dtype)

    def orders(masks):
        if len(masks) < 2:
            return (masks, masks)
        return (masks, [masks[1], masks[0]] + masks[2:])

    def scatter(value, order):
        for first, second in zip(*order):
            half = value.shape[0] // 2
            value = add(value[:half], swap(value[half:], first, second))
        return value

    def gather(value, order):
        for first, second in reversed(list(zip(*order))):
            value = jnp.concatenate([value, swap(value, first, second)], axis=0)
        return value

    wide_at, narrow_at = lax.axis_index("wide"), lax.axis_index("narrow")
    core = wide_at & 1
    flat = wide_at * narrow + narrow_at

    ff_order = orders(wide_masks)
    ff_tables = tuple([owner // (2 * narrow) for owner in places(o, wide // 2)] for o in ff_order)
    masks = narrow_masks + wide_masks
    split = min(len(masks), (width // TILE).bit_length() - 2)
    at_order = orders(masks[:split])
    at_rest = masks[split:]
    blocks = 1 << split
    near = [places(o, blocks) for o in at_order]
    used = [core_mask] + masks[:split]

    def named(owner):
        return sum((1 << b) for b, m in enumerate(used) if owner & m)

    at_tables = tuple(
        [named(o) for o in near[c]] + [named(o ^ core_mask) for o in near[1 - c]] for c in range(2)
    )
    own_block = sum((flat // m & 1) << b for b, m in enumerate(used))
    info = jnp.stack([core, wide_at // 2, own_block]).astype(jnp.int32)

    up_chunk = lax.dynamic_slice(w_up, (0, core * units), (width, units))
    bias_chunk = lax.dynamic_slice(b_up, (core * units,), (units,))
    up_chunk = jnp.concatenate([up_chunk, jnp.broadcast_to(bias_chunk[None], (TILE, units))], axis=0)
    down_chunk = lax.dynamic_slice(w_down, (core * units, 0), (units, width))
    fetched = [(up_chunk, down_chunk)]
    for mask in narrow_masks:
        fetched = fetched + [(swap(u, mask), swap(d, mask)) for u, d in fetched]
    chunks = []
    for up, down in fetched[1:]:
        chunks += [(up, down), (swap(up, core_mask), swap(down, core_mask))]

    row = lambda v: v[None].astype(F32)
    qkv, prob, mixed, residual, second = attend(
        info, tokens_in, row(ln1_gain), row(ln1_bias), w_qkv, w_out, row(ln2_gain), row(ln2_bias), segment_ids, step_ids, pad_mask
    )
    out_part, dsec_part, own_keep, own_send, bown_keep, bown_send = ffn_own(
        info, ff_tables, second, cotangent, w_up, b_up[None], w_down
    )
    rest = ffn_rest(
        info, ff_tables, second, cotangent, out_part, dsec_part, residual, mixed, row(b_down), row(ln2_gain), w_out, chunks
    )
    block_out, gres, gmix, vec, dwout = rest[:5]
    count = len(chunks)
    grads, bgrads = rest[5 : 5 + count], rest[5 + count :]

    held = [add(own_keep, swap(own_send, core_mask))]
    held += [add(grads[2 * j], swap(grads[2 * j + 1], core_mask)) for j in range(narrow - 1)]
    for mask in reversed(narrow_masks):
        held = [add(held[j], swap(held[j + mask], mask)) for j in range(mask)]
    ff_keep = gather(scatter(held[0], ff_order), ff_order)
    ff_other = swap(ff_keep, core_mask)
    grad_w_up, grad_w_down = ffn_end(info, ff_tables, ff_keep, ff_other)

    dqkv, keep, send = attend_back(
        info, at_tables, qkv, prob, gmix, tokens_in, row(ln1_gain), row(ln1_bias), dwout
    )
    keep = scatter(add(keep, swap(send, core_mask)), at_order)
    for mask in at_rest:
        keep = add(keep, swap(keep, mask))
    keep = gather(keep, at_order)
    grad_w_qkv, grad_w_out = attend_end(info, at_tables, keep, swap(keep, core_mask))

    grad_tokens, vec = first_back(info, dqkv, w_qkv, tokens_in, gres, row(ln1_gain), vec)

    b_parts = [(0, bown_keep, bown_send)] + [(j, bgrads[2 * j - 2], bgrads[2 * j - 1]) for j in range(1, narrow)]
    b_all = jnp.zeros((narrow, 2, units), F32)
    for j, mine, other in b_parts:
        both = jnp.where(core == 0, jnp.concatenate([mine, other], 0), jnp.concatenate([other, mine], 0))
        b_all = lax.dynamic_update_slice(b_all, both[None], (narrow_at ^ j, 0, 0))
    vec = jnp.concatenate([vec, b_all.reshape(-1, width)], axis=0)
    for mask in [core_mask] + masks:
        vec = vec + swap(vec, mask)
    b_sum = vec[8:].reshape(narrow, 2 * units)
    grad_b_up = lax.dynamic_slice(b_sum, (narrow_at, 0), (1, 2 * units))[0]
    return (
        block_out,
        grad_tokens,
        vec[3],
        vec[4],
        grad_w_qkv,
        grad_w_out,
        vec[0],
        vec[1],
        grad_w_up,
        grad_b_up,
        grad_w_down,
        vec[2],
    )


def solution(mesh):
    rows = P(("wide", "narrow"), None)
    in_specs = (
        rows, P(), P(), P(), P(), P(), P(), P(None, "narrow"), P("narrow"), P("narrow", None), P(), rows, rows, rows, rows,
    )
    out_specs = (
        rows, rows, P(), P(), P(), P(), P(), P(), P(None, "narrow"), P("narrow"), P("narrow", None), P(),
    )
    wide, narrow = mesh.shape["wide"], mesh.shape["narrow"]
    return jax.shard_map(
        functools.partial(local, wide, narrow), mesh=mesh, in_specs=in_specs, out_specs=out_specs, check_vma=False
    )
```

```python
import functools

import jax
import jax.numpy as jnp
import numpy as np
from jax import lax
from jax.experimental import pallas as pl
from jax.experimental.pallas import tpu as pltpu
from jax.sharding import PartitionSpec as P

HEAD = 64
PAIR = 2 * HEAD
NORM_EPS = 1e-05
BF = jnp.bfloat16
F32 = jnp.float32
AXES = ("wide", "narrow")
LANES = 128
SUMS = 8
TILE = 16
TOKS = 256
VMEM_LIMIT = 50 * 1024 * 1024


def mm(a, b):
    return lax.dot_general(a, b, (((1,), (0,)), ((), ())), preferred_element_type=F32)


def mm_nt(a, b):
    return lax.dot_general(a, b, (((1,), (1,)), ((), ())), preferred_element_type=F32)


def mm_tn(a, b):
    return lax.dot_general(a, b, (((0,), (0,)), ((), ())), preferred_element_type=F32)


def whole(*shape):
    return pl.BlockSpec(shape, lambda *_: (0,) * len(shape))


def rows_of(width, toks=TOKS):
    return pl.BlockSpec((toks, width), lambda i, *_: (i, 0))


def call(kernel, name, grid, in_specs, out_specs, out_shape, scratch, info, args):
    return pl.pallas_call(
        kernel,
        grid_spec=pltpu.PrefetchScalarGridSpec(
            num_scalar_prefetch=1, grid=grid, in_specs=in_specs, out_specs=out_specs, scratch_shapes=scratch
        ),
        out_shape=out_shape,
        compiler_params=pltpu.CompilerParams(vmem_limit_bytes=VMEM_LIMIT),
        cost_estimate=pl.CostEstimate(flops=1000, bytes_accessed=1000, transcendentals=0),
        name=name,
    )(info, *args)


def unit_parts(rows):
    mean = jnp.mean(rows, axis=-1, keepdims=True)
    centered = rows - mean
    inv = lax.rsqrt(jnp.mean(centered * centered, axis=-1, keepdims=True) + NORM_EPS)
    return centered * inv, inv


def norm_back(incoming, unit, inv, gain):
    scaled = incoming * gain
    return inv * (
        scaled
        - jnp.mean(scaled, axis=-1, keepdims=True)
        - unit * jnp.mean(scaled * unit, axis=-1, keepdims=True)
    )


def gelu_pair(x):
    cdf = 0.5 * (1.0 + lax.erf(x * 0.7071067811865476))
    return x * cdf, cdf + x * jnp.exp(-0.5 * x * x) * 0.3989422804014327


def by_head(block):
    lane = lax.broadcasted_iota(jnp.int32, block.shape, 1)
    zero = jnp.zeros_like(block)
    first = lane < HEAD
    return jnp.concatenate([jnp.where(first, block, zero), jnp.where(first, zero, block)], axis=0)


def places(order, blocks):
    bits = blocks.bit_length() - 1
    table = []
    for place in range(blocks):
        owner = 0
        for step in range(bits):
            if place >> (bits - 1 - step) & 1:
                owner ^= order[step]
        table.append(owner)
    return table


def block_at(place, tables, core, own):
    first, second = tables[0][place], tables[1][place]
    if first == second:
        return own ^ first
    return own ^ jnp.where(core == 0, first, second)


def permuted(dst_ref, acc_ref, tables, core, own):
    blocks = len(tables[0])
    size = acc_ref.shape[0] // blocks
    for place in range(blocks):
        block = block_at(place, tables, core, own)
        rows = pl.ds(pl.multiple_of(block * size, size), size)
        dst_ref[place * size : (place + 1) * size, :] = acc_ref[rows, :].astype(dst_ref.dtype)


def attend_kernel(
    info_ref, tok_ref, g1_ref, c1_ref, wqkv_ref, wout_ref, g2_ref, c2_ref, seg_ref, step_ref, pad_ref,
    qkv_ref, prob_ref, mixed_ref, res_ref, second_ref,
):
    slots = seg_ref.shape[1]
    toks, width = tok_ref.shape
    rows = toks // slots
    at = pl.program_id(0)
    tokens = tok_ref[...].astype(F32)
    unit, _ = unit_parts(tokens)
    normed = (unit * g1_ref[...] + c1_ref[...]).astype(BF)
    qkv_ref[...] = mm(normed, wqkv_ref[...]).astype(BF)
    q_id = lax.broadcasted_iota(jnp.int32, (slots, slots), 0)
    k_id = lax.broadcasted_iota(jnp.int32, (slots, slots), 1)
    eye = q_id == k_id
    for r in range(rows):
        here = pl.ds(at * rows + r, 1)
        seg = jnp.broadcast_to(seg_ref[here, :].astype(F32), (slots, slots))
        step = jnp.broadcast_to(step_ref[here, :].astype(F32), (slots, slots))
        live = jnp.broadcast_to(pad_ref[here, :], (slots, slots)) == 0
        visible = ((seg == seg.T) & (step <= step.T) & live) | eye
        span = slice(r * slots, (r + 1) * slots)
        for p in range(width // PAIR):
            cols = slice(p * PAIR, (p + 1) * PAIR)
            q = qkv_ref[span, p * PAIR : (p + 1) * PAIR]
            k = qkv_ref[span, width + p * PAIR : width + (p + 1) * PAIR]
            v = qkv_ref[span, 2 * width + p * PAIR : 2 * width + (p + 1) * PAIR]
            scores = mm_nt(q, by_head(k * HEAD ** (-0.5)))
            halves = []
            for half in (scores[:, :slots], scores[:, slots:]):
                half = jnp.where(visible, half, -1e30)
                weight = jnp.exp(half - jnp.max(half, axis=-1, keepdims=True))
                total = jnp.sum(weight, axis=-1, keepdims=True)
                halves.append((weight * (1.0 / total)).astype(BF))
            prob = jnp.concatenate(halves, axis=1)
            prob_ref[r, p] = prob
            mixed_ref[span, cols] = mm(prob, by_head(v)).astype(BF)
    residual = tokens + mm(mixed_ref[...], wout_ref[...])
    res_ref[...] = residual
    unit, _ = unit_parts(residual)
    second_ref[...] = (unit * g2_ref[...] + c2_ref[...]).astype(BF)


def attend(info, tokens, g1, c1, wqkv, wout, g2, c2, seg, step, pad):
    n, width = tokens.shape
    rows, slots = seg.shape
    per, pairs = TOKS // slots, width // PAIR
    return call(
        attend_kernel,
        "attend",
        (n // TOKS,),
        [rows_of(width), whole(1, width), whole(1, width), whole(*wqkv.shape), whole(*wout.shape)]
        + [whole(1, width)] * 2
        + [whole(rows, slots)] * 3,
        [
            rows_of(3 * width),
            pl.BlockSpec((per, pairs, slots, 2 * slots), lambda i, *_: (i, 0, 0, 0)),
            rows_of(width),
            rows_of(width),
            rows_of(width),
        ],
        [
            jax.ShapeDtypeStruct((n, 3 * width), BF),
            jax.ShapeDtypeStruct((rows, pairs, slots, 2 * slots), BF),
            jax.ShapeDtypeStruct((n, width), BF),
            jax.ShapeDtypeStruct((n, width), F32),
            jax.ShapeDtypeStruct((n, width), BF),
        ],
        [],
        info,
        (tokens, g1, c1, wqkv, wout, g2, c2, seg, step, pad),
    )


def ffn_block(sec, sec_t, dy, dy_t, up, bias, down, acc_ref, bacc_ref, out, dsec):
    units = up.shape[1]
    pre = mm(sec, up) + bias
    hid, slope = gelu_pair(pre)
    hid = hid.astype(BF)
    dpre = (mm_nt(dy, down) * slope).astype(BF)
    acc_ref[:, :units] += mm(sec_t, dpre)
    acc_ref[:, units:] += mm(dy_t, hid)
    bacc_ref[...] += jnp.sum(dpre.astype(F32), axis=0, keepdims=True)
    o = mm(hid, down)
    d = mm_nt(dpre, up)
    return (o if out is None else out + o), (d if dsec is None else dsec + d)


def ffn_own_kernel(tables, info_ref, sec_ref, dy_ref, *refs):
    ups, biases, downs = refs[:2], refs[2:4], refs[4:6]
    out_ref, dsec_ref = refs[6:8]
    grads, bgrads, accs, baccs = refs[8:10], refs[10:12], refs[12:14], refs[14:16]
    at, last = pl.program_id(0), pl.num_programs(0) - 1

    @pl.when(at == 0)
    def _():
        for ref in accs + baccs:
            ref[...] = jnp.zeros_like(ref)

    sec, dy = sec_ref[...], dy_ref[...]
    sec_t, dy_t = sec.T, dy.T
    out = dsec = None
    for i in range(2):
        out, dsec = ffn_block(
            sec, sec_t, dy, dy_t, ups[i][...], biases[i][...].astype(F32), downs[i][...], accs[i], baccs[i], out, dsec
        )
    out_ref[...] = out
    dsec_ref[...] = dsec

    @pl.when(at == last)
    def _():
        core, own = info_ref[0], info_ref[1]
        for i in range(2):
            permuted(grads[i], accs[i], tables, core ^ i, own)
            bgrads[i][...] = baccs[i][...]


def ffn_own(info, tables, second, dy, up, bias, down):
    n, width = second.shape
    units = up.shape[1] // 2
    chunk = lambda i: (lambda t, info: (0, info[0] ^ i))
    return call(
        functools.partial(ffn_own_kernel, tables),
        "ffn_own",
        (n // TOKS,),
        [rows_of(width), rows_of(width)]
        + [pl.BlockSpec((width, units), chunk(i)) for i in range(2)]
        + [pl.BlockSpec((1, units), chunk(i)) for i in range(2)]
        + [pl.BlockSpec((units, width), lambda t, info, i=i: (info[0] ^ i, 0)) for i in range(2)],
        [rows_of(width)] * 2 + [whole(width, 2 * units)] * 2 + [whole(1, units)] * 2,
        [jax.ShapeDtypeStruct((n, width), F32)] * 2
        + [jax.ShapeDtypeStruct((width, 2 * units), BF)] * 2
        + [jax.ShapeDtypeStruct((1, units), F32)] * 2,
        [pltpu.VMEM((width, 2 * units), F32)] * 2 + [pltpu.VMEM((1, units), F32)] * 2,
        info,
        (second, dy, up, up, bias, bias, down, down),
    )


def ffn_rest_kernel(
    tables, count, info_ref, sec_ref, dy_ref, out_part_ref, dsec_part_ref, res_ref, mixed_ref, bdown_ref, g2_ref, wout_ref, *refs
):
    ups, downs = refs[:count], refs[count : 2 * count]
    block_ref, gres_ref, gmix_ref, vec_ref, dwout_ref = refs[2 * count : 2 * count + 5]
    rest = refs[2 * count + 5 :]
    grads, bgrads = rest[:count], rest[count : 2 * count]
    accs, baccs = rest[2 * count : 3 * count], rest[3 * count : 4 * count]
    wacc_ref = rest[4 * count]
    at, last = pl.program_id(0), pl.num_programs(0) - 1
    width = sec_ref.shape[1]

    @pl.when(at == 0)
    def _():
        for ref in accs + baccs + (wacc_ref, vec_ref):
            ref[...] = jnp.zeros_like(ref)

    sec, dy = sec_ref[...], dy_ref[...]
    sec_t, dy_t = sec.T, dy.T
    out, dsec = out_part_ref[...], dsec_part_ref[...]
    for i in range(count):
        bias = ups[i][width : width + TILE, :].astype(F32)[:1]
        out, dsec = ffn_block(sec, sec_t, dy, dy_t, ups[i][:width, :], bias, downs[i][...], accs[i], baccs[i], out, dsec)
    residual = res_ref[...]
    block_ref[...] = (residual + (out + bdown_ref[...])).astype(BF)
    dy32 = dy.astype(F32)
    unit, inv = unit_parts(residual)
    vec_ref[0:1, :] += jnp.sum(dsec * unit, axis=0, keepdims=True)
    vec_ref[1:2, :] += jnp.sum(dsec, axis=0, keepdims=True)
    vec_ref[2:3, :] += jnp.sum(dy32, axis=0, keepdims=True)
    gres = dy32 + norm_back(dsec, unit, inv, g2_ref[...])
    gres_ref[...] = gres
    branch = gres.astype(BF)
    gmix_ref[...] = mm_nt(branch, wout_ref[...]).astype(BF)
    wacc_ref[...] += mm_tn(mixed_ref[...], branch)

    @pl.when(at == last)
    def _():
        core, own = info_ref[0], info_ref[1]
        for i in range(count):
            permuted(grads[i], accs[i], tables, core ^ (i % 2), own)
            bgrads[i][...] = baccs[i][...]
        dwout_ref[...] = wacc_ref[...]


def ffn_rest(info, tables, second, dy, out_part, dsec_part, residual, mixed, bdown, g2, wout, chunks):
    n, width = second.shape
    count = len(chunks)
    units = chunks[0][0].shape[1]
    return call(
        functools.partial(ffn_rest_kernel, tables, count),
        "ffn_rest",
        (n // TOKS,),
        [rows_of(width)] * 6
        + [whole(1, width)] * 2
        + [whole(width, width)]
        + [whole(width + TILE, units)] * count
        + [whole(units, width)] * count,
        [rows_of(width)] * 3
        + [whole(8, width), whole(width, width)]
        + [whole(width, 2 * units)] * count
        + [whole(1, units)] * count,
        [
            jax.ShapeDtypeStruct((n, width), BF),
            jax.ShapeDtypeStruct((n, width), F32),
            jax.ShapeDtypeStruct((n, width), BF),
            jax.ShapeDtypeStruct((8, width), F32),
            jax.ShapeDtypeStruct((width, width), F32),
        ]
        + [jax.ShapeDtypeStruct((width, 2 * units), BF)] * count
        + [jax.ShapeDtypeStruct((1, units), F32)] * count,
        [pltpu.VMEM((width, 2 * units), F32)] * count
        + [pltpu.VMEM((1, units), F32)] * count
        + [pltpu.VMEM((width, width), F32)],
        info,
        (second, dy, out_part, dsec_part, residual, mixed, bdown, g2, wout)
        + tuple(c[0] for c in chunks)
        + tuple(c[1] for c in chunks),
    )


def attend_back_kernel(
    tables, info_ref, qkv_ref, prob_ref, gmix_ref, tok_ref, vec_ref, dwout_ref, grad_ref, dw_keep_ref, dw_send_ref,
    dqkv_ref, acc_ref, row_ref,
):
    at, last = pl.program_id(0), pl.num_programs(0) - 1
    toks, width = tok_ref.shape
    rows, pairs, slots, _ = prob_ref.shape

    @pl.when(at == 0)
    def _():
        acc_ref[:, : 3 * width] = jnp.zeros((width, 3 * width), F32)
        acc_ref[:, 3 * width : 4 * width] = dwout_ref[...]
        row_ref[...] = jnp.zeros_like(row_ref)
        row_ref[SUMS : SUMS + vec_ref.shape[0], :] = vec_ref[...]

    scale = HEAD ** (-0.5)
    for r in range(rows):
        span = slice(r * slots, (r + 1) * slots)
        for p in range(pairs):
            cols = slice(p * PAIR, (p + 1) * PAIR)
            kcols = slice(width + p * PAIR, width + (p + 1) * PAIR)
            vcols = slice(2 * width + p * PAIR, 2 * width + (p + 1) * PAIR)
            q = qkv_ref[span, cols]
            k = qkv_ref[span, kcols]
            v = qkv_ref[span, vcols]
            g = gmix_ref[span, cols]
            prob = prob_ref[r, p]
            dprob = mm_nt(g, by_head(v))
            p32 = prob.astype(F32)
            prod = p32 * dprob
            first = jnp.sum(prod[:, :slots], axis=-1, keepdims=True)
            second = jnp.sum(prod[:, slots:], axis=-1, keepdims=True)
            ds_a = (p32[:, :slots] * (dprob[:, :slots] - first)).astype(BF)
            ds_b = (p32[:, slots:] * (dprob[:, slots:] - second)).astype(BF)
            dqkv_ref[span, cols] = mm(jnp.concatenate([ds_a, ds_b], axis=1), by_head(k * scale)).astype(BF)
            dqkv_ref[span, kcols] = mm_tn(jnp.concatenate([ds_a, ds_b], axis=0), by_head(q * scale)).astype(BF)
            dqkv_ref[span, vcols] = mm_tn(
                jnp.concatenate([prob[:, :slots], prob[:, slots:]], axis=0), by_head(g)
            ).astype(BF)
    unit, _ = unit_parts(tok_ref[...].astype(F32))
    acc_ref[:, : 3 * width] += mm_tn(unit.astype(BF), dqkv_ref[...])
    grad_ref[...] = dqkv_ref[...]
    for i in range(3):
        part = dqkv_ref[:, i * width : (i + 1) * width].astype(F32)
        row_ref[i : i + 1, :] += jnp.sum(part, axis=0, keepdims=True)

    @pl.when(at == last)
    def _():
        core, own = info_ref[0], info_ref[2]
        acc_ref[:, 4 * width :] = row_ref[...].T
        half = width // 2
        size = width // len(tables[0])
        for place in range(len(tables[0])):
            dst = dw_keep_ref if place * size < half else dw_send_ref
            block = block_at(place, tables, core, own)
            rows_at = pl.ds(pl.multiple_of(block * size, size), size)
            to = place * size % half
            dst[to : to + size, :] = acc_ref[rows_at, :].astype(BF)


def attend_back(info, tables, qkv, prob, gmix, tokens, vec, dwout):
    n, width = tokens.shape
    rows, pairs, slots, _ = prob.shape
    per = TOKS // slots
    return call(
        functools.partial(attend_back_kernel, tables),
        "attend_back",
        (n // TOKS,),
        [
            rows_of(3 * width),
            pl.BlockSpec((per, pairs, slots, 2 * slots), lambda i, *_: (i, 0, 0, 0)),
            rows_of(width),
            rows_of(width),
            whole(*vec.shape),
            whole(width, width),
        ],
        [rows_of(3 * width)] + [whole(width // 2, 4 * width + LANES)] * 2,
        [jax.ShapeDtypeStruct((n, 3 * width), BF)] + [jax.ShapeDtypeStruct((width // 2, 4 * width + LANES), BF)] * 2,
        [
            pltpu.VMEM((TOKS, 3 * width), BF),
            pltpu.VMEM((width, 4 * width + LANES), F32),
            pltpu.VMEM((LANES, width), F32),
        ],
        info,
        (qkv, prob, gmix, tokens, vec, dwout),
    )


def first_back_kernel(info_ref, dqkv_ref, wqkv_ref, tok_ref, gres_ref, g1_ref, out_ref):
    dnormed = mm_nt(dqkv_ref[...], wqkv_ref[...])
    unit, inv = unit_parts(tok_ref[...].astype(F32))
    out_ref[...] = gres_ref[...] + norm_back(dnormed, unit, inv, g1_ref[...])


def first_back(info, dqkv, wqkv, tokens, gres, g1):
    n, width = tokens.shape
    return call(
        first_back_kernel,
        "first_back",
        (n // TOKS,),
        [rows_of(3 * width), whole(*wqkv.shape), rows_of(width), rows_of(width), whole(1, width)],
        rows_of(width),
        jax.ShapeDtypeStruct((n, width), F32),
        [],
        info,
        (dqkv, wqkv, tokens, gres, g1),
    )


def ffn_end_kernel(tables, info_ref, keep_ref, other_ref, up_ref, down_ref, full_ref):
    core, own = info_ref[0], info_ref[1]
    units = up_ref.shape[1]
    blocks = len(tables[0])
    size = keep_ref.shape[0] // blocks

    def lay(src_ref, whose):
        for place in range(blocks):
            block = block_at(place, tables, whose, own)
            rows = pl.ds(pl.multiple_of(block * size, size), size)
            part = src_ref[place * size : (place + 1) * size, :].astype(F32)
            up_ref[rows, :] = part[:, :units]
            full_ref[rows, :] = part[:, units:]
        down_ref[...] = full_ref[...].T

    @pl.when(pl.program_id(0) == 0)
    def _():
        lay(keep_ref, core)

    @pl.when(pl.program_id(0) == 1)
    def _():
        lay(other_ref, core ^ 1)


def ffn_end(info, tables, keep, other):
    width, double = keep.shape
    units = double // 2
    return call(
        functools.partial(ffn_end_kernel, tables),
        "ffn_end",
        (2,),
        [whole(width, double)] * 2,
        [
            pl.BlockSpec((width, units), lambda i, info: (0, info[0] ^ i)),
            pl.BlockSpec((units, width), lambda i, info: (info[0] ^ i, 0)),
        ],
        [jax.ShapeDtypeStruct((width, double), F32), jax.ShapeDtypeStruct((double, width), F32)],
        [pltpu.VMEM((width, units), F32)],
        info,
        (keep, other),
    )


def attend_end_kernel(tables, info_ref, keep_ref, other_ref, w_ref, g1_ref, c1_ref, qkv_ref, out_ref, vec_ref, sum_ref, col_ref):
    core, own = info_ref[0], info_ref[2]
    width = out_ref.shape[1]
    blocks = len(tables[0])
    size = out_ref.shape[0] // blocks
    half = out_ref.shape[0] // 2
    for place in range(blocks):
        src = keep_ref if place * size < half else other_ref
        at = place * size % half
        block = block_at(place, tables, core, own)
        rows = pl.ds(pl.multiple_of(block * size, size), size)
        part = src[at : at + size, :].astype(F32)
        sum_ref[rows, :] = part[:, : 3 * width]
        out_ref[rows, :] = part[:, 3 * width : 4 * width]
        col_ref[rows, :] = part[:, 4 * width :]
    vec = col_ref[...].T
    wide_row = jnp.concatenate([vec[i : i + 1, :] for i in range(3)], axis=1)
    pair = jnp.concatenate([g1_ref[...], c1_ref[...], jnp.zeros((LANES - 2, width), F32)], axis=0).T
    gain, bias = pair[:, 0:1], pair[:, 1:2]
    w = w_ref[...].astype(F32)
    sums = sum_ref[...]
    qkv_ref[...] = gain * sums + bias * wide_row
    lane = lax.broadcasted_iota(jnp.int32, (width, LANES), 1)
    d_gain = jnp.sum(w * sums, axis=1, keepdims=True)
    d_bias = jnp.sum(w * wide_row, axis=1, keepdims=True)
    both = jnp.where(lane == 0, d_gain, jnp.where(lane == 1, d_bias, 0.0)).T
    vec_ref[...] = vec[: vec_ref.shape[0], :]
    vec_ref[0:2, :] = both[0:2, :]


def attend_end(info, tables, keep, other, w_qkv, g1, c1, count):
    rows, width = 2 * keep.shape[0], w_qkv.shape[0]
    return call(
        functools.partial(attend_end_kernel, tables),
        "attend_end",
        (1,),
        [whole(*keep.shape)] * 2 + [whole(*w_qkv.shape)] + [whole(1, width)] * 2,
        [whole(rows, 3 * width), whole(rows, width), whole(count, width)],
        [
            jax.ShapeDtypeStruct((rows, 3 * width), F32),
            jax.ShapeDtypeStruct((rows, width), F32),
            jax.ShapeDtypeStruct((count, width), F32),
        ],
        [pltpu.VMEM((rows, 3 * width), F32), pltpu.VMEM((rows, LANES), F32)],
        info,
        (keep, other, w_qkv, g1, c1),
    )


def local(
    wide, narrow, tokens_in, ln1_gain, ln1_bias, w_qkv, w_out, ln2_gain, ln2_bias, w_up, b_up, w_down, b_down, segment_ids,
    step_ids, pad_mask, cotangent,
):
    width = tokens_in.shape[1]
    units = w_up.shape[1] // 2
    core_mask = narrow
    narrow_masks = [1 << b for b in range(narrow.bit_length() - 1)]
    wide_masks = [narrow << b for b in range(1, wide.bit_length() - 1)]

    def swap(value, first, second=None):
        masks = (first, first if second is None else second)
        pairs = [(i, i ^ masks[i // narrow & 1]) for i in range(wide * narrow)]
        return lax.ppermute(value, AXES, pairs)

    def add(a, b):
        return (a.astype(F32) + b.astype(F32)).astype(a.dtype)

    def orders(masks):
        if len(masks) < 2:
            return (masks, masks)
        return (masks, [masks[1], masks[0]] + masks[2:])

    def after(*values):
        return lax.optimization_barrier(values)

    def scatter(value, order, beside=None):
        for step, (first, second) in enumerate(zip(*order)):
            half = value.shape[0] // 2
            value = add(value[:half], swap(value[half:], first, second))
            if beside is not None and step == 0:
                value, beside = after(value, beside)
        return value if beside is None else (value, beside)

    def gather(value, order):
        for first, second in reversed(list(zip(*order))):
            value = jnp.concatenate([value, swap(value, first, second)], axis=0)
        return value

    wide_at, narrow_at = lax.axis_index("wide"), lax.axis_index("narrow")
    core = wide_at & 1
    flat = wide_at * narrow + narrow_at

    ff_order = orders(wide_masks)
    ff_tables = tuple([owner // (2 * narrow) for owner in places(o, wide // 2)] for o in ff_order)
    masks = narrow_masks + wide_masks
    split = min(len(masks), (width // TILE).bit_length() - 2)
    at_order = orders(masks[:split])
    at_rest = masks[split:]
    blocks = 1 << split
    near = [places(o, blocks) for o in at_order]
    used = [core_mask] + masks[:split]

    def named(owner):
        return sum((1 << b) for b, m in enumerate(used) if owner & m)

    at_tables = tuple(
        [named(o) for o in near[c]] + [named(o ^ core_mask) for o in near[1 - c]] for c in range(2)
    )
    own_block = sum((flat // m & 1) << b for b, m in enumerate(used))
    info = jnp.stack([core, wide_at // 2, own_block]).astype(jnp.int32)

    up_chunk = lax.dynamic_slice(w_up, (0, core * units), (width, units))
    bias_chunk = lax.dynamic_slice(b_up, (core * units,), (units,))
    up_chunk = jnp.concatenate([up_chunk, jnp.broadcast_to(bias_chunk[None], (TILE, units))], axis=0)
    down_chunk = lax.dynamic_slice(w_down, (core * units, 0), (units, width))
    fetched = [(up_chunk, down_chunk)]
    for mask in narrow_masks:
        fetched = fetched + [(swap(u, mask), swap(d, mask)) for u, d in fetched]

    row = lambda v: v[None].astype(F32)
    g1, c1, g2 = row(ln1_gain), row(ln1_bias), row(ln2_gain)
    qkv, prob, mixed, residual, second = attend(
        info, tokens_in, g1, c1, w_qkv, w_out, g2, row(ln2_bias), segment_ids, step_ids, pad_mask
    )
    second, fetched = after(second, fetched)
    chunks = []
    for up, down in fetched[1:]:
        chunks += [(up, down), (swap(up, core_mask), swap(down, core_mask))]
    out_part, dsec_part, own_keep, own_send, bown_keep, bown_send = ffn_own(
        info, ff_tables, second, cotangent, w_up, b_up[None], w_down
    )
    rest = ffn_rest(
        info, ff_tables, second, cotangent, out_part, dsec_part, residual, mixed, row(b_down), g2, w_out, chunks
    )
    block_out, gres, gmix, vec, dwout = rest[:5]
    count = len(chunks)
    grads, bgrads = rest[5 : 5 + count], rest[5 + count :]

    b_all = jnp.concatenate([bown_keep, bown_send, *bgrads], axis=0)
    for bit in range(narrow.bit_length()):
        flipped = jnp.flip(b_all.reshape(-1, 2, 1 << bit, units), axis=1).reshape(b_all.shape)
        b_all = jnp.where((narrow_at * 2 + core) >> bit & 1, flipped, b_all)
    vec = jnp.concatenate([vec, b_all.reshape(-1, width)], axis=0)

    held = [add(own_keep, swap(own_send, core_mask))]
    held += [add(grads[2 * j], swap(grads[2 * j + 1], core_mask)) for j in range(narrow - 1)]
    gmix, held = after(gmix, held)
    for mask in reversed(narrow_masks):
        held = [add(held[j], swap(held[j + mask], mask)) for j in range(mask)]

    dqkv, keep, send = attend_back(info, at_tables, qkv, prob, gmix, tokens_in, vec, dwout)
    keep = add(keep, swap(send, core_mask))
    keep, held = after(keep, held)
    grad_tokens = first_back(info, dqkv, w_qkv, tokens_in, gres, g1)
    ff_keep = gather(scatter(held[0], ff_order), ff_order)
    ff_other = swap(ff_keep, core_mask)
    grad_w_up, grad_w_down = ffn_end(info, ff_tables, ff_keep, ff_other)

    keep, grad_tokens = scatter(keep, at_order, grad_tokens)
    for mask in at_rest:
        keep = add(keep, swap(keep, mask))
    keep = gather(keep, at_order)
    grad_w_qkv, grad_w_out, vec = attend_end(
        info, at_tables, keep, swap(keep, core_mask), w_qkv, g1, c1, SUMS + vec.shape[0]
    )
    b_sum = vec[SUMS + 8 :].reshape(narrow, 2 * units)
    grad_b_up = lax.dynamic_slice(b_sum, (narrow_at, 0), (1, 2 * units))[0]
    return (
        block_out,
        grad_tokens,
        vec[0],
        vec[1],
        grad_w_qkv,
        grad_w_out,
        vec[SUMS],
        vec[SUMS + 1],
        grad_w_up,
        grad_b_up,
        grad_w_down,
        vec[SUMS + 2],
    )


def solution(mesh):
    rows = P(("wide", "narrow"), None)
    in_specs = (
        rows, P(), P(), P(), P(), P(), P(), P(None, "narrow"), P("narrow"), P("narrow", None), P(), rows, rows, rows, rows,
    )
    out_specs = (
        rows, rows, P(), P(), P(), P(), P(), P(), P(None, "narrow"), P("narrow"), P("narrow", None), P(),
    )
    wide, narrow = mesh.shape["wide"], mesh.shape["narrow"]
    return jax.shard_map(
        functools.partial(local, wide, narrow), mesh=mesh, in_specs=in_specs, out_specs=out_specs, check_vma=False
    )
```

```python
import functools

import jax
import jax.numpy as jnp
import numpy as np
from jax import lax
from jax.experimental import pallas as pl
from jax.experimental.pallas import tpu as pltpu
from jax.sharding import PartitionSpec as P

HEAD = 64
PAIR = 2 * HEAD
NORM_EPS = 1e-05
BF = jnp.bfloat16
F32 = jnp.float32
AXES = ("wide", "narrow")
LANES = 128
SUMS = 8
TILE = 16
TOKS = 512
VMEM_LIMIT = 24 * 1024 * 1024


def mm(a, b):
    return lax.dot_general(a, b, (((1,), (0,)), ((), ())), preferred_element_type=F32)


def mm_nt(a, b):
    return lax.dot_general(a, b, (((1,), (1,)), ((), ())), preferred_element_type=F32)


def mm_tn(a, b):
    return lax.dot_general(a, b, (((0,), (0,)), ((), ())), preferred_element_type=F32)


def near(*values):
    return tuple(pltpu.with_memory_space_constraint(v, pltpu.VMEM) for v in values)


def far(*values):
    return tuple(pltpu.with_memory_space_constraint(v, pltpu.HBM) for v in values)


def whole(*shape):
    return pl.BlockSpec(shape, lambda *_: (0,) * len(shape))


def rows_of(width, toks=TOKS):
    return pl.BlockSpec((toks, width), lambda i, *_: (i, 0))


def call(kernel, name, grid, in_specs, out_specs, out_shape, scratch, info, args):
    return pl.pallas_call(
        kernel,
        grid_spec=pltpu.PrefetchScalarGridSpec(
            num_scalar_prefetch=1, grid=grid, in_specs=in_specs, out_specs=out_specs, scratch_shapes=scratch
        ),
        out_shape=out_shape,
        compiler_params=pltpu.CompilerParams(vmem_limit_bytes=VMEM_LIMIT),
        cost_estimate=pl.CostEstimate(flops=1000, bytes_accessed=1000, transcendentals=0),
        name=name,
    )(info, *args)


def unit_parts(rows):
    mean = jnp.mean(rows, axis=-1, keepdims=True)
    centered = rows - mean
    inv = lax.rsqrt(jnp.mean(centered * centered, axis=-1, keepdims=True) + NORM_EPS)
    return centered * inv, inv


def norm_back(incoming, unit, inv, gain):
    scaled = incoming * gain
    return inv * (
        scaled
        - jnp.mean(scaled, axis=-1, keepdims=True)
        - unit * jnp.mean(scaled * unit, axis=-1, keepdims=True)
    )


def gelu_pair(x):
    cdf = 0.5 * (1.0 + lax.erf(x * 0.7071067811865476))
    return x * cdf, cdf + x * jnp.exp(-0.5 * x * x) * 0.3989422804014327


def by_head(block):
    lane = lax.broadcasted_iota(jnp.int32, block.shape, 1)
    zero = jnp.zeros_like(block)
    first = lane < HEAD
    return jnp.concatenate([jnp.where(first, block, zero), jnp.where(first, zero, block)], axis=0)


def places(order, blocks):
    bits = blocks.bit_length() - 1
    table = []
    for place in range(blocks):
        owner = 0
        for step in range(bits):
            if place >> (bits - 1 - step) & 1:
                owner ^= order[step]
        table.append(owner)
    return table


def block_at(place, tables, core, own):
    first, second = tables[0][place], tables[1][place]
    if first == second:
        return own ^ first
    return own ^ jnp.where(core == 0, first, second)


def permuted(dst_ref, acc_ref, tables, core, own):
    blocks = len(tables[0])
    size = acc_ref.shape[0] // blocks
    for place in range(blocks):
        block = block_at(place, tables, core, own)
        rows = pl.ds(pl.multiple_of(block * size, size), size)
        dst_ref[place * size : (place + 1) * size, :] = acc_ref[rows, :].astype(dst_ref.dtype)


def attend_kernel(
    info_ref, tok_ref, g1_ref, c1_ref, wqkv_ref, wout_ref, g2_ref, c2_ref, seg_ref, step_ref, pad_ref,
    qkv_ref, prob_ref, mixed_ref, res_ref, second_ref,
):
    slots = seg_ref.shape[1]
    toks, width = tok_ref.shape
    rows = toks // slots
    at = pl.program_id(0)
    tokens = tok_ref[...].astype(F32)
    unit, _ = unit_parts(tokens)
    normed = (unit * g1_ref[...] + c1_ref[...]).astype(BF)
    qkv_ref[...] = mm(normed, wqkv_ref[...]).astype(BF)
    q_id = lax.broadcasted_iota(jnp.int32, (slots, slots), 0)
    k_id = lax.broadcasted_iota(jnp.int32, (slots, slots), 1)
    eye = q_id == k_id
    pairs = width // PAIR
    units = [(r, p) for r in range(rows) for p in range(pairs)]

    def part(r, p, which):
        return qkv_ref[r * slots : (r + 1) * slots, which * width + p * PAIR : which * width + (p + 1) * PAIR]

    masks = []
    for r in range(rows):
        here = pl.ds(at * rows + r, 1)
        seg = jnp.broadcast_to(seg_ref[here, :].astype(F32), (slots, slots))
        step = jnp.broadcast_to(step_ref[here, :].astype(F32), (slots, slots))
        live = jnp.broadcast_to(pad_ref[here, :], (slots, slots)) == 0
        masks.append(((seg == seg.T) & (step <= step.T) & live) | eye)
    scores = [mm_nt(part(r, p, 0), by_head(part(r, p, 1) * HEAD ** (-0.5))) for r, p in units]
    probs = []
    for (r, p), score in zip(units, scores):
        halves = []
        for half in (score[:, :slots], score[:, slots:]):
            half = jnp.where(masks[r], half, -1e30)
            weight = jnp.exp(half - jnp.max(half, axis=-1, keepdims=True))
            total = jnp.sum(weight, axis=-1, keepdims=True)
            halves.append((weight * (1.0 / total)).astype(BF))
        probs.append(jnp.concatenate(halves, axis=1))
    for (r, p), prob in zip(units, probs):
        prob_ref[r, p] = prob
        mixed_ref[r * slots : (r + 1) * slots, p * PAIR : (p + 1) * PAIR] = mm(prob, by_head(part(r, p, 2))).astype(BF)
    residual = tokens + mm(mixed_ref[...], wout_ref[...])
    res_ref[...] = residual
    unit, _ = unit_parts(residual)
    second_ref[...] = (unit * g2_ref[...] + c2_ref[...]).astype(BF)


def attend(info, tokens, g1, c1, wqkv, wout, g2, c2, seg, step, pad):
    n, width = tokens.shape
    rows, slots = seg.shape
    per, pairs = TOKS // slots, width // PAIR
    return call(
        attend_kernel,
        "attend",
        (n // TOKS,),
        [rows_of(width), whole(1, width), whole(1, width), whole(*wqkv.shape), whole(*wout.shape)]
        + [whole(1, width)] * 2
        + [whole(rows, slots)] * 3,
        [
            rows_of(3 * width),
            pl.BlockSpec((per, pairs, slots, 2 * slots), lambda i, *_: (i, 0, 0, 0)),
            rows_of(width),
            rows_of(width),
            rows_of(width),
        ],
        [
            pltpu.HBM((n, 3 * width), BF),
            pltpu.HBM((rows, pairs, slots, 2 * slots), BF),
            pltpu.HBM((n, width), BF),
            pltpu.HBM((n, width), F32),
            pltpu.VMEM((n, width), BF),
        ],
        [],
        info,
        far(tokens, g1, c1) + (wqkv, wout) + far(g2, c2, seg, step, pad),
    )


def ffn_block(sec, sec_t, dy, dy_t, up, bias, down, acc_ref, bacc_ref, out, dsec):
    units = up.shape[1]
    pre = mm(sec, up) + bias
    hid, slope = gelu_pair(pre)
    hid = hid.astype(BF)
    dpre = (mm_nt(dy, down) * slope).astype(BF)
    acc_ref[:, :units] += mm(sec_t, dpre)
    acc_ref[:, units:] += mm(dy_t, hid)
    bacc_ref[...] += jnp.sum(dpre.astype(F32), axis=0, keepdims=True)
    o = mm(hid, down)
    d = mm_nt(dpre, up)
    return (o if out is None else out + o), (d if dsec is None else dsec + d)


def ffn_own_kernel(tables, info_ref, sec_ref, dy_ref, *refs):
    ups, biases, downs = refs[:2], refs[2:4], refs[4:6]
    out_ref, dsec_ref = refs[6:8]
    grads, bgrads, accs, baccs = refs[8:10], refs[10:12], refs[12:14], refs[14:16]
    at, last = pl.program_id(0), pl.num_programs(0) - 1

    @pl.when(at == 0)
    def _():
        for ref in accs + baccs:
            ref[...] = jnp.zeros_like(ref)

    sec, dy = sec_ref[...], dy_ref[...]
    sec_t, dy_t = sec.T, dy.T
    out = dsec = None
    for i in range(2):
        out, dsec = ffn_block(
            sec, sec_t, dy, dy_t, ups[i][...], biases[i][...].astype(F32), downs[i][...], accs[i], baccs[i], out, dsec
        )
    out_ref[...] = out
    dsec_ref[...] = dsec

    @pl.when(at == last)
    def _():
        core, own = info_ref[0], info_ref[1]
        for i in range(2):
            permuted(grads[i], accs[i], tables, core ^ i, own)
            bgrads[i][...] = baccs[i][...]


def ffn_own(info, tables, second, dy, up, bias, down):
    n, width = second.shape
    units = up.shape[1] // 2
    chunk = lambda i: (lambda t, info: (0, info[0] ^ i))
    return call(
        functools.partial(ffn_own_kernel, tables),
        "ffn_own",
        (n // TOKS,),
        [rows_of(width), rows_of(width)]
        + [pl.BlockSpec((width, units), chunk(i)) for i in range(2)]
        + [pl.BlockSpec((1, units), chunk(i)) for i in range(2)]
        + [pl.BlockSpec((units, width), lambda t, info, i=i: (info[0] ^ i, 0)) for i in range(2)],
        [rows_of(width)] * 2 + [whole(width, 2 * units)] * 2 + [whole(1, units)] * 2,
        [pltpu.VMEM((n, width), F32)] * 2
        + [jax.ShapeDtypeStruct((width, 2 * units), BF)] * 2
        + [jax.ShapeDtypeStruct((1, units), F32)] * 2,
        [pltpu.VMEM((width, 2 * units), F32)] * 2 + [pltpu.VMEM((1, units), F32)] * 2,
        info,
        near(second) + far(dy) + (up, up) + far(bias, bias) + (down, down),
    )


def ffn_rest_kernel(
    tables, count, info_ref, sec_ref, dy_ref, out_part_ref, dsec_part_ref, res_ref, mixed_ref, bdown_ref, g2_ref, wout_ref, *refs
):
    ups, downs = refs[:count], refs[count : 2 * count]
    block_ref, gres_ref, gmix_ref, vec_ref, dwout_ref = refs[2 * count : 2 * count + 5]
    rest = refs[2 * count + 5 :]
    grads, bgrads = rest[:count], rest[count : 2 * count]
    accs, baccs = rest[2 * count : 3 * count], rest[3 * count : 4 * count]
    wacc_ref = rest[4 * count]
    at, last = pl.program_id(0), pl.num_programs(0) - 1
    width = sec_ref.shape[1]

    @pl.when(at == 0)
    def _():
        for ref in accs + baccs + (wacc_ref, vec_ref):
            ref[...] = jnp.zeros_like(ref)

    sec, dy = sec_ref[...], dy_ref[...]
    sec_t, dy_t = sec.T, dy.T
    out, dsec = out_part_ref[...], dsec_part_ref[...]
    for i in range(count):
        bias = ups[i][width : width + TILE, :].astype(F32)[:1]
        out, dsec = ffn_block(sec, sec_t, dy, dy_t, ups[i][:width, :], bias, downs[i][...], accs[i], baccs[i], out, dsec)
    residual = res_ref[...]
    block_ref[...] = (residual + (out + bdown_ref[...])).astype(BF)
    dy32 = dy.astype(F32)
    unit, inv = unit_parts(residual)
    vec_ref[0:1, :] += jnp.sum(dsec * unit, axis=0, keepdims=True)
    vec_ref[1:2, :] += jnp.sum(dsec, axis=0, keepdims=True)
    vec_ref[2:3, :] += jnp.sum(dy32, axis=0, keepdims=True)
    gres = dy32 + norm_back(dsec, unit, inv, g2_ref[...])
    gres_ref[...] = gres
    branch = gres.astype(BF)
    gmix_ref[...] = mm_nt(branch, wout_ref[...]).astype(BF)
    wacc_ref[...] += mm_tn(mixed_ref[...], branch)

    @pl.when(at == last)
    def _():
        core, own = info_ref[0], info_ref[1]
        for i in range(count):
            permuted(grads[i], accs[i], tables, core ^ (i % 2), own)
            bgrads[i][...] = baccs[i][...]
        dwout_ref[...] = wacc_ref[...]


def ffn_rest(info, tables, second, dy, out_part, dsec_part, residual, mixed, bdown, g2, wout, chunks):
    n, width = second.shape
    count = len(chunks)
    units = chunks[0][0].shape[1]
    return call(
        functools.partial(ffn_rest_kernel, tables, count),
        "ffn_rest",
        (n // TOKS,),
        [rows_of(width)] * 6
        + [whole(1, width)] * 2
        + [whole(width, width)]
        + [whole(width + TILE, units)] * count
        + [whole(units, width)] * count,
        [rows_of(width)] * 3
        + [whole(8, width), whole(width, width)]
        + [whole(width, 2 * units)] * count
        + [whole(1, units)] * count,
        [
            jax.ShapeDtypeStruct((n, width), BF),
            pltpu.HBM((n, width), F32),
            pltpu.HBM((n, width), BF),
            jax.ShapeDtypeStruct((8, width), F32),
            pltpu.HBM((width, width), F32),
        ]
        + [jax.ShapeDtypeStruct((width, 2 * units), BF)] * count
        + [jax.ShapeDtypeStruct((1, units), F32)] * count,
        [pltpu.VMEM((width, 2 * units), F32)] * count
        + [pltpu.VMEM((1, units), F32)] * count
        + [pltpu.VMEM((width, width), F32)],
        info,
        near(second) + far(dy) + near(out_part, dsec_part) + far(residual, mixed) + far(bdown, g2) + (wout,)
        + tuple(c[0] for c in chunks)
        + tuple(c[1] for c in chunks),
    )


def attend_back_kernel(
    tables, info_ref, qkv_ref, prob_ref, gmix_ref, tok_ref, vec_ref, dwout_ref, grad_ref, dw_keep_ref, dw_send_ref,
    dqkv_ref, acc_ref, row_ref,
):
    at, last = pl.program_id(0), pl.num_programs(0) - 1
    toks, width = tok_ref.shape
    rows, pairs, slots, _ = prob_ref.shape

    @pl.when(at == 0)
    def _():
        acc_ref[:, : 3 * width] = jnp.zeros((width, 3 * width), F32)
        acc_ref[:, 3 * width : 4 * width] = dwout_ref[...]
        row_ref[...] = jnp.zeros_like(row_ref)
        row_ref[SUMS : SUMS + vec_ref.shape[0], :] = vec_ref[...]

    scale = HEAD ** (-0.5)
    units = [(r, p) for r in range(rows) for p in range(pairs)]

    def place(r, p, which):
        return (slice(r * slots, (r + 1) * slots), slice(which * width + p * PAIR, which * width + (p + 1) * PAIR))

    grads = [gmix_ref[place(r, p, 0)] for r, p in units]
    dprobs = [mm_nt(g, by_head(qkv_ref[place(r, p, 2)])) for (r, p), g in zip(units, grads)]
    for (r, p), g in zip(units, grads):
        prob = prob_ref[r, p]
        stacked = jnp.concatenate([prob[:, :slots], prob[:, slots:]], axis=0)
        dqkv_ref[place(r, p, 2)] = mm_tn(stacked, by_head(g)).astype(BF)
    dscores = []
    for (r, p), dprob in zip(units, dprobs):
        p32 = prob_ref[r, p].astype(F32)
        prod = p32 * dprob
        first = jnp.sum(prod[:, :slots], axis=-1, keepdims=True)
        second = jnp.sum(prod[:, slots:], axis=-1, keepdims=True)
        dscores.append((
            (p32[:, :slots] * (dprob[:, :slots] - first)).astype(BF),
            (p32[:, slots:] * (dprob[:, slots:] - second)).astype(BF),
        ))
    for (r, p), ds in zip(units, dscores):
        k = qkv_ref[place(r, p, 1)]
        dqkv_ref[place(r, p, 0)] = mm(jnp.concatenate(ds, axis=1), by_head(k * scale)).astype(BF)
    for (r, p), ds in zip(units, dscores):
        q = qkv_ref[place(r, p, 0)]
        dqkv_ref[place(r, p, 1)] = mm_tn(jnp.concatenate(ds, axis=0), by_head(q * scale)).astype(BF)
    unit, _ = unit_parts(tok_ref[...].astype(F32))
    acc_ref[:, : 3 * width] += mm_tn(unit.astype(BF), dqkv_ref[...])
    grad_ref[...] = dqkv_ref[...]
    for i in range(3):
        part = dqkv_ref[:, i * width : (i + 1) * width].astype(F32)
        row_ref[i : i + 1, :] += jnp.sum(part, axis=0, keepdims=True)

    @pl.when(at == last)
    def _():
        core, own = info_ref[0], info_ref[2]
        acc_ref[:, 4 * width :] = row_ref[...].T
        half = width // 2
        size = width // len(tables[0])
        for place in range(len(tables[0])):
            dst = dw_keep_ref if place * size < half else dw_send_ref
            block = block_at(place, tables, core, own)
            rows_at = pl.ds(pl.multiple_of(block * size, size), size)
            to = place * size % half
            dst[to : to + size, :] = acc_ref[rows_at, :].astype(BF)


def attend_back(info, tables, qkv, prob, gmix, tokens, vec, dwout):
    n, width = tokens.shape
    rows, pairs, slots, _ = prob.shape
    per = TOKS // slots
    return call(
        functools.partial(attend_back_kernel, tables),
        "attend_back",
        (n // TOKS,),
        [
            rows_of(3 * width),
            pl.BlockSpec((per, pairs, slots, 2 * slots), lambda i, *_: (i, 0, 0, 0)),
            rows_of(width),
            rows_of(width),
            whole(*vec.shape),
            whole(width, width),
        ],
        [rows_of(3 * width)] + [whole(width // 2, 4 * width + LANES)] * 2,
        [pltpu.VMEM((n, 3 * width), BF)] + [jax.ShapeDtypeStruct((width // 2, 4 * width + LANES), BF)] * 2,
        [
            pltpu.VMEM((TOKS, 3 * width), BF),
            pltpu.VMEM((width, 4 * width + LANES), F32),
            pltpu.VMEM((LANES, width), F32),
        ],
        info,
        far(qkv, prob, gmix, tokens, vec, dwout),
    )


def first_back_kernel(info_ref, dqkv_ref, wqkv_ref, tok_ref, gres_ref, g1_ref, out_ref):
    dnormed = mm_nt(dqkv_ref[...], wqkv_ref[...])
    unit, inv = unit_parts(tok_ref[...].astype(F32))
    out_ref[...] = gres_ref[...] + norm_back(dnormed, unit, inv, g1_ref[...])


def first_back(info, dqkv, wqkv, tokens, gres, g1):
    n, width = tokens.shape
    return call(
        first_back_kernel,
        "first_back",
        (n // TOKS,),
        [rows_of(3 * width), whole(*wqkv.shape), rows_of(width), rows_of(width), whole(1, width)],
        rows_of(width),
        jax.ShapeDtypeStruct((n, width), F32),
        [],
        info,
        near(dqkv) + (wqkv,) + far(tokens, gres, g1),
    )


def ffn_end_kernel(tables, info_ref, keep_ref, other_ref, up_ref, down_ref, full_ref):
    core, own = info_ref[0], info_ref[1]
    units = up_ref.shape[1]
    blocks = len(tables[0])
    size = keep_ref.shape[0] // blocks

    def lay(src_ref, whose):
        for place in range(blocks):
            block = block_at(place, tables, whose, own)
            rows = pl.ds(pl.multiple_of(block * size, size), size)
            part = src_ref[place * size : (place + 1) * size, :].astype(F32)
            up_ref[rows, :] = part[:, :units]
            full_ref[rows, :] = part[:, units:]
        down_ref[...] = full_ref[...].T

    @pl.when(pl.program_id(0) == 0)
    def _():
        lay(keep_ref, core)

    @pl.when(pl.program_id(0) == 1)
    def _():
        lay(other_ref, core ^ 1)


def ffn_end(info, tables, keep, other):
    width, double = keep.shape
    units = double // 2
    return call(
        functools.partial(ffn_end_kernel, tables),
        "ffn_end",
        (2,),
        [whole(width, double)] * 2,
        [
            pl.BlockSpec((width, units), lambda i, info: (0, info[0] ^ i)),
            pl.BlockSpec((units, width), lambda i, info: (info[0] ^ i, 0)),
        ],
        [jax.ShapeDtypeStruct((width, double), F32), jax.ShapeDtypeStruct((double, width), F32)],
        [pltpu.VMEM((width, units), F32)],
        info,
        (keep, other),
    )


def attend_end_kernel(tables, info_ref, keep_ref, other_ref, w_ref, g1_ref, c1_ref, qkv_ref, out_ref, vec_ref, sum_ref, col_ref):
    core, own = info_ref[0], info_ref[2]
    width = out_ref.shape[1]
    blocks = len(tables[0])
    size = out_ref.shape[0] // blocks
    half = out_ref.shape[0] // 2
    for place in range(blocks):
        src = keep_ref if place * size < half else other_ref
        at = place * size % half
        block = block_at(place, tables, core, own)
        rows = pl.ds(pl.multiple_of(block * size, size), size)
        part = src[at : at + size, :].astype(F32)
        sum_ref[rows, :] = part[:, : 3 * width]
        out_ref[rows, :] = part[:, 3 * width : 4 * width]
        col_ref[rows, :] = part[:, 4 * width :]
    vec = col_ref[...].T
    wide_row = jnp.concatenate([vec[i : i + 1, :] for i in range(3)], axis=1)
    pair = jnp.concatenate([g1_ref[...], c1_ref[...], jnp.zeros((LANES - 2, width), F32)], axis=0).T
    gain, bias = pair[:, 0:1], pair[:, 1:2]
    w = w_ref[...].astype(F32)
    sums = sum_ref[...]
    qkv_ref[...] = gain * sums + bias * wide_row
    lane = lax.broadcasted_iota(jnp.int32, (width, LANES), 1)
    d_gain = jnp.sum(w * sums, axis=1, keepdims=True)
    d_bias = jnp.sum(w * wide_row, axis=1, keepdims=True)
    both = jnp.where(lane == 0, d_gain, jnp.where(lane == 1, d_bias, 0.0)).T
    vec_ref[...] = vec[: vec_ref.shape[0], :]
    vec_ref[0:2, :] = both[0:2, :]


def attend_end(info, tables, keep, other, w_qkv, g1, c1, count):
    rows, width = 2 * keep.shape[0], w_qkv.shape[0]
    return call(
        functools.partial(attend_end_kernel, tables),
        "attend_end",
        (1,),
        [whole(*keep.shape)] * 2 + [whole(*w_qkv.shape)] + [whole(1, width)] * 2,
        [whole(rows, 3 * width), whole(rows, width), whole(count, width)],
        [
            jax.ShapeDtypeStruct((rows, 3 * width), F32),
            jax.ShapeDtypeStruct((rows, width), F32),
            jax.ShapeDtypeStruct((count, width), F32),
        ],
        [pltpu.VMEM((rows, 3 * width), F32), pltpu.VMEM((rows, LANES), F32)],
        info,
        (keep, other, w_qkv, g1, c1),
    )


def local(
    wide, narrow, tokens_in, ln1_gain, ln1_bias, w_qkv, w_out, ln2_gain, ln2_bias, w_up, b_up, w_down, b_down, segment_ids,
    step_ids, pad_mask, cotangent,
):
    width = tokens_in.shape[1]
    units = w_up.shape[1] // 2
    core_mask = narrow
    narrow_masks = [1 << b for b in range(narrow.bit_length() - 1)]
    wide_masks = [narrow << b for b in range(1, wide.bit_length() - 1)]

    def swap(value, first, second=None):
        masks = (first, first if second is None else second)
        pairs = [(i, i ^ masks[i // narrow & 1]) for i in range(wide * narrow)]
        return lax.ppermute(value, AXES, pairs)

    def add(a, b):
        return (a.astype(F32) + b.astype(F32)).astype(a.dtype)

    def orders(masks):
        if len(masks) < 2:
            return (masks, masks)
        return (masks, [masks[1], masks[0]] + masks[2:])

    def after(*values):
        return lax.optimization_barrier(values)

    def scatter(value, order, beside=None):
        for step, (first, second) in enumerate(zip(*order)):
            half = value.shape[0] // 2
            value = add(value[:half], swap(value[half:], first, second))
            if beside is not None and step == 0:
                value, beside = after(value, beside)
        return value if beside is None else (value, beside)

    def gather(value, order):
        for first, second in reversed(list(zip(*order))):
            value = jnp.concatenate([value, swap(value, first, second)], axis=0)
        return value

    wide_at, narrow_at = lax.axis_index("wide"), lax.axis_index("narrow")
    core = wide_at & 1
    flat = wide_at * narrow + narrow_at

    ff_order = orders(wide_masks)
    ff_tables = tuple([owner // (2 * narrow) for owner in places(o, wide // 2)] for o in ff_order)
    masks = narrow_masks + wide_masks
    split = min(len(masks), (width // TILE).bit_length() - 2)
    at_order = orders(masks[:split])
    at_rest = masks[split:]
    blocks = 1 << split
    near = [places(o, blocks) for o in at_order]
    used = [core_mask] + masks[:split]

    def named(owner):
        return sum((1 << b) for b, m in enumerate(used) if owner & m)

    at_tables = tuple(
        [named(o) for o in near[c]] + [named(o ^ core_mask) for o in near[1 - c]] for c in range(2)
    )
    own_block = sum((flat // m & 1) << b for b, m in enumerate(used))
    info = jnp.stack([core, wide_at // 2, own_block]).astype(jnp.int32)

    up_chunk = lax.dynamic_slice(w_up, (0, core * units), (width, units))
    bias_chunk = lax.dynamic_slice(b_up, (core * units,), (units,))
    up_chunk = jnp.concatenate([up_chunk, jnp.broadcast_to(bias_chunk[None], (TILE, units))], axis=0)
    down_chunk = lax.dynamic_slice(w_down, (core * units, 0), (units, width))
    fetched = [(up_chunk, down_chunk)]
    for mask in narrow_masks:
        fetched = fetched + [(swap(u, mask), swap(d, mask)) for u, d in fetched]

    row = lambda v: v[None].astype(F32)
    g1, c1, g2 = row(ln1_gain), row(ln1_bias), row(ln2_gain)
    qkv, prob, mixed, residual, second = attend(
        info, tokens_in, g1, c1, w_qkv, w_out, g2, row(ln2_bias), segment_ids, step_ids, pad_mask
    )
    fetched = after(second, fetched)[1]
    chunks = []
    for up, down in fetched[1:]:
        chunks += [(up, down), (swap(up, core_mask), swap(down, core_mask))]
    out_part, dsec_part, own_keep, own_send, bown_keep, bown_send = ffn_own(
        info, ff_tables, second, cotangent, w_up, b_up[None], w_down
    )
    rest = ffn_rest(
        info, ff_tables, second, cotangent, out_part, dsec_part, residual, mixed, row(b_down), g2, w_out, chunks
    )
    block_out, gres, gmix, vec, dwout = rest[:5]
    count = len(chunks)
    grads, bgrads = rest[5 : 5 + count], rest[5 + count :]

    b_all = jnp.concatenate([bown_keep, bown_send, *bgrads], axis=0)
    for bit in range(narrow.bit_length()):
        flipped = jnp.flip(b_all.reshape(-1, 2, 1 << bit, units), axis=1).reshape(b_all.shape)
        b_all = jnp.where((narrow_at * 2 + core) >> bit & 1, flipped, b_all)
    vec = jnp.concatenate([vec, b_all.reshape(-1, width)], axis=0)

    held = [add(own_keep, swap(own_send, core_mask))]
    held += [add(grads[2 * j], swap(grads[2 * j + 1], core_mask)) for j in range(narrow - 1)]
    gmix, held = after(gmix, held)
    for mask in reversed(narrow_masks):
        held = [add(held[j], swap(held[j + mask], mask)) for j in range(mask)]

    dqkv, keep, send = attend_back(info, at_tables, qkv, prob, gmix, tokens_in, vec, dwout)
    keep = add(keep, swap(send, core_mask))
    keep, held = after(keep, held)
    grad_tokens = first_back(info, dqkv, w_qkv, tokens_in, gres, g1)
    ff_keep = gather(scatter(held[0], ff_order), ff_order)
    ff_other = swap(ff_keep, core_mask)
    grad_w_up, grad_w_down = ffn_end(info, ff_tables, ff_keep, ff_other)

    keep, grad_tokens = scatter(keep, at_order, grad_tokens)
    for mask in at_rest:
        keep = add(keep, swap(keep, mask))
    keep = gather(keep, at_order)
    grad_w_qkv, grad_w_out, vec = attend_end(
        info, at_tables, keep, swap(keep, core_mask), w_qkv, g1, c1, SUMS + vec.shape[0]
    )
    b_sum = vec[SUMS + 8 :].reshape(narrow, 2 * units)
    grad_b_up = lax.dynamic_slice(b_sum, (narrow_at, 0), (1, 2 * units))[0]
    return (
        block_out,
        grad_tokens,
        vec[0],
        vec[1],
        grad_w_qkv,
        grad_w_out,
        vec[SUMS],
        vec[SUMS + 1],
        grad_w_up,
        grad_b_up,
        grad_w_down,
        vec[SUMS + 2],
    )


def solution(mesh):
    rows = P(("wide", "narrow"), None)
    in_specs = (
        rows, P(), P(), P(), P(), P(), P(), P(None, "narrow"), P("narrow"), P("narrow", None), P(), rows, rows, rows, rows,
    )
    out_specs = (
        rows, rows, P(), P(), P(), P(), P(), P(), P(None, "narrow"), P("narrow"), P("narrow", None), P(),
    )
    wide, narrow = mesh.shape["wide"], mesh.shape["narrow"]
    return jax.shard_map(
        functools.partial(local, wide, narrow), mesh=mesh, in_specs=in_specs, out_specs=out_specs, check_vma=False
    )
```

```python
import functools
import itertools

import jax
import jax.numpy as jnp
import numpy as np
from jax import lax
from jax.experimental import pallas as pl
from jax.experimental.pallas import tpu as pltpu
from jax.sharding import PartitionSpec as P

HEAD = 64
PAIR = 2 * HEAD
NORM_EPS = 1e-05
BF = jnp.bfloat16
F32 = jnp.float32
AXES = ("wide", "narrow")
LANES = 128
SUMS = 8
TILE = 16
TOKS = 512
VMEM_LIMIT = 24 * 1024 * 1024


def mm(a, b):
    return lax.dot_general(a, b, (((1,), (0,)), ((), ())), preferred_element_type=F32)


def mm_nt(a, b):
    return lax.dot_general(a, b, (((1,), (1,)), ((), ())), preferred_element_type=F32)


def mm_tn(a, b):
    return lax.dot_general(a, b, (((0,), (0,)), ((), ())), preferred_element_type=F32)


def near(*values):
    return tuple(pltpu.with_memory_space_constraint(v, pltpu.VMEM) for v in values)


def far(*values):
    return tuple(pltpu.with_memory_space_constraint(v, pltpu.HBM) for v in values)


def whole(*shape):
    return pl.BlockSpec(shape, lambda *_: (0,) * len(shape))


def rows_of(width, toks=TOKS):
    return pl.BlockSpec((toks, width), lambda i, *_: (i, 0))


def call(kernel, name, grid, in_specs, out_specs, out_shape, scratch, info, args):
    return pl.pallas_call(
        kernel,
        grid_spec=pltpu.PrefetchScalarGridSpec(
            num_scalar_prefetch=1, grid=grid, in_specs=in_specs, out_specs=out_specs, scratch_shapes=scratch
        ),
        out_shape=out_shape,
        compiler_params=pltpu.CompilerParams(vmem_limit_bytes=VMEM_LIMIT),
        cost_estimate=pl.CostEstimate(flops=1000, bytes_accessed=1000, transcendentals=0),
        name=name,
    )(info, *args)


def unit_parts(rows):
    mean = jnp.mean(rows, axis=-1, keepdims=True)
    centered = rows - mean
    inv = lax.rsqrt(jnp.mean(centered * centered, axis=-1, keepdims=True) + NORM_EPS)
    return centered * inv, inv


def norm_back(incoming, unit, inv, gain):
    scaled = incoming * gain
    return inv * (
        scaled
        - jnp.mean(scaled, axis=-1, keepdims=True)
        - unit * jnp.mean(scaled * unit, axis=-1, keepdims=True)
    )


def gelu_pair(x):
    cdf = 0.5 * (1.0 + lax.erf(x * 0.7071067811865476))
    return x * cdf, cdf + x * jnp.exp(-0.5 * x * x) * 0.3989422804014327


def by_head(block):
    lane = lax.broadcasted_iota(jnp.int32, block.shape, 1)
    zero = jnp.zeros_like(block)
    first = lane < HEAD
    return jnp.concatenate([jnp.where(first, block, zero), jnp.where(first, zero, block)], axis=0)


def places(order, blocks):
    bits = blocks.bit_length() - 1
    table = []
    for place in range(blocks):
        owner = 0
        for step in range(bits):
            if place >> (bits - 1 - step) & 1:
                owner ^= order[step]
        table.append(owner)
    return table


def block_at(place, tables, core, own):
    first, second = tables[0][place], tables[1][place]
    if first == second:
        return own ^ first
    return own ^ jnp.where(core == 0, first, second)


def permuted(dst_ref, acc_ref, tables, core, own):
    blocks = len(tables[0])
    size = acc_ref.shape[0] // blocks
    for place in range(blocks):
        block = block_at(place, tables, core, own)
        rows = pl.ds(pl.multiple_of(block * size, size), size)
        dst_ref[place * size : (place + 1) * size, :] = acc_ref[rows, :].astype(dst_ref.dtype)


def attend_kernel(
    info_ref, tok_ref, g1_ref, c1_ref, wqkv_ref, wout_ref, g2_ref, c2_ref, seg_ref, step_ref, pad_ref,
    qkv_ref, prob_ref, mixed_ref, res_ref, second_ref,
):
    slots = seg_ref.shape[1]
    toks, width = tok_ref.shape
    rows = toks // slots
    at = pl.program_id(0)
    tokens = tok_ref[...].astype(F32)
    unit, _ = unit_parts(tokens)
    normed = (unit * g1_ref[...] + c1_ref[...]).astype(BF)
    qkv_ref[...] = mm(normed, wqkv_ref[...]).astype(BF)
    q_id = lax.broadcasted_iota(jnp.int32, (slots, slots), 0)
    k_id = lax.broadcasted_iota(jnp.int32, (slots, slots), 1)
    eye = q_id == k_id
    pairs = width // PAIR
    units = [(r, p) for r in range(rows) for p in range(pairs)]

    def part(r, p, which):
        return qkv_ref[r * slots : (r + 1) * slots, which * width + p * PAIR : which * width + (p + 1) * PAIR]

    masks = []
    for r in range(rows):
        here = pl.ds(at * rows + r, 1)
        seg = jnp.broadcast_to(seg_ref[here, :].astype(F32), (slots, slots))
        step = jnp.broadcast_to(step_ref[here, :].astype(F32), (slots, slots))
        live = jnp.broadcast_to(pad_ref[here, :], (slots, slots)) == 0
        masks.append(((seg == seg.T) & (step <= step.T) & live) | eye)
    scores = [mm_nt(part(r, p, 0), by_head(part(r, p, 1) * HEAD ** (-0.5))) for r, p in units]
    probs = []
    for (r, p), score in zip(units, scores):
        halves = []
        for half in (score[:, :slots], score[:, slots:]):
            half = jnp.where(masks[r], half, -1e30)
            weight = jnp.exp(half - jnp.max(half, axis=-1, keepdims=True))
            total = jnp.sum(weight, axis=-1, keepdims=True)
            halves.append((weight * (1.0 / total)).astype(BF))
        probs.append(jnp.concatenate(halves, axis=1))
    for (r, p), prob in zip(units, probs):
        prob_ref[r, p] = prob
        mixed_ref[r * slots : (r + 1) * slots, p * PAIR : (p + 1) * PAIR] = mm(prob, by_head(part(r, p, 2))).astype(BF)
    residual = tokens + mm(mixed_ref[...], wout_ref[...])
    res_ref[...] = residual
    unit, _ = unit_parts(residual)
    second_ref[...] = (unit * g2_ref[...] + c2_ref[...]).astype(BF)


def attend(info, tokens, g1, c1, wqkv, wout, g2, c2, seg, step, pad):
    n, width = tokens.shape
    rows, slots = seg.shape
    per, pairs = TOKS // slots, width // PAIR
    return call(
        attend_kernel,
        "attend",
        (n // TOKS,),
        [rows_of(width), whole(1, width), whole(1, width), whole(*wqkv.shape), whole(*wout.shape)]
        + [whole(1, width)] * 2
        + [whole(rows, slots)] * 3,
        [
            rows_of(3 * width),
            pl.BlockSpec((per, pairs, slots, 2 * slots), lambda i, *_: (i, 0, 0, 0)),
            rows_of(width),
            rows_of(width),
            rows_of(width),
        ],
        [
            pltpu.HBM((n, 3 * width), BF),
            pltpu.HBM((rows, pairs, slots, 2 * slots), BF),
            pltpu.HBM((n, width), BF),
            pltpu.HBM((n, width), F32),
            pltpu.VMEM((n, width), BF),
        ],
        [],
        info,
        far(tokens, g1, c1) + (wqkv, wout) + far(g2, c2, seg, step, pad),
    )


def ffn_block(sec, sec_t, dy, dy_t, up, bias, down, acc_ref, bacc_ref, out, dsec):
    units = up.shape[1]
    pre = mm(sec, up) + bias
    hid, slope = gelu_pair(pre)
    hid = hid.astype(BF)
    dpre = (mm_nt(dy, down) * slope).astype(BF)
    acc_ref[:, :units] += mm(sec_t, dpre)
    acc_ref[:, units:] += mm(dy_t, hid)
    bacc_ref[...] += jnp.sum(dpre.astype(F32), axis=0, keepdims=True)
    o = mm(hid, down)
    d = mm_nt(dpre, up)
    return (o if out is None else out + o), (d if dsec is None else dsec + d)


def ffn_own_kernel(tables, info_ref, sec_ref, dy_ref, *refs):
    ups, biases, downs = refs[:2], refs[2:4], refs[4:6]
    out_ref, dsec_ref = refs[6:8]
    grads, bgrads, accs, baccs = refs[8:10], refs[10:12], refs[12:14], refs[14:16]
    at, last = pl.program_id(0), pl.num_programs(0) - 1

    @pl.when(at == 0)
    def _():
        for ref in accs + baccs:
            ref[...] = jnp.zeros_like(ref)

    sec, dy = sec_ref[...], dy_ref[...]
    sec_t, dy_t = sec.T, dy.T
    out = dsec = None
    for i in range(2):
        out, dsec = ffn_block(
            sec, sec_t, dy, dy_t, ups[i][...], biases[i][...].astype(F32), downs[i][...], accs[i], baccs[i], out, dsec
        )
    out_ref[...] = out
    dsec_ref[...] = dsec

    @pl.when(at == last)
    def _():
        core, own = info_ref[0], info_ref[1]
        for i in range(2):
            permuted(grads[i], accs[i], tables, core ^ i, own)
            bgrads[i][...] = baccs[i][...]


def ffn_own(info, tables, second, dy, up, bias, down):
    n, width = second.shape
    units = up.shape[1] // 2
    chunk = lambda i: (lambda t, info: (0, info[0] ^ i))
    return call(
        functools.partial(ffn_own_kernel, tables),
        "ffn_own",
        (n // TOKS,),
        [rows_of(width), rows_of(width)]
        + [pl.BlockSpec((width, units), chunk(i)) for i in range(2)]
        + [pl.BlockSpec((1, units), chunk(i)) for i in range(2)]
        + [pl.BlockSpec((units, width), lambda t, info, i=i: (info[0] ^ i, 0)) for i in range(2)],
        [rows_of(width)] * 2 + [whole(width, 2 * units)] * 2 + [whole(1, units)] * 2,
        [pltpu.VMEM((n, width), F32)] * 2
        + [jax.ShapeDtypeStruct((width, 2 * units), BF)] * 2
        + [jax.ShapeDtypeStruct((1, units), F32)] * 2,
        [pltpu.VMEM((width, 2 * units), F32)] * 2 + [pltpu.VMEM((1, units), F32)] * 2,
        info,
        near(second) + far(dy) + (up, up) + far(bias, bias) + (down, down),
    )


def ffn_rest_kernel(
    tables, count, info_ref, sec_ref, dy_ref, out_part_ref, dsec_part_ref, res_ref, mixed_ref, bdown_ref, g2_ref, wout_ref, *refs
):
    ups, downs = refs[:count], refs[count : 2 * count]
    block_ref, gres_ref, gmix_ref, vec_ref, dwout_ref = refs[2 * count : 2 * count + 5]
    rest = refs[2 * count + 5 :]
    grads, bgrads = rest[:count], rest[count : 2 * count]
    accs, baccs = rest[2 * count : 3 * count], rest[3 * count : 4 * count]
    wacc_ref = rest[4 * count]
    at, last = pl.program_id(0), pl.num_programs(0) - 1
    width = sec_ref.shape[1]

    @pl.when(at == 0)
    def _():
        for ref in accs + baccs + (wacc_ref, vec_ref):
            ref[...] = jnp.zeros_like(ref)

    sec, dy = sec_ref[...], dy_ref[...]
    sec_t, dy_t = sec.T, dy.T
    out, dsec = out_part_ref[...], dsec_part_ref[...]
    for i in range(count):
        bias = ups[i][width : width + TILE, :].astype(F32)[:1]
        out, dsec = ffn_block(sec, sec_t, dy, dy_t, ups[i][:width, :], bias, downs[i][...], accs[i], baccs[i], out, dsec)
    residual = res_ref[...]
    block_ref[...] = (residual + (out + bdown_ref[...])).astype(BF)
    dy32 = dy.astype(F32)
    unit, inv = unit_parts(residual)
    vec_ref[0:1, :] += jnp.sum(dsec * unit, axis=0, keepdims=True)
    vec_ref[1:2, :] += jnp.sum(dsec, axis=0, keepdims=True)
    vec_ref[2:3, :] += jnp.sum(dy32, axis=0, keepdims=True)
    gres = dy32 + norm_back(dsec, unit, inv, g2_ref[...])
    gres_ref[...] = gres
    branch = gres.astype(BF)
    gmix_ref[...] = mm_nt(branch, wout_ref[...]).astype(BF)
    wacc_ref[...] += mm_tn(mixed_ref[...], branch)

    @pl.when(at == last)
    def _():
        core, own = info_ref[0], info_ref[1]
        for i in range(count):
            permuted(grads[i], accs[i], tables, core ^ (i % 2), own)
            bgrads[i][...] = baccs[i][...]
        dwout_ref[...] = wacc_ref[...]


def ffn_rest(info, tables, second, dy, out_part, dsec_part, residual, mixed, bdown, g2, wout, chunks):
    n, width = second.shape
    count = len(chunks)
    units = chunks[0][0].shape[1]
    return call(
        functools.partial(ffn_rest_kernel, tables, count),
        "ffn_rest",
        (n // TOKS,),
        [rows_of(width)] * 6
        + [whole(1, width)] * 2
        + [whole(width, width)]
        + [whole(width + TILE, units)] * count
        + [whole(units, width)] * count,
        [rows_of(width)] * 3
        + [whole(8, width), whole(width, width)]
        + [whole(width, 2 * units)] * count
        + [whole(1, units)] * count,
        [
            jax.ShapeDtypeStruct((n, width), BF),
            pltpu.HBM((n, width), F32),
            pltpu.HBM((n, width), BF),
            jax.ShapeDtypeStruct((8, width), F32),
            pltpu.HBM((width, width), F32),
        ]
        + [jax.ShapeDtypeStruct((width, 2 * units), BF)] * count
        + [jax.ShapeDtypeStruct((1, units), F32)] * count,
        [pltpu.VMEM((width, 2 * units), F32)] * count
        + [pltpu.VMEM((1, units), F32)] * count
        + [pltpu.VMEM((width, width), F32)],
        info,
        near(second) + far(dy) + near(out_part, dsec_part) + far(residual, mixed) + far(bdown, g2) + (wout,)
        + tuple(c[0] for c in chunks)
        + tuple(c[1] for c in chunks),
    )


def attend_back_kernel(
    tables, info_ref, qkv_ref, prob_ref, gmix_ref, tok_ref, vec_ref, dwout_ref, grad_ref, dw_keep_ref, dw_send_ref,
    dqkv_ref, acc_ref, row_ref,
):
    at, last = pl.program_id(0), pl.num_programs(0) - 1
    toks, width = tok_ref.shape
    rows, pairs, slots, _ = prob_ref.shape

    @pl.when(at == 0)
    def _():
        acc_ref[:, : 3 * width] = jnp.zeros((width, 3 * width), F32)
        acc_ref[:, 3 * width : 4 * width] = dwout_ref[...]
        row_ref[...] = jnp.zeros_like(row_ref)
        row_ref[SUMS : SUMS + vec_ref.shape[0], :] = vec_ref[...]

    scale = HEAD ** (-0.5)
    units = [(r, p) for r in range(rows) for p in range(pairs)]

    def place(r, p, which):
        return (slice(r * slots, (r + 1) * slots), slice(which * width + p * PAIR, which * width + (p + 1) * PAIR))

    grads = [gmix_ref[place(r, p, 0)] for r, p in units]
    dprobs = [mm_nt(g, by_head(qkv_ref[place(r, p, 2)])) for (r, p), g in zip(units, grads)]
    for (r, p), g in zip(units, grads):
        prob = prob_ref[r, p]
        stacked = jnp.concatenate([prob[:, :slots], prob[:, slots:]], axis=0)
        dqkv_ref[place(r, p, 2)] = mm_tn(stacked, by_head(g)).astype(BF)
    dscores = []
    for (r, p), dprob in zip(units, dprobs):
        p32 = prob_ref[r, p].astype(F32)
        prod = p32 * dprob
        first = jnp.sum(prod[:, :slots], axis=-1, keepdims=True)
        second = jnp.sum(prod[:, slots:], axis=-1, keepdims=True)
        dscores.append((
            (p32[:, :slots] * (dprob[:, :slots] - first)).astype(BF),
            (p32[:, slots:] * (dprob[:, slots:] - second)).astype(BF),
        ))
    for (r, p), ds in zip(units, dscores):
        k = qkv_ref[place(r, p, 1)]
        dqkv_ref[place(r, p, 0)] = mm(jnp.concatenate(ds, axis=1), by_head(k * scale)).astype(BF)
    for (r, p), ds in zip(units, dscores):
        q = qkv_ref[place(r, p, 0)]
        dqkv_ref[place(r, p, 1)] = mm_tn(jnp.concatenate(ds, axis=0), by_head(q * scale)).astype(BF)
    unit, _ = unit_parts(tok_ref[...].astype(F32))
    acc_ref[:, : 3 * width] += mm_tn(unit.astype(BF), dqkv_ref[...])
    grad_ref[...] = dqkv_ref[...]
    for i in range(3):
        part = dqkv_ref[:, i * width : (i + 1) * width].astype(F32)
        row_ref[i : i + 1, :] += jnp.sum(part, axis=0, keepdims=True)

    @pl.when(at == last)
    def _():
        core, own = info_ref[0], info_ref[2]
        acc_ref[:, 4 * width :] = row_ref[...].T
        half = width // 2
        size = width // len(tables[0])
        for place in range(len(tables[0])):
            dst = dw_keep_ref if place * size < half else dw_send_ref
            block = block_at(place, tables, core, own)
            rows_at = pl.ds(pl.multiple_of(block * size, size), size)
            to = place * size % half
            dst[to : to + size, :] = acc_ref[rows_at, :].astype(BF)


def attend_back(info, tables, qkv, prob, gmix, tokens, vec, dwout):
    n, width = tokens.shape
    rows, pairs, slots, _ = prob.shape
    per = TOKS // slots
    return call(
        functools.partial(attend_back_kernel, tables),
        "attend_back",
        (n // TOKS,),
        [
            rows_of(3 * width),
            pl.BlockSpec((per, pairs, slots, 2 * slots), lambda i, *_: (i, 0, 0, 0)),
            rows_of(width),
            rows_of(width),
            whole(*vec.shape),
            whole(width, width),
        ],
        [rows_of(3 * width)] + [whole(width // 2, 4 * width + LANES)] * 2,
        [pltpu.VMEM((n, 3 * width), BF)] + [jax.ShapeDtypeStruct((width // 2, 4 * width + LANES), BF)] * 2,
        [
            pltpu.VMEM((TOKS, 3 * width), BF),
            pltpu.VMEM((width, 4 * width + LANES), F32),
            pltpu.VMEM((LANES, width), F32),
        ],
        info,
        far(qkv, prob, gmix, tokens, vec, dwout),
    )


def first_back_kernel(info_ref, dqkv_ref, wqkv_ref, tok_ref, gres_ref, g1_ref, out_ref):
    dnormed = mm_nt(dqkv_ref[...], wqkv_ref[...])
    unit, inv = unit_parts(tok_ref[...].astype(F32))
    out_ref[...] = gres_ref[...] + norm_back(dnormed, unit, inv, g1_ref[...])


def first_back(info, dqkv, wqkv, tokens, gres, g1):
    n, width = tokens.shape
    return call(
        first_back_kernel,
        "first_back",
        (n // TOKS,),
        [rows_of(3 * width), whole(*wqkv.shape), rows_of(width), rows_of(width), whole(1, width)],
        rows_of(width),
        jax.ShapeDtypeStruct((n, width), F32),
        [],
        info,
        near(dqkv) + (wqkv,) + far(tokens, gres, g1),
    )


def ffn_end_kernel(tables, info_ref, keep_ref, other_ref, up_ref, down_ref, full_ref):
    core, own = info_ref[0], info_ref[1]
    units = up_ref.shape[1]
    blocks = len(tables[0])
    size = keep_ref.shape[0] // blocks

    def lay(src_ref, whose):
        for place in range(blocks):
            block = block_at(place, tables, whose, own)
            rows = pl.ds(pl.multiple_of(block * size, size), size)
            part = src_ref[place * size : (place + 1) * size, :].astype(F32)
            up_ref[rows, :] = part[:, :units]
            full_ref[rows, :] = part[:, units:]
        down_ref[...] = full_ref[...].T

    @pl.when(pl.program_id(0) == 0)
    def _():
        lay(keep_ref, core)

    @pl.when(pl.program_id(0) == 1)
    def _():
        lay(other_ref, core ^ 1)


def ffn_end(info, tables, keep, other):
    width, double = keep.shape
    units = double // 2
    return call(
        functools.partial(ffn_end_kernel, tables),
        "ffn_end",
        (2,),
        [whole(width, double)] * 2,
        [
            pl.BlockSpec((width, units), lambda i, info: (0, info[0] ^ i)),
            pl.BlockSpec((units, width), lambda i, info: (info[0] ^ i, 0)),
        ],
        [jax.ShapeDtypeStruct((width, double), F32), jax.ShapeDtypeStruct((double, width), F32)],
        [pltpu.VMEM((width, units), F32)],
        info,
        (keep, other),
    )


def attend_end_kernel(tables, info_ref, keep_ref, other_ref, w_ref, g1_ref, c1_ref, qkv_ref, out_ref, vec_ref, sum_ref, col_ref):
    core, own = info_ref[0], info_ref[2]
    width = out_ref.shape[1]
    blocks = len(tables[0])
    size = out_ref.shape[0] // blocks
    half = out_ref.shape[0] // 2
    for place in range(blocks):
        src = keep_ref if place * size < half else other_ref
        at = place * size % half
        block = block_at(place, tables, core, own)
        rows = pl.ds(pl.multiple_of(block * size, size), size)
        part = src[at : at + size, :].astype(F32)
        sum_ref[rows, :] = part[:, : 3 * width]
        out_ref[rows, :] = part[:, 3 * width : 4 * width]
        col_ref[rows, :] = part[:, 4 * width :]
    vec = col_ref[...].T
    wide_row = jnp.concatenate([vec[i : i + 1, :] for i in range(3)], axis=1)
    pair = jnp.concatenate([g1_ref[...], c1_ref[...], jnp.zeros((LANES - 2, width), F32)], axis=0).T
    gain, bias = pair[:, 0:1], pair[:, 1:2]
    w = w_ref[...].astype(F32)
    sums = sum_ref[...]
    qkv_ref[...] = gain * sums + bias * wide_row
    lane = lax.broadcasted_iota(jnp.int32, (width, LANES), 1)
    d_gain = jnp.sum(w * sums, axis=1, keepdims=True)
    d_bias = jnp.sum(w * wide_row, axis=1, keepdims=True)
    both = jnp.where(lane == 0, d_gain, jnp.where(lane == 1, d_bias, 0.0)).T
    vec_ref[...] = vec[: vec_ref.shape[0], :]
    vec_ref[0:2, :] = both[0:2, :]


def attend_end(info, tables, keep, other, w_qkv, g1, c1, count):
    rows, width = 2 * keep.shape[0], w_qkv.shape[0]
    return call(
        functools.partial(attend_end_kernel, tables),
        "attend_end",
        (1,),
        [whole(*keep.shape)] * 2 + [whole(*w_qkv.shape)] + [whole(1, width)] * 2,
        [whole(rows, 3 * width), whole(rows, width), whole(count, width)],
        [
            jax.ShapeDtypeStruct((rows, 3 * width), F32),
            jax.ShapeDtypeStruct((rows, width), F32),
            jax.ShapeDtypeStruct((count, width), F32),
        ],
        [pltpu.VMEM((rows, 3 * width), F32), pltpu.VMEM((rows, LANES), F32)],
        info,
        (keep, other, w_qkv, g1, c1),
    )


def local(
    wide, narrow, tokens_in, ln1_gain, ln1_bias, w_qkv, w_out, ln2_gain, ln2_bias, w_up, b_up, w_down, b_down, segment_ids,
    step_ids, pad_mask, cotangent,
):
    width = tokens_in.shape[1]
    units = w_up.shape[1] // 2
    core_mask = narrow
    narrow_masks = [1 << b for b in range(narrow.bit_length() - 1)]
    wide_masks = [narrow << b for b in range(1, wide.bit_length() - 1)]

    def swap(value, first, second=None):
        masks = (first, first if second is None else second)
        pairs = [(i, i ^ masks[i // narrow & 1]) for i in range(wide * narrow)]
        return lax.ppermute(value, AXES, pairs)

    def add(a, b):
        return (a.astype(F32) + b.astype(F32)).astype(a.dtype)

    def orders(masks):
        if len(masks) < 2:
            return (masks, masks)
        return (masks, [masks[1], masks[0]] + masks[2:])

    def after(*values):
        return lax.optimization_barrier(values)

    def scatters(order):
        def step(first, second, value):
            half = value.shape[0] // 2
            return add(value[:half], swap(value[half:], first, second))

        return [functools.partial(step, *pair) for pair in zip(*order)]

    def exchanges(masks):
        return [lambda value, mask=mask: add(value, swap(value, mask)) for mask in masks]

    def gathers(order):
        def step(first, second, value):
            return jnp.concatenate([value, swap(value, first, second)], axis=0)

        return [functools.partial(step, *pair) for pair in reversed(list(zip(*order)))]

    wide_at, narrow_at = lax.axis_index("wide"), lax.axis_index("narrow")
    core = wide_at & 1
    flat = wide_at * narrow + narrow_at

    def named(owner, used):
        return sum((1 << b) for b, m in enumerate(used) if owner & m)

    def block_of(used):
        return sum((flat // m & 1) << b for b, m in enumerate(used))

    def halved(masks, tiles):
        count = min(len(masks) - 1, tiles.bit_length() - 1)
        return masks[:count], masks[count:]

    ff_used, ff_rest = halved(wide_masks, width // TILE)
    ff_out = orders(ff_used)
    ff_in = (ff_used, ff_used) if narrow == 2 else ff_out
    ff_in_tables, ff_out_tables = (
        tuple([named(owner, ff_used) for owner in places(o, 1 << len(ff_used))] for o in pair) for pair in (ff_in, ff_out)
    )
    at_masks, at_rest = halved(narrow_masks + wide_masks, width // TILE // 2)
    at_order = orders(at_masks)
    at_used = [core_mask] + at_masks
    near_places = [places(o, 1 << len(at_masks)) for o in at_order]
    at_tables = tuple(
        [named(o, at_used) for o in near_places[c]] + [named(o ^ core_mask, at_used) for o in near_places[1 - c]]
        for c in range(2)
    )
    info = jnp.stack([core, block_of(ff_used), block_of(at_used)]).astype(jnp.int32)

    up_chunk = lax.dynamic_slice(w_up, (0, core * units), (width, units))
    bias_chunk = lax.dynamic_slice(b_up, (core * units,), (units,))
    up_chunk = jnp.concatenate([up_chunk, jnp.broadcast_to(bias_chunk[None], (TILE, units))], axis=0)
    down_chunk = lax.dynamic_slice(w_down, (core * units, 0), (units, width))
    fetched = [(up_chunk, down_chunk)]
    for mask in narrow_masks:
        fetched = fetched + [(swap(u, mask), swap(d, mask)) for u, d in fetched]

    row = lambda v: v[None].astype(F32)
    g1, c1, g2 = row(ln1_gain), row(ln1_bias), row(ln2_gain)
    qkv, prob, mixed, residual, second = attend(
        info, tokens_in, g1, c1, w_qkv, w_out, g2, row(ln2_bias), segment_ids, step_ids, pad_mask
    )
    fetched = after(second, fetched)[1]
    chunks = []
    for up, down in fetched[1:]:
        chunks += [(up, down), (swap(up, core_mask), swap(down, core_mask))]
    out_part, dsec_part, own_keep, own_send, bown_keep, bown_send = ffn_own(
        info, ff_in_tables, second, cotangent, w_up, b_up[None], w_down
    )
    rest = ffn_rest(
        info, ff_in_tables, second, cotangent, out_part, dsec_part, residual, mixed, row(b_down), g2, w_out, chunks
    )
    block_out, gres, gmix, vec, dwout = rest[:5]
    count = len(chunks)
    grads, bgrads = rest[5 : 5 + count], rest[5 + count :]

    b_all = jnp.concatenate([bown_keep, bown_send, *bgrads], axis=0)
    for bit in range(narrow.bit_length()):
        flipped = jnp.flip(b_all.reshape(-1, 2, 1 << bit, units), axis=1).reshape(b_all.shape)
        b_all = jnp.where((narrow_at * 2 + core) >> bit & 1, flipped, b_all)
    vec = jnp.concatenate([vec, b_all.reshape(-1, width)], axis=0)

    held = [add(own_keep, swap(own_send, core_mask))]
    held += [add(grads[2 * j], swap(grads[2 * j + 1], core_mask)) for j in range(narrow - 1)]
    if narrow == 2:
        top, mine, other = width // 2, *held
        ff_keep = jnp.where(core == 0, mine, jnp.concatenate([mine[:top], other[:top]], axis=0))
        ff_send = jnp.where(core == 0, other, jnp.concatenate([mine[top:], other[top:]], axis=0))
        gmix, ff_keep, ff_send = after(gmix, ff_keep, ff_send)
        ff_keep = add(ff_keep, swap(ff_send, narrow_masks[0], ff_used[0]))
        ff_left = ([ff_used[0]] + ff_used[1:], narrow_masks + ff_used[1:])
    else:
        gmix, held = after(gmix, held)
        for mask in reversed(narrow_masks):
            held = [add(held[j], swap(held[j + mask], mask)) for j in range(mask)]
        ff_keep, ff_left = held[0], ff_in

    dqkv, keep, send = attend_back(info, at_tables, qkv, prob, gmix, tokens_in, vec, dwout)
    keep, ff_keep = after(add(keep, swap(send, core_mask)), ff_keep)
    grad_tokens = first_back(info, dqkv, w_qkv, tokens_in, gres, g1)
    at_steps = scatters(at_order) + exchanges(at_rest) + gathers(at_order)
    ff_steps = scatters(ff_left) + exchanges(ff_rest) + gathers(ff_out)
    keep, ff_keep, grad_tokens = after(at_steps[0](keep), ff_steps[0](ff_keep), grad_tokens)
    at_steps, ff_steps = at_steps[1:], ff_steps[1:]
    shared = min(len(at_steps), len(ff_steps))
    for at_step, ff_step in zip(at_steps, ff_steps):
        keep, ff_keep = after(at_step(keep), ff_step(ff_keep))
    for ff_step in ff_steps[shared:]:
        ff_keep = ff_step(ff_keep)
    ff_other = swap(ff_keep, core_mask)
    for at_step in at_steps[shared : shared + 1]:
        keep, ff_other = after(at_step(keep), ff_other)
    ff_done = ffn_end(info, ff_out_tables, ff_keep, ff_other)
    for at_step in at_steps[shared + 1 :]:
        keep, ff_done = after(at_step(keep), ff_done)
    grad_w_up, grad_w_down = ff_done

    grad_w_qkv, grad_w_out, vec = attend_end(
        info, at_tables, keep, swap(keep, core_mask), w_qkv, g1, c1, SUMS + vec.shape[0]
    )
    b_sum = vec[SUMS + 8 :].reshape(narrow, 2 * units)
    grad_b_up = lax.dynamic_slice(b_sum, (narrow_at, 0), (1, 2 * units))[0]
    return (
        block_out,
        grad_tokens,
        vec[0],
        vec[1],
        grad_w_qkv,
        grad_w_out,
        vec[SUMS],
        vec[SUMS + 1],
        grad_w_up,
        grad_b_up,
        grad_w_down,
        vec[SUMS + 2],
    )


def solution(mesh):
    rows = P(("wide", "narrow"), None)
    in_specs = (
        rows, P(), P(), P(), P(), P(), P(), P(None, "narrow"), P("narrow"), P("narrow", None), P(), rows, rows, rows, rows,
    )
    out_specs = (
        rows, rows, P(), P(), P(), P(), P(), P(), P(None, "narrow"), P("narrow"), P("narrow", None), P(),
    )
    wide, narrow = mesh.shape["wide"], mesh.shape["narrow"]
    return jax.shard_map(
        functools.partial(local, wide, narrow), mesh=mesh, in_specs=in_specs, out_specs=out_specs, check_vma=False
    )
```

```python
import functools
import itertools

import jax
import jax.numpy as jnp
import numpy as np
from jax import lax
from jax.experimental import pallas as pl
from jax.experimental.pallas import tpu as pltpu
from jax.sharding import PartitionSpec as P

HEAD = 64
PAIR = 2 * HEAD
NORM_EPS = 1e-05
BF = jnp.bfloat16
F32 = jnp.float32
AXES = ("wide", "narrow")
LANES = 128
SUMS = 8
TILE = 16
TOKS = 512
VMEM_LIMIT = 32 * 1024 * 1024


def mm(a, b):
    return lax.dot_general(a, b, (((1,), (0,)), ((), ())), preferred_element_type=F32)


def mm_nt(a, b):
    return lax.dot_general(a, b, (((1,), (1,)), ((), ())), preferred_element_type=F32)


def mm_tn(a, b):
    return lax.dot_general(a, b, (((0,), (0,)), ((), ())), preferred_element_type=F32)


def near(*values):
    return tuple(pltpu.with_memory_space_constraint(v, pltpu.VMEM) for v in values)


def far(*values):
    return tuple(pltpu.with_memory_space_constraint(v, pltpu.HBM) for v in values)


def whole(*shape):
    return pl.BlockSpec(shape, lambda *_: (0,) * len(shape))


def rows_of(width, toks=TOKS):
    return pl.BlockSpec((toks, width), lambda i, *_: (i, 0))


def call(kernel, name, grid, in_specs, out_specs, out_shape, scratch, info, args):
    return pl.pallas_call(
        kernel,
        grid_spec=pltpu.PrefetchScalarGridSpec(
            num_scalar_prefetch=1, grid=grid, in_specs=in_specs, out_specs=out_specs, scratch_shapes=scratch
        ),
        out_shape=out_shape,
        compiler_params=pltpu.CompilerParams(vmem_limit_bytes=VMEM_LIMIT),
        cost_estimate=pl.CostEstimate(flops=1000, bytes_accessed=1000, transcendentals=0),
        name=name,
    )(info, *args)


def unit_parts(rows):
    mean = jnp.mean(rows, axis=-1, keepdims=True)
    centered = rows - mean
    inv = lax.rsqrt(jnp.mean(centered * centered, axis=-1, keepdims=True) + NORM_EPS)
    return centered * inv, inv


def norm_back(incoming, unit, inv, gain):
    scaled = incoming * gain
    return inv * (
        scaled
        - jnp.mean(scaled, axis=-1, keepdims=True)
        - unit * jnp.mean(scaled * unit, axis=-1, keepdims=True)
    )


def gelu_pair(x):
    cdf = 0.5 * (1.0 + lax.erf(x * 0.7071067811865476))
    return x * cdf, cdf + x * jnp.exp(-0.5 * x * x) * 0.3989422804014327


def by_head(block):
    lane = lax.broadcasted_iota(jnp.int32, block.shape, 1)
    zero = jnp.zeros_like(block)
    first = lane < HEAD
    return jnp.concatenate([jnp.where(first, block, zero), jnp.where(first, zero, block)], axis=0)


def places(order, blocks):
    bits = blocks.bit_length() - 1
    table = []
    for place in range(blocks):
        owner = 0
        for step in range(bits):
            if place >> (bits - 1 - step) & 1:
                owner ^= order[step]
        table.append(owner)
    return table


def block_at(place, tables, core, own):
    first, second = tables[0][place], tables[1][place]
    if first == second:
        return own ^ first
    return own ^ jnp.where(core == 0, first, second)


def permuted(dst_ref, acc_ref, chunk, tables, core, own):
    blocks = len(tables[0])
    size = dst_ref.shape[0] // blocks
    for place in range(blocks):
        block = block_at(place, tables, core, own)
        rows = pl.ds(pl.multiple_of(block * size, size), size)
        dst_ref[place * size : (place + 1) * size, :] = acc_ref[chunk, rows, :].astype(dst_ref.dtype)


def attend_kernel(
    info_ref, tok_ref, g1_ref, c1_ref, wqkv_ref, wout_ref, g2_ref, c2_ref, seg_ref, step_ref, pad_ref,
    qkv_ref, prob_ref, mixed_ref, res_ref, second_ref,
):
    slots = seg_ref.shape[1]
    toks, width = tok_ref.shape
    rows = toks // slots
    at = pl.program_id(0)
    tokens = tok_ref[...].astype(F32)
    unit, _ = unit_parts(tokens)
    normed = (unit * g1_ref[...] + c1_ref[...]).astype(BF)
    qkv_ref[...] = mm(normed, wqkv_ref[...]).astype(BF)
    q_id = lax.broadcasted_iota(jnp.int32, (slots, slots), 0)
    k_id = lax.broadcasted_iota(jnp.int32, (slots, slots), 1)
    eye = q_id == k_id
    pairs = width // PAIR
    units = [(r, p) for r in range(rows) for p in range(pairs)]

    def part(r, p, which):
        return qkv_ref[r * slots : (r + 1) * slots, which * width + p * PAIR : which * width + (p + 1) * PAIR]

    masks = []
    for r in range(rows):
        here = pl.ds(at * rows + r, 1)
        seg = jnp.broadcast_to(seg_ref[here, :].astype(F32), (slots, slots))
        step = jnp.broadcast_to(step_ref[here, :].astype(F32), (slots, slots))
        live = jnp.broadcast_to(pad_ref[here, :], (slots, slots)) == 0
        masks.append(((seg == seg.T) & (step <= step.T) & live) | eye)
    scores = [mm_nt(part(r, p, 0), by_head(part(r, p, 1) * HEAD ** (-0.5))) for r, p in units]
    probs = []
    for (r, p), score in zip(units, scores):
        halves = []
        for half in (score[:, :slots], score[:, slots:]):
            half = jnp.where(masks[r], half, -1e30)
            weight = jnp.exp(half - jnp.max(half, axis=-1, keepdims=True))
            total = jnp.sum(weight, axis=-1, keepdims=True)
            halves.append((weight * (1.0 / total)).astype(BF))
        probs.append(jnp.concatenate(halves, axis=1))
    for (r, p), prob in zip(units, probs):
        prob_ref[r, p] = prob
        mixed_ref[r * slots : (r + 1) * slots, p * PAIR : (p + 1) * PAIR] = mm(prob, by_head(part(r, p, 2))).astype(BF)
    residual = tokens + mm(mixed_ref[...], wout_ref[...])
    res_ref[...] = residual
    unit, _ = unit_parts(residual)
    second_ref[...] = (unit * g2_ref[...] + c2_ref[...]).astype(BF)


def attend(info, tokens, g1, c1, wqkv, wout, g2, c2, seg, step, pad):
    n, width = tokens.shape
    rows, slots = seg.shape
    per, pairs = TOKS // slots, width // PAIR
    return call(
        attend_kernel,
        "attend",
        (n // TOKS,),
        [rows_of(width), whole(1, width), whole(1, width), whole(*wqkv.shape), whole(*wout.shape)]
        + [whole(1, width)] * 2
        + [whole(rows, slots)] * 3,
        [
            rows_of(3 * width),
            pl.BlockSpec((per, pairs, slots, 2 * slots), lambda i, *_: (i, 0, 0, 0)),
            rows_of(width),
            rows_of(width),
            rows_of(width),
        ],
        [
            pltpu.HBM((n, 3 * width), BF),
            pltpu.HBM((rows, pairs, slots, 2 * slots), BF),
            pltpu.HBM((n, width), BF),
            pltpu.HBM((n, width), F32),
            pltpu.VMEM((n, width), BF),
        ],
        [],
        info,
        far(tokens, g1, c1) + (wqkv, wout) + far(g2, c2, seg, step, pad),
    )


def pack_kernel(info_ref, up_ref, bias_ref, down_ref, up_out, down_out):
    width = up_ref.shape[0]
    up_out[:width, :] = up_ref[...]
    up_out[width:, :] = jnp.broadcast_to(bias_ref[...], (TILE, bias_ref.shape[1]))
    down_out[...] = down_ref[...]


def pack(info, up, bias, down):
    width, units = up.shape[0], up.shape[1] // 2
    return call(
        pack_kernel,
        "pack",
        (1,),
        [
            pl.BlockSpec((width, units), lambda t, info: (0, info[0])),
            pl.BlockSpec((1, units), lambda t, info: (0, info[0])),
            pl.BlockSpec((units, width), lambda t, info: (info[0], 0)),
        ],
        [whole(width + TILE, units), whole(units, width)],
        [jax.ShapeDtypeStruct((width + TILE, units), BF), jax.ShapeDtypeStruct((units, width), BF)],
        [],
        info,
        far(up, bias, down),
    )


def ffn_block(sec, dy, up, bias, down, acc_ref, bacc_ref):
    pre = mm(sec, up) + bias
    dhid = mm_nt(dy, down)
    hid, slope = gelu_pair(pre)
    hid = hid.astype(BF)
    dpre = (dhid * slope).astype(BF)
    grad_up = mm(sec.T, dpre)
    grad_down = mm(dy.T, hid)
    sums = jnp.sum(dpre.astype(F32), axis=0, keepdims=True)
    chunks, _, double = acc_ref.shape
    units = double // 2
    for i in range(chunks):
        cols = slice(i * units, (i + 1) * units)
        acc_ref[i, :, :units] += grad_up[:, cols]
        acc_ref[i, :, units:] += grad_down[:, cols]
        bacc_ref[i : i + 1, :] += sums[:, cols]
    return mm(hid, down), mm_nt(dpre, up)


def ffn_own_kernel(
    tables, info_ref, sec_ref, dy_ref, up_ref, bias_ref, down_ref, out_ref, dsec_ref, keep_ref, send_ref, bias_out, acc_ref
):
    at, last = pl.program_id(0), pl.num_programs(0) - 1

    @pl.when(at == 0)
    def _():
        acc_ref[...] = jnp.zeros_like(acc_ref)
        bias_out[...] = jnp.zeros_like(bias_out)

    out, dsec = ffn_block(
        sec_ref[...], dy_ref[...], up_ref[...], bias_ref[...].astype(F32), down_ref[...], acc_ref, bias_out
    )
    out_ref[...] = out
    dsec_ref[...] = dsec

    @pl.when(at == last)
    def _():
        core, own, other = info_ref[0], info_ref[1], info_ref[2]
        permuted(keep_ref, acc_ref, core, tables, core, own)
        permuted(send_ref, acc_ref, core ^ 1, tables, core ^ 1, other)


def ffn_own(info, tables, second, dy, up, bias, down):
    n, width = second.shape
    units = up.shape[1] // 2
    return call(
        functools.partial(ffn_own_kernel, tables),
        "ffn_own",
        (n // TOKS,),
        [rows_of(width), rows_of(width), whole(*up.shape), whole(*bias.shape), whole(*down.shape)],
        [rows_of(width)] * 2 + [whole(width, 2 * units)] * 2 + [whole(2, units)],
        [pltpu.VMEM((n, width), F32)] * 2
        + [jax.ShapeDtypeStruct((width, 2 * units), BF)] * 2
        + [jax.ShapeDtypeStruct((2, units), F32)],
        [pltpu.VMEM((2, width, 2 * units), F32)],
        info,
        near(second) + far(dy) + (up,) + far(bias) + (down,),
    )


def ffn_rest_kernel(
    tables, count, info_ref, sec_ref, dy_ref, out_part_ref, dsec_part_ref, res_ref, mixed_ref, bdown_ref, g2_ref, wout_ref, *refs
):
    ups, downs = refs[:count], refs[count : 2 * count]
    block_ref, gres_ref, gmix_ref, vec_ref, dwout_ref, bias_out = refs[2 * count : 2 * count + 6]
    grads = refs[2 * count + 6 : 3 * count + 6]
    acc_ref, up_ref, bias_ref, down_ref = refs[3 * count + 6 :]
    at, last = pl.program_id(0), pl.num_programs(0) - 1
    width, units = wout_ref.shape[0], ups[0].shape[1]

    @pl.when(at == 0)
    def _():
        for ref in (acc_ref, bias_out, vec_ref, dwout_ref):
            ref[...] = jnp.zeros_like(ref)
        for i in range(count):
            cols = slice(i * units, (i + 1) * units)
            up_ref[:, cols] = ups[i][:width, :]
            bias_ref[:, cols] = ups[i][width : width + TILE, :].astype(F32)[:8]
            down_ref[cols, :] = downs[i][...]

    dy = dy_ref[...]
    out, dsec = ffn_block(sec_ref[...], dy, up_ref[...], bias_ref[0:1, :], down_ref[...], acc_ref, bias_out)
    out += out_part_ref[...]
    dsec += dsec_part_ref[...]
    residual = res_ref[...]
    block_ref[...] = (residual + (out + bdown_ref[...])).astype(BF)
    dy32 = dy.astype(F32)
    unit, inv = unit_parts(residual)
    vec_ref[0:1, :] += jnp.sum(dsec * unit, axis=0, keepdims=True)
    vec_ref[1:2, :] += jnp.sum(dsec, axis=0, keepdims=True)
    vec_ref[2:3, :] += jnp.sum(dy32, axis=0, keepdims=True)
    gres = dy32 + norm_back(dsec, unit, inv, g2_ref[...])
    gres_ref[...] = gres
    branch = gres.astype(BF)
    gmix_ref[...] = mm_nt(branch, wout_ref[...]).astype(BF)
    dwout_ref[...] += mm_tn(mixed_ref[...], branch)

    @pl.when(at == last)
    def _():
        core, own, other = info_ref[0], info_ref[1], info_ref[2]
        for i in range(count):
            permuted(grads[i], acc_ref, i, tables, core ^ (i % 2), other if i % 2 else own)


def ffn_rest(info, tables, second, dy, out_part, dsec_part, residual, mixed, bdown, g2, wout, chunks):
    n, width = second.shape
    count = len(chunks)
    units = chunks[0][0].shape[1]
    return call(
        functools.partial(ffn_rest_kernel, tables, count),
        "ffn_rest",
        (n // TOKS,),
        [rows_of(width)] * 6
        + [whole(1, width)] * 2
        + [whole(width, width)]
        + [whole(width + TILE, units)] * count
        + [whole(units, width)] * count,
        [rows_of(width)] * 3
        + [whole(8, width), whole(width, width), whole(count, units)]
        + [whole(width, 2 * units)] * count,
        [
            jax.ShapeDtypeStruct((n, width), BF),
            pltpu.HBM((n, width), F32),
            pltpu.HBM((n, width), BF),
            jax.ShapeDtypeStruct((8, width), F32),
            pltpu.HBM((width, width), F32),
            jax.ShapeDtypeStruct((count, units), F32),
        ]
        + [jax.ShapeDtypeStruct((width, 2 * units), BF)] * count,
        [
            pltpu.VMEM((count, width, 2 * units), F32),
            pltpu.VMEM((width, count * units), BF),
            pltpu.VMEM((8, count * units), F32),
            pltpu.VMEM((count * units, width), BF),
        ],
        info,
        near(second)
        + far(dy)
        + near(out_part, dsec_part)
        + far(residual, mixed, bdown, g2)
        + (wout,)
        + tuple(c[0] for c in chunks)
        + tuple(c[1] for c in chunks),
    )


def mix_kernel(info_ref, mine_ref, other_ref, got_ref, keep_ref, send_ref):
    top = mine_ref.shape[0] // 2
    both = (other_ref[...].astype(F32) + got_ref[...].astype(F32)).astype(BF)
    keep_ref[:top, :] = mine_ref[:top, :]

    @pl.when(info_ref[0] == 0)
    def _():
        keep_ref[top:, :] = mine_ref[top:, :]
        send_ref[...] = both

    @pl.when(info_ref[0] == 1)
    def _():
        keep_ref[top:, :] = both[:top, :]
        send_ref[:top, :] = mine_ref[top:, :]
        send_ref[top:, :] = both[top:, :]


def mix(info, mine, other, got):
    return call(
        mix_kernel,
        "mix",
        (1,),
        [whole(*mine.shape)] * 3,
        [whole(*mine.shape)] * 2,
        [jax.ShapeDtypeStruct(mine.shape, BF)] * 2,
        [],
        info,
        (mine, other, got),
    )


def attend_back_kernel(
    tables, info_ref, qkv_ref, prob_ref, gmix_ref, tok_ref, vec_ref, dwout_ref, grad_ref, dw_keep_ref, dw_send_ref,
    dqkv_ref, acc_ref, row_ref,
):
    at, last = pl.program_id(0), pl.num_programs(0) - 1
    toks, width = tok_ref.shape
    rows, pairs, slots, _ = prob_ref.shape

    @pl.when(at == 0)
    def _():
        acc_ref[:, : 3 * width] = jnp.zeros((width, 3 * width), F32)
        acc_ref[:, 3 * width : 4 * width] = dwout_ref[...]
        row_ref[...] = jnp.zeros_like(row_ref)
        row_ref[SUMS : SUMS + vec_ref.shape[0], :] = vec_ref[...]

    scale = HEAD ** (-0.5)
    units = [(r, p) for r in range(rows) for p in range(pairs)]

    def place(r, p, which):
        return (slice(r * slots, (r + 1) * slots), slice(which * width + p * PAIR, which * width + (p + 1) * PAIR))

    grads = [gmix_ref[place(r, p, 0)] for r, p in units]
    dprobs = [mm_nt(g, by_head(qkv_ref[place(r, p, 2)])) for (r, p), g in zip(units, grads)]
    for (r, p), g in zip(units, grads):
        prob = prob_ref[r, p]
        stacked = jnp.concatenate([prob[:, :slots], prob[:, slots:]], axis=0)
        dqkv_ref[place(r, p, 2)] = mm_tn(stacked, by_head(g)).astype(BF)
    dscores = []
    for (r, p), dprob in zip(units, dprobs):
        p32 = prob_ref[r, p].astype(F32)
        prod = p32 * dprob
        first = jnp.sum(prod[:, :slots], axis=-1, keepdims=True)
        second = jnp.sum(prod[:, slots:], axis=-1, keepdims=True)
        dscores.append((
            (p32[:, :slots] * (dprob[:, :slots] - first)).astype(BF),
            (p32[:, slots:] * (dprob[:, slots:] - second)).astype(BF),
        ))
    for (r, p), ds in zip(units, dscores):
        k = qkv_ref[place(r, p, 1)]
        dqkv_ref[place(r, p, 0)] = mm(jnp.concatenate(ds, axis=1), by_head(k * scale)).astype(BF)
    for (r, p), ds in zip(units, dscores):
        q = qkv_ref[place(r, p, 0)]
        dqkv_ref[place(r, p, 1)] = mm_tn(jnp.concatenate(ds, axis=0), by_head(q * scale)).astype(BF)
    unit, _ = unit_parts(tok_ref[...].astype(F32))
    acc_ref[:, : 3 * width] += mm_tn(unit.astype(BF), dqkv_ref[...])
    grad_ref[...] = dqkv_ref[...]
    for i in range(3):
        part = dqkv_ref[:, i * width : (i + 1) * width].astype(F32)
        row_ref[i : i + 1, :] += jnp.sum(part, axis=0, keepdims=True)

    @pl.when(at == last)
    def _():
        core, own, other = info_ref[0], info_ref[3], info_ref[4]
        acc_ref[:, 4 * width :] = row_ref[...].T
        half = width // 2
        size = width // len(tables[0])
        for place in range(len(tables[0])):
            dst = dw_keep_ref if place * size < half else dw_send_ref
            block = block_at(place, tables, core, own if place * size < half else other)
            rows_at = pl.ds(pl.multiple_of(block * size, size), size)
            to = place * size % half
            dst[to : to + size, :] = acc_ref[rows_at, :].astype(BF)


def attend_back(info, tables, qkv, prob, gmix, tokens, vec, dwout):
    n, width = tokens.shape
    rows, pairs, slots, _ = prob.shape
    per = TOKS // slots
    return call(
        functools.partial(attend_back_kernel, tables),
        "attend_back",
        (n // TOKS,),
        [
            rows_of(3 * width),
            pl.BlockSpec((per, pairs, slots, 2 * slots), lambda i, *_: (i, 0, 0, 0)),
            rows_of(width),
            rows_of(width),
            whole(*vec.shape),
            whole(width, width),
        ],
        [rows_of(3 * width)] + [whole(width // 2, 4 * width + LANES)] * 2,
        [pltpu.VMEM((n, 3 * width), BF)] + [jax.ShapeDtypeStruct((width // 2, 4 * width + LANES), BF)] * 2,
        [
            pltpu.VMEM((TOKS, 3 * width), BF),
            pltpu.VMEM((width, 4 * width + LANES), F32),
            pltpu.VMEM((LANES, width), F32),
        ],
        info,
        far(qkv, prob, gmix, tokens, vec, dwout),
    )


def first_back_kernel(info_ref, dqkv_ref, wqkv_ref, tok_ref, gres_ref, g1_ref, out_ref):
    dnormed = mm_nt(dqkv_ref[...], wqkv_ref[...])
    unit, inv = unit_parts(tok_ref[...].astype(F32))
    out_ref[...] = gres_ref[...] + norm_back(dnormed, unit, inv, g1_ref[...])


def first_back(info, dqkv, wqkv, tokens, gres, g1):
    n, width = tokens.shape
    return call(
        first_back_kernel,
        "first_back",
        (n // TOKS,),
        [rows_of(3 * width), whole(*wqkv.shape), rows_of(width), rows_of(width), whole(1, width)],
        rows_of(width),
        jax.ShapeDtypeStruct((n, width), F32),
        [],
        info,
        near(dqkv) + (wqkv,) + far(tokens, gres, g1),
    )


def ffn_end_kernel(tables, info_ref, keep_ref, other_ref, up_ref, down_ref, full_ref):
    core = info_ref[0]
    units = up_ref.shape[1]
    blocks = len(tables[0])
    size = keep_ref.shape[0] // blocks

    def lay(src_ref, whose, base):
        for place in range(blocks):
            block = block_at(place, tables, whose, base)
            rows = pl.ds(pl.multiple_of(block * size, size), size)
            part = src_ref[place * size : (place + 1) * size, :].astype(F32)
            up_ref[rows, :] = part[:, :units]
            full_ref[rows, :] = part[:, units:]
        down_ref[...] = full_ref[...].T

    @pl.when(pl.program_id(0) == 0)
    def _():
        lay(keep_ref, core, info_ref[1])

    @pl.when(pl.program_id(0) == 1)
    def _():
        lay(other_ref, core ^ 1, info_ref[2])


def ffn_end(info, tables, keep, other):
    width, double = keep.shape
    units = double // 2
    return call(
        functools.partial(ffn_end_kernel, tables),
        "ffn_end",
        (2,),
        [whole(width, double)] * 2,
        [
            pl.BlockSpec((width, units), lambda i, info: (0, info[0] ^ i)),
            pl.BlockSpec((units, width), lambda i, info: (info[0] ^ i, 0)),
        ],
        [jax.ShapeDtypeStruct((width, double), F32), jax.ShapeDtypeStruct((double, width), F32)],
        [pltpu.VMEM((width, units), F32)],
        info,
        (keep, other),
    )


def attend_end_kernel(
    tables, shares, info_ref, keep_ref, other_ref, w_ref, g1_ref, c1_ref, qkv_hbm, out_hbm, *refs
):
    vec_refs, (qkv_ref, out_ref, col_ref, row_ref, sems) = refs[:6], refs[6:]
    core, own, away = info_ref[0], info_ref[3], info_ref[4]
    width = out_ref.shape[1]
    blocks = len(tables[0])
    size = out_ref.shape[0] // blocks
    half = out_ref.shape[0] // 2
    spots = []
    for place in range(blocks):
        mine = place * size < half
        block = block_at(place, tables, core, own if mine else away)
        at = place * size % half
        spots.append((keep_ref if mine else other_ref, slice(at, at + size), pl.multiple_of(block * size, size)))
    copies = []
    for i, (src, rows, to) in enumerate(spots):
        to = pl.ds(to, size)
        col_ref[to, :] = src[rows, 4 * width :].astype(F32)
        out_ref[rows if src is keep_ref else slice(rows.start + half, rows.stop + half), :] = src[
            rows, 3 * width : 4 * width
        ].astype(F32)
    for i, (src, rows, to) in enumerate(spots):
        rows = rows if src is keep_ref else slice(rows.start + half, rows.stop + half)
        copies.append(pltpu.make_async_copy(out_ref.at[rows, :], out_hbm.at[pl.ds(to, size), :], sems.at[i]))
        copies[-1].start()
    vec = col_ref[...].T
    row_ref[...] = vec
    wide_row = jnp.concatenate([vec[i : i + 1, :] for i in range(3)], axis=1)
    pair = jnp.concatenate([g1_ref[...], c1_ref[...], jnp.zeros((LANES - 2, width), F32)], axis=0).T
    col_ref[...] = pair
    lane = lax.broadcasted_iota(jnp.int32, (size, LANES), 1)
    for i, (src, rows, to) in enumerate(spots):
        here = pl.ds(to, size)
        gain_bias = col_ref[here, :]
        gain, bias = gain_bias[:, 0:1], gain_bias[:, 1:2]
        sums = src[rows, : 3 * width].astype(F32)
        w = w_ref[here, :].astype(F32)
        rows = rows if src is keep_ref else slice(rows.start + half, rows.stop + half)
        qkv_ref[rows, :] = gain * sums + bias * wide_row
        copies.append(pltpu.make_async_copy(qkv_ref.at[rows, :], qkv_hbm.at[here, :], sems.at[blocks + i]))
        copies[-1].start()
        d_gain = jnp.sum(w * sums, axis=1, keepdims=True)
        d_bias = jnp.sum(w * wide_row, axis=1, keepdims=True)
        col_ref[here, :] = jnp.where(lane == 0, d_gain, jnp.where(lane == 1, d_bias, 0.0))
    both = col_ref[...].T
    flat = lambda row: row.reshape(row.shape[1])
    vec_refs[0][...] = flat(both[0:1, :])
    vec_refs[1][...] = flat(both[1:2, :])
    for i in range(3):
        vec_refs[2 + i][...] = flat(vec[SUMS + i : SUMS + i + 1, :])
    units = vec_refs[5].shape[0]
    if units >= width:
        first = SUMS + 8 + info_ref[5] * (units // width)
        for i in range(units // width):
            vec_refs[5][i * width : (i + 1) * width] = flat(row_ref[pl.ds(first + i, 1), :])
    else:
        row = row_ref[pl.ds(SUMS + 8 + info_ref[5] // shares, 1), :]
        share = row[:, :units]
        for i in range(1, shares):
            share = jnp.where(info_ref[5] % shares == i, row[:, i * units : (i + 1) * units], share)
        vec_refs[5][...] = flat(share)
    for copy in copies:
        copy.wait()


def attend_end(info, tables, keep, other, w_qkv, g1, c1, units):
    rows, width = 2 * keep.shape[0], w_qkv.shape[0]
    blocks = len(tables[0])
    return call(
        functools.partial(attend_end_kernel, tables, max(1, width // units)),
        "attend_end",
        (1,),
        [whole(*keep.shape)] * 2 + [whole(*w_qkv.shape)] + [whole(1, width)] * 2,
        [pl.BlockSpec(memory_space=pl.ANY)] * 2 + [whole(width)] * 5 + [whole(units)],
        [jax.ShapeDtypeStruct((rows, 3 * width), F32), jax.ShapeDtypeStruct((rows, width), F32)]
        + [jax.ShapeDtypeStruct((width,), F32)] * 5
        + [jax.ShapeDtypeStruct((units,), F32)],
        [
            pltpu.VMEM((rows, 3 * width), F32),
            pltpu.VMEM((rows, width), F32),
            pltpu.VMEM((rows, LANES), F32),
            pltpu.VMEM((LANES, width), F32),
            pltpu.SemaphoreType.DMA((2 * blocks,)),
        ],
        info,
        (keep, other, w_qkv) + far(g1, c1),
    )


def local(
    wide, narrow, tokens_in, ln1_gain, ln1_bias, w_qkv, w_out, ln2_gain, ln2_bias, w_up, b_up, w_down, b_down, segment_ids,
    step_ids, pad_mask, cotangent,
):
    width = tokens_in.shape[1]
    units = w_up.shape[1] // 2
    core_mask = narrow
    narrow_masks = [1 << b for b in range(narrow.bit_length() - 1)]
    wide_masks = [narrow << b for b in range(1, wide.bit_length() - 1)]

    def swap(value, first, second=None):
        masks = (first, first if second is None else second)
        pairs = [(i, i ^ masks[i // narrow & 1]) for i in range(wide * narrow)]
        return lax.ppermute(value, AXES, pairs)

    def add(a, b):
        return (a.astype(F32) + b.astype(F32)).astype(a.dtype)

    def after(*values):
        return lax.optimization_barrier(values)

    def scatters(order):
        def step(first, second, value):
            half = value.shape[0] // 2
            return add(value[:half], swap(value[half:], first, second))

        return [functools.partial(step, *pair) for pair in zip(*order)]

    def exchanges(order):
        def step(first, second, value):
            return add(value, swap(value, first, second))

        return [functools.partial(step, *pair) for pair in zip(*order)]

    def gathers(order):
        def step(first, second, value):
            return jnp.concatenate([value, swap(value, first, second)], axis=0)

        return [functools.partial(step, *pair) for pair in reversed(list(zip(*order)))]

    wide_at, narrow_at = lax.axis_index("wide"), lax.axis_index("narrow")
    core = wide_at & 1
    flat = wide_at * narrow + narrow_at

    def named(owner, used):
        return sum((1 << b) for b, m in enumerate(used) if owner & m)

    def block_of(used):
        return sum(((flat & m) != 0).astype(jnp.int32) << b for b, m in enumerate(used))

    def split_at(pair, count):
        return tuple(o[:count] for o in pair), tuple(o[count:] for o in pair)

    def by_core(values):
        return jnp.where(core == 0, values[0], values[1]), jnp.where(core == 0, values[1], values[0])

    if narrow == 2 and len(wide_masks) == 3:
        y, low, high = wide_masks
        ff_in, ff_rest = ([y, high], [y, low]), ([low], [high])
        ff_out = ([y, high], [low, y])
        at_order = ([1, y, low], [y, 1, high])
        at_rest = ([high], [low])
    else:
        ff_in, ff_rest = split_at((wide_masks, wide_masks), min(len(wide_masks) - 1, (width // TILE).bit_length() - 1))
        ff_out = ff_in
        masks = narrow_masks + wide_masks
        at_order, at_rest = split_at((masks, masks), min(len(masks) - 1, (width // TILE // 2).bit_length() - 1))
    ff_used = tuple(sorted(o) for o in ff_in)
    ff_in_tables, ff_out_tables = (
        tuple([named(owner, ff_used[c]) for owner in places(pair[c], 1 << len(ff_used[c]))] for c in range(2))
        for pair in (ff_in, ff_out)
    )
    at_used = tuple([core_mask] + sorted(o) for o in at_order)
    at_places = [places(o, 1 << len(o)) for o in at_order]
    at_tables = tuple(
        [named(o, at_used[c]) for o in at_places[c]]
        + [named(o ^ core_mask, at_used[1 - c]) for o in at_places[1 - c]]
        for c in range(2)
    )
    ff_block = by_core([block_of(used) for used in ff_used])
    at_block = by_core([block_of(used) for used in at_used])
    info = jnp.stack([core, *ff_block, *at_block, narrow_at]).astype(jnp.int32)

    packed, tokens_in = after(pack(info, w_up, b_up[None], w_down), tokens_in)
    fetched = [packed]
    for mask in narrow_masks:
        fetched = fetched + [(swap(u, mask), swap(d, mask)) for u, d in fetched]

    row = lambda v: v[None].astype(F32)
    g1, c1, g2 = row(ln1_gain), row(ln1_bias), row(ln2_gain)
    qkv, prob, mixed, residual, second = attend(
        info, tokens_in, g1, c1, w_qkv, w_out, g2, row(ln2_bias), segment_ids, step_ids, pad_mask
    )
    out_part, dsec_part, own_keep, own_send, bias_own = ffn_own(
        info, ff_in_tables, second, cotangent, w_up, b_up[None], w_down
    )
    own_send, fetched = after(own_send, fetched)
    chunks = []
    for up, down in fetched[1:]:
        chunks += [(up, down), (swap(up, core_mask), swap(down, core_mask))]
    own_keep, second = after(add(own_keep, swap(own_send, core_mask)), second)
    rest = ffn_rest(
        info, ff_in_tables, second, cotangent, out_part, dsec_part, residual, mixed, row(b_down), g2, w_out, chunks
    )
    block_out, gres, gmix, vec, dwout, bias_rest = rest[:6]
    grads = rest[6:]

    b_rest = bias_rest.reshape(-1, 2, units)
    b_rest = jnp.where(core == 0, b_rest, jnp.flip(b_rest, axis=1))
    b_all = jnp.concatenate([bias_own[None], b_rest], axis=0)
    for bit in range(narrow.bit_length() - 1):
        flipped = jnp.flip(b_all.reshape(-1, 2, (1 << bit) * 2, units), axis=1).reshape(b_all.shape)
        b_all = jnp.where(narrow_at >> bit & 1, flipped, b_all)
    vec = jnp.concatenate([vec, b_all.reshape(-1, width)], axis=0)

    got = [swap(grads[2 * j + 1], core_mask) for j in range(narrow - 1)]
    if narrow == 2 and len(wide_masks) == 3:
        ff_keep, ff_send = mix(info, own_keep, grads[0], got[0])
        gmix, ff_keep, ff_send = after(gmix, ff_keep, ff_send)
        ff_keep = add(ff_keep, swap(ff_send, 1, y))
        ff_left = ([y, high], [1, low])
    else:
        held = [own_keep] + [add(grads[2 * j], got[j]) for j in range(narrow - 1)]
        gmix, held = after(gmix, held)
        for mask in reversed(narrow_masks):
            held = [add(held[j], swap(held[j + mask], mask)) for j in range(mask)]
        ff_keep, ff_left = held[0], ff_in

    dqkv, keep, send = attend_back(info, at_tables, qkv, prob, gmix, tokens_in, vec, dwout)
    keep, ff_keep = after(add(keep, swap(send, core_mask)), ff_keep)
    grad_tokens = first_back(info, dqkv, w_qkv, tokens_in, gres, g1)
    at_steps = scatters(at_order) + exchanges(at_rest) + gathers(at_order)
    ff_steps = scatters(ff_left) + exchanges(ff_rest) + gathers(ff_out)
    keep, ff_keep, grad_tokens = after(at_steps[0](keep), ff_steps[0](ff_keep), grad_tokens)
    at_steps, ff_steps = at_steps[1:], ff_steps[1:]
    shared = min(len(at_steps), len(ff_steps))
    for at_step, ff_step in zip(at_steps, ff_steps):
        keep, ff_keep = after(at_step(keep), ff_step(ff_keep))
    for ff_step in ff_steps[shared:]:
        ff_keep = ff_step(ff_keep)
    ff_other = swap(ff_keep, core_mask)
    for at_step in at_steps[shared : shared + 1]:
        keep, ff_other = after(at_step(keep), ff_other)
    ff_done = ffn_end(info, ff_out_tables, ff_keep, ff_other)
    for at_step in at_steps[shared + 1 :]:
        keep, ff_done = after(at_step(keep), ff_done)
    grad_w_up, grad_w_down = ff_done

    grad_w_qkv, grad_w_out, d_gain1, d_bias1, d_gain2, d_bias2, d_bdown, grad_b_up = attend_end(
        info, at_tables, keep, swap(keep, core_mask), w_qkv, g1, c1, 2 * units
    )
    return (
        block_out, grad_tokens, d_gain1, d_bias1, grad_w_qkv, grad_w_out, d_gain2, d_bias2, grad_w_up, grad_b_up, grad_w_down,
        d_bdown,
    )


def solution(mesh):
    rows = P(("wide", "narrow"), None)
    in_specs = (
        rows, P(), P(), P(), P(), P(), P(), P(None, "narrow"), P("narrow"), P("narrow", None), P(), rows, rows, rows, rows,
    )
    out_specs = (
        rows, rows, P(), P(), P(), P(), P(), P(), P(None, "narrow"), P("narrow"), P("narrow", None), P(),
    )
    wide, narrow = mesh.shape["wide"], mesh.shape["narrow"]
    return jax.shard_map(
        functools.partial(local, wide, narrow), mesh=mesh, in_specs=in_specs, out_specs=out_specs, check_vma=False
    )
```

```python
import functools
import itertools

import jax
import jax.numpy as jnp
import numpy as np
from jax import lax
from jax.experimental import pallas as pl
from jax.experimental.pallas import tpu as pltpu
from jax.sharding import PartitionSpec as P

HEAD = 64
PAIR = 2 * HEAD
NORM_EPS = 1e-05
BF = jnp.bfloat16
F32 = jnp.float32
AXES = ("wide", "narrow")
LANES = 128
SUMS = 8
TILE = 16
TOKS = 512
VMEM_LIMIT = 32 * 1024 * 1024


def mm(a, b):
    return lax.dot_general(a, b, (((1,), (0,)), ((), ())), preferred_element_type=F32)


def mm_nt(a, b):
    return lax.dot_general(a, b, (((1,), (1,)), ((), ())), preferred_element_type=F32)


def mm_tn(a, b):
    return lax.dot_general(a, b, (((0,), (0,)), ((), ())), preferred_element_type=F32)


def near(*values):
    return tuple(pltpu.with_memory_space_constraint(v, pltpu.VMEM) for v in values)


def far(*values):
    return tuple(pltpu.with_memory_space_constraint(v, pltpu.HBM) for v in values)


def whole(*shape):
    return pl.BlockSpec(shape, lambda *_: (0,) * len(shape))


def rows_of(width, toks=TOKS):
    return pl.BlockSpec((toks, width), lambda i, *_: (i, 0))


def call(kernel, name, grid, in_specs, out_specs, out_shape, scratch, info, args):
    return pl.pallas_call(
        kernel,
        grid_spec=pltpu.PrefetchScalarGridSpec(
            num_scalar_prefetch=1, grid=grid, in_specs=in_specs, out_specs=out_specs, scratch_shapes=scratch
        ),
        out_shape=out_shape,
        compiler_params=pltpu.CompilerParams(vmem_limit_bytes=VMEM_LIMIT),
        cost_estimate=pl.CostEstimate(flops=1000, bytes_accessed=1000, transcendentals=0),
        name=name,
    )(info, *args)


def unit_parts(rows):
    mean = jnp.mean(rows, axis=-1, keepdims=True)
    centered = rows - mean
    inv = lax.rsqrt(jnp.mean(centered * centered, axis=-1, keepdims=True) + NORM_EPS)
    return centered * inv, inv


def norm_back(incoming, unit, inv, gain):
    scaled = incoming * gain
    return inv * (
        scaled
        - jnp.mean(scaled, axis=-1, keepdims=True)
        - unit * jnp.mean(scaled * unit, axis=-1, keepdims=True)
    )


def gelu_pair(x):
    cdf = 0.5 * (1.0 + lax.erf(x * 0.7071067811865476))
    return x * cdf, cdf + x * jnp.exp(-0.5 * x * x) * 0.3989422804014327


def by_head(block):
    lane = lax.broadcasted_iota(jnp.int32, block.shape, 1)
    zero = jnp.zeros_like(block)
    first = lane < HEAD
    return jnp.concatenate([jnp.where(first, block, zero), jnp.where(first, zero, block)], axis=0)


def places(order, blocks):
    bits = blocks.bit_length() - 1
    table = []
    for place in range(blocks):
        owner = 0
        for step in range(bits):
            if place >> (bits - 1 - step) & 1:
                owner ^= order[step]
        table.append(owner)
    return table


def block_at(place, tables, core, own):
    first, second = tables[0][place], tables[1][place]
    if first == second:
        return own ^ first
    return own ^ jnp.where(core == 0, first, second)


def permuted(dst_ref, acc_ref, chunk, tables, core, own, turned=0):
    blocks = len(tables[0])
    size = dst_ref.shape[0] // blocks
    for place in range(blocks):
        block = block_at(place, tables, core, own)
        rows = pl.ds(pl.multiple_of(block * size, size), size)
        to = pl.ds(pl.multiple_of(((place + turned * (blocks // 2)) & (blocks - 1)) * size, size), size)
        dst_ref[to, :] = acc_ref[chunk, rows, :].astype(dst_ref.dtype)


def attend_kernel(
    info_ref, tok_ref, g1_ref, c1_ref, wqkv_ref, wout_ref, g2_ref, c2_ref, seg_ref, step_ref, pad_ref,
    qkv_ref, prob_ref, mixed_ref, res_ref, second_ref,
):
    slots = seg_ref.shape[1]
    toks, width = tok_ref.shape
    rows = toks // slots
    at = pl.program_id(0)
    tokens = tok_ref[...].astype(F32)
    unit, _ = unit_parts(tokens)
    normed = (unit * g1_ref[...] + c1_ref[...]).astype(BF)
    qkv_ref[...] = mm(normed, wqkv_ref[...]).astype(BF)
    q_id = lax.broadcasted_iota(jnp.int32, (slots, slots), 0)
    k_id = lax.broadcasted_iota(jnp.int32, (slots, slots), 1)
    eye = q_id == k_id
    pairs = width // PAIR
    units = [(r, p) for r in range(rows) for p in range(pairs)]

    def part(r, p, which):
        return qkv_ref[r * slots : (r + 1) * slots, which * width + p * PAIR : which * width + (p + 1) * PAIR]

    masks = []
    for r in range(rows):
        here = pl.ds(at * rows + r, 1)
        seg = jnp.broadcast_to(seg_ref[here, :].astype(F32), (slots, slots))
        step = jnp.broadcast_to(step_ref[here, :].astype(F32), (slots, slots))
        live = jnp.broadcast_to(pad_ref[here, :], (slots, slots)) == 0
        masks.append(((seg == seg.T) & (step <= step.T) & live) | eye)
    scores = [mm_nt(part(r, p, 0), by_head(part(r, p, 1) * HEAD ** (-0.5))) for r, p in units]
    probs = []
    for (r, p), score in zip(units, scores):
        halves = []
        for half in (score[:, :slots], score[:, slots:]):
            half = jnp.where(masks[r], half, -1e30)
            weight = jnp.exp(half - jnp.max(half, axis=-1, keepdims=True))
            total = jnp.sum(weight, axis=-1, keepdims=True)
            halves.append((weight * (1.0 / total)).astype(BF))
        probs.append(jnp.concatenate(halves, axis=1))
    for (r, p), prob in zip(units, probs):
        prob_ref[r, p] = prob
        mixed_ref[r * slots : (r + 1) * slots, p * PAIR : (p + 1) * PAIR] = mm(prob, by_head(part(r, p, 2))).astype(BF)
    residual = tokens + mm(mixed_ref[...], wout_ref[...])
    res_ref[...] = residual
    unit, _ = unit_parts(residual)
    second_ref[...] = (unit * g2_ref[...] + c2_ref[...]).astype(BF)


def attend(info, tokens, g1, c1, wqkv, wout, g2, c2, seg, step, pad):
    n, width = tokens.shape
    rows, slots = seg.shape
    per, pairs = TOKS // slots, width // PAIR
    return call(
        attend_kernel,
        "attend",
        (n // TOKS,),
        [rows_of(width), whole(1, width), whole(1, width), whole(*wqkv.shape), whole(*wout.shape)]
        + [whole(1, width)] * 2
        + [whole(rows, slots)] * 3,
        [
            rows_of(3 * width),
            pl.BlockSpec((per, pairs, slots, 2 * slots), lambda i, *_: (i, 0, 0, 0)),
            rows_of(width),
            rows_of(width),
            rows_of(width),
        ],
        [
            pltpu.HBM((n, 3 * width), BF),
            pltpu.HBM((rows, pairs, slots, 2 * slots), BF),
            pltpu.HBM((n, width), BF),
            pltpu.HBM((n, width), F32),
            pltpu.VMEM((n, width), BF),
        ],
        [],
        info,
        far(tokens, g1, c1) + (wqkv, wout) + far(g2, c2, seg, step, pad),
    )


def pack_kernel(info_ref, up_ref, bias_ref, down_ref, up_out, down_out):
    width = up_ref.shape[0]
    up_out[:width, :] = up_ref[...]
    units = up_ref.shape[1]
    bias = bias_ref[...].reshape(1, 2 * units)
    bias = jnp.where(info_ref[0] == 0, bias[:, :units], bias[:, units:])
    up_out[width:, :] = jnp.broadcast_to(bias, (TILE, units))
    down_out[...] = down_ref[...]


def pack(info, up, bias, down):
    width, units = up.shape[0], up.shape[1] // 2
    return call(
        pack_kernel,
        "pack",
        (1,),
        [
            pl.BlockSpec((width, units), lambda t, info: (0, info[0])),
            whole(2 * units),
            pl.BlockSpec((units, width), lambda t, info: (info[0], 0)),
        ],
        [whole(width + TILE, units), whole(units, width)],
        [jax.ShapeDtypeStruct((width + TILE, units), BF), jax.ShapeDtypeStruct((units, width), BF)],
        [],
        info,
        far(up, bias, down),
    )


def ffn_block(sec, dy, up, bias, down, acc_ref, bacc_ref):
    pre = mm(sec, up) + bias
    dhid = mm_nt(dy, down)
    hid, slope = gelu_pair(pre)
    hid = hid.astype(BF)
    dpre = (dhid * slope).astype(BF)
    grad_up = mm(sec.T, dpre)
    grad_down = mm(dy.T, hid)
    sums = jnp.sum(dpre.astype(F32), axis=0, keepdims=True)
    chunks, _, double = acc_ref.shape
    units = double // 2
    for i in range(chunks):
        cols = slice(i * units, (i + 1) * units)
        acc_ref[i, :, :units] += grad_up[:, cols]
        acc_ref[i, :, units:] += grad_down[:, cols]
        bacc_ref[i : i + 1, :] += sums[:, cols]
    return mm(hid, down), mm_nt(dpre, up)


def ffn_own_kernel(
    tables, mixing, info_ref, sec_ref, dy_ref, up_ref, bias_ref, down_ref, out_ref, dsec_ref, keep_ref, send_ref, bias_out,
    acc_ref,
):
    at, last = pl.program_id(0), pl.num_programs(0) - 1

    @pl.when(at == 0)
    def _():
        acc_ref[...] = jnp.zeros_like(acc_ref)
        bias_out[...] = jnp.zeros_like(bias_out)

    bias = bias_ref[...].astype(F32).reshape(1, up_ref.shape[1])
    out_ref[...], dsec_ref[...] = ffn_block(
        sec_ref[...], dy_ref[...], up_ref[...], bias, down_ref[...], acc_ref, bias_out
    )

    @pl.when(at == last)
    def _():
        core, own, other = info_ref[0], info_ref[1], info_ref[2]
        permuted(keep_ref, acc_ref, core, tables, core, own)
        permuted(send_ref, acc_ref, core ^ 1, tables, core ^ 1, other, core ^ 1 if mixing else 0)


def ffn_own(info, tables, mixing, second, dy, up, bias, down):
    n, width = second.shape
    units = up.shape[1] // 2
    return call(
        functools.partial(ffn_own_kernel, tables, mixing),
        "ffn_own",
        (n // TOKS,),
        [rows_of(width), rows_of(width), whole(*up.shape), whole(*bias.shape), whole(*down.shape)],
        [rows_of(width)] * 2 + [whole(width, 2 * units)] * 2 + [whole(2, units)],
        [pltpu.VMEM((n, width), F32)] * 2
        + [jax.ShapeDtypeStruct((width, 2 * units), BF)] * 2
        + [jax.ShapeDtypeStruct((2, units), F32)],
        [pltpu.VMEM((2, width, 2 * units), F32)],
        info,
        near(second) + far(dy) + (up,) + far(bias) + (down,),
    )


def ffn_rest_kernel(
    tables, count, mixing, info_ref, sec_ref, dy_ref, out_part_ref, dsec_part_ref, res_ref, mixed_ref, bdown_ref, g2_ref,
    wout_ref, mine_ref, *refs
):
    ups, downs = refs[:count], refs[count : 2 * count]
    block_ref, gres_ref, gmix_ref, vec_ref, dwout_ref, bias_out = refs[2 * count : 2 * count + 6]
    *grads, acc_ref, up_ref, bias_ref, down_ref = refs[2 * count + 6 :]
    at, last = pl.program_id(0), pl.num_programs(0) - 1
    width, units = wout_ref.shape[0], ups[0].shape[1]

    @pl.when(at == 0)
    def _():
        for ref in (acc_ref, bias_out, vec_ref, dwout_ref):
            ref[...] = jnp.zeros_like(ref)
        for i in range(count):
            cols = slice(i * units, (i + 1) * units)
            up_ref[:, cols] = ups[i][:width, :]
            bias_ref[:, cols] = ups[i][width : width + TILE, :].astype(F32)[:8]
            down_ref[cols, :] = downs[i][...]

    dy = dy_ref[...]
    out, dsec = ffn_block(sec_ref[...], dy, up_ref[...], bias_ref[0:1, :], down_ref[...], acc_ref, bias_out)
    out += out_part_ref[...]
    dsec += dsec_part_ref[...]
    residual = res_ref[...]
    block_ref[...] = (residual + (out + bdown_ref[...])).astype(BF)
    dy32 = dy.astype(F32)
    unit, inv = unit_parts(residual)
    vec_ref[0:1, :] += jnp.sum(dsec * unit, axis=0, keepdims=True)
    vec_ref[1:2, :] += jnp.sum(dsec, axis=0, keepdims=True)
    vec_ref[2:3, :] += jnp.sum(dy32, axis=0, keepdims=True)
    gres = dy32 + norm_back(dsec, unit, inv, g2_ref[...])
    gres_ref[...] = gres
    branch = gres.astype(BF)
    gmix_ref[...] = mm_nt(branch, wout_ref[...]).astype(BF)
    dwout_ref[...] += mm_tn(mixed_ref[...], branch)

    @pl.when(at == last)
    def _():
        core = info_ref[0]
        blocks = len(tables[0])
        size = width // blocks

        def rows_at(i, place):
            block = block_at(place, tables, core ^ (i % 2), info_ref[1 + i % 2])
            rows = pl.ds(pl.multiple_of(block * size, size), size)
            return acc_ref[i, rows, :].astype(BF)

        def put(ref, row, part):
            ref[row : row + size, :] = part

        for i in range(1 if mixing else 0, count):
            for place in range(blocks):
                put(grads[i + 1 if mixing else i], place * size, rows_at(i, place))
        if not mixing:
            return
        keep_ref, send_ref = grads[:2]
        half = width // 2
        for place in range(blocks // 2, blocks):
            put(send_ref, place * size, rows_at(0, place))

        @pl.when(core == 0)
        def _():
            for place in range(blocks // 2):
                put(send_ref, place * size, rows_at(0, place))
            keep_ref[...] = mine_ref[...]

        @pl.when(core == 1)
        def _():
            for place in range(blocks // 2):
                put(keep_ref, place * size, rows_at(0, place))
            keep_ref[half:, :] = mine_ref[:half, :]
            send_ref[:half, :] = mine_ref[half:, :]


def ffn_rest(
    info, tables, mixing, second, dy, out_part, dsec_part, residual, mixed, bdown, g2, wout, mine, chunks
):
    n, width = second.shape
    count = len(chunks)
    units = chunks[0][0].shape[1]
    return call(
        functools.partial(ffn_rest_kernel, tables, count, mixing),
        "ffn_rest",
        (n // TOKS,),
        [rows_of(width)] * 6
        + [whole(1, width)] * 2
        + [whole(width, width), whole(*mine.shape)]
        + [whole(width + TILE, units)] * count
        + [whole(units, width)] * count,
        [rows_of(width)] * 3
        + [whole(8, width), whole(width, width), whole(count, units)]
        + [whole(width, 2 * units)] * (count + mixing),
        [
            jax.ShapeDtypeStruct((n, width), BF),
            pltpu.HBM((n, width), F32),
            pltpu.HBM((n, width), BF),
            jax.ShapeDtypeStruct((8, width), F32),
            pltpu.HBM((width, width), F32),
            jax.ShapeDtypeStruct((count, units), F32),
        ]
        + [jax.ShapeDtypeStruct((width, 2 * units), BF)] * (count + mixing),
        [
            pltpu.VMEM((count, width, 2 * units), F32),
            pltpu.VMEM((width, count * units), BF),
            pltpu.VMEM((8, count * units), F32),
            pltpu.VMEM((count * units, width), BF),
        ],
        info,
        near(second)
        + far(dy)
        + near(out_part, dsec_part)
        + far(residual, mixed, bdown, g2)
        + (wout, mine)
        + tuple(c[0] for c in chunks)
        + tuple(c[1] for c in chunks),
    )


def attend_back_kernel(
    tables, info_ref, qkv_ref, prob_ref, gmix_ref, tok_ref, vec_ref, dwout_ref, grad_ref, dw_keep_ref, dw_send_ref,
    dqkv_ref, acc_ref, row_ref,
):
    at, last = pl.program_id(0), pl.num_programs(0) - 1
    toks, width = tok_ref.shape
    rows, pairs, slots, _ = prob_ref.shape

    @pl.when(at == 0)
    def _():
        acc_ref[:, : 3 * width] = jnp.zeros((width, 3 * width), F32)
        acc_ref[:, 3 * width : 4 * width] = dwout_ref[...]
        row_ref[...] = jnp.zeros_like(row_ref)
        row_ref[SUMS : SUMS + vec_ref.shape[0], :] = vec_ref[...]

    scale = HEAD ** (-0.5)
    units = [(r, p) for r in range(rows) for p in range(pairs)]

    def place(r, p, which):
        return (slice(r * slots, (r + 1) * slots), slice(which * width + p * PAIR, which * width + (p + 1) * PAIR))

    grads = [gmix_ref[place(r, p, 0)] for r, p in units]
    dprobs = [mm_nt(g, by_head(qkv_ref[place(r, p, 2)])) for (r, p), g in zip(units, grads)]
    for (r, p), g in zip(units, grads):
        prob = prob_ref[r, p]
        stacked = jnp.concatenate([prob[:, :slots], prob[:, slots:]], axis=0)
        dqkv_ref[place(r, p, 2)] = mm_tn(stacked, by_head(g)).astype(BF)
    dscores = []
    for (r, p), dprob in zip(units, dprobs):
        p32 = prob_ref[r, p].astype(F32)
        prod = p32 * dprob
        first = jnp.sum(prod[:, :slots], axis=-1, keepdims=True)
        second = jnp.sum(prod[:, slots:], axis=-1, keepdims=True)
        dscores.append((
            (p32[:, :slots] * (dprob[:, :slots] - first)).astype(BF),
            (p32[:, slots:] * (dprob[:, slots:] - second)).astype(BF),
        ))
    for (r, p), ds in zip(units, dscores):
        k = qkv_ref[place(r, p, 1)]
        dqkv_ref[place(r, p, 0)] = mm(jnp.concatenate(ds, axis=1), by_head(k * scale)).astype(BF)
    for (r, p), ds in zip(units, dscores):
        q = qkv_ref[place(r, p, 0)]
        dqkv_ref[place(r, p, 1)] = mm_tn(jnp.concatenate(ds, axis=0), by_head(q * scale)).astype(BF)
    unit, _ = unit_parts(tok_ref[...].astype(F32))
    acc_ref[:, : 3 * width] += mm_tn(unit.astype(BF), dqkv_ref[...])
    grad_ref[...] = dqkv_ref[...]
    for i in range(3):
        part = dqkv_ref[:, i * width : (i + 1) * width].astype(F32)
        row_ref[i : i + 1, :] += jnp.sum(part, axis=0, keepdims=True)

    @pl.when(at == last)
    def _():
        core, own, other = info_ref[0], info_ref[3], info_ref[4]
        acc_ref[:, 4 * width :] = row_ref[...].T
        half = width // 2
        size = width // len(tables[0])
        for place in range(len(tables[0])):
            dst = dw_keep_ref if place * size < half else dw_send_ref
            block = block_at(place, tables, core, own if place * size < half else other)
            rows_at = pl.ds(pl.multiple_of(block * size, size), size)
            to = place * size % half
            dst[to : to + size, :] = acc_ref[rows_at, :].astype(BF)


def attend_back(info, tables, qkv, prob, gmix, tokens, vec, dwout):
    n, width = tokens.shape
    rows, pairs, slots, _ = prob.shape
    per = TOKS // slots
    return call(
        functools.partial(attend_back_kernel, tables),
        "attend_back",
        (n // TOKS,),
        [
            rows_of(3 * width),
            pl.BlockSpec((per, pairs, slots, 2 * slots), lambda i, *_: (i, 0, 0, 0)),
            rows_of(width),
            rows_of(width),
            whole(*vec.shape),
            whole(width, width),
        ],
        [rows_of(3 * width)] + [whole(width // 2, 4 * width + LANES)] * 2,
        [pltpu.VMEM((n, 3 * width), BF)] + [jax.ShapeDtypeStruct((width // 2, 4 * width + LANES), BF)] * 2,
        [
            pltpu.VMEM((TOKS, 3 * width), BF),
            pltpu.VMEM((width, 4 * width + LANES), F32),
            pltpu.VMEM((LANES, width), F32),
        ],
        info,
        far(qkv, prob, gmix, tokens, vec, dwout),
    )


def first_back_kernel(info_ref, dqkv_ref, wqkv_ref, tok_ref, gres_ref, g1_ref, out_ref):
    dnormed = mm_nt(dqkv_ref[...], wqkv_ref[...])
    unit, inv = unit_parts(tok_ref[...].astype(F32))
    out_ref[...] = gres_ref[...] + norm_back(dnormed, unit, inv, g1_ref[...])


def first_back(info, dqkv, wqkv, tokens, gres, g1):
    n, width = tokens.shape
    return call(
        first_back_kernel,
        "first_back",
        (n // TOKS,),
        [rows_of(3 * width), whole(*wqkv.shape), rows_of(width), rows_of(width), whole(1, width)],
        rows_of(width),
        jax.ShapeDtypeStruct((n, width), F32),
        [],
        info,
        near(dqkv) + (wqkv,) + far(tokens, gres, g1),
    )


def ffn_end_kernel(tables, info_ref, keep_ref, other_ref, up_ref, down_ref, full_ref):
    core = info_ref[0]
    units = up_ref.shape[1]
    blocks = len(tables[0])
    size = keep_ref.shape[0] // blocks

    def lay(src_ref, whose, base):
        for place in range(blocks):
            block = block_at(place, tables, whose, base)
            rows = pl.ds(pl.multiple_of(block * size, size), size)
            part = src_ref[place * size : (place + 1) * size, :].astype(F32)
            up_ref[rows, :] = part[:, :units]
            full_ref[rows, :] = part[:, units:]
        down_ref[...] = full_ref[...].T

    @pl.when(pl.program_id(0) == 0)
    def _():
        lay(keep_ref, core, info_ref[1])

    @pl.when(pl.program_id(0) == 1)
    def _():
        lay(other_ref, core ^ 1, info_ref[2])


def ffn_end(info, tables, keep, other):
    width, double = keep.shape
    units = double // 2
    return call(
        functools.partial(ffn_end_kernel, tables),
        "ffn_end",
        (2,),
        [whole(width, double)] * 2,
        [
            pl.BlockSpec((width, units), lambda i, info: (0, info[0] ^ i)),
            pl.BlockSpec((units, width), lambda i, info: (info[0] ^ i, 0)),
        ],
        [jax.ShapeDtypeStruct((width, double), F32), jax.ShapeDtypeStruct((double, width), F32)],
        [pltpu.VMEM((width, units), F32)],
        info,
        (keep, other),
    )


def attend_end_kernel(
    tables, shares, info_ref, keep_ref, other_ref, w_ref, g1_ref, c1_ref, qkv_hbm, out_hbm, *refs
):
    vec_refs, (qkv_ref, out_ref, col_ref, row_ref, sems) = refs[:6], refs[6:]
    core, own, away = info_ref[0], info_ref[3], info_ref[4]
    width = out_ref.shape[1]
    blocks = len(tables[0])
    size = out_ref.shape[0] // blocks
    half = out_ref.shape[0] // 2
    spots = []
    for place in range(blocks):
        mine = place * size < half
        block = block_at(place, tables, core, own if mine else away)
        at = place * size % half
        spots.append((keep_ref if mine else other_ref, slice(at, at + size), pl.multiple_of(block * size, size)))
    copies = []
    for i, (src, rows, to) in enumerate(spots):
        to = pl.ds(to, size)
        col_ref[to, :] = src[rows, 4 * width :].astype(F32)
        out_ref[rows if src is keep_ref else slice(rows.start + half, rows.stop + half), :] = src[
            rows, 3 * width : 4 * width
        ].astype(F32)
    for i, (src, rows, to) in enumerate(spots):
        rows = rows if src is keep_ref else slice(rows.start + half, rows.stop + half)
        copies.append(pltpu.make_async_copy(out_ref.at[rows, :], out_hbm.at[pl.ds(to, size), :], sems.at[i]))
        copies[-1].start()
    vec = col_ref[...].T
    row_ref[...] = vec
    wide_row = jnp.concatenate([vec[i : i + 1, :] for i in range(3)], axis=1)
    pair = jnp.concatenate([g1_ref[...], c1_ref[...], jnp.zeros((LANES - 2, width), F32)], axis=0).T
    col_ref[...] = pair
    lane = lax.broadcasted_iota(jnp.int32, (size, LANES), 1)
    for i, (src, rows, to) in enumerate(spots):
        here = pl.ds(to, size)
        gain_bias = col_ref[here, :]
        gain, bias = gain_bias[:, 0:1], gain_bias[:, 1:2]
        sums = src[rows, : 3 * width].astype(F32)
        w = w_ref[here, :].astype(F32)
        rows = rows if src is keep_ref else slice(rows.start + half, rows.stop + half)
        qkv_ref[rows, :] = gain * sums + bias * wide_row
        copies.append(pltpu.make_async_copy(qkv_ref.at[rows, :], qkv_hbm.at[here, :], sems.at[blocks + i]))
        copies[-1].start()
        d_gain = jnp.sum(w * sums, axis=1, keepdims=True)
        d_bias = jnp.sum(w * wide_row, axis=1, keepdims=True)
        col_ref[here, :] = jnp.where(lane == 0, d_gain, jnp.where(lane == 1, d_bias, 0.0))
    both = col_ref[...].T
    flat = lambda row: row.reshape(row.shape[1])
    vec_refs[0][...] = flat(both[0:1, :])
    vec_refs[1][...] = flat(both[1:2, :])
    for i in range(3):
        vec_refs[2 + i][...] = flat(vec[SUMS + i : SUMS + i + 1, :])
    units = vec_refs[5].shape[0]
    if units >= width:
        first = SUMS + 8 + info_ref[5] * (units // width)
        for i in range(units // width):
            vec_refs[5][i * width : (i + 1) * width] = flat(row_ref[pl.ds(first + i, 1), :])
    else:
        row = row_ref[pl.ds(SUMS + 8 + info_ref[5] // shares, 1), :]
        share = row[:, :units]
        for i in range(1, shares):
            share = jnp.where(info_ref[5] % shares == i, row[:, i * units : (i + 1) * units], share)
        vec_refs[5][...] = flat(share)
    for copy in copies:
        copy.wait()


def attend_end(info, tables, keep, other, w_qkv, g1, c1, units):
    rows, width = 2 * keep.shape[0], w_qkv.shape[0]
    blocks = len(tables[0])
    return call(
        functools.partial(attend_end_kernel, tables, max(1, width // units)),
        "attend_end",
        (1,),
        [whole(*keep.shape)] * 2 + [whole(*w_qkv.shape)] + [whole(1, width)] * 2,
        [pl.BlockSpec(memory_space=pl.ANY)] * 2 + [whole(width)] * 5 + [whole(units)],
        [jax.ShapeDtypeStruct((rows, 3 * width), F32), jax.ShapeDtypeStruct((rows, width), F32)]
        + [jax.ShapeDtypeStruct((width,), F32)] * 5
        + [jax.ShapeDtypeStruct((units,), F32)],
        [
            pltpu.VMEM((rows, 3 * width), F32),
            pltpu.VMEM((rows, width), F32),
            pltpu.VMEM((rows, LANES), F32),
            pltpu.VMEM((LANES, width), F32),
            pltpu.SemaphoreType.DMA((2 * blocks,)),
        ],
        info,
        (keep, other, w_qkv) + far(g1, c1),
    )


def local(
    wide, narrow, tokens_in, ln1_gain, ln1_bias, w_qkv, w_out, ln2_gain, ln2_bias, w_up, b_up, w_down, b_down, segment_ids,
    step_ids, pad_mask, cotangent,
):
    width = tokens_in.shape[1]
    units = w_up.shape[1] // 2
    core_mask = narrow
    narrow_masks = [1 << b for b in range(narrow.bit_length() - 1)]
    wide_masks = [narrow << b for b in range(1, wide.bit_length() - 1)]

    def swap(value, first, second=None):
        masks = (first, first if second is None else second)
        pairs = [(i, i ^ masks[i // narrow & 1]) for i in range(wide * narrow)]
        return lax.ppermute(value, AXES, pairs)

    def add(a, b):
        return (a.astype(F32) + b.astype(F32)).astype(a.dtype)

    def after(*values):
        return lax.optimization_barrier(values)

    def scatters(order):
        def step(first, second, value):
            half = value.shape[0] // 2
            return add(value[:half], swap(value[half:], first, second))

        return [functools.partial(step, *pair) for pair in zip(*order)]

    def exchanges(order):
        def step(first, second, value):
            return add(value, swap(value, first, second))

        return [functools.partial(step, *pair) for pair in zip(*order)]

    def gathers(order):
        def step(first, second, value):
            return jnp.concatenate([value, swap(value, first, second)], axis=0)

        return [functools.partial(step, *pair) for pair in reversed(list(zip(*order)))]

    wide_at, narrow_at = lax.axis_index("wide"), lax.axis_index("narrow")
    core = wide_at & 1
    flat = wide_at * narrow + narrow_at

    def named(owner, used):
        return sum((1 << b) for b, m in enumerate(used) if owner & m)

    def block_of(used):
        return sum(((flat & m) != 0).astype(jnp.int32) << b for b, m in enumerate(used))

    def split_at(pair, count):
        return tuple(o[:count] for o in pair), tuple(o[count:] for o in pair)

    def by_core(values):
        return jnp.where(core == 0, values[0], values[1]), jnp.where(core == 0, values[1], values[0])

    mixing = narrow == 2 and len(wide_masks) == 3
    if mixing:
        y, low, high = wide_masks
        ff_in, ff_rest = ([y, low], [y, low]), ([high], [high])
        ff_out = ([y, low], [low, y])
        at_order = ([1, y, low], [y, 1, low])
        at_rest = ([high], [high])
    else:
        ff_in, ff_rest = split_at((wide_masks, wide_masks), min(len(wide_masks) - 1, (width // TILE).bit_length() - 1))
        ff_out = ff_in
        masks = narrow_masks + wide_masks
        at_order, at_rest = split_at((masks, masks), min(len(masks) - 1, (width // TILE // 2).bit_length() - 1))
    ff_used = tuple(sorted(o) for o in ff_in)
    ff_in_tables, ff_out_tables = (
        tuple([named(owner, ff_used[c]) for owner in places(pair[c], 1 << len(ff_used[c]))] for c in range(2))
        for pair in (ff_in, ff_out)
    )
    at_used = tuple([core_mask] + sorted(o) for o in at_order)
    at_places = [places(o, 1 << len(o)) for o in at_order]
    at_tables = tuple(
        [named(o, at_used[c]) for o in at_places[c]]
        + [named(o ^ core_mask, at_used[1 - c]) for o in at_places[1 - c]]
        for c in range(2)
    )
    ff_block = by_core([block_of(used) for used in ff_used])
    at_block = by_core([block_of(used) for used in at_used])
    info = jnp.stack([core, *ff_block, *at_block, narrow_at]).astype(jnp.int32)

    packed, tokens_in = after(pack(info, w_up, b_up, w_down), tokens_in)
    fetched = [packed]
    for mask in narrow_masks:
        fetched = fetched + [(swap(u, mask), swap(d, mask)) for u, d in fetched]

    row = lambda v: v[None].astype(F32)
    g1, c1, g2 = row(ln1_gain), row(ln1_bias), row(ln2_gain)
    qkv, prob, mixed, residual, second = attend(
        info, tokens_in, g1, c1, w_qkv, w_out, g2, row(ln2_bias), segment_ids, step_ids, pad_mask
    )
    out_part, dsec_part, own_keep, own_send, bias_own = ffn_own(
        info, ff_in_tables, mixing, second, cotangent, w_up, b_up, w_down
    )
    own_send, fetched = after(own_send, fetched)
    chunks = []
    for up, down in fetched[1:]:
        chunks += [(up, down), (swap(up, core_mask), swap(down, core_mask))]
    rest = ffn_rest(
        info, ff_in_tables, mixing, second, cotangent, out_part, dsec_part, residual, mixed, row(b_down), g2, w_out, own_keep,
        chunks,
    )
    block_out, gres, gmix, vec, dwout, bias_rest = rest[:6]
    grads = rest[6:]

    b_rest = bias_rest.reshape(-1, 2, units)
    b_rest = jnp.where(core == 0, b_rest, jnp.flip(b_rest, axis=1))
    b_all = jnp.concatenate([bias_own[None], b_rest], axis=0)
    for bit in range(narrow.bit_length() - 1):
        flipped = jnp.flip(b_all.reshape(-1, 2, (1 << bit) * 2, units), axis=1).reshape(b_all.shape)
        b_all = jnp.where(narrow_at >> bit & 1, flipped, b_all)
    vec = jnp.concatenate([vec, b_all.reshape(-1, width)], axis=0)

    if mixing:
        ff_keep, ff_send, away = grads
        got_own, got = swap(own_send, core_mask), swap(away, core_mask)
        chunk = (core == 0) | (lax.broadcasted_iota(jnp.int32, got.shape, 0) >= width // 2)
        ff_send = add(ff_send, jnp.where(chunk, got, got_own))
        gmix, ff_send = after(gmix, ff_send)
        ff_got = swap(ff_send, 1, y)
        top = width // 2
        ff_keep = add(ff_keep, jnp.where(chunk, got_own, got))
        ff_send = add(jnp.where(core == 0, ff_keep[top:], ff_keep[:top]), ff_got[top:])
        ff_keep = add(jnp.where(core == 0, ff_keep[:top], ff_keep[top:]), ff_got[:top])
    else:
        held = [add(own_keep, swap(own_send, core_mask))] + [add(grads[2 * j], swap(grads[2 * j + 1], core_mask)) for j in range(narrow - 1)]
        gmix, held = after(gmix, held)
        for mask in reversed(narrow_masks):
            held = [add(held[j], swap(held[j + mask], mask)) for j in range(mask)]
        ff_keep = ff_send = held[0]

    dqkv, keep, send = attend_back(info, at_tables, qkv, prob, gmix, tokens_in, vec, dwout)
    keep, ff_keep, ff_send = after(add(keep, swap(send, core_mask)), ff_keep, ff_send)
    grad_tokens = first_back(info, dqkv, w_qkv, tokens_in, gres, g1)
    at_steps = scatters(at_order) + exchanges(at_rest) + gathers(at_order)
    ff_steps = exchanges(ff_rest) + gathers(ff_out)
    if mixing:
        ff_keep = add(ff_keep, swap(ff_send, y, 1))
        ff_steps = scatters(([low], [low])) + ff_steps
    else:
        first, *ff_steps = scatters(ff_in) + ff_steps
        ff_keep = first(ff_keep)
    keep, ff_keep, grad_tokens = after(at_steps[0](keep), ff_keep, grad_tokens)
    at_steps = at_steps[1:]
    shared = min(len(at_steps), len(ff_steps))
    for at_step, ff_step in zip(at_steps, ff_steps):
        keep, ff_keep = after(at_step(keep), ff_step(ff_keep))
    for ff_step in ff_steps[shared:]:
        ff_keep = ff_step(ff_keep)
    ff_other = swap(ff_keep, core_mask)
    for at_step in at_steps[shared : shared + 1]:
        keep, ff_other = after(at_step(keep), ff_other)
    ff_done = ffn_end(info, ff_out_tables, ff_keep, ff_other)
    for at_step in at_steps[shared + 1 :]:
        keep, ff_done = after(at_step(keep), ff_done)
    grad_w_up, grad_w_down = ff_done

    grad_w_qkv, grad_w_out, d_gain1, d_bias1, d_gain2, d_bias2, d_bdown, grad_b_up = attend_end(
        info, at_tables, keep, swap(keep, core_mask), w_qkv, g1, c1, 2 * units
    )
    return (
        block_out, grad_tokens, d_gain1, d_bias1, grad_w_qkv, grad_w_out, d_gain2, d_bias2, grad_w_up, grad_b_up, grad_w_down,
        d_bdown,
    )


def solution(mesh):
    rows = P(("wide", "narrow"), None)
    in_specs = (
        rows, P(), P(), P(), P(), P(), P(), P(None, "narrow"), P("narrow"), P("narrow", None), P(), rows, rows, rows, rows,
    )
    out_specs = (
        rows, rows, P(), P(), P(), P(), P(), P(), P(None, "narrow"), P("narrow"), P("narrow", None), P(),
    )
    wide, narrow = mesh.shape["wide"], mesh.shape["narrow"]
    return jax.shard_map(
        functools.partial(local, wide, narrow), mesh=mesh, in_specs=in_specs, out_specs=out_specs, check_vma=False
    )
```

```python
import functools
import itertools

import jax
import jax.numpy as jnp
import numpy as np
from jax import lax
from jax.experimental import pallas as pl
from jax.experimental.pallas import tpu as pltpu
from jax.sharding import PartitionSpec as P

HEAD = 64
PAIR = 2 * HEAD
NORM_EPS = 1e-05
BF = jnp.bfloat16
F32 = jnp.float32
AXES = ("wide", "narrow")
LANES = 128
SUMS = 8
TILE = 16
TOKS = 512
VMEM_LIMIT = 30 * 1024 * 1024


def mm(a, b):
    return lax.dot_general(a, b, (((1,), (0,)), ((), ())), preferred_element_type=F32)


def mm_nt(a, b):
    return lax.dot_general(a, b, (((1,), (1,)), ((), ())), preferred_element_type=F32)


def mm_tn(a, b):
    return lax.dot_general(a, b, (((0,), (0,)), ((), ())), preferred_element_type=F32)


def near(*values):
    return tuple(pltpu.with_memory_space_constraint(v, pltpu.VMEM) for v in values)


def far(*values):
    return tuple(pltpu.with_memory_space_constraint(v, pltpu.HBM) for v in values)


def whole(*shape):
    return pl.BlockSpec(shape, lambda *_: (0,) * len(shape))


def rows_of(width, toks=TOKS):
    return pl.BlockSpec((toks, width), lambda i, *_: (i, 0))


def call(kernel, name, grid, in_specs, out_specs, out_shape, scratch, info, args):
    return pl.pallas_call(
        kernel,
        grid_spec=pltpu.PrefetchScalarGridSpec(
            num_scalar_prefetch=1, grid=grid, in_specs=in_specs, out_specs=out_specs, scratch_shapes=scratch
        ),
        out_shape=out_shape,
        compiler_params=pltpu.CompilerParams(vmem_limit_bytes=VMEM_LIMIT),
        cost_estimate=pl.CostEstimate(flops=1000, bytes_accessed=1000, transcendentals=0),
        name=name,
    )(info, *args)


def unit_parts(rows):
    mean = jnp.mean(rows, axis=-1, keepdims=True)
    centered = rows - mean
    inv = lax.rsqrt(jnp.mean(centered * centered, axis=-1, keepdims=True) + NORM_EPS)
    return centered * inv, inv


def norm_back(incoming, unit, inv, gain):
    scaled = incoming * gain
    return inv * (
        scaled
        - jnp.mean(scaled, axis=-1, keepdims=True)
        - unit * jnp.mean(scaled * unit, axis=-1, keepdims=True)
    )


def gelu_pair(x):
    cdf = 0.5 * (1.0 + lax.erf(x * 0.7071067811865476))
    return x * cdf, cdf + x * jnp.exp(-0.5 * x * x) * 0.3989422804014327


def by_head(block):
    lane = lax.broadcasted_iota(jnp.int32, block.shape, 1)
    zero = jnp.zeros_like(block)
    first = lane < HEAD
    return jnp.concatenate([jnp.where(first, block, zero), jnp.where(first, zero, block)], axis=0)


def places(order, blocks):
    bits = blocks.bit_length() - 1
    table = []
    for place in range(blocks):
        owner = 0
        for step in range(bits):
            if place >> (bits - 1 - step) & 1:
                owner ^= order[step]
        table.append(owner)
    return table


def block_at(place, tables, core, own):
    first, second = tables[0][place], tables[1][place]
    if first == second:
        return own ^ first
    return own ^ jnp.where(core == 0, first, second)


def permuted(dst_ref, acc_ref, chunk, tables, core, own, turned=0):
    blocks = len(tables[0])
    size = dst_ref.shape[0] // blocks
    for place in range(blocks):
        block = block_at(place, tables, core, own)
        rows = pl.ds(pl.multiple_of(block * size, size), size)
        to = pl.ds(pl.multiple_of(((place + turned * (blocks // 2)) & (blocks - 1)) * size, size), size)
        dst_ref[to, :] = acc_ref[chunk, rows, :].astype(dst_ref.dtype)


def attend_kernel(
    info_ref, tok_ref, g1_ref, c1_ref, wqkv_ref, wout_ref, g2_ref, c2_ref, seg_ref, step_ref, pad_ref,
    qkv_ref, prob_ref, mixed_ref, res_ref, second_ref,
):
    slots = seg_ref.shape[1]
    toks, width = tok_ref.shape
    rows = toks // slots
    at = pl.program_id(0)
    tokens = tok_ref[...].astype(F32)
    unit, _ = unit_parts(tokens)
    normed = (unit * g1_ref[...] + c1_ref[...]).astype(BF)
    qkv_ref[...] = mm(normed, wqkv_ref[...]).astype(BF)
    q_id = lax.broadcasted_iota(jnp.int32, (slots, slots), 0)
    k_id = lax.broadcasted_iota(jnp.int32, (slots, slots), 1)
    eye = q_id == k_id
    pairs = width // PAIR
    units = [(r, p) for r in range(rows) for p in range(pairs)]

    def part(r, p, which):
        return qkv_ref[r * slots : (r + 1) * slots, which * width + p * PAIR : which * width + (p + 1) * PAIR]

    masks = []
    for r in range(rows):
        here = pl.ds(at * rows + r, 1)
        seg = jnp.broadcast_to(seg_ref[here, :].astype(F32), (slots, slots))
        step = jnp.broadcast_to(step_ref[here, :].astype(F32), (slots, slots))
        live = jnp.broadcast_to(pad_ref[here, :], (slots, slots)) == 0
        masks.append(((seg == seg.T) & (step <= step.T) & live) | eye)
    scores = [mm_nt(part(r, p, 0), by_head(part(r, p, 1) * HEAD ** (-0.5))) for r, p in units]
    probs = []
    for (r, p), score in zip(units, scores):
        halves = []
        for half in (score[:, :slots], score[:, slots:]):
            half = jnp.where(masks[r], half, -1e30)
            weight = jnp.exp(half - jnp.max(half, axis=-1, keepdims=True))
            total = jnp.sum(weight, axis=-1, keepdims=True)
            halves.append((weight * (1.0 / total)).astype(BF))
        probs.append(jnp.concatenate(halves, axis=1))
    for (r, p), prob in zip(units, probs):
        prob_ref[r, p] = prob
        mixed_ref[r * slots : (r + 1) * slots, p * PAIR : (p + 1) * PAIR] = mm(prob, by_head(part(r, p, 2))).astype(BF)
    residual = tokens + mm(mixed_ref[...], wout_ref[...])
    res_ref[...] = residual
    unit, _ = unit_parts(residual)
    second_ref[...] = (unit * g2_ref[...] + c2_ref[...]).astype(BF)


def attend(info, tokens, g1, c1, wqkv, wout, g2, c2, seg, step, pad):
    n, width = tokens.shape
    rows, slots = seg.shape
    per, pairs = TOKS // slots, width // PAIR
    return call(
        attend_kernel,
        "attend",
        (n // TOKS,),
        [rows_of(width), whole(1, width), whole(1, width), whole(*wqkv.shape), whole(*wout.shape)]
        + [whole(1, width)] * 2
        + [whole(rows, slots)] * 3,
        [
            rows_of(3 * width),
            pl.BlockSpec((per, pairs, slots, 2 * slots), lambda i, *_: (i, 0, 0, 0)),
            rows_of(width),
            rows_of(width),
            rows_of(width),
        ],
        [
            pltpu.HBM((n, 3 * width), BF),
            pltpu.HBM((rows, pairs, slots, 2 * slots), BF),
            pltpu.HBM((n, width), BF),
            pltpu.HBM((n, width), F32),
            pltpu.VMEM((n, width), BF),
        ],
        [],
        info,
        far(tokens, g1, c1) + (wqkv, wout) + far(g2, c2, seg, step, pad),
    )


def pack_kernel(info_ref, up_ref, bias_ref, down_ref, up_out, down_out):
    width = up_ref.shape[0]
    up_out[:width, :] = up_ref[...]
    units = up_ref.shape[1]
    bias = bias_ref[...].reshape(1, 2 * units)
    bias = jnp.where(info_ref[0] == 0, bias[:, :units], bias[:, units:])
    up_out[width:, :] = jnp.broadcast_to(bias, (TILE, units))
    down_out[...] = down_ref[...]


def pack(info, up, bias, down):
    width, units = up.shape[0], up.shape[1] // 2
    return call(
        pack_kernel,
        "pack",
        (1,),
        [
            pl.BlockSpec((width, units), lambda t, info: (0, info[0])),
            whole(2 * units),
            pl.BlockSpec((units, width), lambda t, info: (info[0], 0)),
        ],
        [whole(width + TILE, units), whole(units, width)],
        [jax.ShapeDtypeStruct((width + TILE, units), BF), jax.ShapeDtypeStruct((units, width), BF)],
        [],
        info,
        far(up, bias, down),
    )


def ffn_block(sec, dy, up, bias, down, acc_ref, bacc_ref):
    pre = mm(sec, up) + bias
    dhid = mm_nt(dy, down)
    hid, slope = gelu_pair(pre)
    hid = hid.astype(BF)
    dpre = (dhid * slope).astype(BF)
    grad_up = mm(sec.T, dpre)
    grad_down = mm(dy.T, hid)
    sums = jnp.sum(dpre.astype(F32), axis=0, keepdims=True)
    chunks, _, double = acc_ref.shape
    units = double // 2
    for i in range(chunks):
        cols = slice(i * units, (i + 1) * units)
        acc_ref[i, :, :units] += grad_up[:, cols]
        acc_ref[i, :, units:] += grad_down[:, cols]
        bacc_ref[i : i + 1, :] += sums[:, cols]
    return mm(hid, down), mm_nt(dpre, up)


def ffn_own_kernel(
    tables, mixing, info_ref, sec_ref, dy_ref, up_ref, bias_ref, down_ref, out_ref, dsec_ref, keep_ref, send_ref, bias_out,
    acc_ref,
):
    at, last = pl.program_id(0), pl.num_programs(0) - 1

    @pl.when(at == 0)
    def _():
        acc_ref[...] = jnp.zeros_like(acc_ref)
        bias_out[...] = jnp.zeros_like(bias_out)

    bias = bias_ref[...].astype(F32).reshape(1, up_ref.shape[1])
    out_ref[...], dsec_ref[...] = ffn_block(
        sec_ref[...], dy_ref[...], up_ref[...], bias, down_ref[...], acc_ref, bias_out
    )

    @pl.when(at == last)
    def _():
        core, own, other = info_ref[0], info_ref[1], info_ref[2]
        permuted(keep_ref, acc_ref, core, tables, core, own)
        permuted(send_ref, acc_ref, core ^ 1, tables, core ^ 1, other, core ^ 1 if mixing else 0)


def ffn_own(info, tables, mixing, second, dy, up, bias, down):
    n, width = second.shape
    units = up.shape[1] // 2
    return call(
        functools.partial(ffn_own_kernel, tables, mixing),
        "ffn_own",
        (n // TOKS,),
        [rows_of(width), rows_of(width), whole(*up.shape), whole(*bias.shape), whole(*down.shape)],
        [rows_of(width)] * 2 + [whole(width, 2 * units)] * 2 + [whole(2, units)],
        [pltpu.VMEM((n, width), F32)] * 2
        + [jax.ShapeDtypeStruct((width, 2 * units), BF)] * 2
        + [jax.ShapeDtypeStruct((2, units), F32)],
        [pltpu.VMEM((2, width, 2 * units), F32)],
        info,
        near(second) + far(dy) + (up,) + far(bias) + (down,),
    )


def ffn_rest_kernel(
    tables, count, mixing, info_ref, sec_ref, dy_ref, out_part_ref, dsec_part_ref, res_ref, mixed_ref, bdown_ref, g2_ref,
    wout_ref, mine_ref, *refs
):
    ups, downs = refs[:count], refs[count : 2 * count]
    block_ref, gres_ref, gmix_ref, vec_ref, dwout_ref, bias_out = refs[2 * count : 2 * count + 6]
    *grads, acc_ref, up_ref, bias_ref, down_ref = refs[2 * count + 6 :]
    at, last = pl.program_id(0), pl.num_programs(0) - 1
    width, units = wout_ref.shape[0], ups[0].shape[1]

    @pl.when(at == 0)
    def _():
        for ref in (acc_ref, bias_out, vec_ref, dwout_ref):
            ref[...] = jnp.zeros_like(ref)
        for i in range(count):
            cols = slice(i * units, (i + 1) * units)
            up_ref[:, cols] = ups[i][:width, :]
            bias_ref[:, cols] = ups[i][width : width + TILE, :].astype(F32)[:8]
            down_ref[cols, :] = downs[i][...]

    dy = dy_ref[...]
    out, dsec = ffn_block(sec_ref[...], dy, up_ref[...], bias_ref[0:1, :], down_ref[...], acc_ref, bias_out)
    out += out_part_ref[...]
    dsec += dsec_part_ref[...]
    residual = res_ref[...]
    block_ref[...] = (residual + (out + bdown_ref[...])).astype(BF)
    dy32 = dy.astype(F32)
    unit, inv = unit_parts(residual)
    vec_ref[0:1, :] += jnp.sum(dsec * unit, axis=0, keepdims=True)
    vec_ref[1:2, :] += jnp.sum(dsec, axis=0, keepdims=True)
    vec_ref[2:3, :] += jnp.sum(dy32, axis=0, keepdims=True)
    gres = dy32 + norm_back(dsec, unit, inv, g2_ref[...])
    gres_ref[...] = gres
    branch = gres.astype(BF)
    gmix_ref[...] = mm_nt(branch, wout_ref[...]).astype(BF)
    dwout_ref[...] += mm_tn(mixed_ref[...], branch)

    @pl.when(at == last)
    def _():
        core = info_ref[0]
        blocks = len(tables[0])
        size = width // blocks

        def rows_at(i, place):
            block = block_at(place, tables, core ^ (i % 2), info_ref[1 + i % 2])
            rows = pl.ds(pl.multiple_of(block * size, size), size)
            return acc_ref[i, rows, :].astype(BF)

        def put(ref, row, part):
            ref[row : row + size, :] = part

        for i in range(1 if mixing else 0, count):
            for place in range(blocks):
                put(grads[i + 1 if mixing else i], place * size, rows_at(i, place))
        if not mixing:
            return
        keep_ref, send_ref = grads[:2]
        half = width // 2
        for place in range(blocks // 2, blocks):
            put(send_ref, place * size, rows_at(0, place))

        @pl.when(core == 0)
        def _():
            for place in range(blocks // 2):
                put(send_ref, place * size, rows_at(0, place))
            keep_ref[...] = mine_ref[...]

        @pl.when(core == 1)
        def _():
            for place in range(blocks // 2):
                put(keep_ref, place * size, rows_at(0, place))
            keep_ref[half:, :] = mine_ref[:half, :]
            send_ref[:half, :] = mine_ref[half:, :]


def ffn_rest(
    info, tables, mixing, second, dy, out_part, dsec_part, residual, mixed, bdown, g2, wout, mine, chunks
):
    n, width = second.shape
    count = len(chunks)
    units = chunks[0][0].shape[1]
    return call(
        functools.partial(ffn_rest_kernel, tables, count, mixing),
        "ffn_rest",
        (n // TOKS,),
        [rows_of(width)] * 6
        + [whole(1, width)] * 2
        + [whole(width, width), whole(*mine.shape)]
        + [whole(width + TILE, units)] * count
        + [whole(units, width)] * count,
        [rows_of(width)] * 3
        + [whole(8, width), whole(width, width), whole(count, units)]
        + [whole(width, 2 * units)] * (count + mixing),
        [
            jax.ShapeDtypeStruct((n, width), BF),
            pltpu.HBM((n, width), F32),
            pltpu.HBM((n, width), BF),
            jax.ShapeDtypeStruct((8, width), F32),
            pltpu.HBM((width, width), F32),
            jax.ShapeDtypeStruct((count, units), F32),
        ]
        + [jax.ShapeDtypeStruct((width, 2 * units), BF)] * (count + mixing),
        [
            pltpu.VMEM((count, width, 2 * units), F32),
            pltpu.VMEM((width, count * units), BF),
            pltpu.VMEM((8, count * units), F32),
            pltpu.VMEM((count * units, width), BF),
        ],
        info,
        near(second)
        + far(dy)
        + near(out_part, dsec_part)
        + far(residual, mixed, bdown, g2)
        + (wout, mine)
        + tuple(c[0] for c in chunks)
        + tuple(c[1] for c in chunks),
    )


def attend_back_kernel(
    tables, info_ref, qkv_ref, prob_ref, gmix_ref, tok_ref, vec_ref, dwout_ref, grad_ref, dw_keep_ref, dw_send_ref,
    dqkv_ref, acc_ref, row_ref,
):
    at, last = pl.program_id(0), pl.num_programs(0) - 1
    toks, width = tok_ref.shape
    rows, pairs, slots, _ = prob_ref.shape

    @pl.when(at == 0)
    def _():
        acc_ref[:, : 3 * width] = jnp.zeros((width, 3 * width), F32)
        acc_ref[:, 3 * width : 4 * width] = dwout_ref[...]
        row_ref[...] = jnp.zeros_like(row_ref)
        row_ref[SUMS : SUMS + vec_ref.shape[0], :] = vec_ref[...]

    scale = HEAD ** (-0.5)
    units = [(r, p) for r in range(rows) for p in range(pairs)]

    def place(r, p, which):
        return (slice(r * slots, (r + 1) * slots), slice(which * width + p * PAIR, which * width + (p + 1) * PAIR))

    grads = [gmix_ref[place(r, p, 0)] for r, p in units]
    dprobs = [mm_nt(g, by_head(qkv_ref[place(r, p, 2)])) for (r, p), g in zip(units, grads)]
    for (r, p), g in zip(units, grads):
        prob = prob_ref[r, p]
        stacked = jnp.concatenate([prob[:, :slots], prob[:, slots:]], axis=0)
        dqkv_ref[place(r, p, 2)] = mm_tn(stacked, by_head(g)).astype(BF)
    dscores = []
    for (r, p), dprob in zip(units, dprobs):
        p32 = prob_ref[r, p].astype(F32)
        prod = p32 * dprob
        first = jnp.sum(prod[:, :slots], axis=-1, keepdims=True)
        second = jnp.sum(prod[:, slots:], axis=-1, keepdims=True)
        dscores.append((
            (p32[:, :slots] * (dprob[:, :slots] - first)).astype(BF),
            (p32[:, slots:] * (dprob[:, slots:] - second)).astype(BF),
        ))
    for (r, p), ds in zip(units, dscores):
        k = qkv_ref[place(r, p, 1)]
        dqkv_ref[place(r, p, 0)] = mm(jnp.concatenate(ds, axis=1), by_head(k * scale)).astype(BF)
    for (r, p), ds in zip(units, dscores):
        q = qkv_ref[place(r, p, 0)]
        dqkv_ref[place(r, p, 1)] = mm_tn(jnp.concatenate(ds, axis=0), by_head(q * scale)).astype(BF)
    unit, _ = unit_parts(tok_ref[...].astype(F32))
    acc_ref[:, : 3 * width] += mm_tn(unit.astype(BF), dqkv_ref[...])
    grad_ref[...] = dqkv_ref[...]
    for i in range(3):
        part = dqkv_ref[:, i * width : (i + 1) * width].astype(F32)
        row_ref[i : i + 1, :] += jnp.sum(part, axis=0, keepdims=True)

    @pl.when(at == last)
    def _():
        core, own, other = info_ref[0], info_ref[3], info_ref[4]
        acc_ref[:, 4 * width :] = row_ref[...].T
        half = width // 2
        size = width // len(tables[0])
        for place in range(len(tables[0])):
            dst = dw_keep_ref if place * size < half else dw_send_ref
            block = block_at(place, tables, core, own if place * size < half else other)
            rows_at = pl.ds(pl.multiple_of(block * size, size), size)
            to = place * size % half
            dst[to : to + size, :] = acc_ref[rows_at, :].astype(BF)


def attend_back(info, tables, qkv, prob, gmix, tokens, vec, dwout):
    n, width = tokens.shape
    rows, pairs, slots, _ = prob.shape
    per = TOKS // slots
    return call(
        functools.partial(attend_back_kernel, tables),
        "attend_back",
        (n // TOKS,),
        [
            rows_of(3 * width),
            pl.BlockSpec((per, pairs, slots, 2 * slots), lambda i, *_: (i, 0, 0, 0)),
            rows_of(width),
            rows_of(width),
            whole(*vec.shape),
            whole(width, width),
        ],
        [rows_of(3 * width)] + [whole(width // 2, 4 * width + LANES)] * 2,
        [pltpu.VMEM((n, 3 * width), BF)] + [jax.ShapeDtypeStruct((width // 2, 4 * width + LANES), BF)] * 2,
        [
            pltpu.VMEM((TOKS, 3 * width), BF),
            pltpu.VMEM((width, 4 * width + LANES), F32),
            pltpu.VMEM((LANES, width), F32),
        ],
        info,
        far(qkv, prob, gmix, tokens, vec, dwout),
    )


def first_back_kernel(info_ref, dqkv_ref, wqkv_ref, tok_ref, gres_ref, g1_ref, out_ref):
    dnormed = mm_nt(dqkv_ref[...], wqkv_ref[...])
    unit, inv = unit_parts(tok_ref[...].astype(F32))
    out_ref[...] = gres_ref[...] + norm_back(dnormed, unit, inv, g1_ref[...])


def first_back(info, dqkv, wqkv, tokens, gres, g1):
    n, width = tokens.shape
    return call(
        first_back_kernel,
        "first_back",
        (n // TOKS,),
        [rows_of(3 * width), whole(*wqkv.shape), rows_of(width), rows_of(width), whole(1, width)],
        rows_of(width),
        jax.ShapeDtypeStruct((n, width), F32),
        [],
        info,
        near(dqkv) + (wqkv,) + far(tokens, gres, g1),
    )


def ffn_end_kernel(tables, info_ref, keep_ref, other_ref, up_ref, down_ref, full_ref):
    core = info_ref[0]
    units = up_ref.shape[1]
    blocks = len(tables[0])
    size = keep_ref.shape[0] // blocks

    def lay(src_ref, whose, base):
        for place in range(blocks):
            block = block_at(place, tables, whose, base)
            rows = pl.ds(pl.multiple_of(block * size, size), size)
            part = src_ref[place * size : (place + 1) * size, :].astype(F32)
            up_ref[rows, :] = part[:, :units]
            full_ref[rows, :] = part[:, units:]
        down_ref[...] = full_ref[...].T

    @pl.when(pl.program_id(0) == 0)
    def _():
        lay(keep_ref, core, info_ref[1])

    @pl.when(pl.program_id(0) == 1)
    def _():
        lay(other_ref, core ^ 1, info_ref[2])


def ffn_end(info, tables, keep, other):
    width, double = keep.shape
    units = double // 2
    return call(
        functools.partial(ffn_end_kernel, tables),
        "ffn_end",
        (2,),
        [whole(width, double)] * 2,
        [
            pl.BlockSpec((width, units), lambda i, info: (0, info[0] ^ i)),
            pl.BlockSpec((units, width), lambda i, info: (info[0] ^ i, 0)),
        ],
        [jax.ShapeDtypeStruct((width, double), F32), jax.ShapeDtypeStruct((double, width), F32)],
        [pltpu.VMEM((width, units), F32)],
        info,
        (keep, other),
    )


def attend_end_kernel(
    tables, shares, info_ref, keep_ref, other_ref, w_ref, g1_ref, c1_ref, qkv_hbm, out_hbm, *refs
):
    vec_refs, (qkv_ref, out_ref, col_ref, row_ref, sems) = refs[:6], refs[6:]
    core, own, away = info_ref[0], info_ref[3], info_ref[4]
    width = out_ref.shape[1]
    blocks = len(tables[0])
    size = out_ref.shape[0] // blocks
    half = out_ref.shape[0] // 2
    spots = []
    for place in range(blocks):
        mine = place * size < half
        block = block_at(place, tables, core, own if mine else away)
        at = place * size % half
        spots.append((keep_ref if mine else other_ref, slice(at, at + size), pl.multiple_of(block * size, size)))
    copies = []
    for i, (src, rows, to) in enumerate(spots):
        to = pl.ds(to, size)
        col_ref[to, :] = src[rows, 4 * width :].astype(F32)
        out_ref[rows if src is keep_ref else slice(rows.start + half, rows.stop + half), :] = src[
            rows, 3 * width : 4 * width
        ].astype(F32)
    for i, (src, rows, to) in enumerate(spots):
        rows = rows if src is keep_ref else slice(rows.start + half, rows.stop + half)
        copies.append(pltpu.make_async_copy(out_ref.at[rows, :], out_hbm.at[pl.ds(to, size), :], sems.at[i]))
        copies[-1].start()
    vec = col_ref[...].T
    row_ref[...] = vec
    wide_row = jnp.concatenate([vec[i : i + 1, :] for i in range(3)], axis=1)
    pair = jnp.concatenate([g1_ref[...], c1_ref[...], jnp.zeros((LANES - 2, width), F32)], axis=0).T
    col_ref[...] = pair
    lane = lax.broadcasted_iota(jnp.int32, (size, LANES), 1)
    for i, (src, rows, to) in enumerate(spots):
        here = pl.ds(to, size)
        gain_bias = col_ref[here, :]
        gain, bias = gain_bias[:, 0:1], gain_bias[:, 1:2]
        sums = src[rows, : 3 * width].astype(F32)
        w = w_ref[here, :].astype(F32)
        rows = rows if src is keep_ref else slice(rows.start + half, rows.stop + half)
        qkv_ref[rows, :] = gain * sums + bias * wide_row
        copies.append(pltpu.make_async_copy(qkv_ref.at[rows, :], qkv_hbm.at[here, :], sems.at[blocks + i]))
        copies[-1].start()
        d_gain = jnp.sum(w * sums, axis=1, keepdims=True)
        d_bias = jnp.sum(w * wide_row, axis=1, keepdims=True)
        col_ref[here, :] = jnp.where(lane == 0, d_gain, jnp.where(lane == 1, d_bias, 0.0))
    both = col_ref[...].T
    flat = lambda row: row.reshape(row.shape[1])
    vec_refs[0][...] = flat(both[0:1, :])
    vec_refs[1][...] = flat(both[1:2, :])
    for i in range(3):
        vec_refs[2 + i][...] = flat(vec[SUMS + i : SUMS + i + 1, :])
    units = vec_refs[5].shape[0]
    if units >= width:
        first = SUMS + 8 + info_ref[5] * (units // width)
        for i in range(units // width):
            vec_refs[5][i * width : (i + 1) * width] = flat(row_ref[pl.ds(first + i, 1), :])
    else:
        row = row_ref[pl.ds(SUMS + 8 + info_ref[5] // shares, 1), :]
        share = row[:, :units]
        for i in range(1, shares):
            share = jnp.where(info_ref[5] % shares == i, row[:, i * units : (i + 1) * units], share)
        vec_refs[5][...] = flat(share)
    for copy in copies:
        copy.wait()


def attend_end(info, tables, keep, other, w_qkv, g1, c1, units):
    rows, width = 2 * keep.shape[0], w_qkv.shape[0]
    blocks = len(tables[0])
    return call(
        functools.partial(attend_end_kernel, tables, max(1, width // units)),
        "attend_end",
        (1,),
        [whole(*keep.shape)] * 2 + [whole(*w_qkv.shape)] + [whole(1, width)] * 2,
        [pl.BlockSpec(memory_space=pl.ANY)] * 2 + [whole(width)] * 5 + [whole(units)],
        [jax.ShapeDtypeStruct((rows, 3 * width), F32), jax.ShapeDtypeStruct((rows, width), F32)]
        + [jax.ShapeDtypeStruct((width,), F32)] * 5
        + [jax.ShapeDtypeStruct((units,), F32)],
        [
            pltpu.VMEM((rows, 3 * width), F32),
            pltpu.VMEM((rows, width), F32),
            pltpu.VMEM((rows, LANES), F32),
            pltpu.VMEM((LANES, width), F32),
            pltpu.SemaphoreType.DMA((2 * blocks,)),
        ],
        info,
        (keep, other, w_qkv) + far(g1, c1),
    )


def local(
    wide, narrow, tokens_in, ln1_gain, ln1_bias, w_qkv, w_out, ln2_gain, ln2_bias, w_up, b_up, w_down, b_down, segment_ids,
    step_ids, pad_mask, cotangent,
):
    width = tokens_in.shape[1]
    units = w_up.shape[1] // 2
    core_mask = narrow
    narrow_masks = [1 << b for b in range(narrow.bit_length() - 1)]
    wide_masks = [narrow << b for b in range(1, wide.bit_length() - 1)]

    def swap(value, first, second=None):
        masks = (first, first if second is None else second)
        pairs = [(i, i ^ masks[i // narrow & 1]) for i in range(wide * narrow)]
        return lax.ppermute(value, AXES, pairs)

    def add(a, b):
        return (a.astype(F32) + b.astype(F32)).astype(a.dtype)

    def after(*values):
        return lax.optimization_barrier(values)

    def steps_of(halved, exchanged, gathered):
        pairs = lambda order: list(zip(*order))
        return (
            [("halve", *pair) for pair in pairs(halved)]
            + [("exchange", *pair) for pair in pairs(exchanged)]
            + [("gather", *pair) for pair in reversed(pairs(gathered))]
        )

    def start(value, step):
        kind, *masks = step
        if kind == "halve":
            half = value.shape[0] // 2
            return value[:half], swap(value[half:], *masks)
        return value, swap(value, *masks)

    def finish(kept, got, step):
        if step[0] == "gather":
            return jnp.concatenate([kept, got], axis=0)
        return (kept, got) if step[0] == "core" else add(kept, got)

    wide_at, narrow_at = lax.axis_index("wide"), lax.axis_index("narrow")
    core = wide_at & 1
    flat = wide_at * narrow + narrow_at

    def named(owner, used):
        return sum((1 << b) for b, m in enumerate(used) if owner & m)

    def block_of(used):
        return sum(((flat & m) != 0).astype(jnp.int32) << b for b, m in enumerate(used))

    def split_at(pair, count):
        return tuple(o[:count] for o in pair), tuple(o[count:] for o in pair)

    def by_core(values):
        return jnp.where(core == 0, values[0], values[1]), jnp.where(core == 0, values[1], values[0])

    mixing = narrow == 2 and len(wide_masks) == 3
    if mixing:
        y, low, high = wide_masks
        ff_in, ff_rest, ff_out = ([y, high], [y, low]), ([low], [high]), ([high, y], [low, y])
        at_in, at_rest, at_out = ([low, y, 1], [high, 1, y]), ([high], [low]), ([y, 1, low], [1, y, high])
        turns = "FAFAAFAFAAFAFA"
    else:
        ff_in, ff_rest = split_at((wide_masks, wide_masks), min(len(wide_masks) - 1, (width // TILE).bit_length() - 1))
        masks = narrow_masks + wide_masks
        at_in, at_rest = split_at((masks, masks), min(len(masks) - 1, (width // TILE // 2).bit_length() - 1))
        ff_out, at_out, turns = ff_in, at_in, ""
    ff_used = tuple(sorted(o) for o in ff_in)
    ff_in_tables, ff_out_tables = (
        tuple([named(owner, ff_used[c]) for owner in places(pair[c], 1 << len(ff_used[c]))] for c in range(2))
        for pair in (ff_in, ff_out)
    )
    at_used = tuple([core_mask] + sorted(o) for o in at_in)

    def at_tables(order):
        owners = [places(o, 1 << len(o)) for o in order]
        return tuple(
            [named(o, at_used[c]) for o in owners[c]] + [named(o ^ core_mask, at_used[1 - c]) for o in owners[1 - c]]
            for c in range(2)
        )

    ff_block = by_core([block_of(used) for used in ff_used])
    at_block = by_core([block_of(used) for used in at_used])
    info = jnp.stack([core, *ff_block, *at_block, narrow_at]).astype(jnp.int32)

    packed, tokens_in = after(pack(info, w_up, b_up, w_down), tokens_in)
    fetched = [packed]
    for mask in narrow_masks:
        fetched = fetched + [(swap(u, mask), swap(d, mask)) for u, d in fetched]

    row = lambda v: v[None].astype(F32)
    g1, c1, g2 = row(ln1_gain), row(ln1_bias), row(ln2_gain)
    qkv, prob, mixed, residual, second = attend(
        info, tokens_in, g1, c1, w_qkv, w_out, g2, row(ln2_bias), segment_ids, step_ids, pad_mask
    )
    out_part, dsec_part, own_keep, own_send, bias_own = ffn_own(
        info, ff_in_tables, mixing, second, cotangent, w_up, b_up, w_down
    )
    own_send, fetched = after(own_send, fetched)
    chunks = []
    for up, down in fetched[1:]:
        chunks += [(up, down), (swap(up, core_mask), swap(down, core_mask))]
    rest = ffn_rest(
        info, ff_in_tables, mixing, second, cotangent, out_part, dsec_part, residual, mixed, row(b_down), g2, w_out, own_keep,
        chunks,
    )
    block_out, gres, gmix, vec, dwout, bias_rest = rest[:6]
    grads = rest[6:]

    b_rest = bias_rest.reshape(-1, 2, units)
    b_rest = jnp.where(core == 0, b_rest, jnp.flip(b_rest, axis=1))
    b_all = jnp.concatenate([bias_own[None], b_rest], axis=0)
    for bit in range(narrow.bit_length() - 1):
        flipped = jnp.flip(b_all.reshape(-1, 2, (1 << bit) * 2, units), axis=1).reshape(b_all.shape)
        b_all = jnp.where(narrow_at >> bit & 1, flipped, b_all)
    vec = jnp.concatenate([vec, b_all.reshape(-1, width)], axis=0)

    if mixing:
        ff_keep, ff_send, away = grads
        got_own, got = swap(own_send, core_mask), swap(away, core_mask)
        chunk = (core == 0) | (lax.broadcasted_iota(jnp.int32, got.shape, 0) >= width // 2)
        ff_send = add(ff_send, jnp.where(chunk, got, got_own))
        gmix, ff_send = after(gmix, ff_send)
        ff_got, ff_keep, got_own, got = after(swap(ff_send, 1, y), ff_keep, got_own, got)
        top = width // 2
        ff_keep = add(ff_keep, jnp.where(chunk, got_own, got))
        ff_send = add(jnp.where(core == 0, ff_keep[top:], ff_keep[:top]), ff_got[top:])
        ff_keep = add(jnp.where(core == 0, ff_keep[:top], ff_keep[top:]), ff_got[:top])
    else:
        held = [add(own_keep, swap(own_send, core_mask))] + [add(grads[2 * j], swap(grads[2 * j + 1], core_mask)) for j in range(narrow - 1)]
        gmix, held = after(gmix, held)
        for mask in reversed(narrow_masks):
            held = [add(held[j], swap(held[j + mask], mask)) for j in range(mask)]
        ff_keep = ff_send = held[0]

    dqkv, keep, send = attend_back(info, at_tables(at_in), qkv, prob, gmix, tokens_in, vec, dwout)
    keep, ff_keep, ff_send = after(add(keep, swap(send, core_mask)), ff_keep, ff_send)
    grad_tokens = first_back(info, dqkv, w_qkv, tokens_in, gres, g1)
    steps = {
        "A": steps_of(at_in, at_rest, at_out) + [("core", core_mask)],
        "F": steps_of(ff_in, ff_rest, ff_out) + [("core", core_mask)],
    }
    if mixing:
        steps["F"] = [("halve", y, 1)] + steps["F"][1:]
        first = (ff_keep, swap(ff_send, y, 1))
    else:
        first = start(ff_keep, steps["F"][0])
    turns = turns or "".join(a + f for a, f in itertools.zip_longest("A" * len(steps["A"]), "F" * len(steps["F"]), fillvalue=""))
    under_way = {"A": start(keep, steps["A"][0]), "F": first}
    done, beside = (), (grad_tokens,)
    for turn in turns:
        other = "A" if turn == "F" else "F"
        kept, got = under_way.pop(turn)
        if other in under_way:
            other_kept, other_got = under_way[other]
            kept, other_kept, *beside = after(kept, other_kept, *beside)
            under_way[other] = other_kept, other_got
        else:
            kept, *beside = after(kept, *beside)
        if len(beside) == 1:
            (grad_tokens,), beside = beside, ()
        elif beside:
            (grad_w_up, grad_w_down), beside = beside, ()
        step, *steps[turn] = steps[turn]
        value = finish(kept, got, step)
        if steps[turn]:
            under_way[turn] = start(value, steps[turn][0])
        elif turn == "F":
            beside = ffn_end(info, ff_out_tables, *value)
        else:
            done = value
    grad_w_qkv, grad_w_out, d_gain1, d_bias1, d_gain2, d_bias2, d_bdown, grad_b_up = attend_end(
        info, at_tables(at_out), *done, w_qkv, g1, c1, 2 * units
    )
    return (
        block_out, grad_tokens, d_gain1, d_bias1, grad_w_qkv, grad_w_out, d_gain2, d_bias2, grad_w_up, grad_b_up, grad_w_down,
        d_bdown,
    )


def solution(mesh):
    rows = P(("wide", "narrow"), None)
    in_specs = (
        rows, P(), P(), P(), P(), P(), P(), P(None, "narrow"), P("narrow"), P("narrow", None), P(), rows, rows, rows, rows,
    )
    out_specs = (
        rows, rows, P(), P(), P(), P(), P(), P(), P(None, "narrow"), P("narrow"), P("narrow", None), P(),
    )
    wide, narrow = mesh.shape["wide"], mesh.shape["narrow"]
    return jax.shard_map(
        functools.partial(local, wide, narrow), mesh=mesh, in_specs=in_specs, out_specs=out_specs, check_vma=False
    )
```

```python
import functools
import itertools

import jax
import jax.numpy as jnp
import numpy as np
from jax import lax
from jax.experimental import pallas as pl
from jax.experimental.pallas import tpu as pltpu
from jax.sharding import PartitionSpec as P

HEAD = 64
PAIR = 2 * HEAD
NORM_EPS = 1e-05
BF = jnp.bfloat16
F32 = jnp.float32
AXES = ("wide", "narrow")
LANES = 128
SUMS = 8
TILE = 16
TOKS = 512
VMEM_LIMIT = 30 * 1024 * 1024
REST_LIMIT = 36 * 1024 * 1024


def mm(a, b):
    return lax.dot_general(a, b, (((1,), (0,)), ((), ())), preferred_element_type=F32)


def mm_nt(a, b):
    return lax.dot_general(a, b, (((1,), (1,)), ((), ())), preferred_element_type=F32)


def mm_tn(a, b):
    return lax.dot_general(a, b, (((0,), (0,)), ((), ())), preferred_element_type=F32)


def near(*values):
    return tuple(pltpu.with_memory_space_constraint(v, pltpu.VMEM) for v in values)


def far(*values):
    return tuple(pltpu.with_memory_space_constraint(v, pltpu.HBM) for v in values)


def whole(*shape):
    return pl.BlockSpec(shape, lambda *_: (0,) * len(shape))


def rows_of(width, toks=TOKS):
    return pl.BlockSpec((toks, width), lambda i, *_: (i, 0))


def call(kernel, name, grid, in_specs, out_specs, out_shape, scratch, info, args, vmem=VMEM_LIMIT):
    return pl.pallas_call(
        kernel,
        grid_spec=pltpu.PrefetchScalarGridSpec(
            num_scalar_prefetch=1, grid=grid, in_specs=in_specs, out_specs=out_specs, scratch_shapes=scratch
        ),
        out_shape=out_shape,
        compiler_params=pltpu.CompilerParams(vmem_limit_bytes=vmem),
        cost_estimate=pl.CostEstimate(flops=1000, bytes_accessed=1000, transcendentals=0),
        name=name,
    )(info, *args)


def unit_parts(rows):
    mean = jnp.mean(rows, axis=-1, keepdims=True)
    centered = rows - mean
    inv = lax.rsqrt(jnp.mean(centered * centered, axis=-1, keepdims=True) + NORM_EPS)
    return centered * inv, inv


def norm_back(incoming, unit, inv, gain):
    scaled = incoming * gain
    return inv * (
        scaled
        - jnp.mean(scaled, axis=-1, keepdims=True)
        - unit * jnp.mean(scaled * unit, axis=-1, keepdims=True)
    )


def gelu_pair(x):
    cdf = 0.5 * (1.0 + lax.erf(x * 0.7071067811865476))
    return x * cdf, cdf + x * jnp.exp(-0.5 * x * x) * 0.3989422804014327


def by_head(block):
    lane = lax.broadcasted_iota(jnp.int32, block.shape, 1)
    zero = jnp.zeros_like(block)
    first = lane < HEAD
    return jnp.concatenate([jnp.where(first, block, zero), jnp.where(first, zero, block)], axis=0)


def places(order, blocks):
    bits = blocks.bit_length() - 1
    table = []
    for place in range(blocks):
        owner = 0
        for step in range(bits):
            if place >> (bits - 1 - step) & 1:
                owner ^= order[step]
        table.append(owner)
    return table


def block_at(place, tables, core, own):
    first, second = tables[0][place], tables[1][place]
    if first == second:
        return own ^ first
    return own ^ jnp.where(core == 0, first, second)


def place_of(block, tables, core, own):
    wanted = own ^ block
    places_by_core = [[table.index(owner) for owner in range(len(table))] for table in tables]
    place = jnp.int32(0)
    for owner in range(len(tables[0])):
        first, second = places_by_core[0][owner], places_by_core[1][owner]
        place = jnp.where(wanted == owner, jnp.where(core == 0, first, second), place)
    return place


def permuted(dst_ref, acc_ref, chunk, tables, core, own, turned=0):
    blocks = len(tables[0])
    size = dst_ref.shape[0] // blocks
    for place in range(blocks):
        block = block_at(place, tables, core, own)
        rows = pl.ds(pl.multiple_of(block * size, size), size)
        to = pl.ds(pl.multiple_of(((place + turned * (blocks // 2)) & (blocks - 1)) * size, size), size)
        dst_ref[to, :] = acc_ref[chunk, rows, :].astype(dst_ref.dtype)


def attend_kernel(
    info_ref, tok_ref, g1_ref, c1_ref, wqkv_ref, wout_ref, g2_ref, c2_ref, seg_ref, step_ref, pad_ref,
    qkv_ref, prob_ref, mixed_ref, res_ref, second_ref,
):
    slots = seg_ref.shape[1]
    toks, width = tok_ref.shape
    rows = toks // slots
    at = pl.program_id(0)
    tokens = tok_ref[...].astype(F32)
    unit, _ = unit_parts(tokens)
    normed = (unit * g1_ref[...] + c1_ref[...]).astype(BF)
    qkv_ref[...] = mm(normed, wqkv_ref[...]).astype(BF)
    q_id = lax.broadcasted_iota(jnp.int32, (slots, slots), 0)
    k_id = lax.broadcasted_iota(jnp.int32, (slots, slots), 1)
    eye = q_id == k_id
    pairs = width // PAIR
    units = [(r, p) for r in range(rows) for p in range(pairs)]

    def part(r, p, which):
        return qkv_ref[r * slots : (r + 1) * slots, which * width + p * PAIR : which * width + (p + 1) * PAIR]

    masks = []
    for r in range(rows):
        here = pl.ds(at * rows + r, 1)
        seg = jnp.broadcast_to(seg_ref[here, :].astype(F32), (slots, slots))
        step = jnp.broadcast_to(step_ref[here, :].astype(F32), (slots, slots))
        live = jnp.broadcast_to(pad_ref[here, :], (slots, slots)) == 0
        masks.append(((seg == seg.T) & (step <= step.T) & live) | eye)
    scores = [mm_nt(part(r, p, 0), by_head(part(r, p, 1) * HEAD ** (-0.5))) for r, p in units]
    probs = []
    for (r, p), score in zip(units, scores):
        halves = []
        for half in (score[:, :slots], score[:, slots:]):
            half = jnp.where(masks[r], half, -1e30)
            weight = jnp.exp(half - jnp.max(half, axis=-1, keepdims=True))
            total = jnp.sum(weight, axis=-1, keepdims=True)
            halves.append((weight * (1.0 / total)).astype(BF))
        probs.append(jnp.concatenate(halves, axis=1))
    for (r, p), prob in zip(units, probs):
        prob_ref[r, p] = prob
        mixed_ref[r * slots : (r + 1) * slots, p * PAIR : (p + 1) * PAIR] = mm(prob, by_head(part(r, p, 2))).astype(BF)
    residual = tokens + mm(mixed_ref[...], wout_ref[...])
    res_ref[...] = residual
    unit, _ = unit_parts(residual)
    second_ref[...] = (unit * g2_ref[...] + c2_ref[...]).astype(BF)


def attend(info, tokens, g1, c1, wqkv, wout, g2, c2, seg, step, pad):
    n, width = tokens.shape
    rows, slots = seg.shape
    per, pairs = TOKS // slots, width // PAIR
    return call(
        attend_kernel,
        "attend",
        (n // TOKS,),
        [rows_of(width), whole(1, width), whole(1, width), whole(*wqkv.shape), whole(*wout.shape)]
        + [whole(1, width)] * 2
        + [whole(rows, slots)] * 3,
        [
            rows_of(3 * width),
            pl.BlockSpec((per, pairs, slots, 2 * slots), lambda i, *_: (i, 0, 0, 0)),
            rows_of(width),
            rows_of(width),
            rows_of(width),
        ],
        [
            pltpu.HBM((n, 3 * width), BF),
            pltpu.HBM((rows, pairs, slots, 2 * slots), BF),
            pltpu.HBM((n, width), BF),
            pltpu.HBM((n, width), F32),
            pltpu.VMEM((n, width), BF),
        ],
        [],
        info,
        far(tokens, g1, c1) + (wqkv, wout) + far(g2, c2, seg, step, pad),
    )


def pack_kernel(info_ref, up_ref, bias_ref, down_ref, up_out, down_out):
    width = up_ref.shape[0]
    up_out[:width, :] = up_ref[...]
    units = up_ref.shape[1]
    bias = bias_ref[...].reshape(1, 2 * units)
    bias = jnp.where(info_ref[0] == 0, bias[:, :units], bias[:, units:])
    up_out[width:, :] = jnp.broadcast_to(bias, (TILE, units))
    down_out[...] = down_ref[...]


def pack(info, up, bias, down):
    width, units = up.shape[0], up.shape[1] // 2
    return call(
        pack_kernel,
        "pack",
        (1,),
        [
            pl.BlockSpec((width, units), lambda t, info: (0, info[0])),
            whole(2 * units),
            pl.BlockSpec((units, width), lambda t, info: (info[0], 0)),
        ],
        [whole(width + TILE, units), whole(units, width)],
        [jax.ShapeDtypeStruct((width + TILE, units), BF), jax.ShapeDtypeStruct((units, width), BF)],
        [],
        info,
        far(up, bias, down),
    )


def ffn_block(sec, dy, up, bias, down, acc_ref, bacc_ref):
    pre = mm(sec, up) + bias
    dhid = mm_nt(dy, down)
    hid, slope = gelu_pair(pre)
    hid = hid.astype(BF)
    dpre = (dhid * slope).astype(BF)
    grad_up = mm(sec.T, dpre)
    grad_down = mm(dy.T, hid)
    sums = jnp.sum(dpre.astype(F32), axis=0, keepdims=True)
    chunks, _, double = acc_ref.shape
    units = double // 2
    for i in range(chunks):
        cols = slice(i * units, (i + 1) * units)
        acc_ref[i, :, :units] += grad_up[:, cols]
        acc_ref[i, :, units:] += grad_down[:, cols]
        bacc_ref[i : i + 1, :] += sums[:, cols]
    return hid, dpre


def ffn_own_kernel(
    tables, mixing, info_ref, sec_ref, dy_ref, up_ref, bias_ref, down_ref, out_ref, dsec_ref, keep_ref, send_ref, bias_out,
    acc_ref,
):
    at, last = pl.program_id(0), pl.num_programs(0) - 1

    @pl.when(at == 0)
    def _():
        acc_ref[...] = jnp.zeros_like(acc_ref)
        bias_out[...] = jnp.zeros_like(bias_out)

    bias = bias_ref[...].astype(F32).reshape(1, up_ref.shape[1])
    hid, dpre = ffn_block(sec_ref[...], dy_ref[...], up_ref[...], bias, down_ref[...], acc_ref, bias_out)
    out_ref[...] = mm(hid, down_ref[...])
    dsec_ref[...] = mm_nt(dpre, up_ref[...])

    @pl.when(at == last)
    def _():
        core, own, other = info_ref[0], info_ref[1], info_ref[2]
        permuted(keep_ref, acc_ref, core, tables, core, own)
        permuted(send_ref, acc_ref, core ^ 1, tables, core ^ 1, other, core ^ 1 if mixing else 0)


def ffn_own(info, tables, mixing, second, dy, up, bias, down):
    n, width = second.shape
    units = up.shape[1] // 2
    return call(
        functools.partial(ffn_own_kernel, tables, mixing),
        "ffn_own",
        (n // TOKS,),
        [rows_of(width), rows_of(width), whole(*up.shape), whole(*bias.shape), whole(*down.shape)],
        [rows_of(width)] * 2 + [whole(width, 2 * units)] * 2 + [whole(2, units)],
        [pltpu.VMEM((n, width), F32)] * 2
        + [pltpu.HBM((width, 2 * units), BF)] * 2
        + [jax.ShapeDtypeStruct((2, units), F32)],
        [pltpu.VMEM((2, width, 2 * units), F32)],
        info,
        near(second) + far(dy) + (up,) + far(bias) + (down,),
    )


def ffn_rest_kernel(
    tables, count, mixing, info_ref, sec_in, dy_in, out_in, dsec_in, res_in, mixed_in, mine_ref, bdown_ref, g2_ref, wout_ref, *refs
):
    ups, downs = refs[:count], refs[count : 2 * count]
    block_out, gres_out, gmix_out, vec_ref, dwout_ref, bias_out = refs[2 * count : 2 * count + 6]
    grads, refs = refs[2 * count + 6 : 3 * count + 6 + mixing], refs[3 * count + 6 + mixing :]
    sec_ref, dy_ref, out_ref, dsec_ref, res_ref, mixed_ref, branch_ref, up_ref, bias_ref, down_ref, laid_ref, sems = refs
    n, width = sec_ref.shape
    units = down_ref.shape[0] // count
    core = info_ref[0]
    half = width // 2
    top, low = pl.ds(0, half), pl.ds(half, half)
    used = iter(range(sems.shape[0]))

    def move(*pairs):
        copies = [pltpu.make_async_copy(*pair, sems.at[next(used)]) for pair in pairs]
        for copy in copies:
            copy.start()
        return copies

    def arrived(copies):
        for copy in copies:
            copy.wait()

    def by_core(first, *sets):
        def each(act):
            for odd, pairs in enumerate(sets):

                @pl.when(core == odd)
                def _(pairs=pairs):
                    for i, pair in enumerate(pairs):
                        act(pltpu.make_async_copy(*pair, sems.at[first + i]))

        return lambda: each(lambda copy: copy.start()), lambda: each(lambda copy: copy.wait())

    cols = [pl.ds(i * units, units) for i in range(count)]
    first = move(
        (sec_in, sec_ref),
        *[(ups[i].at[pl.ds(0, width), :], up_ref.at[:, cols[i]]) for i in range(count)],
        *[(ups[i].at[pl.ds(width, TILE), :], bias_ref.at[:, cols[i]]) for i in range(count)],
    )
    second = move((dy_in, dy_ref), *[(downs[i], down_ref.at[cols[i], :]) for i in range(count)])
    third = move((out_in, out_ref), (dsec_in, dsec_ref), (res_in, res_ref), (mixed_in, mixed_ref))
    if mixing:
        keep_ref, send_ref, away_ref = grads
        own_start, own_wait = by_core(
            next(used),
            [(mine_ref, keep_ref)],
            [(mine_ref.at[top], keep_ref.at[low]), (mine_ref.at[low], send_ref.at[top])],
        )
        next(used)
        chunk_start, chunk_wait = by_core(
            next(used),
            [(laid_ref.at[0], send_ref)],
            [(laid_ref.at[0, top], keep_ref.at[top]), (laid_ref.at[0, low], send_ref.at[low])],
        )
        next(used)
        own_start()

    arrived(first)
    toks = n if count <= 2 else n // 2
    grad_up = grad_down = sums = None
    parts = []
    for t in range(n // toks):
        rows = slice(t * toks, (t + 1) * toks)
        sec = sec_ref[rows, :]
        pre = mm(sec, up_ref[...]) + bias_ref[...].astype(F32)[:1]
        if t == 0:
            arrived(second)
        dy = dy_ref[rows, :]
        dhid = mm_nt(dy, down_ref[...])
        hid, slope = gelu_pair(pre)
        hid = hid.astype(BF)
        dpre = (dhid * slope).astype(BF)
        more = (mm(sec.T, dpre), mm(dy.T, hid), jnp.sum(dpre.astype(F32), axis=0, keepdims=True))
        if t:
            more = (grad_up + more[0], grad_down + more[1], sums + more[2])
        grad_up, grad_down, sums = more
        parts.append((hid, dpre))
    blocks = len(tables[0])
    size = width // blocks
    for i in range(count):
        at = slice(i * units, (i + 1) * units)
        bias_out[i : i + 1, :] = sums[:, at]
        for block in range(blocks):
            owner = core ^ (i % 2)
            place = place_of(block, tables, owner, info_ref[1 + i % 2])
            to = pl.ds(pl.multiple_of(place * size, size), size)
            rows = slice(block * size, (block + 1) * size)
            laid_ref[i, to, :units] = grad_up[rows, at].astype(BF)
            laid_ref[i, to, units:] = grad_down[rows, at].astype(BF)
    if mixing:
        chunk_start()
        gone = move((laid_ref.at[1], away_ref))
    else:
        gone = move(*[(laid_ref.at[i], grads[i]) for i in range(count)])

    arrived(third)
    step = min(TOKS // 2, toks)
    for t, (hid, dpre) in enumerate(parts):
        out_all, dsec_all = mm(hid, down_ref[...]), mm_nt(dpre, up_ref[...])
        for r in range(0, toks, step):
            rows = slice(t * toks + r, t * toks + r + step)
            span = pl.ds(rows.start, step)
            dy32 = dy_ref[rows, :].astype(F32)
            residual = res_ref[rows, :]
            dsec = dsec_all[r : r + step] + dsec_ref[rows, :]
            dy_ref[rows, :] = (residual + (out_all[r : r + step] + out_ref[rows, :] + bdown_ref[...])).astype(BF)
            unit, inv = unit_parts(residual)
            sums = [jnp.sum(v, axis=0, keepdims=True) for v in (dsec * unit, dsec, dy32)]
            for i, row in enumerate(sums):
                if rows.start:
                    vec_ref[i : i + 1, :] += row
                else:
                    vec_ref[i : i + 1, :] = row
            gres = dy32 + norm_back(dsec, unit, inv, g2_ref[...])
            out_ref[rows, :] = gres
            branch_ref[rows, :] = gres.astype(BF)
            gone += move((dy_ref.at[span, :], block_out.at[span, :]), (out_ref.at[span, :], gres_out.at[span, :]))
    vec_ref[3:, :] = jnp.zeros((vec_ref.shape[0] - 3, width), F32)
    sec_ref[...] = mm_nt(branch_ref[...], wout_ref[...]).astype(BF)
    gone += move((sec_ref, gmix_out))
    dwout_ref[...] = mm_tn(mixed_ref[...], branch_ref[...])
    arrived(gone)
    if mixing:
        own_wait()
        chunk_wait()


def ffn_rest(info, tables, mixing, second, dy, out_part, dsec_part, residual, mixed, bdown, g2, wout, mine, chunks):
    n, width = second.shape
    count = len(chunks)
    units = chunks[0][0].shape[1]
    anywhere = pl.BlockSpec(memory_space=pl.ANY)
    return call(
        functools.partial(ffn_rest_kernel, tables, count, mixing),
        "ffn_rest",
        (1,),
        [anywhere] * 7 + [whole(1, width)] * 2 + [whole(width, width)] + [anywhere] * (2 * count),
        [anywhere] * 3 + [whole(8, width), whole(width, width), whole(count, units)] + [anywhere] * (count + mixing),
        [
            jax.ShapeDtypeStruct((n, width), BF),
            pltpu.HBM((n, width), F32),
            pltpu.HBM((n, width), BF),
            jax.ShapeDtypeStruct((8, width), F32),
            pltpu.HBM((width, width), F32),
            jax.ShapeDtypeStruct((count, units), F32),
        ]
        + [jax.ShapeDtypeStruct((width, 2 * units), BF)] * (count + mixing),
        [
            pltpu.VMEM((n, width), BF),
            pltpu.VMEM((n, width), BF),
            pltpu.VMEM((n, width), F32),
            pltpu.VMEM((n, width), F32),
            pltpu.VMEM((n, width), F32),
            pltpu.VMEM((n, width), BF),
            pltpu.VMEM((n, width), BF),
            pltpu.VMEM((width, count * units), BF),
            pltpu.VMEM((TILE, count * units), BF),
            pltpu.VMEM((count * units, width), BF),
            pltpu.VMEM((count, width, 2 * units), BF),
            pltpu.SemaphoreType.DMA((24 + 4 * count,)),
        ],
        info,
        near(second)
        + far(dy)
        + near(out_part, dsec_part)
        + far(residual, mixed, mine, bdown, g2)
        + (wout,)
        + tuple(c[0] for c in chunks)
        + tuple(c[1] for c in chunks),
        REST_LIMIT if count <= 2 else 56 * 1024 * 1024,
    )


def join_kernel(info_ref, send_ref, got_ref, own_ref, out_ref):
    half = send_ref.shape[0] // 2
    out_ref[half:, :] = (send_ref[half:, :].astype(F32) + got_ref[half:, :].astype(F32)).astype(BF)

    @pl.when(info_ref[0] == 0)
    def _():
        out_ref[:half, :] = (send_ref[:half, :].astype(F32) + got_ref[:half, :].astype(F32)).astype(BF)

    @pl.when(info_ref[0] == 1)
    def _():
        out_ref[:half, :] = (send_ref[:half, :].astype(F32) + own_ref[:half, :].astype(F32)).astype(BF)


def split_kernel(info_ref, keep_ref, got_ref, own_ref, arrived_ref, keep_out, send_out):
    half = keep_ref.shape[0] // 2
    top, low = slice(0, half), slice(half, 2 * half)

    def total(*parts):
        value = parts[0].astype(F32)
        for part in parts[1:]:
            value += part.astype(F32)
        return value.astype(BF)

    @pl.when(info_ref[0] == 0)
    def _():
        keep_out[...] = total(keep_ref[top, :], own_ref[top, :], arrived_ref[top, :])
        send_out[...] = total(keep_ref[low, :], own_ref[low, :], arrived_ref[low, :])

    @pl.when(info_ref[0] == 1)
    def _():
        keep_out[...] = total(keep_ref[low, :], own_ref[low, :], arrived_ref[top, :])
        send_out[...] = total(keep_ref[top, :], got_ref[top, :], arrived_ref[low, :])


def direct(kernel, name, info, out_shape, args):
    return pl.pallas_call(
        kernel,
        in_specs=[pl.BlockSpec(memory_space=pltpu.SMEM)] + [pl.BlockSpec(memory_space=pltpu.VMEM)] * len(args),
        out_specs=jax.tree.map(lambda _: pl.BlockSpec(memory_space=pltpu.VMEM), out_shape),
        out_shape=out_shape,
        compiler_params=pltpu.CompilerParams(vmem_limit_bytes=VMEM_LIMIT),
        cost_estimate=pl.CostEstimate(flops=1000, bytes_accessed=1000, transcendentals=0),
        name=name,
    )(info, *args)


def join(info, send, got, own):
    return direct(join_kernel, "join", info, jax.ShapeDtypeStruct(send.shape, BF), (send, got, own))


def split(info, keep, got, own, arrived):
    shape = jax.ShapeDtypeStruct((keep.shape[0] // 2, keep.shape[1]), BF)
    return direct(split_kernel, "split", info, [shape, shape], (keep, got, own, arrived))


def attend_back_kernel(
    tables, info_ref, qkv_ref, prob_ref, gmix_ref, tok_ref, vec_ref, dwout_ref, grad_ref, dw_keep_ref, dw_send_ref,
    dqkv_ref, acc_ref, row_ref,
):
    at, last = pl.program_id(0), pl.num_programs(0) - 1
    toks, width = tok_ref.shape
    rows, pairs, slots, _ = prob_ref.shape

    @pl.when(at == 0)
    def _():
        acc_ref[:, : 3 * width] = jnp.zeros((width, 3 * width), F32)
        acc_ref[:, 3 * width : 4 * width] = dwout_ref[...]
        row_ref[...] = jnp.zeros_like(row_ref)
        row_ref[SUMS : SUMS + vec_ref.shape[0], :] = vec_ref[...]

    scale = HEAD ** (-0.5)
    units = [(r, p) for r in range(rows) for p in range(pairs)]

    def place(r, p, which):
        return (slice(r * slots, (r + 1) * slots), slice(which * width + p * PAIR, which * width + (p + 1) * PAIR))

    grads = [gmix_ref[place(r, p, 0)] for r, p in units]
    dprobs = [mm_nt(g, by_head(qkv_ref[place(r, p, 2)])) for (r, p), g in zip(units, grads)]
    for (r, p), g in zip(units, grads):
        prob = prob_ref[r, p]
        stacked = jnp.concatenate([prob[:, :slots], prob[:, slots:]], axis=0)
        dqkv_ref[place(r, p, 2)] = mm_tn(stacked, by_head(g)).astype(BF)
    dscores = []
    for (r, p), dprob in zip(units, dprobs):
        p32 = prob_ref[r, p].astype(F32)
        prod = p32 * dprob
        first = jnp.sum(prod[:, :slots], axis=-1, keepdims=True)
        second = jnp.sum(prod[:, slots:], axis=-1, keepdims=True)
        dscores.append((
            (p32[:, :slots] * (dprob[:, :slots] - first)).astype(BF),
            (p32[:, slots:] * (dprob[:, slots:] - second)).astype(BF),
        ))
    for (r, p), ds in zip(units, dscores):
        k = qkv_ref[place(r, p, 1)]
        dqkv_ref[place(r, p, 0)] = mm(jnp.concatenate(ds, axis=1), by_head(k * scale)).astype(BF)
    for (r, p), ds in zip(units, dscores):
        q = qkv_ref[place(r, p, 0)]
        dqkv_ref[place(r, p, 1)] = mm_tn(jnp.concatenate(ds, axis=0), by_head(q * scale)).astype(BF)
    unit, _ = unit_parts(tok_ref[...].astype(F32))
    acc_ref[:, : 3 * width] += mm_tn(unit.astype(BF), dqkv_ref[...])
    grad_ref[...] = dqkv_ref[...]
    for i in range(3):
        part = dqkv_ref[:, i * width : (i + 1) * width].astype(F32)
        row_ref[i : i + 1, :] += jnp.sum(part, axis=0, keepdims=True)

    @pl.when(at == last)
    def _():
        core, own, other = info_ref[0], info_ref[3], info_ref[4]
        acc_ref[:, 4 * width :] = row_ref[...].T
        half = width // 2
        size = width // len(tables[0])
        for place in range(len(tables[0])):
            dst = dw_keep_ref if place * size < half else dw_send_ref
            block = block_at(place, tables, core, own if place * size < half else other)
            rows_at = pl.ds(pl.multiple_of(block * size, size), size)
            to = place * size % half
            dst[to : to + size, :] = acc_ref[rows_at, :].astype(BF)


def attend_back(info, tables, qkv, prob, gmix, tokens, vec, dwout):
    n, width = tokens.shape
    rows, pairs, slots, _ = prob.shape
    per = TOKS // slots
    return call(
        functools.partial(attend_back_kernel, tables),
        "attend_back",
        (n // TOKS,),
        [
            rows_of(3 * width),
            pl.BlockSpec((per, pairs, slots, 2 * slots), lambda i, *_: (i, 0, 0, 0)),
            rows_of(width),
            rows_of(width),
            whole(*vec.shape),
            whole(width, width),
        ],
        [rows_of(3 * width)] + [whole(width // 2, 4 * width + LANES)] * 2,
        [pltpu.VMEM((n, 3 * width), BF)] + [jax.ShapeDtypeStruct((width // 2, 4 * width + LANES), BF)] * 2,
        [
            pltpu.VMEM((TOKS, 3 * width), BF),
            pltpu.VMEM((width, 4 * width + LANES), F32),
            pltpu.VMEM((LANES, width), F32),
        ],
        info,
        far(qkv, prob, gmix, tokens, vec, dwout),
    )


def first_back_kernel(info_ref, dqkv_ref, wqkv_ref, tok_ref, gres_ref, g1_ref, out_ref):
    dnormed = mm_nt(dqkv_ref[...], wqkv_ref[...])
    unit, inv = unit_parts(tok_ref[...].astype(F32))
    out_ref[...] = gres_ref[...] + norm_back(dnormed, unit, inv, g1_ref[...])


def first_back(info, dqkv, wqkv, tokens, gres, g1):
    n, width = tokens.shape
    return call(
        first_back_kernel,
        "first_back",
        (n // TOKS,),
        [rows_of(3 * width), whole(*wqkv.shape), rows_of(width), rows_of(width), whole(1, width)],
        rows_of(width),
        jax.ShapeDtypeStruct((n, width), F32),
        [],
        info,
        near(dqkv) + (wqkv,) + far(tokens, gres, g1),
    )


def ffn_end_kernel(tables, info_ref, keep_ref, other_ref, up_ref, down_ref, full_ref):
    core = info_ref[0]
    units = up_ref.shape[1]
    blocks = len(tables[0])
    size = keep_ref.shape[0] // blocks

    def lay(src_ref, whose, base):
        for place in range(blocks):
            block = block_at(place, tables, whose, base)
            rows = pl.ds(pl.multiple_of(block * size, size), size)
            part = src_ref[place * size : (place + 1) * size, :].astype(F32)
            up_ref[rows, :] = part[:, :units]
            full_ref[rows, :] = part[:, units:]
        down_ref[...] = full_ref[...].T

    @pl.when(pl.program_id(0) == 0)
    def _():
        lay(keep_ref, core, info_ref[1])

    @pl.when(pl.program_id(0) == 1)
    def _():
        lay(other_ref, core ^ 1, info_ref[2])


def ffn_end(info, tables, keep, other):
    width, double = keep.shape
    units = double // 2
    return call(
        functools.partial(ffn_end_kernel, tables),
        "ffn_end",
        (2,),
        [whole(width, double)] * 2,
        [
            pl.BlockSpec((width, units), lambda i, info: (0, info[0] ^ i)),
            pl.BlockSpec((units, width), lambda i, info: (info[0] ^ i, 0)),
        ],
        [jax.ShapeDtypeStruct((width, double), F32), jax.ShapeDtypeStruct((double, width), F32)],
        [pltpu.VMEM((width, units), F32)],
        info,
        (keep, other),
    )


def attend_end_kernel(
    tables, shares, info_ref, keep_ref, other_ref, w_ref, g1_ref, c1_ref, qkv_hbm, out_hbm, *refs
):
    vec_refs, (qkv_ref, out_ref, col_ref, row_ref, sems) = refs[:6], refs[6:]
    core, own, away = info_ref[0], info_ref[3], info_ref[4]
    width = out_ref.shape[1]
    blocks = len(tables[0])
    size = out_ref.shape[0] // blocks
    half = out_ref.shape[0] // 2
    spots = []
    for place in range(blocks):
        mine = place * size < half
        block = block_at(place, tables, core, own if mine else away)
        at = place * size % half
        spots.append((keep_ref if mine else other_ref, slice(at, at + size), pl.multiple_of(block * size, size)))
    copies = []
    for i, (src, rows, to) in enumerate(spots):
        to = pl.ds(to, size)
        col_ref[to, :] = src[rows, 4 * width :].astype(F32)
        out_ref[rows if src is keep_ref else slice(rows.start + half, rows.stop + half), :] = src[
            rows, 3 * width : 4 * width
        ].astype(F32)
    for i, (src, rows, to) in enumerate(spots):
        rows = rows if src is keep_ref else slice(rows.start + half, rows.stop + half)
        copies.append(pltpu.make_async_copy(out_ref.at[rows, :], out_hbm.at[pl.ds(to, size), :], sems.at[i]))
        copies[-1].start()
    vec = col_ref[...].T
    row_ref[...] = vec
    wide_row = jnp.concatenate([vec[i : i + 1, :] for i in range(3)], axis=1)
    pair = jnp.concatenate([g1_ref[...], c1_ref[...], jnp.zeros((LANES - 2, width), F32)], axis=0).T
    col_ref[...] = pair
    lane = lax.broadcasted_iota(jnp.int32, (size, LANES), 1)
    for i, (src, rows, to) in enumerate(spots):
        here = pl.ds(to, size)
        gain_bias = col_ref[here, :]
        gain, bias = gain_bias[:, 0:1], gain_bias[:, 1:2]
        sums = src[rows, : 3 * width].astype(F32)
        w = w_ref[here, :].astype(F32)
        rows = rows if src is keep_ref else slice(rows.start + half, rows.stop + half)
        qkv_ref[rows, :] = gain * sums + bias * wide_row
        copies.append(pltpu.make_async_copy(qkv_ref.at[rows, :], qkv_hbm.at[here, :], sems.at[blocks + i]))
        copies[-1].start()
        d_gain = jnp.sum(w * sums, axis=1, keepdims=True)
        d_bias = jnp.sum(w * wide_row, axis=1, keepdims=True)
        col_ref[here, :] = jnp.where(lane == 0, d_gain, jnp.where(lane == 1, d_bias, 0.0))
    both = col_ref[...].T
    flat = lambda row: row.reshape(row.shape[1])
    vec_refs[0][...] = flat(both[0:1, :])
    vec_refs[1][...] = flat(both[1:2, :])
    for i in range(3):
        vec_refs[2 + i][...] = flat(vec[SUMS + i : SUMS + i + 1, :])
    units = vec_refs[5].shape[0]
    if units >= width:
        first = SUMS + 8 + info_ref[5] * (units // width)
        for i in range(units // width):
            vec_refs[5][i * width : (i + 1) * width] = flat(row_ref[pl.ds(first + i, 1), :])
    else:
        row = row_ref[pl.ds(SUMS + 8 + info_ref[5] // shares, 1), :]
        share = row[:, :units]
        for i in range(1, shares):
            share = jnp.where(info_ref[5] % shares == i, row[:, i * units : (i + 1) * units], share)
        vec_refs[5][...] = flat(share)
    for copy in copies:
        copy.wait()


def attend_end(info, tables, keep, other, w_qkv, g1, c1, units):
    rows, width = 2 * keep.shape[0], w_qkv.shape[0]
    blocks = len(tables[0])
    return call(
        functools.partial(attend_end_kernel, tables, max(1, width // units)),
        "attend_end",
        (1,),
        [whole(*keep.shape)] * 2 + [whole(*w_qkv.shape)] + [whole(1, width)] * 2,
        [pl.BlockSpec(memory_space=pl.ANY)] * 2 + [whole(width)] * 5 + [whole(units)],
        [jax.ShapeDtypeStruct((rows, 3 * width), F32), jax.ShapeDtypeStruct((rows, width), F32)]
        + [jax.ShapeDtypeStruct((width,), F32)] * 5
        + [jax.ShapeDtypeStruct((units,), F32)],
        [
            pltpu.VMEM((rows, 3 * width), F32),
            pltpu.VMEM((rows, width), F32),
            pltpu.VMEM((rows, LANES), F32),
            pltpu.VMEM((LANES, width), F32),
            pltpu.SemaphoreType.DMA((2 * blocks,)),
        ],
        info,
        (keep, other, w_qkv) + far(g1, c1),
    )


def local(
    wide, narrow, tokens_in, ln1_gain, ln1_bias, w_qkv, w_out, ln2_gain, ln2_bias, w_up, b_up, w_down, b_down, segment_ids,
    step_ids, pad_mask, cotangent,
):
    width = tokens_in.shape[1]
    units = w_up.shape[1] // 2
    core_mask = narrow
    narrow_masks = [1 << b for b in range(narrow.bit_length() - 1)]
    wide_masks = [narrow << b for b in range(1, wide.bit_length() - 1)]

    def swap(value, first, second=None):
        masks = (first, first if second is None else second)
        pairs = [(i, i ^ masks[i // narrow & 1]) for i in range(wide * narrow)]
        return lax.ppermute(value, AXES, pairs)

    def add(a, b):
        return (a.astype(F32) + b.astype(F32)).astype(a.dtype)

    def after(*values):
        return lax.optimization_barrier(values)

    def steps_of(halved, exchanged, gathered):
        pairs = lambda order: list(zip(*order))
        return (
            [("halve", *pair) for pair in pairs(halved)]
            + [("exchange", *pair) for pair in pairs(exchanged)]
            + [("gather", *pair) for pair in reversed(pairs(gathered))]
        )

    def start(value, step):
        kind, *masks = step
        if kind == "halve":
            half = value.shape[0] // 2
            return value[:half], swap(value[half:], *masks)
        return value, swap(value, *masks)

    def finish(kept, got, step):
        if step[0] == "gather":
            return jnp.concatenate([kept, got], axis=0)
        return (kept, got) if step[0] == "core" else add(kept, got)

    wide_at, narrow_at = lax.axis_index("wide"), lax.axis_index("narrow")
    core = wide_at & 1
    flat = wide_at * narrow + narrow_at

    def named(owner, used):
        return sum((1 << b) for b, m in enumerate(used) if owner & m)

    def block_of(used):
        return sum(((flat & m) != 0).astype(jnp.int32) << b for b, m in enumerate(used))

    def split_at(pair, count):
        return tuple(o[:count] for o in pair), tuple(o[count:] for o in pair)

    def by_core(values):
        return jnp.where(core == 0, values[0], values[1]), jnp.where(core == 0, values[1], values[0])

    mixing = narrow == 2 and len(wide_masks) == 3
    if mixing:
        y, low, high = wide_masks
        ff_in, ff_rest, ff_out = ([y, low], [y, low]), ([high], [high]), ([y, low], [y, low])
        at_in, at_rest, at_out = ([y, 1, low], [low, y, 1]), ([high], [high]), ([y, 1, low], [low, 1, y])
        turns = "FAFAAFAFAAFFAA"
    else:
        ff_in, ff_rest = split_at((wide_masks, wide_masks), min(len(wide_masks) - 1, (width // TILE).bit_length() - 1))
        masks = narrow_masks + wide_masks
        at_in, at_rest = split_at((masks, masks), min(len(masks) - 1, (width // TILE // 2).bit_length() - 1))
        ff_out, at_out, turns = ff_in, at_in, ""
    ff_used = tuple(sorted(o) for o in ff_in)
    ff_in_tables, ff_out_tables = (
        tuple([named(owner, ff_used[c]) for owner in places(pair[c], 1 << len(ff_used[c]))] for c in range(2))
        for pair in (ff_in, ff_out)
    )
    at_used = tuple([core_mask] + sorted(o) for o in at_in)

    def at_tables(order):
        owners = [places(o, 1 << len(o)) for o in order]
        return tuple(
            [named(o, at_used[c]) for o in owners[c]] + [named(o ^ core_mask, at_used[1 - c]) for o in owners[1 - c]]
            for c in range(2)
        )

    ff_block = by_core([block_of(used) for used in ff_used])
    at_block = by_core([block_of(used) for used in at_used])
    info = jnp.stack([core, *ff_block, *at_block, narrow_at]).astype(jnp.int32)

    packed, tokens_in = after(pack(info, w_up, b_up, w_down), tokens_in)
    fetched = [packed]
    for mask in narrow_masks:
        fetched = fetched + [(swap(u, mask), swap(d, mask)) for u, d in fetched]

    row = lambda v: v[None].astype(F32)
    g1, c1, g2 = row(ln1_gain), row(ln1_bias), row(ln2_gain)
    qkv, prob, mixed, residual, second = attend(
        info, tokens_in, g1, c1, w_qkv, w_out, g2, row(ln2_bias), segment_ids, step_ids, pad_mask
    )
    out_part, dsec_part, own_keep, own_send, bias_own = ffn_own(
        info, ff_in_tables, mixing, second, cotangent, w_up, b_up, w_down
    )
    own_send, fetched = after(own_send, fetched)
    chunks = []
    for up, down in fetched[1:]:
        chunks += [(up, down), (swap(up, core_mask), swap(down, core_mask))]
    rest = ffn_rest(
        info, ff_in_tables, mixing, second, cotangent, out_part, dsec_part, residual, mixed, row(b_down), g2, w_out, own_keep,
        chunks,
    )
    block_out, gres, gmix, vec, dwout, bias_rest = rest[:6]
    grads = rest[6:]

    b_rest = bias_rest.reshape(-1, 2, units)
    b_rest = jnp.where(core == 0, b_rest, jnp.flip(b_rest, axis=1))
    b_all = jnp.concatenate([bias_own[None], b_rest], axis=0)
    for bit in range(narrow.bit_length() - 1):
        flipped = jnp.flip(b_all.reshape(-1, 2, (1 << bit) * 2, units), axis=1).reshape(b_all.shape)
        b_all = jnp.where(narrow_at >> bit & 1, flipped, b_all)
    vec = jnp.concatenate([vec, b_all.reshape(-1, width)], axis=0)

    if mixing:
        ff_keep, ff_send, away = grads
        got_own, got = swap(own_send, core_mask), swap(away, core_mask)
        ff_send = join(info, ff_send, got, got_own)
        gmix, ff_send = after(gmix, ff_send)
        ff_got = swap(ff_send, 1, y)
    else:
        held = [add(own_keep, swap(own_send, core_mask))] + [add(grads[2 * j], swap(grads[2 * j + 1], core_mask)) for j in range(narrow - 1)]
        gmix, held = after(gmix, held)
        for mask in reversed(narrow_masks):
            held = [add(held[j], swap(held[j + mask], mask)) for j in range(mask)]
        ff_keep = held[0]

    dqkv, keep, send = attend_back(info, at_tables(at_in), qkv, prob, gmix, tokens_in, vec, dwout)
    if mixing:
        send, ff_got = after(send, ff_got)
        ff_keep, ff_send = split(info, ff_keep, got, got_own, ff_got)
    keep = add(keep, swap(send, core_mask))
    grad_tokens = first_back(info, dqkv, w_qkv, tokens_in, gres, g1)
    steps = {
        "A": steps_of(at_in, at_rest, at_out) + [("core", core_mask)],
        "F": steps_of(ff_in, ff_rest, ff_out) + [("core", core_mask)],
    }
    if mixing:
        steps["F"] = [("halve", y, 1)] + steps["F"][1:]
        first = (ff_keep, swap(ff_send, y, 1))
    else:
        first = start(ff_keep, steps["F"][0])
    turns = turns or "".join(a + f for a, f in itertools.zip_longest("A" * len(steps["A"]), "F" * len(steps["F"]), fillvalue=""))
    under_way = {"A": start(keep, steps["A"][0]), "F": first}
    done, beside = (), (grad_tokens,)
    for turn in turns:
        other = "A" if turn == "F" else "F"
        kept, got = under_way.pop(turn)
        if other in under_way:
            other_kept, other_got = under_way[other]
            kept, other_kept, *beside = after(kept, other_kept, *beside)
            under_way[other] = other_kept, other_got
        else:
            kept, *beside = after(kept, *beside)
        if len(beside) == 1:
            (grad_tokens,), beside = beside, ()
        elif beside:
            (grad_w_up, grad_w_down), beside = beside, ()
        step, *steps[turn] = steps[turn]
        value = finish(kept, got, step)
        if steps[turn]:
            under_way[turn] = start(value, steps[turn][0])
        elif turn == "F":
            beside = ffn_end(info, ff_out_tables, *value)
        else:
            done = value
    grad_w_qkv, grad_w_out, d_gain1, d_bias1, d_gain2, d_bias2, d_bdown, grad_b_up = attend_end(
        info, at_tables(at_out), *done, w_qkv, g1, c1, 2 * units
    )
    return (
        block_out, grad_tokens, d_gain1, d_bias1, grad_w_qkv, grad_w_out, d_gain2, d_bias2, grad_w_up, grad_b_up, grad_w_down,
        d_bdown,
    )


def solution(mesh):
    rows = P(("wide", "narrow"), None)
    in_specs = (
        rows, P(), P(), P(), P(), P(), P(), P(None, "narrow"), P("narrow"), P("narrow", None), P(), rows, rows, rows, rows,
    )
    out_specs = (
        rows, rows, P(), P(), P(), P(), P(), P(), P(None, "narrow"), P("narrow"), P("narrow", None), P(),
    )
    wide, narrow = mesh.shape["wide"], mesh.shape["narrow"]
    return jax.shard_map(
        functools.partial(local, wide, narrow), mesh=mesh, in_specs=in_specs, out_specs=out_specs, check_vma=False
    )
```

```python
import functools
import itertools

import jax
import jax.numpy as jnp
import numpy as np
from jax import lax
from jax.experimental import pallas as pl
from jax.experimental.pallas import tpu as pltpu
from jax.sharding import PartitionSpec as P

HEAD = 64
PAIR = 2 * HEAD
NORM_EPS = 1e-05
BF = jnp.bfloat16
F32 = jnp.float32
AXES = ("wide", "narrow")
LANES = 128
SUMS = 8
TILE = 16
TOKS = 512
VMEM_LIMIT = 30 * 1024 * 1024
REST_LIMIT = 36 * 1024 * 1024


def mm(a, b):
    return lax.dot_general(a, b, (((1,), (0,)), ((), ())), preferred_element_type=F32)


def mm_nt(a, b):
    return lax.dot_general(a, b, (((1,), (1,)), ((), ())), preferred_element_type=F32)


def mm_tn(a, b):
    return lax.dot_general(a, b, (((0,), (0,)), ((), ())), preferred_element_type=F32)


def near(*values):
    return tuple(pltpu.with_memory_space_constraint(v, pltpu.VMEM) for v in values)


def far(*values):
    return tuple(pltpu.with_memory_space_constraint(v, pltpu.HBM) for v in values)


def whole(*shape):
    return pl.BlockSpec(shape, lambda *_: (0,) * len(shape))


def rows_of(width, toks=TOKS):
    return pl.BlockSpec((toks, width), lambda i, *_: (i, 0))


def call(kernel, name, grid, in_specs, out_specs, out_shape, scratch, info, args, vmem=VMEM_LIMIT):
    return pl.pallas_call(
        kernel,
        grid_spec=pltpu.PrefetchScalarGridSpec(
            num_scalar_prefetch=1, grid=grid, in_specs=in_specs, out_specs=out_specs, scratch_shapes=scratch
        ),
        out_shape=out_shape,
        compiler_params=pltpu.CompilerParams(vmem_limit_bytes=vmem),
        cost_estimate=pl.CostEstimate(flops=1000, bytes_accessed=1000, transcendentals=0),
        name=name,
    )(info, *args)


def unit_parts(rows):
    mean = jnp.mean(rows, axis=-1, keepdims=True)
    centered = rows - mean
    inv = lax.rsqrt(jnp.mean(centered * centered, axis=-1, keepdims=True) + NORM_EPS)
    return centered * inv, inv


def norm_back(incoming, unit, inv, gain):
    scaled = incoming * gain
    return inv * (
        scaled
        - jnp.mean(scaled, axis=-1, keepdims=True)
        - unit * jnp.mean(scaled * unit, axis=-1, keepdims=True)
    )


def gelu_pair(x):
    cdf = 0.5 * (1.0 + lax.erf(x * 0.7071067811865476))
    return x * cdf, cdf + x * jnp.exp(-0.5 * x * x) * 0.3989422804014327


def by_head(block):
    lane = lax.broadcasted_iota(jnp.int32, block.shape, 1)
    zero = jnp.zeros_like(block)
    first = lane < HEAD
    return jnp.concatenate([jnp.where(first, block, zero), jnp.where(first, zero, block)], axis=0)


def places(order, blocks):
    bits = blocks.bit_length() - 1
    table = []
    for place in range(blocks):
        owner = 0
        for step in range(bits):
            if place >> (bits - 1 - step) & 1:
                owner ^= order[step]
        table.append(owner)
    return table


def block_at(place, tables, core, own):
    first, second = tables[0][place], tables[1][place]
    if first == second:
        return own ^ first
    return own ^ jnp.where(core == 0, first, second)


def place_of(block, tables, core, own):
    wanted = own ^ block
    places_by_core = [[table.index(owner) for owner in range(len(table))] for table in tables]
    place = jnp.int32(0)
    for owner in range(len(tables[0])):
        first, second = places_by_core[0][owner], places_by_core[1][owner]
        place = jnp.where(wanted == owner, jnp.where(core == 0, first, second), place)
    return place


def permuted(dst_ref, acc_ref, chunk, tables, core, own, turned=0):
    blocks = len(tables[0])
    size = dst_ref.shape[0] // blocks
    for place in range(blocks):
        block = block_at(place, tables, core, own)
        rows = pl.ds(pl.multiple_of(block * size, size), size)
        to = pl.ds(pl.multiple_of(((place + turned * (blocks // 2)) & (blocks - 1)) * size, size), size)
        dst_ref[to, :] = acc_ref[chunk, rows, :].astype(dst_ref.dtype)


def attend_kernel(
    info_ref, tok_ref, g1_ref, c1_ref, wqkv_ref, wout_ref, g2_ref, c2_ref, seg_ref, step_ref, pad_ref,
    qkv_ref, prob_ref, mixed_ref, res_ref, second_ref,
):
    slots = seg_ref.shape[1]
    toks, width = tok_ref.shape
    rows = toks // slots
    at = pl.program_id(0)
    tokens = tok_ref[...].astype(F32)
    unit, _ = unit_parts(tokens)
    normed = (unit * g1_ref[...] + c1_ref[...]).astype(BF)
    qkv_ref[...] = mm(normed, wqkv_ref[...]).astype(BF)
    q_id = lax.broadcasted_iota(jnp.int32, (slots, slots), 0)
    k_id = lax.broadcasted_iota(jnp.int32, (slots, slots), 1)
    eye = q_id == k_id
    pairs = width // PAIR
    units = [(r, p) for r in range(rows) for p in range(pairs)]

    def part(r, p, which):
        return qkv_ref[r * slots : (r + 1) * slots, which * width + p * PAIR : which * width + (p + 1) * PAIR]

    masks = []
    for r in range(rows):
        here = pl.ds(at * rows + r, 1)
        seg = jnp.broadcast_to(seg_ref[here, :].astype(F32), (slots, slots))
        step = jnp.broadcast_to(step_ref[here, :].astype(F32), (slots, slots))
        live = jnp.broadcast_to(pad_ref[here, :].astype(F32), (slots, slots)).T == 0
        masks.append(((seg == seg.T) & (step.T <= step) & live) | eye)
    scores = [mm_nt(part(r, p, 1), by_head(part(r, p, 0) * HEAD ** (-0.5))) for r, p in units]
    probs = []
    for (r, p), score in zip(units, scores):
        halves = []
        for half in (score[:, :slots], score[:, slots:]):
            half = jnp.where(masks[r], half, -1e30)
            weight = jnp.exp(half - jnp.max(half, axis=0, keepdims=True))
            total = jnp.sum(weight, axis=0, keepdims=True)
            halves.append((weight * (1.0 / total)).astype(BF))
        probs.append(halves)
    for (r, p), halves in zip(units, probs):
        prob_ref[r, p] = jnp.concatenate(halves, axis=1)
        mixed = mm_tn(jnp.concatenate(halves, axis=0), by_head(part(r, p, 2)))
        mixed_ref[r * slots : (r + 1) * slots, p * PAIR : (p + 1) * PAIR] = mixed.astype(BF)
    residual = tokens + mm(mixed_ref[...], wout_ref[...])
    res_ref[...] = residual
    unit, _ = unit_parts(residual)
    second_ref[...] = (unit * g2_ref[...] + c2_ref[...]).astype(BF)


def attend(info, tokens, g1, c1, wqkv, wout, g2, c2, seg, step, pad):
    n, width = tokens.shape
    rows, slots = seg.shape
    per, pairs = TOKS // slots, width // PAIR
    return call(
        attend_kernel,
        "attend",
        (n // TOKS,),
        [rows_of(width), whole(1, width), whole(1, width), whole(*wqkv.shape), whole(*wout.shape)]
        + [whole(1, width)] * 2
        + [whole(rows, slots)] * 3,
        [
            rows_of(3 * width),
            pl.BlockSpec((per, pairs, slots, 2 * slots), lambda i, *_: (i, 0, 0, 0)),
            rows_of(width),
            rows_of(width),
            rows_of(width),
        ],
        [
            pltpu.HBM((n, 3 * width), BF),
            pltpu.HBM((rows, pairs, slots, 2 * slots), BF),
            pltpu.HBM((n, width), BF),
            pltpu.HBM((n, width), F32),
            pltpu.VMEM((n, width), BF),
        ],
        [],
        info,
        far(tokens, g1, c1) + (wqkv, wout) + far(g2, c2, seg, step, pad),
    )


def pack_kernel(info_ref, up_ref, bias_ref, down_ref, up_out, down_out):
    width = up_ref.shape[0]
    up_out[:width, :] = up_ref[...]
    units = up_ref.shape[1]
    bias = bias_ref[...].reshape(1, 2 * units)
    bias = jnp.where(info_ref[0] == 0, bias[:, :units], bias[:, units:])
    up_out[width:, :] = jnp.broadcast_to(bias, (TILE, units))
    down_out[...] = down_ref[...]


def pack(info, up, bias, down):
    width, units = up.shape[0], up.shape[1] // 2
    return call(
        pack_kernel,
        "pack",
        (1,),
        [
            pl.BlockSpec((width, units), lambda t, info: (0, info[0])),
            whole(2 * units),
            pl.BlockSpec((units, width), lambda t, info: (info[0], 0)),
        ],
        [whole(width + TILE, units), whole(units, width)],
        [jax.ShapeDtypeStruct((width + TILE, units), BF), jax.ShapeDtypeStruct((units, width), BF)],
        [],
        info,
        far(up, bias, down),
    )


def ffn_block(sec, dy, up, bias, down, acc_ref, bacc_ref):
    pre = mm(sec, up) + bias
    dhid = mm_nt(dy, down)
    hid, slope = gelu_pair(pre)
    hid = hid.astype(BF)
    dpre = (dhid * slope).astype(BF)
    grad_up = mm(sec.T, dpre)
    grad_down = mm(dy.T, hid)
    sums = jnp.sum(dpre.astype(F32), axis=0, keepdims=True)
    chunks, _, double = acc_ref.shape
    units = double // 2
    for i in range(chunks):
        cols = slice(i * units, (i + 1) * units)
        acc_ref[i, :, :units] += grad_up[:, cols]
        acc_ref[i, :, units:] += grad_down[:, cols]
        bacc_ref[i : i + 1, :] += sums[:, cols]
    return hid, dpre


def ffn_own_kernel(
    tables, mixing, info_ref, sec_ref, dy_ref, up_ref, bias_ref, down_ref, out_ref, dsec_ref, keep_ref, send_ref, bias_out,
    acc_ref,
):
    at, last = pl.program_id(0), pl.num_programs(0) - 1

    @pl.when(at == 0)
    def _():
        acc_ref[...] = jnp.zeros_like(acc_ref)
        bias_out[...] = jnp.zeros_like(bias_out)

    bias = bias_ref[...].astype(F32).reshape(1, up_ref.shape[1])
    hid, dpre = ffn_block(sec_ref[...], dy_ref[...], up_ref[...], bias, down_ref[...], acc_ref, bias_out)
    out_ref[...] = mm(hid, down_ref[...])
    dsec_ref[...] = mm_nt(dpre, up_ref[...])

    @pl.when(at == last)
    def _():
        core, own, other = info_ref[0], info_ref[1], info_ref[2]
        permuted(keep_ref, acc_ref, core, tables, core, own)
        permuted(send_ref, acc_ref, core ^ 1, tables, core ^ 1, other, core ^ 1 if mixing else 0)


def ffn_own(info, tables, mixing, second, dy, up, bias, down):
    n, width = second.shape
    units = up.shape[1] // 2
    return call(
        functools.partial(ffn_own_kernel, tables, mixing),
        "ffn_own",
        (n // TOKS,),
        [rows_of(width), rows_of(width), whole(*up.shape), whole(*bias.shape), whole(*down.shape)],
        [rows_of(width)] * 2 + [whole(width, 2 * units)] * 2 + [whole(2, units)],
        [pltpu.VMEM((n, width), F32)] * 2
        + [pltpu.HBM((width, 2 * units), BF)] * 2
        + [jax.ShapeDtypeStruct((2, units), F32)],
        [pltpu.VMEM((2, width, 2 * units), F32)],
        info,
        near(second) + far(dy) + (up,) + far(bias) + (down,),
    )


def ffn_rest_kernel(
    tables, count, mixing, info_ref, sec_in, dy_in, out_in, dsec_in, res_in, mixed_in, mine_ref, bdown_ref, g2_ref, wout_ref, *refs
):
    ups, downs = refs[:count], refs[count : 2 * count]
    block_out, gres_out, gmix_out, vec_ref, dwout_ref, bias_out = refs[2 * count : 2 * count + 6]
    grads, refs = refs[2 * count + 6 : 3 * count + 6 + mixing], refs[3 * count + 6 + mixing :]
    sec_ref, dy_ref, out_ref, dsec_ref, res_ref, mixed_ref, branch_ref, up_ref, bias_ref, down_ref, laid_ref, sems = refs
    n, width = sec_ref.shape
    units = down_ref.shape[0] // count
    core = info_ref[0]
    half = width // 2
    top, low = pl.ds(0, half), pl.ds(half, half)
    used = iter(range(sems.shape[0]))

    def move(*pairs):
        copies = [pltpu.make_async_copy(*pair, sems.at[next(used)]) for pair in pairs]
        for copy in copies:
            copy.start()
        return copies

    def arrived(copies):
        for copy in copies:
            copy.wait()

    def by_core(first, *sets):
        def each(act):
            for odd, pairs in enumerate(sets):

                @pl.when(core == odd)
                def _(pairs=pairs):
                    for i, pair in enumerate(pairs):
                        act(pltpu.make_async_copy(*pair, sems.at[first + i]))

        return lambda: each(lambda copy: copy.start()), lambda: each(lambda copy: copy.wait())

    cols = [pl.ds(i * units, units) for i in range(count)]
    first = move(
        (sec_in, sec_ref),
        *[(ups[i].at[pl.ds(0, width), :], up_ref.at[:, cols[i]]) for i in range(count)],
        *[(ups[i].at[pl.ds(width, TILE), :], bias_ref.at[:, cols[i]]) for i in range(count)],
    )
    second = move((dy_in, dy_ref), *[(downs[i], down_ref.at[cols[i], :]) for i in range(count)])
    third = move((out_in, out_ref), (dsec_in, dsec_ref), (res_in, res_ref), (mixed_in, mixed_ref))
    if mixing:
        keep_ref, send_ref, away_ref = grads
        own_start, own_wait = by_core(
            next(used),
            [(mine_ref, keep_ref)],
            [(mine_ref.at[top], keep_ref.at[low]), (mine_ref.at[low], send_ref.at[top])],
        )
        next(used)
        chunk_start, chunk_wait = by_core(
            next(used),
            [(laid_ref.at[0], send_ref)],
            [(laid_ref.at[0, top], keep_ref.at[top]), (laid_ref.at[0, low], send_ref.at[low])],
        )
        next(used)
        own_start()

    arrived(first)
    toks = n if count <= 2 else n // 2
    grad_up = grad_down = sums = None
    parts = []
    for t in range(n // toks):
        rows = slice(t * toks, (t + 1) * toks)
        sec = sec_ref[rows, :]
        pre = mm(sec, up_ref[...]) + bias_ref[...].astype(F32)[:1]
        if t == 0:
            arrived(second)
        dy = dy_ref[rows, :]
        dhid = mm_nt(dy, down_ref[...])
        hid, slope = gelu_pair(pre)
        hid = hid.astype(BF)
        dpre = (dhid * slope).astype(BF)
        more = (mm(sec.T, dpre), mm(dy.T, hid), jnp.sum(dpre.astype(F32), axis=0, keepdims=True))
        if t:
            more = (grad_up + more[0], grad_down + more[1], sums + more[2])
        grad_up, grad_down, sums = more
        parts.append((hid, dpre))
    blocks = len(tables[0])
    size = width // blocks
    for i in range(count):
        at = slice(i * units, (i + 1) * units)
        bias_out[i : i + 1, :] = sums[:, at]
        for block in range(blocks):
            owner = core ^ (i % 2)
            place = place_of(block, tables, owner, info_ref[1 + i % 2])
            to = pl.ds(pl.multiple_of(place * size, size), size)
            rows = slice(block * size, (block + 1) * size)
            laid_ref[i, to, :units] = grad_up[rows, at].astype(BF)
            laid_ref[i, to, units:] = grad_down[rows, at].astype(BF)
    if mixing:
        chunk_start()
        gone = move((laid_ref.at[1], away_ref))
    else:
        gone = move(*[(laid_ref.at[i], grads[i]) for i in range(count)])

    arrived(third)
    step = min(TOKS // 2, toks)
    for t, (hid, dpre) in enumerate(parts):
        out_all, dsec_all = mm(hid, down_ref[...]), mm_nt(dpre, up_ref[...])
        for r in range(0, toks, step):
            rows = slice(t * toks + r, t * toks + r + step)
            span = pl.ds(rows.start, step)
            dy32 = dy_ref[rows, :].astype(F32)
            residual = res_ref[rows, :]
            dsec = dsec_all[r : r + step] + dsec_ref[rows, :]
            dy_ref[rows, :] = (residual + (out_all[r : r + step] + out_ref[rows, :] + bdown_ref[...])).astype(BF)
            unit, inv = unit_parts(residual)
            sums = [jnp.sum(v, axis=0, keepdims=True) for v in (dsec * unit, dsec, dy32)]
            for i, row in enumerate(sums):
                if rows.start:
                    vec_ref[i : i + 1, :] += row
                else:
                    vec_ref[i : i + 1, :] = row
            gres = dy32 + norm_back(dsec, unit, inv, g2_ref[...])
            out_ref[rows, :] = gres
            branch_ref[rows, :] = gres.astype(BF)
            gone += move((dy_ref.at[span, :], block_out.at[span, :]), (out_ref.at[span, :], gres_out.at[span, :]))
    vec_ref[3:, :] = jnp.zeros((vec_ref.shape[0] - 3, width), F32)
    sec_ref[...] = mm_nt(branch_ref[...], wout_ref[...]).astype(BF)
    gone += move((sec_ref, gmix_out))
    dwout_ref[...] = mm_tn(mixed_ref[...], branch_ref[...])
    arrived(gone)
    if mixing:
        own_wait()
        chunk_wait()


def ffn_rest(info, tables, mixing, second, dy, out_part, dsec_part, residual, mixed, bdown, g2, wout, mine, chunks):
    n, width = second.shape
    count = len(chunks)
    units = chunks[0][0].shape[1]
    anywhere = pl.BlockSpec(memory_space=pl.ANY)
    return call(
        functools.partial(ffn_rest_kernel, tables, count, mixing),
        "ffn_rest",
        (1,),
        [anywhere] * 7 + [whole(1, width)] * 2 + [whole(width, width)] + [anywhere] * (2 * count),
        [anywhere] * 3 + [whole(8, width), whole(width, width), whole(count, units)] + [anywhere] * (count + mixing),
        [
            jax.ShapeDtypeStruct((n, width), BF),
            pltpu.HBM((n, width), F32),
            pltpu.HBM((n, width), BF),
            jax.ShapeDtypeStruct((8, width), F32),
            pltpu.HBM((width, width), F32),
            jax.ShapeDtypeStruct((count, units), F32),
        ]
        + [jax.ShapeDtypeStruct((width, 2 * units), BF)] * (count + mixing),
        [
            pltpu.VMEM((n, width), BF),
            pltpu.VMEM((n, width), BF),
            pltpu.VMEM((n, width), F32),
            pltpu.VMEM((n, width), F32),
            pltpu.VMEM((n, width), F32),
            pltpu.VMEM((n, width), BF),
            pltpu.VMEM((n, width), BF),
            pltpu.VMEM((width, count * units), BF),
            pltpu.VMEM((TILE, count * units), BF),
            pltpu.VMEM((count * units, width), BF),
            pltpu.VMEM((count, width, 2 * units), BF),
            pltpu.SemaphoreType.DMA((24 + 4 * count,)),
        ],
        info,
        near(second)
        + far(dy)
        + near(out_part, dsec_part)
        + far(residual, mixed, mine, bdown, g2)
        + (wout,)
        + tuple(c[0] for c in chunks)
        + tuple(c[1] for c in chunks),
        REST_LIMIT if count <= 2 else 56 * 1024 * 1024,
    )


def join_kernel(info_ref, send_ref, got_ref, own_ref, out_ref):
    half = send_ref.shape[0] // 2
    out_ref[half:, :] = (send_ref[half:, :].astype(F32) + got_ref[half:, :].astype(F32)).astype(BF)

    @pl.when(info_ref[0] == 0)
    def _():
        out_ref[:half, :] = (send_ref[:half, :].astype(F32) + got_ref[:half, :].astype(F32)).astype(BF)

    @pl.when(info_ref[0] == 1)
    def _():
        out_ref[:half, :] = (send_ref[:half, :].astype(F32) + own_ref[:half, :].astype(F32)).astype(BF)


def split_kernel(info_ref, keep_ref, got_ref, own_ref, arrived_ref, keep_out, send_out):
    half = keep_ref.shape[0] // 2
    top, low = slice(0, half), slice(half, 2 * half)

    def total(*parts):
        value = parts[0].astype(F32)
        for part in parts[1:]:
            value += part.astype(F32)
        return value.astype(BF)

    @pl.when(info_ref[0] == 0)
    def _():
        keep_out[...] = total(keep_ref[top, :], own_ref[top, :], arrived_ref[top, :])
        send_out[...] = total(keep_ref[low, :], own_ref[low, :], arrived_ref[low, :])

    @pl.when(info_ref[0] == 1)
    def _():
        keep_out[...] = total(keep_ref[low, :], own_ref[low, :], arrived_ref[top, :])
        send_out[...] = total(keep_ref[top, :], got_ref[top, :], arrived_ref[low, :])


def direct(kernel, name, info, out_shape, args):
    return pl.pallas_call(
        kernel,
        in_specs=[pl.BlockSpec(memory_space=pltpu.SMEM)] + [pl.BlockSpec(memory_space=pltpu.VMEM)] * len(args),
        out_specs=jax.tree.map(lambda _: pl.BlockSpec(memory_space=pltpu.VMEM), out_shape),
        out_shape=out_shape,
        compiler_params=pltpu.CompilerParams(vmem_limit_bytes=VMEM_LIMIT),
        cost_estimate=pl.CostEstimate(flops=1000, bytes_accessed=1000, transcendentals=0),
        name=name,
    )(info, *args)


def join(info, send, got, own):
    return direct(join_kernel, "join", info, jax.ShapeDtypeStruct(send.shape, BF), (send, got, own))


def split(info, keep, got, own, arrived):
    shape = jax.ShapeDtypeStruct((keep.shape[0] // 2, keep.shape[1]), BF)
    return direct(split_kernel, "split", info, [shape, shape], (keep, got, own, arrived))


def attend_back_kernel(
    tables, info_ref, qkv_ref, prob_ref, gmix_ref, tok_ref, vec_ref, dwout_ref, grad_ref, dw_keep_ref, dw_send_ref,
    dqkv_ref, acc_ref, row_ref,
):
    at, last = pl.program_id(0), pl.num_programs(0) - 1
    toks, width = tok_ref.shape
    rows, pairs, slots, _ = prob_ref.shape

    @pl.when(at == 0)
    def _():
        acc_ref[:, : 3 * width] = jnp.zeros((width, 3 * width), F32)
        acc_ref[:, 3 * width : 4 * width] = dwout_ref[...]
        row_ref[...] = jnp.zeros_like(row_ref)
        row_ref[SUMS : SUMS + vec_ref.shape[0], :] = vec_ref[...]

    scale = HEAD ** (-0.5)
    units = [(r, p) for r in range(rows) for p in range(pairs)]

    def place(r, p, which):
        return (slice(r * slots, (r + 1) * slots), slice(which * width + p * PAIR, which * width + (p + 1) * PAIR))

    grads = [gmix_ref[place(r, p, 0)] for r, p in units]
    by_grad = [by_head(g) for g in grads]
    dprobs = [mm_nt(qkv_ref[place(r, p, 2)], g) for (r, p), g in zip(units, by_grad)]
    for (r, p), g in zip(units, by_grad):
        dqkv_ref[place(r, p, 2)] = mm(prob_ref[r, p], g).astype(BF)
    dscores = []
    for (r, p), dprob in zip(units, dprobs):
        p32 = prob_ref[r, p].astype(F32)
        dscores.append((p32 * (dprob - jnp.sum(p32 * dprob, axis=0, keepdims=True))).astype(BF))
    for (r, p), ds in zip(units, dscores):
        q = qkv_ref[place(r, p, 0)]
        dqkv_ref[place(r, p, 1)] = mm(ds, by_head(q * scale)).astype(BF)
    for (r, p), ds in zip(units, dscores):
        k = qkv_ref[place(r, p, 1)]
        stacked = jnp.concatenate([ds[:, :slots], ds[:, slots:]], axis=0)
        dqkv_ref[place(r, p, 0)] = mm_tn(stacked, by_head(k * scale)).astype(BF)
    unit, _ = unit_parts(tok_ref[...].astype(F32))
    acc_ref[:, : 3 * width] += mm_tn(unit.astype(BF), dqkv_ref[...])
    grad_ref[...] = dqkv_ref[...]
    for i in range(3):
        part = dqkv_ref[:, i * width : (i + 1) * width].astype(F32)
        row_ref[i : i + 1, :] += jnp.sum(part, axis=0, keepdims=True)

    @pl.when(at == last)
    def _():
        core, own, other = info_ref[0], info_ref[3], info_ref[4]
        acc_ref[:, 4 * width :] = row_ref[...].T
        half = width // 2
        size = width // len(tables[0])
        for place in range(len(tables[0])):
            dst = dw_keep_ref if place * size < half else dw_send_ref
            block = block_at(place, tables, core, own if place * size < half else other)
            rows_at = pl.ds(pl.multiple_of(block * size, size), size)
            to = place * size % half
            dst[to : to + size, :] = acc_ref[rows_at, :].astype(BF)


def attend_back(info, tables, qkv, prob, gmix, tokens, vec, dwout):
    n, width = tokens.shape
    rows, pairs, slots, _ = prob.shape
    per = TOKS // slots
    return call(
        functools.partial(attend_back_kernel, tables),
        "attend_back",
        (n // TOKS,),
        [
            rows_of(3 * width),
            pl.BlockSpec((per, pairs, slots, 2 * slots), lambda i, *_: (i, 0, 0, 0)),
            rows_of(width),
            rows_of(width),
            whole(*vec.shape),
            whole(width, width),
        ],
        [rows_of(3 * width)] + [whole(width // 2, 4 * width + LANES)] * 2,
        [pltpu.VMEM((n, 3 * width), BF)] + [jax.ShapeDtypeStruct((width // 2, 4 * width + LANES), BF)] * 2,
        [
            pltpu.VMEM((TOKS, 3 * width), BF),
            pltpu.VMEM((width, 4 * width + LANES), F32),
            pltpu.VMEM((LANES, width), F32),
        ],
        info,
        far(qkv, prob, gmix, tokens, vec, dwout),
    )


def first_back_kernel(info_ref, dqkv_ref, wqkv_ref, tok_ref, gres_ref, g1_ref, out_ref):
    dnormed = mm_nt(dqkv_ref[...], wqkv_ref[...])
    unit, inv = unit_parts(tok_ref[...].astype(F32))
    out_ref[...] = gres_ref[...] + norm_back(dnormed, unit, inv, g1_ref[...])


def first_back(info, dqkv, wqkv, tokens, gres, g1):
    n, width = tokens.shape
    return call(
        first_back_kernel,
        "first_back",
        (n // TOKS,),
        [rows_of(3 * width), whole(*wqkv.shape), rows_of(width), rows_of(width), whole(1, width)],
        rows_of(width),
        jax.ShapeDtypeStruct((n, width), F32),
        [],
        info,
        near(dqkv) + (wqkv,) + far(tokens, gres, g1),
    )


def ffn_end_kernel(tables, info_ref, keep_ref, other_ref, up_ref, down_ref, full_ref):
    core = info_ref[0]
    units = up_ref.shape[1]
    blocks = len(tables[0])
    size = keep_ref.shape[0] // blocks

    def lay(src_ref, whose, base):
        for place in range(blocks):
            block = block_at(place, tables, whose, base)
            rows = pl.ds(pl.multiple_of(block * size, size), size)
            part = src_ref[place * size : (place + 1) * size, :].astype(F32)
            up_ref[rows, :] = part[:, :units]
            full_ref[rows, :] = part[:, units:]
        down_ref[...] = full_ref[...].T

    @pl.when(pl.program_id(0) == 0)
    def _():
        lay(keep_ref, core, info_ref[1])

    @pl.when(pl.program_id(0) == 1)
    def _():
        lay(other_ref, core ^ 1, info_ref[2])


def ffn_end(info, tables, keep, other):
    width, double = keep.shape
    units = double // 2
    return call(
        functools.partial(ffn_end_kernel, tables),
        "ffn_end",
        (2,),
        [whole(width, double)] * 2,
        [
            pl.BlockSpec((width, units), lambda i, info: (0, info[0] ^ i)),
            pl.BlockSpec((units, width), lambda i, info: (info[0] ^ i, 0)),
        ],
        [jax.ShapeDtypeStruct((width, double), F32), jax.ShapeDtypeStruct((double, width), F32)],
        [pltpu.VMEM((width, units), F32)],
        info,
        (keep, other),
    )


def attend_end_kernel(
    tables, shares, info_ref, *refs
):
    quarters, (w_hbm, g1_ref, c1_ref, qkv_hbm, out_hbm), refs = refs[:4], refs[4:9], refs[9:]
    vec_refs, (qkv_ref, out_ref, col_ref, row_ref, w_ref, sems) = refs[:6], refs[6:]
    core, own, away = info_ref[0], info_ref[3], info_ref[4]
    weights = pltpu.make_async_copy(w_hbm, w_ref, sems.at[2 * len(tables[0])])
    weights.start()
    width = out_ref.shape[1]
    blocks = len(tables[0])
    size = out_ref.shape[0] // blocks
    quarter = out_ref.shape[0] // 4
    spots = []
    for place in range(blocks):
        row = place * size
        block = block_at(place, tables, core, own if row < 2 * quarter else away)
        at = row % quarter
        spots.append((quarters[row // quarter], slice(at, at + size), slice(row, row + size), pl.multiple_of(block * size, size)))
    copies = []
    for i, (src, rows, here, to) in enumerate(spots):
        col_ref[pl.ds(to, size), :] = src[rows, 4 * width :].astype(F32)
        out_ref[here, :] = src[rows, 3 * width : 4 * width].astype(F32)
        copies.append(pltpu.make_async_copy(out_ref.at[here, :], out_hbm.at[pl.ds(to, size), :], sems.at[i]))
        copies[-1].start()
    vec = col_ref[...].T
    row_ref[...] = vec
    wide_row = jnp.concatenate([vec[i : i + 1, :] for i in range(3)], axis=1)
    pair = jnp.concatenate([g1_ref[...], c1_ref[...], jnp.zeros((LANES - 2, width), F32)], axis=0).T
    col_ref[...] = pair
    lane = lax.broadcasted_iota(jnp.int32, (size, LANES), 1)
    for i, (src, rows, here, to) in enumerate(spots):
        gain_bias = col_ref[pl.ds(to, size), :]
        sums = src[rows, : 3 * width].astype(F32)
        qkv_ref[here, :] = gain_bias[:, 0:1] * sums + gain_bias[:, 1:2] * wide_row
        copies.append(pltpu.make_async_copy(qkv_ref.at[here, :], qkv_hbm.at[pl.ds(to, size), :], sems.at[blocks + i]))
        copies[-1].start()
    weights.wait()
    for src, rows, _, to in spots:
        here = pl.ds(to, size)
        sums = src[rows, : 3 * width].astype(F32)
        w = w_ref[here, :].astype(F32)
        d_gain = jnp.sum(w * sums, axis=1, keepdims=True)
        d_bias = jnp.sum(w * wide_row, axis=1, keepdims=True)
        col_ref[here, :] = jnp.where(lane == 0, d_gain, jnp.where(lane == 1, d_bias, 0.0))
    both = col_ref[...].T
    flat = lambda row: row.reshape(row.shape[1])
    vec_refs[0][...] = flat(both[0:1, :])
    vec_refs[1][...] = flat(both[1:2, :])
    for i in range(3):
        vec_refs[2 + i][...] = flat(vec[SUMS + i : SUMS + i + 1, :])
    units = vec_refs[5].shape[0]
    if units >= width:
        first = SUMS + 8 + info_ref[5] * (units // width)
        for i in range(units // width):
            vec_refs[5][i * width : (i + 1) * width] = flat(row_ref[pl.ds(first + i, 1), :])
    else:
        row = row_ref[pl.ds(SUMS + 8 + info_ref[5] // shares, 1), :]
        share = row[:, :units]
        for i in range(1, shares):
            share = jnp.where(info_ref[5] % shares == i, row[:, i * units : (i + 1) * units], share)
        vec_refs[5][...] = flat(share)
    for copy in copies:
        copy.wait()


def attend_end(info, tables, quarters, w_qkv, g1, c1, units):
    rows, width = 4 * quarters[0].shape[0], w_qkv.shape[0]
    blocks = len(tables[0])
    return call(
        functools.partial(attend_end_kernel, tables, max(1, width // units)),
        "attend_end",
        (1,),
        [whole(*quarters[0].shape)] * 4 + [pl.BlockSpec(memory_space=pl.ANY)] + [whole(1, width)] * 2,
        [pl.BlockSpec(memory_space=pl.ANY)] * 2 + [whole(width)] * 5 + [whole(units)],
        [jax.ShapeDtypeStruct((rows, 3 * width), F32), jax.ShapeDtypeStruct((rows, width), F32)]
        + [jax.ShapeDtypeStruct((width,), F32)] * 5
        + [jax.ShapeDtypeStruct((units,), F32)],
        [
            pltpu.VMEM((rows, 3 * width), F32),
            pltpu.VMEM((rows, width), F32),
            pltpu.VMEM((rows, LANES), F32),
            pltpu.VMEM((LANES, width), F32),
            pltpu.VMEM(w_qkv.shape, BF),
            pltpu.SemaphoreType.DMA((2 * blocks + 1,)),
        ],
        info,
        tuple(quarters) + far(w_qkv, g1, c1),
    )


def local(
    wide, narrow, tokens_in, ln1_gain, ln1_bias, w_qkv, w_out, ln2_gain, ln2_bias, w_up, b_up, w_down, b_down, segment_ids,
    step_ids, pad_mask, cotangent,
):
    width = tokens_in.shape[1]
    units = w_up.shape[1] // 2
    core_mask = narrow
    narrow_masks = [1 << b for b in range(narrow.bit_length() - 1)]
    wide_masks = [narrow << b for b in range(1, wide.bit_length() - 1)]

    def swap(value, first, second=None):
        masks = (first, first if second is None else second)
        pairs = [(i, i ^ masks[i // narrow & 1]) for i in range(wide * narrow)]
        return lax.ppermute(value, AXES, pairs)

    def add(a, b):
        return (a.astype(F32) + b.astype(F32)).astype(a.dtype)

    def after(*values):
        return lax.optimization_barrier(values)

    def steps_of(halved, exchanged, gathered):
        pairs = lambda order: list(zip(*order))
        return (
            [("halve", *pair) for pair in pairs(halved)]
            + [("exchange", *pair) for pair in pairs(exchanged)]
            + [("gather", *pair) for pair in reversed(pairs(gathered))]
        )

    def start(value, step):
        kind, *masks = step
        if kind == "halve":
            half = value.shape[0] // 2
            return value[:half], swap(value[half:], *masks)
        return value, swap(value, *masks)

    def finish(kept, got, step):
        if step[0] == "gather":
            return jnp.concatenate([kept, got], axis=0)
        return add(kept, got) if step[0] in ("halve", "exchange") else (kept, got)

    wide_at, narrow_at = lax.axis_index("wide"), lax.axis_index("narrow")
    core = wide_at & 1
    flat = wide_at * narrow + narrow_at

    def named(owner, used):
        return sum((1 << b) for b, m in enumerate(used) if owner & m)

    def block_of(used):
        return sum(((flat & m) != 0).astype(jnp.int32) << b for b, m in enumerate(used))

    def split_at(pair, count):
        return tuple(o[:count] for o in pair), tuple(o[count:] for o in pair)

    def by_core(values):
        return jnp.where(core == 0, values[0], values[1]), jnp.where(core == 0, values[1], values[0])

    mixing = narrow == 2 and len(wide_masks) == 3
    if mixing:
        y, low, high = wide_masks
        ff_in, ff_rest, ff_out = ([y, low], [y, low]), ([high], [high]), ([y, low], [y, low])
        at_in, at_rest, at_out = ([y, 1, low], [low, y, 1]), ([high], [high]), ([y, 1, low], [low, 1, y])
        turns = "FAFAAFAFAAFFAA"
    else:
        ff_in, ff_rest = split_at((wide_masks, wide_masks), min(len(wide_masks) - 1, (width // TILE).bit_length() - 1))
        masks = narrow_masks + wide_masks
        at_in, at_rest = split_at((masks, masks), min(len(masks) - 1, (width // TILE // 2).bit_length() - 1))
        ff_out, at_out, turns = ff_in, at_in, ""
    ff_used = tuple(sorted(o) for o in ff_in)
    ff_in_tables, ff_out_tables = (
        tuple([named(owner, ff_used[c]) for owner in places(pair[c], 1 << len(ff_used[c]))] for c in range(2))
        for pair in (ff_in, ff_out)
    )
    at_used = tuple([core_mask] + sorted(o) for o in at_in)

    def at_tables(order):
        owners = [places(o, 1 << len(o)) for o in order]
        return tuple(
            [named(o, at_used[c]) for o in owners[c]] + [named(o ^ core_mask, at_used[1 - c]) for o in owners[1 - c]]
            for c in range(2)
        )

    ff_block = by_core([block_of(used) for used in ff_used])
    at_block = by_core([block_of(used) for used in at_used])
    info = jnp.stack([core, *ff_block, *at_block, narrow_at]).astype(jnp.int32)

    packed, tokens_in = after(pack(info, w_up, b_up, w_down), tokens_in)
    fetched = [packed]
    for mask in narrow_masks:
        fetched = fetched + [(swap(u, mask), swap(d, mask)) for u, d in fetched]

    row = lambda v: v[None].astype(F32)
    g1, c1, g2 = row(ln1_gain), row(ln1_bias), row(ln2_gain)
    qkv, prob, mixed, residual, second = attend(
        info, tokens_in, g1, c1, w_qkv, w_out, g2, row(ln2_bias), segment_ids, step_ids, pad_mask
    )
    out_part, dsec_part, own_keep, own_send, bias_own = ffn_own(
        info, ff_in_tables, mixing, second, cotangent, w_up, b_up, w_down
    )
    own_send, fetched = after(own_send, fetched)
    chunks = []
    for up, down in fetched[1:]:
        chunks += [(up, down), (swap(up, core_mask), swap(down, core_mask))]
    rest = ffn_rest(
        info, ff_in_tables, mixing, second, cotangent, out_part, dsec_part, residual, mixed, row(b_down), g2, w_out, own_keep,
        chunks,
    )
    block_out, gres, gmix, vec, dwout, bias_rest = rest[:6]
    grads = rest[6:]

    b_rest = bias_rest.reshape(-1, 2, units)
    b_rest = jnp.where(core == 0, b_rest, jnp.flip(b_rest, axis=1))
    b_all = jnp.concatenate([bias_own[None], b_rest], axis=0)
    for bit in range(narrow.bit_length() - 1):
        flipped = jnp.flip(b_all.reshape(-1, 2, (1 << bit) * 2, units), axis=1).reshape(b_all.shape)
        b_all = jnp.where(narrow_at >> bit & 1, flipped, b_all)
    vec = jnp.concatenate([vec, b_all.reshape(-1, width)], axis=0)

    if mixing:
        ff_keep, ff_send, away = grads
        got_own, got = swap(own_send, core_mask), swap(away, core_mask)
        ff_send = join(info, ff_send, got, got_own)
        gmix, ff_send = after(gmix, ff_send)
        ff_got = swap(ff_send, 1, y)
    else:
        held = [add(own_keep, swap(own_send, core_mask))] + [add(grads[2 * j], swap(grads[2 * j + 1], core_mask)) for j in range(narrow - 1)]
        gmix, held = after(gmix, held)
        for mask in reversed(narrow_masks):
            held = [add(held[j], swap(held[j + mask], mask)) for j in range(mask)]
        ff_keep = held[0]

    dqkv, keep, send = attend_back(info, at_tables(at_in), qkv, prob, gmix, tokens_in, vec, dwout)
    if mixing:
        send, ff_got = after(send, ff_got)
        ff_keep, ff_send = split(info, ff_keep, got, got_own, ff_got)
    keep = add(keep, swap(send, core_mask))
    grad_tokens = first_back(info, dqkv, w_qkv, tokens_in, gres, g1)
    steps = {
        "A": steps_of(at_in, at_rest, at_out)[:-1] + [("last", *steps_of(at_in, at_rest, at_out)[-1][1:]), ("core", core_mask)],
        "F": steps_of(ff_in, ff_rest, ff_out) + [("core", core_mask)],
    }
    if mixing:
        steps["F"] = [("halve", y, 1)] + steps["F"][1:]
        first = (ff_keep, swap(ff_send, y, 1))
    else:
        first = start(ff_keep, steps["F"][0])
    turns = turns or "".join(a + f for a, f in itertools.zip_longest("A" * len(steps["A"]), "F" * len(steps["F"]), fillvalue=""))
    under_way = {"A": start(keep, steps["A"][0]), "F": first}
    done, beside = (), (grad_tokens,)
    for turn in turns:
        other = "A" if turn == "F" else "F"
        kept, got = under_way.pop(turn)
        if other in under_way:
            other_kept, other_got = under_way[other]
            kept, other_kept, *beside = after(kept, other_kept, *beside)
            under_way[other] = other_kept, other_got
        else:
            kept, got, *beside = after(kept, got, *beside)
        if len(beside) == 1:
            (grad_tokens,), beside = beside, ()
        elif beside:
            (grad_w_up, grad_w_down), beside = beside, ()
        step, *steps[turn] = steps[turn]
        if step[0] == "last":
            got, crossed = after(got, crossed)
        value = finish(kept, got, step)
        if step[0] == "last":
            under_way[turn] = value, swap(got, core_mask)
        elif steps[turn]:
            under_way[turn] = start(value, steps[turn][0])
            if steps[turn][0][0] == "last":
                crossed = swap(value, core_mask)
        elif turn == "F":
            beside = ffn_end(info, ff_out_tables, *value)
        else:
            done = (*value[0], crossed, value[1])
    grad_w_qkv, grad_w_out, d_gain1, d_bias1, d_gain2, d_bias2, d_bdown, grad_b_up = attend_end(
        info, at_tables(at_out), done, w_qkv, g1, c1, 2 * units
    )
    return (
        block_out, grad_tokens, d_gain1, d_bias1, grad_w_qkv, grad_w_out, d_gain2, d_bias2, grad_w_up, grad_b_up, grad_w_down,
        d_bdown,
    )


def solution(mesh):
    rows = P(("wide", "narrow"), None)
    in_specs = (
        rows, P(), P(), P(), P(), P(), P(), P(None, "narrow"), P("narrow"), P("narrow", None), P(), rows, rows, rows, rows,
    )
    out_specs = (
        rows, rows, P(), P(), P(), P(), P(), P(), P(None, "narrow"), P("narrow"), P("narrow", None), P(),
    )
    wide, narrow = mesh.shape["wide"], mesh.shape["narrow"]
    return jax.shard_map(
        functools.partial(local, wide, narrow), mesh=mesh, in_specs=in_specs, out_specs=out_specs, check_vma=False
    )
```

```python
import functools
import itertools

import jax
import jax.numpy as jnp
import numpy as np
from jax import lax
from jax.experimental import pallas as pl
from jax.experimental.pallas import tpu as pltpu
from jax.sharding import PartitionSpec as P

HEAD = 64
PAIR = 2 * HEAD
NORM_EPS = 1e-05
BF = jnp.bfloat16
F32 = jnp.float32
AXES = ("wide", "narrow")
LANES = 128
SUMS = 8
TILE = 16
TOKS = 512
VMEM_LIMIT = 30 * 1024 * 1024
REST_LIMIT = 36 * 1024 * 1024


def mm(a, b):
    return lax.dot_general(a, b, (((1,), (0,)), ((), ())), preferred_element_type=F32)


def mm_nt(a, b):
    return lax.dot_general(a, b, (((1,), (1,)), ((), ())), preferred_element_type=F32)


def mm_tn(a, b):
    return lax.dot_general(a, b, (((0,), (0,)), ((), ())), preferred_element_type=F32)


def near(*values):
    return tuple(pltpu.with_memory_space_constraint(v, pltpu.VMEM) for v in values)


def far(*values):
    return tuple(pltpu.with_memory_space_constraint(v, pltpu.HBM) for v in values)


def whole(*shape):
    return pl.BlockSpec(shape, lambda *_: (0,) * len(shape))


def rows_of(width, toks=TOKS):
    return pl.BlockSpec((toks, width), lambda i, *_: (i, 0))


def call(kernel, name, grid, in_specs, out_specs, out_shape, scratch, info, args, vmem=VMEM_LIMIT):
    return pl.pallas_call(
        kernel,
        grid_spec=pltpu.PrefetchScalarGridSpec(
            num_scalar_prefetch=1, grid=grid, in_specs=in_specs, out_specs=out_specs, scratch_shapes=scratch
        ),
        out_shape=out_shape,
        compiler_params=pltpu.CompilerParams(vmem_limit_bytes=vmem),
        cost_estimate=pl.CostEstimate(flops=1000, bytes_accessed=1000, transcendentals=0),
        name=name,
    )(info, *args)


def unit_parts(rows):
    mean = jnp.mean(rows, axis=-1, keepdims=True)
    centered = rows - mean
    inv = lax.rsqrt(jnp.mean(centered * centered, axis=-1, keepdims=True) + NORM_EPS)
    return centered * inv, inv


def norm_back(incoming, unit, inv, gain):
    scaled = incoming * gain
    return inv * (
        scaled
        - jnp.mean(scaled, axis=-1, keepdims=True)
        - unit * jnp.mean(scaled * unit, axis=-1, keepdims=True)
    )


def gelu_pair(x):
    cdf = 0.5 * (1.0 + lax.erf(x * 0.7071067811865476))
    return x * cdf, cdf + x * jnp.exp(-0.5 * x * x) * 0.3989422804014327


def by_head(block):
    lane = lax.broadcasted_iota(jnp.int32, block.shape, 1)
    zero = jnp.zeros_like(block)
    first = lane < HEAD
    return jnp.concatenate([jnp.where(first, block, zero), jnp.where(first, zero, block)], axis=0)


def places(order, blocks):
    bits = blocks.bit_length() - 1
    table = []
    for place in range(blocks):
        owner = 0
        for step in range(bits):
            if place >> (bits - 1 - step) & 1:
                owner ^= order[step]
        table.append(owner)
    return table


def block_at(place, tables, core, own):
    first, second = tables[0][place], tables[1][place]
    if first == second:
        return own ^ first
    return own ^ jnp.where(core == 0, first, second)


def place_of(block, tables, core, own):
    wanted = own ^ block
    places_by_core = [[table.index(owner) for owner in range(len(table))] for table in tables]
    place = jnp.int32(0)
    for owner in range(len(tables[0])):
        first, second = places_by_core[0][owner], places_by_core[1][owner]
        place = jnp.where(wanted == owner, jnp.where(core == 0, first, second), place)
    return place


def permuted(dst_ref, acc_ref, chunk, tables, core, own, turned=0):
    blocks = len(tables[0])
    size = dst_ref.shape[0] // blocks
    for place in range(blocks):
        block = block_at(place, tables, core, own)
        rows = pl.ds(pl.multiple_of(block * size, size), size)
        to = pl.ds(pl.multiple_of(((place + turned * (blocks // 2)) & (blocks - 1)) * size, size), size)
        dst_ref[to, :] = acc_ref[chunk, rows, :].astype(dst_ref.dtype)


def attend_kernel(
    info_ref, tok_ref, g1_ref, c1_ref, wqkv_ref, wout_ref, g2_ref, c2_ref, seg_ref, step_ref, pad_ref,
    qkv_ref, prob_ref, mixed_ref, res_ref, second_ref,
):
    slots = seg_ref.shape[1]
    toks, width = tok_ref.shape
    rows = toks // slots
    at = pl.program_id(0)
    tokens = tok_ref[...].astype(F32)
    unit, _ = unit_parts(tokens)
    normed = (unit * g1_ref[...] + c1_ref[...]).astype(BF)
    qkv_ref[...] = mm(normed, wqkv_ref[...]).astype(BF)
    q_id = lax.broadcasted_iota(jnp.int32, (slots, slots), 0)
    k_id = lax.broadcasted_iota(jnp.int32, (slots, slots), 1)
    eye = q_id == k_id
    pairs = width // PAIR
    units = [(r, p) for r in range(rows) for p in range(pairs)]

    def part(r, p, which):
        return qkv_ref[r * slots : (r + 1) * slots, which * width + p * PAIR : which * width + (p + 1) * PAIR]

    masks = []
    for r in range(rows):
        here = pl.ds(at * rows + r, 1)
        seg = jnp.broadcast_to(seg_ref[here, :].astype(F32), (slots, slots))
        step = jnp.broadcast_to(step_ref[here, :].astype(F32), (slots, slots))
        live = jnp.broadcast_to(pad_ref[here, :].astype(F32), (slots, slots)).T == 0
        masks.append(((seg == seg.T) & (step.T <= step) & live) | eye)
    scores = [mm_nt(part(r, p, 1), by_head(part(r, p, 0) * HEAD ** (-0.5))) for r, p in units]
    probs = []
    for (r, p), score in zip(units, scores):
        halves = []
        for half in (score[:, :slots], score[:, slots:]):
            half = jnp.where(masks[r], half, -1e30)
            weight = jnp.exp(half - jnp.max(half, axis=0, keepdims=True))
            total = jnp.sum(weight, axis=0, keepdims=True)
            halves.append((weight * (1.0 / total)).astype(BF))
        probs.append(halves)
    for (r, p), halves in zip(units, probs):
        prob_ref[r, p] = jnp.concatenate(halves, axis=1)
        mixed = mm_tn(jnp.concatenate(halves, axis=0), by_head(part(r, p, 2)))
        mixed_ref[r * slots : (r + 1) * slots, p * PAIR : (p + 1) * PAIR] = mixed.astype(BF)
    residual = tokens + mm(mixed_ref[...], wout_ref[...])
    res_ref[...] = residual
    unit, _ = unit_parts(residual)
    second_ref[...] = (unit * g2_ref[...] + c2_ref[...]).astype(BF)


def attend(info, tokens, g1, c1, wqkv, wout, g2, c2, seg, step, pad):
    n, width = tokens.shape
    rows, slots = seg.shape
    per, pairs = TOKS // slots, width // PAIR
    return call(
        attend_kernel,
        "attend",
        (n // TOKS,),
        [rows_of(width), whole(1, width), whole(1, width), whole(*wqkv.shape), whole(*wout.shape)]
        + [whole(1, width)] * 2
        + [whole(rows, slots)] * 3,
        [
            rows_of(3 * width),
            pl.BlockSpec((per, pairs, slots, 2 * slots), lambda i, *_: (i, 0, 0, 0)),
            rows_of(width),
            rows_of(width),
            rows_of(width),
        ],
        [
            pltpu.HBM((n, 3 * width), BF),
            pltpu.HBM((rows, pairs, slots, 2 * slots), BF),
            pltpu.HBM((n, width), BF),
            pltpu.HBM((n, width), F32),
            pltpu.VMEM((n, width), BF),
        ],
        [],
        info,
        far(tokens, g1, c1) + (wqkv, wout) + far(g2, c2, seg, step, pad),
    )


def pack_kernel(info_ref, up_ref, bias_ref, down_ref, up_out, down_out):
    width = up_ref.shape[0]
    up_out[:width, :] = up_ref[...]
    units = up_ref.shape[1]
    bias = bias_ref[...].reshape(1, 2 * units)
    bias = jnp.where(info_ref[0] == 0, bias[:, :units], bias[:, units:])
    up_out[width:, :] = jnp.broadcast_to(bias, (TILE, units))
    down_out[...] = down_ref[...]


def pack(info, up, bias, down):
    width, units = up.shape[0], up.shape[1] // 2
    return call(
        pack_kernel,
        "pack",
        (1,),
        [
            pl.BlockSpec((width, units), lambda t, info: (0, info[0])),
            whole(2 * units),
            pl.BlockSpec((units, width), lambda t, info: (info[0], 0)),
        ],
        [whole(width + TILE, units), whole(units, width)],
        [jax.ShapeDtypeStruct((width + TILE, units), BF), jax.ShapeDtypeStruct((units, width), BF)],
        [],
        info,
        far(up, bias, down),
    )


def ffn_block(sec, dy, up, bias, down, acc_ref, bacc_ref):
    pre = mm(sec, up) + bias
    dhid = mm_nt(dy, down)
    hid, slope = gelu_pair(pre)
    hid = hid.astype(BF)
    dpre = (dhid * slope).astype(BF)
    grad_up = mm(sec.T, dpre)
    grad_down = mm(dy.T, hid)
    sums = jnp.sum(dpre.astype(F32), axis=0, keepdims=True)
    chunks, _, double = acc_ref.shape
    units = double // 2
    for i in range(chunks):
        cols = slice(i * units, (i + 1) * units)
        acc_ref[i, :, :units] += grad_up[:, cols]
        acc_ref[i, :, units:] += grad_down[:, cols]
        bacc_ref[i : i + 1, :] += sums[:, cols]
    return hid, dpre


def ffn_own_kernel(
    tables, mixing, info_ref, sec_ref, dy_ref, up_ref, bias_ref, down_ref, out_ref, dsec_ref, keep_ref, send_ref, bias_out,
    acc_ref,
):
    at, last = pl.program_id(0), pl.num_programs(0) - 1

    @pl.when(at == 0)
    def _():
        acc_ref[...] = jnp.zeros_like(acc_ref)
        bias_out[...] = jnp.zeros_like(bias_out)

    bias = bias_ref[...].astype(F32).reshape(1, up_ref.shape[1])
    hid, dpre = ffn_block(sec_ref[...], dy_ref[...], up_ref[...], bias, down_ref[...], acc_ref, bias_out)
    out_ref[...] = mm(hid, down_ref[...])
    dsec_ref[...] = mm_nt(dpre, up_ref[...])

    @pl.when(at == last)
    def _():
        core, own, other = info_ref[0], info_ref[1], info_ref[2]
        permuted(keep_ref, acc_ref, core, tables, core, own)
        permuted(send_ref, acc_ref, core ^ 1, tables, core ^ 1, other, core ^ 1 if mixing else 0)


def ffn_own(info, tables, mixing, second, dy, up, bias, down):
    n, width = second.shape
    units = up.shape[1] // 2
    return call(
        functools.partial(ffn_own_kernel, tables, mixing),
        "ffn_own",
        (n // TOKS,),
        [rows_of(width), rows_of(width), whole(*up.shape), whole(*bias.shape), whole(*down.shape)],
        [rows_of(width)] * 2 + [whole(width, 2 * units)] * 2 + [whole(2, units)],
        [pltpu.VMEM((n, width), F32)] * 2
        + [pltpu.HBM((width, 2 * units), BF)] * 2
        + [pltpu.HBM((2, units), F32)],
        [pltpu.VMEM((2, width, 2 * units), F32)],
        info,
        near(second) + far(dy) + (up,) + far(bias) + (down,),
    )


def ffn_rest_kernel(
    tables, count, mixing, info_ref, sec_in, dy_in, out_in, dsec_in, res_in, mixed_in, mine_ref, bdown_ref, g2_ref, wout_ref, *refs
):
    ups, downs = refs[:count], refs[count : 2 * count]
    block_out, gres_out, gmix_out, vec_ref, dwout_ref, bias_out = refs[2 * count : 2 * count + 6]
    grads, refs = refs[2 * count + 6 : 3 * count + 6 + mixing], refs[3 * count + 6 + mixing :]
    sec_ref, dy_ref, out_ref, dsec_ref, res_ref, mixed_ref, branch_ref, up_ref, bias_ref, down_ref, laid_ref, sems = refs
    n, width = sec_ref.shape
    units = down_ref.shape[0] // count
    core = info_ref[0]
    half = width // 2
    top, low = pl.ds(0, half), pl.ds(half, half)
    used = iter(range(sems.shape[0]))

    def move(*pairs):
        copies = [pltpu.make_async_copy(*pair, sems.at[next(used)]) for pair in pairs]
        for copy in copies:
            copy.start()
        return copies

    def arrived(copies):
        for copy in copies:
            copy.wait()

    def by_core(first, *sets):
        def each(act):
            for odd, pairs in enumerate(sets):

                @pl.when(core == odd)
                def _(pairs=pairs):
                    for i, pair in enumerate(pairs):
                        act(pltpu.make_async_copy(*pair, sems.at[first + i]))

        return lambda: each(lambda copy: copy.start()), lambda: each(lambda copy: copy.wait())

    cols = [pl.ds(i * units, units) for i in range(count)]
    first = move(
        (sec_in, sec_ref),
        *[(ups[i].at[pl.ds(0, width), :], up_ref.at[:, cols[i]]) for i in range(count)],
        *[(ups[i].at[pl.ds(width, TILE), :], bias_ref.at[:, cols[i]]) for i in range(count)],
    )
    second = move((dy_in, dy_ref), *[(downs[i], down_ref.at[cols[i], :]) for i in range(count)])
    third = move((out_in, out_ref), (dsec_in, dsec_ref), (res_in, res_ref), (mixed_in, mixed_ref))
    if mixing:
        keep_ref, send_ref, away_ref = grads
        own_start, own_wait = by_core(
            next(used),
            [(mine_ref, keep_ref)],
            [(mine_ref.at[top], keep_ref.at[low]), (mine_ref.at[low], send_ref.at[top])],
        )
        next(used)
        chunk_start, chunk_wait = by_core(
            next(used),
            [(laid_ref.at[0], send_ref)],
            [(laid_ref.at[0, top], keep_ref.at[top]), (laid_ref.at[0, low], send_ref.at[low])],
        )
        next(used)
        own_start()

    arrived(first)
    toks = n if count <= 2 else n // 2
    grad_up = grad_down = sums = None
    parts = []
    for t in range(n // toks):
        rows = slice(t * toks, (t + 1) * toks)
        sec = sec_ref[rows, :]
        pre = mm(sec, up_ref[...]) + bias_ref[...].astype(F32)[:1]
        if t == 0:
            arrived(second)
        dy = dy_ref[rows, :]
        dhid = mm_nt(dy, down_ref[...])
        hid, slope = gelu_pair(pre)
        hid = hid.astype(BF)
        dpre = (dhid * slope).astype(BF)
        more = (mm(sec.T, dpre), mm(dy.T, hid), jnp.sum(dpre.astype(F32), axis=0, keepdims=True))
        if t:
            more = (grad_up + more[0], grad_down + more[1], sums + more[2])
        grad_up, grad_down, sums = more
        parts.append((hid, dpre))
    blocks = len(tables[0])
    size = width // blocks
    for i in range(count):
        at = slice(i * units, (i + 1) * units)
        bias_out[i : i + 1, :] = sums[:, at]
        for block in range(blocks):
            owner = core ^ (i % 2)
            place = place_of(block, tables, owner, info_ref[1 + i % 2])
            to = pl.ds(pl.multiple_of(place * size, size), size)
            rows = slice(block * size, (block + 1) * size)
            laid_ref[i, to, :units] = grad_up[rows, at].astype(BF)
            laid_ref[i, to, units:] = grad_down[rows, at].astype(BF)
    if mixing:
        chunk_start()
        gone = move((laid_ref.at[1], away_ref))
    else:
        gone = move(*[(laid_ref.at[i], grads[i]) for i in range(count)])

    arrived(third)
    step = min(TOKS // 2, toks)
    for t, (hid, dpre) in enumerate(parts):
        out_all, dsec_all = mm(hid, down_ref[...]), mm_nt(dpre, up_ref[...])
        for r in range(0, toks, step):
            rows = slice(t * toks + r, t * toks + r + step)
            span = pl.ds(rows.start, step)
            dy32 = dy_ref[rows, :].astype(F32)
            residual = res_ref[rows, :]
            dsec = dsec_all[r : r + step] + dsec_ref[rows, :]
            dy_ref[rows, :] = (residual + (out_all[r : r + step] + out_ref[rows, :] + bdown_ref[...])).astype(BF)
            unit, inv = unit_parts(residual)
            sums = [jnp.sum(v, axis=0, keepdims=True) for v in (dsec * unit, dsec, dy32)]
            for i, row in enumerate(sums):
                if rows.start:
                    vec_ref[i : i + 1, :] += row
                else:
                    vec_ref[i : i + 1, :] = row
            gres = dy32 + norm_back(dsec, unit, inv, g2_ref[...])
            out_ref[rows, :] = gres
            branch_ref[rows, :] = gres.astype(BF)
            gone += move((dy_ref.at[span, :], block_out.at[span, :]), (out_ref.at[span, :], gres_out.at[span, :]))
    vec_ref[3:, :] = jnp.zeros((vec_ref.shape[0] - 3, width), F32)
    sec_ref[...] = mm_nt(branch_ref[...], wout_ref[...]).astype(BF)
    gone += move((sec_ref, gmix_out))
    dwout_ref[...] = mm_tn(mixed_ref[...], branch_ref[...])
    arrived(gone)
    if mixing:
        own_wait()
        chunk_wait()


def ffn_rest(info, tables, mixing, second, dy, out_part, dsec_part, residual, mixed, bdown, g2, wout, mine, chunks):
    n, width = second.shape
    count = len(chunks)
    units = chunks[0][0].shape[1]
    anywhere = pl.BlockSpec(memory_space=pl.ANY)
    return call(
        functools.partial(ffn_rest_kernel, tables, count, mixing),
        "ffn_rest",
        (1,),
        [anywhere] * 7 + [whole(1, width)] * 2 + [whole(width, width)] + [anywhere] * (2 * count),
        [anywhere] * 3 + [whole(8, width), whole(width, width), whole(count, units)] + [anywhere] * (count + mixing),
        [
            jax.ShapeDtypeStruct((n, width), BF),
            pltpu.HBM((n, width), F32),
            pltpu.HBM((n, width), BF),
            pltpu.HBM((8, width), F32),
            pltpu.HBM((width, width), F32),
            pltpu.HBM((count, units), F32),
        ]
        + [jax.ShapeDtypeStruct((width, 2 * units), BF)] * (count + mixing),
        [
            pltpu.VMEM((n, width), BF),
            pltpu.VMEM((n, width), BF),
            pltpu.VMEM((n, width), F32),
            pltpu.VMEM((n, width), F32),
            pltpu.VMEM((n, width), F32),
            pltpu.VMEM((n, width), BF),
            pltpu.VMEM((n, width), BF),
            pltpu.VMEM((width, count * units), BF),
            pltpu.VMEM((TILE, count * units), BF),
            pltpu.VMEM((count * units, width), BF),
            pltpu.VMEM((count, width, 2 * units), BF),
            pltpu.SemaphoreType.DMA((24 + 4 * count,)),
        ],
        info,
        near(second)
        + far(dy)
        + near(out_part, dsec_part)
        + far(residual, mixed, mine, bdown, g2)
        + (wout,)
        + tuple(c[0] for c in chunks)
        + tuple(c[1] for c in chunks),
        REST_LIMIT if count <= 2 else 56 * 1024 * 1024,
    )


def join_kernel(info_ref, send_ref, got_ref, own_ref, out_ref):
    half = send_ref.shape[0] // 2
    out_ref[half:, :] = (send_ref[half:, :].astype(F32) + got_ref[half:, :].astype(F32)).astype(BF)

    @pl.when(info_ref[0] == 0)
    def _():
        out_ref[:half, :] = (send_ref[:half, :].astype(F32) + got_ref[:half, :].astype(F32)).astype(BF)

    @pl.when(info_ref[0] == 1)
    def _():
        out_ref[:half, :] = (send_ref[:half, :].astype(F32) + own_ref[:half, :].astype(F32)).astype(BF)


def split_kernel(info_ref, keep_ref, got_ref, own_ref, arrived_ref, keep_out, send_out):
    half = keep_ref.shape[0] // 2
    top, low = slice(0, half), slice(half, 2 * half)

    def total(*parts):
        value = parts[0].astype(F32)
        for part in parts[1:]:
            value += part.astype(F32)
        return value.astype(BF)

    @pl.when(info_ref[0] == 0)
    def _():
        keep_out[...] = total(keep_ref[top, :], own_ref[top, :], arrived_ref[top, :])
        send_out[...] = total(keep_ref[low, :], own_ref[low, :], arrived_ref[low, :])

    @pl.when(info_ref[0] == 1)
    def _():
        keep_out[...] = total(keep_ref[low, :], own_ref[low, :], arrived_ref[top, :])
        send_out[...] = total(keep_ref[top, :], got_ref[top, :], arrived_ref[low, :])


def direct(kernel, name, info, out_shape, args):
    return pl.pallas_call(
        kernel,
        in_specs=[pl.BlockSpec(memory_space=pltpu.SMEM)] + [pl.BlockSpec(memory_space=pltpu.VMEM)] * len(args),
        out_specs=jax.tree.map(lambda _: pl.BlockSpec(memory_space=pltpu.VMEM), out_shape),
        out_shape=out_shape,
        compiler_params=pltpu.CompilerParams(vmem_limit_bytes=VMEM_LIMIT),
        cost_estimate=pl.CostEstimate(flops=1000, bytes_accessed=1000, transcendentals=0),
        name=name,
    )(info, *args)


def join(info, send, got, own):
    return direct(join_kernel, "join", info, jax.ShapeDtypeStruct(send.shape, BF), (send, got, own))


def split(info, keep, got, own, arrived):
    shape = jax.ShapeDtypeStruct((keep.shape[0] // 2, keep.shape[1]), BF)
    return direct(split_kernel, "split", info, [shape, shape], (keep, got, own, arrived))


def attend_back_kernel(
    tables, info_ref, qkv_ref, prob_ref, gmix_ref, tok_ref, dwout_ref, vec_ref, *refs
):
    *sums, grad_ref, dw_keep_ref, dw_send_ref, dqkv_ref, acc_ref, row_ref = refs
    at, last = pl.program_id(0), pl.num_programs(0) - 1
    toks, width = tok_ref.shape
    rows, pairs, slots, _ = prob_ref.shape

    @pl.when(at == 0)
    def _():
        acc_ref[:, : 3 * width] = jnp.zeros((width, 3 * width), F32)
        acc_ref[:, 3 * width : 4 * width] = dwout_ref[...]
        row_ref[...] = jnp.zeros_like(row_ref)
        row_ref[SUMS : SUMS + vec_ref.shape[0], :] = vec_ref[...]
        if sums:
            own_ref, rest_ref = sums
            first = SUMS + vec_ref.shape[0]
            for i in range(2):
                row_ref[pl.ds(first + 2 * info_ref[5] + i, 1), :] = own_ref[i : i + 1, :]
                row_ref[pl.ds(first + 2 * (info_ref[5] ^ 1) + (info_ref[0] ^ i), 1), :] = rest_ref[i : i + 1, :]

    scale = HEAD ** (-0.5)
    units = [(r, p) for r in range(rows) for p in range(pairs)]

    def place(r, p, which):
        return (slice(r * slots, (r + 1) * slots), slice(which * width + p * PAIR, which * width + (p + 1) * PAIR))

    grads = [gmix_ref[place(r, p, 0)] for r, p in units]
    by_grad = [by_head(g) for g in grads]
    dprobs = [mm_nt(qkv_ref[place(r, p, 2)], g) for (r, p), g in zip(units, by_grad)]
    for (r, p), g in zip(units, by_grad):
        dqkv_ref[place(r, p, 2)] = mm(prob_ref[r, p], g).astype(BF)
    dscores = []
    for (r, p), dprob in zip(units, dprobs):
        p32 = prob_ref[r, p].astype(F32)
        dscores.append((p32 * (dprob - jnp.sum(p32 * dprob, axis=0, keepdims=True))).astype(BF))
    for (r, p), ds in zip(units, dscores):
        q = qkv_ref[place(r, p, 0)]
        dqkv_ref[place(r, p, 1)] = mm(ds, by_head(q * scale)).astype(BF)
    for (r, p), ds in zip(units, dscores):
        k = qkv_ref[place(r, p, 1)]
        stacked = jnp.concatenate([ds[:, :slots], ds[:, slots:]], axis=0)
        dqkv_ref[place(r, p, 0)] = mm_tn(stacked, by_head(k * scale)).astype(BF)
    unit, _ = unit_parts(tok_ref[...].astype(F32))
    acc_ref[:, : 3 * width] += mm_tn(unit.astype(BF), dqkv_ref[...])
    grad_ref[...] = dqkv_ref[...]
    for i in range(3):
        part = dqkv_ref[:, i * width : (i + 1) * width].astype(F32)
        row_ref[i : i + 1, :] += jnp.sum(part, axis=0, keepdims=True)

    @pl.when(at == last)
    def _():
        core, own, other = info_ref[0], info_ref[3], info_ref[4]
        acc_ref[:, 4 * width :] = row_ref[...].T
        half = width // 2
        size = width // len(tables[0])
        for place in range(len(tables[0])):
            dst = dw_keep_ref if place * size < half else dw_send_ref
            block = block_at(place, tables, core, own if place * size < half else other)
            rows_at = pl.ds(pl.multiple_of(block * size, size), size)
            to = place * size % half
            dst[to : to + size, :] = acc_ref[rows_at, :].astype(BF)


def attend_back(info, tables, qkv, prob, gmix, tokens, dwout, *vecs):
    n, width = tokens.shape
    rows, pairs, slots, _ = prob.shape
    per = TOKS // slots
    return call(
        functools.partial(attend_back_kernel, tables),
        "attend_back",
        (n // TOKS,),
        [
            rows_of(3 * width),
            pl.BlockSpec((per, pairs, slots, 2 * slots), lambda i, *_: (i, 0, 0, 0)),
            rows_of(width),
            rows_of(width),
            whole(width, width),
        ]
        + [whole(*vec.shape) for vec in vecs],
        [rows_of(3 * width)] + [whole(width // 2, 4 * width + LANES)] * 2,
        [pltpu.VMEM((n, 3 * width), BF)] + [jax.ShapeDtypeStruct((width // 2, 4 * width + LANES), BF)] * 2,
        [
            pltpu.VMEM((TOKS, 3 * width), BF),
            pltpu.VMEM((width, 4 * width + LANES), F32),
            pltpu.VMEM((LANES, width), F32),
        ],
        info,
        far(qkv, prob, gmix, tokens, dwout, *vecs),
    )


def first_back_kernel(info_ref, dqkv_ref, wqkv_ref, tok_ref, gres_ref, g1_ref, out_ref):
    dnormed = mm_nt(dqkv_ref[...], wqkv_ref[...])
    unit, inv = unit_parts(tok_ref[...].astype(F32))
    out_ref[...] = gres_ref[...] + norm_back(dnormed, unit, inv, g1_ref[...])


def first_back(info, dqkv, wqkv, tokens, gres, g1):
    n, width = tokens.shape
    return call(
        first_back_kernel,
        "first_back",
        (n // TOKS,),
        [rows_of(3 * width), whole(*wqkv.shape), rows_of(width), rows_of(width), whole(1, width)],
        rows_of(width),
        jax.ShapeDtypeStruct((n, width), F32),
        [],
        info,
        near(dqkv) + (wqkv,) + far(tokens, gres, g1),
    )


def ffn_end_kernel(tables, info_ref, keep_ref, other_ref, up_ref, down_ref, full_ref):
    core = info_ref[0]
    units = up_ref.shape[1]
    blocks = len(tables[0])
    size = keep_ref.shape[0] // blocks

    def lay(src_ref, whose, base):
        for place in range(blocks):
            block = block_at(place, tables, whose, base)
            rows = pl.ds(pl.multiple_of(block * size, size), size)
            part = src_ref[place * size : (place + 1) * size, :].astype(F32)
            up_ref[rows, :] = part[:, :units]
            full_ref[rows, :] = part[:, units:]
        down_ref[...] = full_ref[...].T

    @pl.when(pl.program_id(0) == 0)
    def _():
        lay(keep_ref, core, info_ref[1])

    @pl.when(pl.program_id(0) == 1)
    def _():
        lay(other_ref, core ^ 1, info_ref[2])


def ffn_end(info, tables, keep, other):
    width, double = keep.shape
    units = double // 2
    return call(
        functools.partial(ffn_end_kernel, tables),
        "ffn_end",
        (2,),
        [whole(width, double)] * 2,
        [
            pl.BlockSpec((width, units), lambda i, info: (0, info[0] ^ i)),
            pl.BlockSpec((units, width), lambda i, info: (info[0] ^ i, 0)),
        ],
        [jax.ShapeDtypeStruct((width, double), F32), jax.ShapeDtypeStruct((double, width), F32)],
        [pltpu.VMEM((width, units), F32)],
        info,
        (keep, other),
    )


def attend_end_kernel(
    tables, shares, info_ref, *refs
):
    quarters, (w_hbm, g1_ref, c1_ref, qkv_hbm, out_hbm), refs = refs[:4], refs[4:9], refs[9:]
    vec_refs, (qkv_ref, out_ref, col_ref, row_ref, w_ref, sems) = refs[:6], refs[6:]
    core, own, away = info_ref[0], info_ref[3], info_ref[4]
    weights = pltpu.make_async_copy(w_hbm, w_ref, sems.at[2 * len(tables[0])])
    weights.start()
    width = out_ref.shape[1]
    blocks = len(tables[0])
    size = out_ref.shape[0] // blocks
    quarter = out_ref.shape[0] // 4
    spots = []
    for place in range(blocks):
        row = place * size
        block = block_at(place, tables, core, own if row < 2 * quarter else away)
        at = row % quarter
        spots.append((quarters[row // quarter], slice(at, at + size), slice(row, row + size), pl.multiple_of(block * size, size)))
    copies = []
    for i, (src, rows, here, to) in enumerate(spots):
        col_ref[pl.ds(to, size), :] = src[rows, 4 * width :].astype(F32)
        out_ref[here, :] = src[rows, 3 * width : 4 * width].astype(F32)
        copies.append(pltpu.make_async_copy(out_ref.at[here, :], out_hbm.at[pl.ds(to, size), :], sems.at[i]))
        copies[-1].start()
    vec = col_ref[...].T
    row_ref[...] = vec
    wide_row = jnp.concatenate([vec[i : i + 1, :] for i in range(3)], axis=1)
    pair = jnp.concatenate([g1_ref[...], c1_ref[...], jnp.zeros((LANES - 2, width), F32)], axis=0).T
    col_ref[...] = pair
    lane = lax.broadcasted_iota(jnp.int32, (size, LANES), 1)
    for i, (src, rows, here, to) in enumerate(spots):
        gain_bias = col_ref[pl.ds(to, size), :]
        sums = src[rows, : 3 * width].astype(F32)
        qkv_ref[here, :] = gain_bias[:, 0:1] * sums + gain_bias[:, 1:2] * wide_row
        copies.append(pltpu.make_async_copy(qkv_ref.at[here, :], qkv_hbm.at[pl.ds(to, size), :], sems.at[blocks + i]))
        copies[-1].start()
    weights.wait()
    for src, rows, _, to in spots:
        here = pl.ds(to, size)
        sums = src[rows, : 3 * width].astype(F32)
        w = w_ref[here, :].astype(F32)
        d_gain = jnp.sum(w * sums, axis=1, keepdims=True)
        d_bias = jnp.sum(w * wide_row, axis=1, keepdims=True)
        col_ref[here, :] = jnp.where(lane == 0, d_gain, jnp.where(lane == 1, d_bias, 0.0))
    both = col_ref[...].T
    flat = lambda row: row.reshape(row.shape[1])
    vec_refs[0][...] = flat(both[0:1, :])
    vec_refs[1][...] = flat(both[1:2, :])
    for i in range(3):
        vec_refs[2 + i][...] = flat(vec[SUMS + i : SUMS + i + 1, :])
    units = vec_refs[5].shape[0]
    if units >= width:
        first = SUMS + 8 + info_ref[5] * (units // width)
        for i in range(units // width):
            vec_refs[5][i * width : (i + 1) * width] = flat(row_ref[pl.ds(first + i, 1), :])
    else:
        row = row_ref[pl.ds(SUMS + 8 + info_ref[5] // shares, 1), :]
        share = row[:, :units]
        for i in range(1, shares):
            share = jnp.where(info_ref[5] % shares == i, row[:, i * units : (i + 1) * units], share)
        vec_refs[5][...] = flat(share)
    for copy in copies:
        copy.wait()


def attend_end(info, tables, quarters, w_qkv, g1, c1, units):
    rows, width = 4 * quarters[0].shape[0], w_qkv.shape[0]
    blocks = len(tables[0])
    return call(
        functools.partial(attend_end_kernel, tables, max(1, width // units)),
        "attend_end",
        (1,),
        [whole(*quarters[0].shape)] * 4 + [pl.BlockSpec(memory_space=pl.ANY)] + [whole(1, width)] * 2,
        [pl.BlockSpec(memory_space=pl.ANY)] * 2 + [whole(width)] * 5 + [whole(units)],
        [jax.ShapeDtypeStruct((rows, 3 * width), F32), jax.ShapeDtypeStruct((rows, width), F32)]
        + [jax.ShapeDtypeStruct((width,), F32)] * 5
        + [jax.ShapeDtypeStruct((units,), F32)],
        [
            pltpu.VMEM((rows, 3 * width), F32),
            pltpu.VMEM((rows, width), F32),
            pltpu.VMEM((rows, LANES), F32),
            pltpu.VMEM((LANES, width), F32),
            pltpu.VMEM(w_qkv.shape, BF),
            pltpu.SemaphoreType.DMA((2 * blocks + 1,)),
        ],
        info,
        tuple(quarters) + far(w_qkv, g1, c1),
    )


def local(
    wide, narrow, tokens_in, ln1_gain, ln1_bias, w_qkv, w_out, ln2_gain, ln2_bias, w_up, b_up, w_down, b_down, segment_ids,
    step_ids, pad_mask, cotangent,
):
    width = tokens_in.shape[1]
    units = w_up.shape[1] // 2
    core_mask = narrow
    narrow_masks = [1 << b for b in range(narrow.bit_length() - 1)]
    wide_masks = [narrow << b for b in range(1, wide.bit_length() - 1)]

    def swap(value, first, second=None):
        masks = (first, first if second is None else second)
        pairs = [(i, i ^ masks[i // narrow & 1]) for i in range(wide * narrow)]
        return lax.ppermute(value, AXES, pairs)

    def add(a, b):
        return (a.astype(F32) + b.astype(F32)).astype(a.dtype)

    def after(*values):
        return lax.optimization_barrier(values)

    def steps_of(halved, exchanged, gathered):
        pairs = lambda order: list(zip(*order))
        return (
            [("halve", *pair) for pair in pairs(halved)]
            + [("exchange", *pair) for pair in pairs(exchanged)]
            + [("gather", *pair) for pair in reversed(pairs(gathered))]
        )

    def start(value, step):
        kind, *masks = step
        if kind == "halve":
            half = value.shape[0] // 2
            return value[:half], swap(value[half:], *masks)
        return value, swap(value, *masks)

    def finish(kept, got, step):
        if step[0] == "gather":
            return jnp.concatenate([kept, got], axis=0)
        return add(kept, got) if step[0] in ("halve", "exchange") else (kept, got)

    wide_at, narrow_at = lax.axis_index("wide"), lax.axis_index("narrow")
    core = wide_at & 1
    flat = wide_at * narrow + narrow_at

    def named(owner, used):
        return sum((1 << b) for b, m in enumerate(used) if owner & m)

    def block_of(used):
        return sum(((flat & m) != 0).astype(jnp.int32) << b for b, m in enumerate(used))

    def split_at(pair, count):
        return tuple(o[:count] for o in pair), tuple(o[count:] for o in pair)

    def by_core(values):
        return jnp.where(core == 0, values[0], values[1]), jnp.where(core == 0, values[1], values[0])

    mixing = narrow == 2 and len(wide_masks) == 3
    if mixing:
        y, low, high = wide_masks
        ff_in, ff_rest, ff_out = ([y, low], [y, low]), ([high], [high]), ([low, y], [low, y])
        at_in, at_rest, at_out = ([y, 1, low], [low, y, 1]), ([high], [high]), ([y, 1, low], [low, 1, y])
        turns = "FAFAAFAFAAFFAA"
    else:
        ff_in, ff_rest = split_at((wide_masks, wide_masks), min(len(wide_masks) - 1, (width // TILE).bit_length() - 1))
        masks = narrow_masks + wide_masks
        at_in, at_rest = split_at((masks, masks), min(len(masks) - 1, (width // TILE // 2).bit_length() - 1))
        ff_out, at_out, turns = ff_in, at_in, ""
    ff_used = tuple(sorted(o) for o in ff_in)
    ff_in_tables, ff_out_tables = (
        tuple([named(owner, ff_used[c]) for owner in places(pair[c], 1 << len(ff_used[c]))] for c in range(2))
        for pair in (ff_in, ff_out)
    )
    at_used = tuple([core_mask] + sorted(o) for o in at_in)

    def at_tables(order):
        owners = [places(o, 1 << len(o)) for o in order]
        return tuple(
            [named(o, at_used[c]) for o in owners[c]] + [named(o ^ core_mask, at_used[1 - c]) for o in owners[1 - c]]
            for c in range(2)
        )

    ff_block = by_core([block_of(used) for used in ff_used])
    at_block = by_core([block_of(used) for used in at_used])
    info = jnp.stack([core, *ff_block, *at_block, narrow_at]).astype(jnp.int32)

    packed, tokens_in = after(pack(info, w_up, b_up, w_down), tokens_in)
    fetched = [packed]
    for mask in narrow_masks:
        fetched = fetched + [(swap(u, mask), swap(d, mask)) for u, d in fetched]

    row = lambda v: v[None].astype(F32)
    g1, c1, g2 = row(ln1_gain), row(ln1_bias), row(ln2_gain)
    qkv, prob, mixed, residual, second = attend(
        info, tokens_in, g1, c1, w_qkv, w_out, g2, row(ln2_bias), segment_ids, step_ids, pad_mask
    )
    out_part, dsec_part, own_keep, own_send, bias_own = ffn_own(
        info, ff_in_tables, mixing, second, cotangent, w_up, b_up, w_down
    )
    own_send, fetched = after(own_send, fetched)
    chunks = []
    for up, down in fetched[1:]:
        chunks += [(up, down), (swap(up, core_mask), swap(down, core_mask))]
    rest = ffn_rest(
        info, ff_in_tables, mixing, second, cotangent, out_part, dsec_part, residual, mixed, row(b_down), g2, w_out, own_keep,
        chunks,
    )
    block_out, gres, gmix, vec, dwout, bias_rest = rest[:6]
    grads = rest[6:]

    if narrow == 2 and units == width:
        vecs = (vec, bias_own, bias_rest)
    else:
        b_rest = bias_rest.reshape(-1, 2, units)
        b_rest = jnp.where(core == 0, b_rest, jnp.flip(b_rest, axis=1))
        b_all = jnp.concatenate([bias_own[None], b_rest], axis=0)
        for bit in range(narrow.bit_length() - 1):
            flipped = jnp.flip(b_all.reshape(-1, 2, (1 << bit) * 2, units), axis=1).reshape(b_all.shape)
            b_all = jnp.where(narrow_at >> bit & 1, flipped, b_all)
        vecs = (jnp.concatenate([vec, b_all.reshape(-1, width)], axis=0),)

    if mixing:
        ff_keep, ff_send, away = grads
        got_own, got = swap(own_send, core_mask), swap(away, core_mask)
        ff_send = join(info, ff_send, got, got_own)
        gmix, ff_send = after(gmix, ff_send)
        ff_got = swap(ff_send, 1, y)
    else:
        held = [add(own_keep, swap(own_send, core_mask))] + [add(grads[2 * j], swap(grads[2 * j + 1], core_mask)) for j in range(narrow - 1)]
        gmix, held = after(gmix, held)
        for mask in reversed(narrow_masks):
            held = [add(held[j], swap(held[j + mask], mask)) for j in range(mask)]
        ff_keep = held[0]

    dqkv, keep, send = attend_back(info, at_tables(at_in), qkv, prob, gmix, tokens_in, dwout, *vecs)
    if mixing:
        send, ff_got = after(send, ff_got)
        ff_keep, ff_send = split(info, ff_keep, got, got_own, ff_got)
    keep = add(keep, swap(send, core_mask))
    grad_tokens = first_back(info, dqkv, w_qkv, tokens_in, gres, g1)
    steps = {
        "A": steps_of(at_in, at_rest, at_out)[:-1] + [("last", *steps_of(at_in, at_rest, at_out)[-1][1:]), ("core", core_mask)],
        "F": steps_of(ff_in, ff_rest, ff_out) + [("core", core_mask)],
    }
    if mixing:
        steps["F"] = [("halve", y, 1)] + steps["F"][1:]
        first = (ff_keep, swap(ff_send, y, 1))
    else:
        first = start(ff_keep, steps["F"][0])
    turns = turns or "".join(a + f for a, f in itertools.zip_longest("A" * len(steps["A"]), "F" * len(steps["F"]), fillvalue=""))
    under_way = {"A": start(keep, steps["A"][0]), "F": first}
    done, beside = (), (grad_tokens,)
    for turn in turns:
        other = "A" if turn == "F" else "F"
        kept, got = under_way.pop(turn)
        if other in under_way:
            other_kept, other_got = under_way[other]
            kept, other_kept, *beside = after(kept, other_kept, *beside)
            under_way[other] = other_kept, other_got
        else:
            kept, got, *beside = after(kept, got, *beside)
        if len(beside) == 1:
            (grad_tokens,), beside = beside, ()
        elif beside:
            (grad_w_up, grad_w_down), beside = beside, ()
        step, *steps[turn] = steps[turn]
        if step[0] == "last":
            got, crossed = after(got, crossed)
        value = finish(kept, got, step)
        if step[0] == "last":
            under_way[turn] = value, swap(got, core_mask)
        elif steps[turn]:
            under_way[turn] = start(value, steps[turn][0])
            if steps[turn][0][0] == "last":
                crossed = swap(value, core_mask)
        elif turn == "F":
            beside = ffn_end(info, ff_out_tables, *value)
        else:
            done = (*value[0], crossed, value[1])
    grad_w_qkv, grad_w_out, d_gain1, d_bias1, d_gain2, d_bias2, d_bdown, grad_b_up = attend_end(
        info, at_tables(at_out), done, w_qkv, g1, c1, 2 * units
    )
    return (
        block_out, grad_tokens, d_gain1, d_bias1, grad_w_qkv, grad_w_out, d_gain2, d_bias2, grad_w_up, grad_b_up, grad_w_down,
        d_bdown,
    )


def solution(mesh):
    rows = P(("wide", "narrow"), None)
    in_specs = (
        rows, P(), P(), P(), P(), P(), P(), P(None, "narrow"), P("narrow"), P("narrow", None), P(), rows, rows, rows, rows,
    )
    out_specs = (
        rows, rows, P(), P(), P(), P(), P(), P(), P(None, "narrow"), P("narrow"), P("narrow", None), P(),
    )
    wide, narrow = mesh.shape["wide"], mesh.shape["narrow"]
    return jax.shard_map(
        functools.partial(local, wide, narrow), mesh=mesh, in_specs=in_specs, out_specs=out_specs, check_vma=False
    )
```

```python
import functools
import itertools

import jax
import jax.numpy as jnp
import numpy as np
from jax import lax
from jax.experimental import pallas as pl
from jax.experimental.pallas import tpu as pltpu
from jax.sharding import PartitionSpec as P

HEAD = 64
PAIR = 2 * HEAD
NORM_EPS = 1e-05
BF = jnp.bfloat16
F32 = jnp.float32
AXES = ("wide", "narrow")
LANES = 128
SUMS = 8
TILE = 16
TOKS = 512
VMEM_LIMIT = 30 * 1024 * 1024
REST_LIMIT = 36 * 1024 * 1024


def mm(a, b):
    return lax.dot_general(a, b, (((1,), (0,)), ((), ())), preferred_element_type=F32)


def mm_nt(a, b):
    return lax.dot_general(a, b, (((1,), (1,)), ((), ())), preferred_element_type=F32)


def mm_tn(a, b):
    return lax.dot_general(a, b, (((0,), (0,)), ((), ())), preferred_element_type=F32)


def near(*values):
    return tuple(pltpu.with_memory_space_constraint(v, pltpu.VMEM) for v in values)


def far(*values):
    return tuple(pltpu.with_memory_space_constraint(v, pltpu.HBM) for v in values)


def whole(*shape):
    return pl.BlockSpec(shape, lambda *_: (0,) * len(shape))


def rows_of(width, toks=TOKS):
    return pl.BlockSpec((toks, width), lambda i, *_: (i, 0))


def call(kernel, name, grid, in_specs, out_specs, out_shape, scratch, info, args, vmem=VMEM_LIMIT, aliases=()):
    return pl.pallas_call(
        kernel,
        grid_spec=pltpu.PrefetchScalarGridSpec(
            num_scalar_prefetch=1, grid=grid, in_specs=in_specs, out_specs=out_specs, scratch_shapes=scratch
        ),
        out_shape=out_shape,
        input_output_aliases=dict(aliases),
        compiler_params=pltpu.CompilerParams(vmem_limit_bytes=vmem),
        cost_estimate=pl.CostEstimate(flops=1000, bytes_accessed=1000, transcendentals=0),
        name=name,
    )(info, *args)


def unit_parts(rows):
    mean = jnp.mean(rows, axis=-1, keepdims=True)
    centered = rows - mean
    inv = lax.rsqrt(jnp.mean(centered * centered, axis=-1, keepdims=True) + NORM_EPS)
    return centered * inv, inv


def norm_back(incoming, unit, inv, gain):
    scaled = incoming * gain
    return inv * (
        scaled
        - jnp.mean(scaled, axis=-1, keepdims=True)
        - unit * jnp.mean(scaled * unit, axis=-1, keepdims=True)
    )


def gelu_pair(x):
    cdf = 0.5 * (1.0 + lax.erf(x * 0.7071067811865476))
    return x * cdf, cdf + x * jnp.exp(-0.5 * x * x) * 0.3989422804014327


def by_head(block):
    lane = lax.broadcasted_iota(jnp.int32, block.shape, 1)
    zero = jnp.zeros_like(block)
    first = lane < HEAD
    return jnp.concatenate([jnp.where(first, block, zero), jnp.where(first, zero, block)], axis=0)


def places(order, blocks):
    bits = blocks.bit_length() - 1
    table = []
    for place in range(blocks):
        owner = 0
        for step in range(bits):
            if place >> (bits - 1 - step) & 1:
                owner ^= order[step]
        table.append(owner)
    return table


def block_at(place, tables, core, own):
    first, second = tables[0][place], tables[1][place]
    if first == second:
        return own ^ first
    return own ^ jnp.where(core == 0, first, second)


def place_of(block, tables, core, own):
    wanted = own ^ block
    places_by_core = [[table.index(owner) for owner in range(len(table))] for table in tables]
    place = jnp.int32(0)
    for owner in range(len(tables[0])):
        first, second = places_by_core[0][owner], places_by_core[1][owner]
        place = jnp.where(wanted == owner, jnp.where(core == 0, first, second), place)
    return place


def permuted(dst_ref, acc_ref, chunk, tables, core, own, turned=0):
    blocks = len(tables[0])
    size = dst_ref.shape[0] // blocks
    for place in range(blocks):
        block = block_at(place, tables, core, own)
        rows = pl.ds(pl.multiple_of(block * size, size), size)
        to = pl.ds(pl.multiple_of(((place + turned * (blocks // 2)) & (blocks - 1)) * size, size), size)
        dst_ref[to, :] = acc_ref[chunk, rows, :].astype(dst_ref.dtype)


def attend_kernel(
    info_ref, tok_ref, g1_ref, c1_ref, wqkv_ref, wout_ref, g2_ref, c2_ref, seg_ref, step_ref, pad_ref,
    qkv_ref, prob_ref, mixed_ref, res_ref, second_ref,
):
    slots = seg_ref.shape[1]
    toks, width = tok_ref.shape
    rows = toks // slots
    at = pl.program_id(0)
    tokens = tok_ref[...].astype(F32)
    unit, _ = unit_parts(tokens)
    normed = (unit * g1_ref[...] + c1_ref[...]).astype(BF)
    qkv_ref[...] = mm(normed, wqkv_ref[...]).astype(BF)
    q_id = lax.broadcasted_iota(jnp.int32, (slots, slots), 0)
    k_id = lax.broadcasted_iota(jnp.int32, (slots, slots), 1)
    eye = q_id == k_id
    pairs = width // PAIR
    units = [(r, p) for r in range(rows) for p in range(pairs)]

    def part(r, p, which):
        return qkv_ref[r * slots : (r + 1) * slots, which * width + p * PAIR : which * width + (p + 1) * PAIR]

    masks = []
    for r in range(rows):
        here = pl.ds(at * rows + r, 1)
        seg = jnp.broadcast_to(seg_ref[here, :].astype(F32), (slots, slots))
        step = jnp.broadcast_to(step_ref[here, :].astype(F32), (slots, slots))
        live = jnp.broadcast_to(pad_ref[here, :].astype(F32), (slots, slots)).T == 0
        masks.append(((seg == seg.T) & (step.T <= step) & live) | eye)
    scores = [mm_nt(part(r, p, 1), by_head(part(r, p, 0) * HEAD ** (-0.5))) for r, p in units]
    probs = []
    for (r, p), score in zip(units, scores):
        halves = []
        for half in (score[:, :slots], score[:, slots:]):
            half = jnp.where(masks[r], half, -1e30)
            weight = jnp.exp(half - jnp.max(half, axis=0, keepdims=True))
            total = jnp.sum(weight, axis=0, keepdims=True)
            halves.append((weight * (1.0 / total)).astype(BF))
        probs.append(halves)
    for (r, p), halves in zip(units, probs):
        prob_ref[r, p] = jnp.concatenate(halves, axis=1)
        mixed = mm_tn(jnp.concatenate(halves, axis=0), by_head(part(r, p, 2)))
        mixed_ref[r * slots : (r + 1) * slots, p * PAIR : (p + 1) * PAIR] = mixed.astype(BF)
    residual = tokens + mm(mixed_ref[...], wout_ref[...])
    res_ref[...] = residual
    unit, _ = unit_parts(residual)
    second_ref[...] = (unit * g2_ref[...] + c2_ref[...]).astype(BF)


def attend(info, tokens, g1, c1, wqkv, wout, g2, c2, seg, step, pad):
    n, width = tokens.shape
    rows, slots = seg.shape
    per, pairs = TOKS // slots, width // PAIR
    return call(
        attend_kernel,
        "attend",
        (n // TOKS,),
        [rows_of(width), whole(1, width), whole(1, width), whole(*wqkv.shape), whole(*wout.shape)]
        + [whole(1, width)] * 2
        + [whole(rows, slots)] * 3,
        [
            rows_of(3 * width),
            pl.BlockSpec((per, pairs, slots, 2 * slots), lambda i, *_: (i, 0, 0, 0)),
            rows_of(width),
            rows_of(width),
            rows_of(width),
        ],
        [
            pltpu.HBM((n, 3 * width), BF),
            pltpu.HBM((rows, pairs, slots, 2 * slots), BF),
            pltpu.HBM((n, width), BF),
            pltpu.HBM((n, width), F32),
            pltpu.VMEM((n, width), BF),
        ],
        [],
        info,
        far(tokens, g1, c1) + (wqkv, wout) + far(g2, c2, seg, step, pad),
    )


def pack_kernel(info_ref, up_ref, bias_ref, down_ref, up_out, down_out):
    width = up_ref.shape[0]
    up_out[:width, :] = up_ref[...]
    units = up_ref.shape[1]
    bias = bias_ref[...].reshape(1, 2 * units)
    bias = jnp.where(info_ref[0] == 0, bias[:, :units], bias[:, units:])
    up_out[width:, :] = jnp.broadcast_to(bias, (TILE, units))
    down_out[...] = down_ref[...]


def pack(info, up, bias, down):
    width, units = up.shape[0], up.shape[1] // 2
    return call(
        pack_kernel,
        "pack",
        (1,),
        [
            pl.BlockSpec((width, units), lambda t, info: (0, info[0])),
            whole(2 * units),
            pl.BlockSpec((units, width), lambda t, info: (info[0], 0)),
        ],
        [whole(width + TILE, units), whole(units, width)],
        [jax.ShapeDtypeStruct((width + TILE, units), BF), jax.ShapeDtypeStruct((units, width), BF)],
        [],
        info,
        far(up, bias, down),
    )


def ffn_block(sec, dy, up, bias, down, acc_ref, bacc_ref):
    pre = mm(sec, up) + bias
    dhid = mm_nt(dy, down)
    hid, slope = gelu_pair(pre)
    hid = hid.astype(BF)
    dpre = (dhid * slope).astype(BF)
    grad_up = mm(sec.T, dpre)
    grad_down = mm(dy.T, hid)
    sums = jnp.sum(dpre.astype(F32), axis=0, keepdims=True)
    chunks, _, double = acc_ref.shape
    units = double // 2
    for i in range(chunks):
        cols = slice(i * units, (i + 1) * units)
        acc_ref[i, :, :units] += grad_up[:, cols]
        acc_ref[i, :, units:] += grad_down[:, cols]
        bacc_ref[i : i + 1, :] += sums[:, cols]
    return hid, dpre


def ffn_own_kernel(
    tables, mixing, info_ref, sec_ref, dy_ref, up_ref, bias_ref, down_ref, out_ref, dsec_ref, keep_ref, send_ref, bias_out,
    acc_ref,
):
    at, last = pl.program_id(0), pl.num_programs(0) - 1

    @pl.when(at == 0)
    def _():
        acc_ref[...] = jnp.zeros_like(acc_ref)
        bias_out[...] = jnp.zeros_like(bias_out)

    bias = bias_ref[...].astype(F32).reshape(1, up_ref.shape[1])
    hid, dpre = ffn_block(sec_ref[...], dy_ref[...], up_ref[...], bias, down_ref[...], acc_ref, bias_out)
    out_ref[...] = mm(hid, down_ref[...])
    dsec_ref[...] = mm_nt(dpre, up_ref[...])

    @pl.when(at == last)
    def _():
        core, own, other = info_ref[0], info_ref[1], info_ref[2]
        permuted(keep_ref, acc_ref, core, tables, core, own)
        permuted(send_ref, acc_ref, core ^ 1, tables, core ^ 1, other, core ^ 1 if mixing else 0)


def ffn_own(info, tables, mixing, second, dy, up, bias, down):
    n, width = second.shape
    units = up.shape[1] // 2
    return call(
        functools.partial(ffn_own_kernel, tables, mixing),
        "ffn_own",
        (n // TOKS,),
        [rows_of(width), rows_of(width), whole(*up.shape), whole(*bias.shape), whole(*down.shape)],
        [rows_of(width)] * 2 + [whole(width, 2 * units)] * 2 + [whole(2, units)],
        [pltpu.VMEM((n, width), F32)] * 2
        + [pltpu.HBM((width, 2 * units), BF)] * 2
        + [pltpu.HBM((2, units), F32)],
        [pltpu.VMEM((2, width, 2 * units), F32)],
        info,
        near(second) + far(dy) + (up,) + far(bias) + (down,),
    )


def ffn_rest_kernel(
    tables, count, mixing, info_ref, sec_in, dy_in, out_in, dsec_in, res_in, mixed_in, mine_ref, bdown_ref, g2_ref, wout_ref, *refs
):
    ups, downs = refs[:count], refs[count : 2 * count]
    block_out, gres_out, gmix_out, vec_ref, dwout_ref, bias_out = refs[2 * count : 2 * count + 6]
    grads, refs = refs[2 * count + 6 : 3 * count + 6 + mixing], refs[3 * count + 6 + mixing :]
    sec_ref, dy_ref, out_ref, dsec_ref, res_ref, mixed_ref, branch_ref, up_ref, bias_ref, down_ref, laid_ref, sems = refs
    n, width = sec_ref.shape
    units = down_ref.shape[0] // count
    core = info_ref[0]
    half = width // 2
    top, low = pl.ds(0, half), pl.ds(half, half)
    used = iter(range(sems.shape[0]))

    def move(*pairs):
        copies = [pltpu.make_async_copy(*pair, sems.at[next(used)]) for pair in pairs]
        for copy in copies:
            copy.start()
        return copies

    def arrived(copies):
        for copy in copies:
            copy.wait()

    def by_core(first, *sets):
        def each(act):
            for odd, pairs in enumerate(sets):

                @pl.when(core == odd)
                def _(pairs=pairs):
                    for i, pair in enumerate(pairs):
                        act(pltpu.make_async_copy(*pair, sems.at[first + i]))

        return lambda: each(lambda copy: copy.start()), lambda: each(lambda copy: copy.wait())

    cols = [pl.ds(i * units, units) for i in range(count)]
    first = move(
        (sec_in, sec_ref),
        *[(ups[i].at[pl.ds(0, width), :], up_ref.at[:, cols[i]]) for i in range(count)],
        *[(ups[i].at[pl.ds(width, TILE), :], bias_ref.at[:, cols[i]]) for i in range(count)],
    )
    second = move((dy_in, dy_ref), *[(downs[i], down_ref.at[cols[i], :]) for i in range(count)])
    third = move((out_in, out_ref), (dsec_in, dsec_ref), (res_in, res_ref), (mixed_in, mixed_ref))
    if mixing:
        keep_ref, send_ref, away_ref = grads
        own_start, own_wait = by_core(
            next(used),
            [(mine_ref, keep_ref)],
            [(mine_ref.at[top], keep_ref.at[low]), (mine_ref.at[low], send_ref.at[top])],
        )
        next(used)
        chunk_start, chunk_wait = by_core(
            next(used),
            [(laid_ref.at[0], send_ref)],
            [(laid_ref.at[0, top], keep_ref.at[top]), (laid_ref.at[0, low], send_ref.at[low])],
        )
        next(used)
        own_start()

    arrived(first)
    toks = n if count <= 2 else n // 2
    grad_up = grad_down = sums = None
    parts = []
    for t in range(n // toks):
        rows = slice(t * toks, (t + 1) * toks)
        sec = sec_ref[rows, :]
        pre = mm(sec, up_ref[...]) + bias_ref[...].astype(F32)[:1]
        if t == 0:
            arrived(second)
        dy = dy_ref[rows, :]
        dhid = mm_nt(dy, down_ref[...])
        hid, slope = gelu_pair(pre)
        hid = hid.astype(BF)
        dpre = (dhid * slope).astype(BF)
        more = (mm(sec.T, dpre), mm(dy.T, hid), jnp.sum(dpre.astype(F32), axis=0, keepdims=True))
        if t:
            more = (grad_up + more[0], grad_down + more[1], sums + more[2])
        grad_up, grad_down, sums = more
        parts.append((hid, dpre))
    blocks = len(tables[0])
    size = width // blocks
    for i in range(count):
        at = slice(i * units, (i + 1) * units)
        bias_out[i : i + 1, :] = sums[:, at]
        for block in range(blocks):
            owner = core ^ (i % 2)
            place = place_of(block, tables, owner, info_ref[1 + i % 2])
            to = pl.ds(pl.multiple_of(place * size, size), size)
            rows = slice(block * size, (block + 1) * size)
            laid_ref[i, to, :units] = grad_up[rows, at].astype(BF)
            laid_ref[i, to, units:] = grad_down[rows, at].astype(BF)
    if mixing:
        chunk_start()
        gone = move((laid_ref.at[1], away_ref))
    else:
        gone = move(*[(laid_ref.at[i], grads[i]) for i in range(count)])

    arrived(third)
    step = min(TOKS // 2, toks)
    for t, (hid, dpre) in enumerate(parts):
        out_all, dsec_all = mm(hid, down_ref[...]), mm_nt(dpre, up_ref[...])
        for r in range(0, toks, step):
            rows = slice(t * toks + r, t * toks + r + step)
            span = pl.ds(rows.start, step)
            dy32 = dy_ref[rows, :].astype(F32)
            residual = res_ref[rows, :]
            dsec = dsec_all[r : r + step] + dsec_ref[rows, :]
            dy_ref[rows, :] = (residual + (out_all[r : r + step] + out_ref[rows, :] + bdown_ref[...])).astype(BF)
            unit, inv = unit_parts(residual)
            sums = [jnp.sum(v, axis=0, keepdims=True) for v in (dsec * unit, dsec, dy32)]
            for i, row in enumerate(sums):
                if rows.start:
                    vec_ref[i : i + 1, :] += row
                else:
                    vec_ref[i : i + 1, :] = row
            gres = dy32 + norm_back(dsec, unit, inv, g2_ref[...])
            out_ref[rows, :] = gres
            branch_ref[rows, :] = gres.astype(BF)
            gone += move((dy_ref.at[span, :], block_out.at[span, :]), (out_ref.at[span, :], gres_out.at[span, :]))
    vec_ref[3:, :] = jnp.zeros((vec_ref.shape[0] - 3, width), F32)
    sec_ref[...] = mm_nt(branch_ref[...], wout_ref[...]).astype(BF)
    gone += move((sec_ref, gmix_out))
    dwout_ref[...] = mm_tn(mixed_ref[...], branch_ref[...])
    arrived(gone)
    if mixing:
        own_wait()
        chunk_wait()


def ffn_rest(info, tables, mixing, second, dy, out_part, dsec_part, residual, mixed, bdown, g2, wout, mine, chunks):
    n, width = second.shape
    count = len(chunks)
    units = chunks[0][0].shape[1]
    anywhere = pl.BlockSpec(memory_space=pl.ANY)
    return call(
        functools.partial(ffn_rest_kernel, tables, count, mixing),
        "ffn_rest",
        (1,),
        [anywhere] * 7 + [whole(1, width)] * 2 + [whole(width, width)] + [anywhere] * (2 * count),
        [anywhere] * 3 + [whole(8, width), whole(width, width), whole(count, units)] + [anywhere] * (count + mixing),
        [
            jax.ShapeDtypeStruct((n, width), BF),
            pltpu.HBM((n, width), F32),
            pltpu.HBM((n, width), BF),
            pltpu.HBM((8, width), F32),
            pltpu.HBM((width, width), F32),
            pltpu.HBM((count, units), F32),
        ]
        + [jax.ShapeDtypeStruct((width, 2 * units), BF)] * (count + mixing),
        [
            pltpu.VMEM((n, width), BF),
            pltpu.VMEM((n, width), BF),
            pltpu.VMEM((n, width), F32),
            pltpu.VMEM((n, width), F32),
            pltpu.VMEM((n, width), F32),
            pltpu.VMEM((n, width), BF),
            pltpu.VMEM((n, width), BF),
            pltpu.VMEM((width, count * units), BF),
            pltpu.VMEM((TILE, count * units), BF),
            pltpu.VMEM((count * units, width), BF),
            pltpu.VMEM((count, width, 2 * units), BF),
            pltpu.SemaphoreType.DMA((24 + 4 * count,)),
        ],
        info,
        near(second)
        + far(dy)
        + near(out_part, dsec_part)
        + far(residual, mixed, mine, bdown, g2)
        + (wout,)
        + tuple(c[0] for c in chunks)
        + tuple(c[1] for c in chunks),
        REST_LIMIT if count <= 2 else 56 * 1024 * 1024,
    )


def join_kernel(info_ref, send_ref, got_ref, own_ref, out_ref):
    half = send_ref.shape[0] // 2
    out_ref[half:, :] = (send_ref[half:, :].astype(F32) + got_ref[half:, :].astype(F32)).astype(BF)

    @pl.when(info_ref[0] == 0)
    def _():
        out_ref[:half, :] = (send_ref[:half, :].astype(F32) + got_ref[:half, :].astype(F32)).astype(BF)

    @pl.when(info_ref[0] == 1)
    def _():
        out_ref[:half, :] = (send_ref[:half, :].astype(F32) + own_ref[:half, :].astype(F32)).astype(BF)


def split_kernel(info_ref, keep_ref, got_ref, own_ref, arrived_ref, keep_out, send_out):
    half = keep_ref.shape[0] // 2
    top, low = slice(0, half), slice(half, 2 * half)

    def total(*parts):
        value = parts[0].astype(F32)
        for part in parts[1:]:
            value += part.astype(F32)
        return value.astype(BF)

    @pl.when(info_ref[0] == 0)
    def _():
        keep_out[...] = total(keep_ref[top, :], own_ref[top, :], arrived_ref[top, :])
        send_out[...] = total(keep_ref[low, :], own_ref[low, :], arrived_ref[low, :])

    @pl.when(info_ref[0] == 1)
    def _():
        keep_out[...] = total(keep_ref[low, :], own_ref[low, :], arrived_ref[top, :])
        send_out[...] = total(keep_ref[top, :], got_ref[top, :], arrived_ref[low, :])


def direct(kernel, name, info, out_shape, args):
    return pl.pallas_call(
        kernel,
        in_specs=[pl.BlockSpec(memory_space=pltpu.SMEM)] + [pl.BlockSpec(memory_space=pltpu.VMEM)] * len(args),
        out_specs=jax.tree.map(lambda _: pl.BlockSpec(memory_space=pltpu.VMEM), out_shape),
        out_shape=out_shape,
        compiler_params=pltpu.CompilerParams(vmem_limit_bytes=VMEM_LIMIT),
        cost_estimate=pl.CostEstimate(flops=1000, bytes_accessed=1000, transcendentals=0),
        name=name,
    )(info, *args)


def join(info, send, got, own):
    return direct(join_kernel, "join", info, jax.ShapeDtypeStruct(send.shape, BF), (send, got, own))


def split(info, keep, got, own, arrived):
    shape = jax.ShapeDtypeStruct((keep.shape[0] // 2, keep.shape[1]), BF)
    return direct(split_kernel, "split", info, [shape, shape], (keep, got, own, arrived))


def attend_back_kernel(
    tables, info_ref, qkv_ref, prob_ref, gmix_ref, tok_ref, g1_ref, c1_ref, wqkv_ref, dwout_ref, vec_ref,
    *refs,
):
    *sums, grad_ref, dw_keep_ref, dw_send_ref, dqkv_ref, acc_ref, row_ref = refs
    at, last = pl.program_id(0), pl.num_programs(0) - 1
    toks, width = tok_ref.shape
    rows, pairs, slots, _ = prob_ref.shape

    @pl.when(at == 0)
    def _():
        acc_ref[:, : 3 * width] = jnp.zeros((width, 3 * width), F32)
        acc_ref[:, 3 * width : 4 * width] = dwout_ref[...]
        row_ref[...] = jnp.zeros_like(row_ref)
        row_ref[SUMS : SUMS + vec_ref.shape[0], :] = vec_ref[...]
        if sums:
            own_ref, rest_ref = sums
            first = SUMS + vec_ref.shape[0]
            for i in range(2):
                row_ref[pl.ds(first + 2 * info_ref[5] + i, 1), :] = own_ref[i : i + 1, :]
                row_ref[pl.ds(first + 2 * (info_ref[5] ^ 1) + (info_ref[0] ^ i), 1), :] = rest_ref[i : i + 1, :]

    scale = HEAD ** (-0.5)
    units = [(r, p) for r in range(rows) for p in range(pairs)]

    def place(r, p, which):
        return (slice(r * slots, (r + 1) * slots), slice(which * width + p * PAIR, which * width + (p + 1) * PAIR))

    grads = [gmix_ref[place(r, p, 0)] for r, p in units]
    by_grad = [by_head(g) for g in grads]
    dprobs = [mm_nt(qkv_ref[place(r, p, 2)], g) for (r, p), g in zip(units, by_grad)]
    for (r, p), g in zip(units, by_grad):
        dqkv_ref[place(r, p, 2)] = mm(prob_ref[r, p], g).astype(BF)
    dscores = []
    for (r, p), dprob in zip(units, dprobs):
        p32 = prob_ref[r, p].astype(F32)
        dscores.append((p32 * (dprob - jnp.sum(p32 * dprob, axis=0, keepdims=True))).astype(BF))
    for (r, p), ds in zip(units, dscores):
        q = qkv_ref[place(r, p, 0)]
        dqkv_ref[place(r, p, 1)] = mm(ds, by_head(q * scale)).astype(BF)
    for (r, p), ds in zip(units, dscores):
        k = qkv_ref[place(r, p, 1)]
        stacked = jnp.concatenate([ds[:, :slots], ds[:, slots:]], axis=0)
        dqkv_ref[place(r, p, 0)] = mm_tn(stacked, by_head(k * scale)).astype(BF)
    unit, _ = unit_parts(tok_ref[...].astype(F32))
    acc_ref[:, : 3 * width] += mm_tn(unit.astype(BF), dqkv_ref[...])
    grad_ref[...] = dqkv_ref[...]
    for i in range(3):
        part = dqkv_ref[:, i * width : (i + 1) * width].astype(F32)
        row_ref[i : i + 1, :] += jnp.sum(part, axis=0, keepdims=True)

    @pl.when(at == last)
    def _():
        core, own, other = info_ref[0], info_ref[3], info_ref[4]
        row_ref[5:6, :] = g1_ref[...]
        row_ref[6:7, :] = c1_ref[...]
        wide_row = jnp.concatenate([row_ref[i : i + 1, :] for i in range(3)], axis=1)
        step = width // 4
        for r in range(0, width, step):
            w = wqkv_ref[r : r + step, :].astype(F32)
            sums = acc_ref[r : r + step, : 3 * width]
            d_gain = jnp.sum(w * sums, axis=1, keepdims=True)
            d_bias = jnp.sum(w * wide_row, axis=1, keepdims=True)
            lane = lax.broadcasted_iota(jnp.int32, (step, LANES), 1)
            others = row_ref[:, r : r + step].T
            acc_ref[r : r + step, : 3 * width] = others[:, 5:6] * sums + others[:, 6:7] * wide_row
            acc_ref[r : r + step, 4 * width :] = jnp.where(lane == 3, d_gain, jnp.where(lane == 4, d_bias, others))
        half = width // 2
        size = width // len(tables[0])
        for place in range(len(tables[0])):
            dst = dw_keep_ref if place * size < half else dw_send_ref
            block = block_at(place, tables, core, own if place * size < half else other)
            rows_at = pl.ds(pl.multiple_of(block * size, size), size)
            to = place * size % half
            dst[to : to + size, :] = acc_ref[rows_at, :].astype(BF)


def attend_back(info, tables, qkv, prob, gmix, tokens, g1, c1, wqkv, dwout, *vecs):
    n, width = tokens.shape
    rows, pairs, slots, _ = prob.shape
    per = TOKS // slots
    return call(
        functools.partial(attend_back_kernel, tables),
        "attend_back",
        (n // TOKS,),
        [
            rows_of(3 * width),
            pl.BlockSpec((per, pairs, slots, 2 * slots), lambda i, *_: (i, 0, 0, 0)),
            rows_of(width),
            rows_of(width),
            whole(1, width),
            whole(1, width),
            whole(*wqkv.shape),
            whole(width, width),
        ]
        + [whole(*vec.shape) for vec in vecs],
        [rows_of(3 * width)] + [whole(width // 2, 4 * width + LANES)] * 2,
        [pltpu.VMEM((n, 3 * width), BF)] + [jax.ShapeDtypeStruct((width // 2, 4 * width + LANES), BF)] * 2,
        [
            pltpu.VMEM((TOKS, 3 * width), BF),
            pltpu.VMEM((width, 4 * width + LANES), F32),
            pltpu.VMEM((LANES, width), F32),
        ],
        info,
        far(qkv, prob, gmix, tokens, g1, c1, wqkv, dwout, *vecs),
    )


def first_back_kernel(info_ref, dqkv_ref, wqkv_ref, tok_ref, gres_ref, g1_ref, out_ref):
    dnormed = mm_nt(dqkv_ref[...], wqkv_ref[...])
    unit, inv = unit_parts(tok_ref[...].astype(F32))
    out_ref[...] = gres_ref[...] + norm_back(dnormed, unit, inv, g1_ref[...])


def first_back(info, dqkv, wqkv, tokens, gres, g1):
    n, width = tokens.shape
    return call(
        first_back_kernel,
        "first_back",
        (n // TOKS,),
        [rows_of(3 * width), whole(*wqkv.shape), rows_of(width), rows_of(width), whole(1, width)],
        rows_of(width),
        jax.ShapeDtypeStruct((n, width), F32),
        [],
        info,
        near(dqkv) + (wqkv,) + far(tokens, gres, g1),
    )


def ffn_end_kernel(tables, info_ref, keep_ref, other_ref, up_ref, down_ref, full_ref):
    core = info_ref[0]
    units = up_ref.shape[1]
    blocks = len(tables[0])
    size = keep_ref.shape[0] // blocks

    def lay(src_ref, whose, base):
        for place in range(blocks):
            block = block_at(place, tables, whose, base)
            rows = pl.ds(pl.multiple_of(block * size, size), size)
            part = src_ref[place * size : (place + 1) * size, :].astype(F32)
            up_ref[rows, :] = part[:, :units]
            full_ref[rows, :] = part[:, units:]
        down_ref[...] = full_ref[...].T

    @pl.when(pl.program_id(0) == 0)
    def _():
        lay(keep_ref, core, info_ref[1])

    @pl.when(pl.program_id(0) == 1)
    def _():
        lay(other_ref, core ^ 1, info_ref[2])


def ffn_end(info, tables, keep, other):
    width, double = keep.shape
    units = double // 2
    return call(
        functools.partial(ffn_end_kernel, tables),
        "ffn_end",
        (2,),
        [whole(width, double)] * 2,
        [
            pl.BlockSpec((width, units), lambda i, info: (0, info[0] ^ i)),
            pl.BlockSpec((units, width), lambda i, info: (info[0] ^ i, 0)),
        ],
        [jax.ShapeDtypeStruct((width, double), F32), jax.ShapeDtypeStruct((double, width), F32)],
        [pltpu.VMEM((width, units), F32)],
        info,
        (keep, other),
    )


def attend_end_kernel(tables, which, shares, info_ref, *refs):
    quarters, refs = refs[: 2 + 2 * which], refs[2 + 2 * which + 2 * which :]
    qkv_hbm, out_hbm, *refs = refs
    vec_refs, (qkv_ref, out_ref, *refs, sems) = refs[: 6 * which], refs[6 * which :]
    core = info_ref[0]
    width = out_ref.shape[1]
    blocks = len(tables[0])
    quarter = quarters[0].shape[0]
    size = 4 * quarter // blocks
    spots = []
    for place in range(blocks):
        row = place * size
        side, half = row // (2 * quarter), row // quarter % 2
        block = block_at(place, tables, core, info_ref[3 + side])
        at = row % quarter
        src = quarters[side + 2 * half * which] if half <= which else None
        spots.append((half, src, at, side * quarter + at, pl.multiple_of(block * size, size)))
    copies = []
    for half, src, at, row, to in spots:
        if half != which:
            continue
        here, there = pl.ds(row, size), pl.ds(to, size)
        for ref, hbm, cols in ((qkv_ref, qkv_hbm, slice(0, 3 * width)), (out_ref, out_hbm, slice(3 * width, 4 * width))):
            ref[row : row + size, :] = src[at : at + size, cols].astype(F32)
            copies.append(pltpu.make_async_copy(ref.at[here, :], hbm.at[there, :], sems.at[len(copies)]))
            copies[-1].start()
    if which:
        col_ref, row_ref = refs
        for half, src, at, _, to in spots:
            col_ref[pl.ds(to, size), :] = src[at : at + size, 4 * width :].astype(F32)
        vec = col_ref[...].T
        row_ref[...] = vec
        flat = lambda row: row.reshape(row.shape[1])
        for i, at in enumerate((3, 4, SUMS, SUMS + 1, SUMS + 2)):
            vec_refs[i][...] = flat(vec[at : at + 1, :])
        units = vec_refs[5].shape[0]
        if units >= width:
            first = SUMS + 8 + info_ref[5] * (units // width)
            for i in range(units // width):
                vec_refs[5][i * width : (i + 1) * width] = flat(row_ref[pl.ds(first + i, 1), :])
        else:
            row = row_ref[pl.ds(SUMS + 8 + info_ref[5] // shares, 1), :]
            share = row[:, :units]
            for i in range(1, shares):
                share = jnp.where(info_ref[5] % shares == i, row[:, i * units : (i + 1) * units], share)
            vec_refs[5][...] = flat(share)
    for copy in copies:
        copy.wait()


def attend_end(info, tables, quarters, width, units, written=()):
    rows = 4 * quarters[0].shape[0]
    which = 1 if written else 0
    anywhere = pl.BlockSpec(memory_space=pl.ANY)
    return call(
        functools.partial(attend_end_kernel, tables, which, max(1, width // units)),
        "attend_end",
        (1,),
        [whole(*quarters[0].shape)] * len(quarters) + [anywhere] * len(written),
        [anywhere] * 2 + ([whole(width)] * 5 + [whole(units)]) * which,
        [jax.ShapeDtypeStruct((rows, 3 * width), F32), jax.ShapeDtypeStruct((rows, width), F32)]
        + ([jax.ShapeDtypeStruct((width,), F32)] * 5 + [jax.ShapeDtypeStruct((units,), F32)]) * which,
        [pltpu.VMEM((rows // 2, 3 * width), F32), pltpu.VMEM((rows // 2, width), F32)]
        + [pltpu.VMEM((rows, LANES), F32), pltpu.VMEM((LANES, width), F32)] * which
        + [pltpu.SemaphoreType.DMA((len(tables[0]),))],
        info,
        (*quarters, *written),
        aliases=[(1 + len(quarters) + i, i) for i in range(len(written))],
    )


def local(
    wide, narrow, tokens_in, ln1_gain, ln1_bias, w_qkv, w_out, ln2_gain, ln2_bias, w_up, b_up, w_down, b_down, segment_ids,
    step_ids, pad_mask, cotangent,
):
    width = tokens_in.shape[1]
    units = w_up.shape[1] // 2
    core_mask = narrow
    narrow_masks = [1 << b for b in range(narrow.bit_length() - 1)]
    wide_masks = [narrow << b for b in range(1, wide.bit_length() - 1)]

    def swap(value, first, second=None):
        masks = (first, first if second is None else second)
        pairs = [(i, i ^ masks[i // narrow & 1]) for i in range(wide * narrow)]
        return lax.ppermute(value, AXES, pairs)

    def add(a, b):
        return (a.astype(F32) + b.astype(F32)).astype(a.dtype)

    def after(*values):
        return lax.optimization_barrier(values)

    def steps_of(halved, exchanged, gathered):
        pairs = lambda order: list(zip(*order))
        return (
            [("halve", *pair) for pair in pairs(halved)]
            + [("exchange", *pair) for pair in pairs(exchanged)]
            + [("gather", *pair) for pair in reversed(pairs(gathered))]
        )

    def start(value, step):
        kind, *masks = step
        if kind == "halve":
            half = value.shape[0] // 2
            return value[:half], swap(value[half:], *masks)
        return value, swap(value, *masks)

    def finish(kept, got, step):
        if step[0] == "gather":
            return jnp.concatenate([kept, got], axis=0)
        return add(kept, got) if step[0] in ("halve", "exchange") else (kept, got)

    wide_at, narrow_at = lax.axis_index("wide"), lax.axis_index("narrow")
    core = wide_at & 1
    flat = wide_at * narrow + narrow_at

    def named(owner, used):
        return sum((1 << b) for b, m in enumerate(used) if owner & m)

    def block_of(used):
        return sum(((flat & m) != 0).astype(jnp.int32) << b for b, m in enumerate(used))

    def split_at(pair, count):
        return tuple(o[:count] for o in pair), tuple(o[count:] for o in pair)

    def by_core(values):
        return jnp.where(core == 0, values[0], values[1]), jnp.where(core == 0, values[1], values[0])

    mixing = narrow == 2 and len(wide_masks) == 3
    if mixing:
        y, low, high = wide_masks
        ff_in, ff_rest, ff_out = ([y, low], [y, low]), ([high], [high]), ([low, y], [low, y])
        at_in, at_rest, at_out = ([y, 1, low], [low, y, 1]), ([high], [high]), ([y, 1, low], [low, 1, y])
        turns = "FAFAAFAFAAFFAA"
    else:
        ff_in, ff_rest = split_at((wide_masks, wide_masks), min(len(wide_masks) - 1, (width // TILE).bit_length() - 1))
        masks = narrow_masks + wide_masks
        at_in, at_rest = split_at((masks, masks), min(len(masks) - 1, (width // TILE // 2).bit_length() - 1))
        ff_out, at_out, turns = ff_in, at_in, ""
    ff_used = tuple(sorted(o) for o in ff_in)
    ff_in_tables, ff_out_tables = (
        tuple([named(owner, ff_used[c]) for owner in places(pair[c], 1 << len(ff_used[c]))] for c in range(2))
        for pair in (ff_in, ff_out)
    )
    at_used = tuple([core_mask] + sorted(o) for o in at_in)

    def at_tables(order):
        owners = [places(o, 1 << len(o)) for o in order]
        return tuple(
            [named(o, at_used[c]) for o in owners[c]] + [named(o ^ core_mask, at_used[1 - c]) for o in owners[1 - c]]
            for c in range(2)
        )

    ff_block = by_core([block_of(used) for used in ff_used])
    at_block = by_core([block_of(used) for used in at_used])
    info = jnp.stack([core, *ff_block, *at_block, narrow_at]).astype(jnp.int32)

    packed, tokens_in = after(pack(info, w_up, b_up, w_down), tokens_in)
    fetched = [packed]
    for mask in narrow_masks:
        fetched = fetched + [(swap(u, mask), swap(d, mask)) for u, d in fetched]

    row = lambda v: v[None].astype(F32)
    g1, c1, g2 = row(ln1_gain), row(ln1_bias), row(ln2_gain)
    qkv, prob, mixed, residual, second = attend(
        info, tokens_in, g1, c1, w_qkv, w_out, g2, row(ln2_bias), segment_ids, step_ids, pad_mask
    )
    out_part, dsec_part, own_keep, own_send, bias_own = ffn_own(
        info, ff_in_tables, mixing, second, cotangent, w_up, b_up, w_down
    )
    own_send, fetched = after(own_send, fetched)
    chunks = []
    for up, down in fetched[1:]:
        chunks += [(up, down), (swap(up, core_mask), swap(down, core_mask))]
    rest = ffn_rest(
        info, ff_in_tables, mixing, second, cotangent, out_part, dsec_part, residual, mixed, row(b_down), g2, w_out, own_keep,
        chunks,
    )
    block_out, gres, gmix, vec, dwout, bias_rest = rest[:6]
    grads = rest[6:]

    if narrow == 2 and units == width:
        vecs = (vec, bias_own, bias_rest)
    else:
        b_rest = bias_rest.reshape(-1, 2, units)
        b_rest = jnp.where(core == 0, b_rest, jnp.flip(b_rest, axis=1))
        b_all = jnp.concatenate([bias_own[None], b_rest], axis=0)
        for bit in range(narrow.bit_length() - 1):
            flipped = jnp.flip(b_all.reshape(-1, 2, (1 << bit) * 2, units), axis=1).reshape(b_all.shape)
            b_all = jnp.where(narrow_at >> bit & 1, flipped, b_all)
        vecs = (jnp.concatenate([vec, b_all.reshape(-1, width)], axis=0),)

    if mixing:
        ff_keep, ff_send, away = grads
        got_own, got = swap(own_send, core_mask), swap(away, core_mask)
        ff_send = join(info, ff_send, got, got_own)
        gmix, ff_send = after(gmix, ff_send)
        ff_got = swap(ff_send, 1, y)
    else:
        held = [add(own_keep, swap(own_send, core_mask))] + [add(grads[2 * j], swap(grads[2 * j + 1], core_mask)) for j in range(narrow - 1)]
        gmix, held = after(gmix, held)
        for mask in reversed(narrow_masks):
            held = [add(held[j], swap(held[j + mask], mask)) for j in range(mask)]
        ff_keep = held[0]

    dqkv, keep, send = attend_back(info, at_tables(at_in), qkv, prob, gmix, tokens_in, g1, c1, w_qkv, dwout, *vecs)
    if mixing:
        send, ff_got = after(send, ff_got)
        ff_keep, ff_send = split(info, ff_keep, got, got_own, ff_got)
    keep = add(keep, swap(send, core_mask))
    grad_tokens = first_back(info, dqkv, w_qkv, tokens_in, gres, g1)
    steps = {
        "A": steps_of(at_in, at_rest, at_out)[:-1] + [("last", *steps_of(at_in, at_rest, at_out)[-1][1:]), ("core", core_mask)],
        "F": steps_of(ff_in, ff_rest, ff_out) + [("core", core_mask)],
    }
    if mixing:
        steps["F"] = [("halve", y, 1)] + steps["F"][1:]
        first = (ff_keep, swap(ff_send, y, 1))
    else:
        first = start(ff_keep, steps["F"][0])
    turns = turns or "".join(a + f for a, f in itertools.zip_longest("A" * len(steps["A"]), "F" * len(steps["F"]), fillvalue=""))
    under_way = {"A": start(keep, steps["A"][0]), "F": first}
    done, beside = (), (grad_tokens,)
    for turn in turns:
        other = "A" if turn == "F" else "F"
        kept, got = under_way.pop(turn)
        if other in under_way:
            other_kept, other_got = under_way[other]
            kept, other_kept, *beside = after(kept, other_kept, *beside)
            under_way[other] = other_kept, other_got
        else:
            kept, *beside = after(kept, *beside)
        if len(beside) == 1:
            (grad_tokens,), beside = beside, ()
        elif beside:
            (grad_w_up, grad_w_down), beside = beside, ()
        step, *steps[turn] = steps[turn]
        if step[0] == "last":
            written = attend_end(info, at_tables(at_out), (kept, crossed), width, 2 * units)
            got, written = after(got, written)
        value = finish(kept, got, step)
        if step[0] == "last":
            under_way[turn] = value, swap(got, core_mask)
        elif steps[turn]:
            under_way[turn] = start(value, steps[turn][0])
            if steps[turn][0][0] == "last":
                crossed = swap(value, core_mask)
        elif turn == "F":
            beside = ffn_end(info, ff_out_tables, *value)
        else:
            done = (value[0][0], crossed, value[0][1], value[1])
    grad_w_qkv, grad_w_out, d_gain1, d_bias1, d_gain2, d_bias2, d_bdown, grad_b_up = attend_end(
        info, at_tables(at_out), done, width, 2 * units, written
    )
    return (
        block_out, grad_tokens, d_gain1, d_bias1, grad_w_qkv, grad_w_out, d_gain2, d_bias2, grad_w_up, grad_b_up, grad_w_down,
        d_bdown,
    )


def solution(mesh):
    rows = P(("wide", "narrow"), None)
    in_specs = (
        rows, P(), P(), P(), P(), P(), P(), P(None, "narrow"), P("narrow"), P("narrow", None), P(), rows, rows, rows, rows,
    )
    out_specs = (
        rows, rows, P(), P(), P(), P(), P(), P(), P(None, "narrow"), P("narrow"), P("narrow", None), P(),
    )
    wide, narrow = mesh.shape["wide"], mesh.shape["narrow"]
    return jax.shard_map(
        functools.partial(local, wide, narrow), mesh=mesh, in_specs=in_specs, out_specs=out_specs, check_vma=False
    )
```

```python
import functools
import itertools

import jax
import jax.numpy as jnp
import numpy as np
from jax import lax
from jax.experimental import pallas as pl
from jax.experimental.pallas import tpu as pltpu
from jax.sharding import PartitionSpec as P

HEAD = 64
PAIR = 2 * HEAD
NORM_EPS = 1e-05
BF = jnp.bfloat16
F32 = jnp.float32
AXES = ("wide", "narrow")
LANES = 128
SUMS = 8
TILE = 16
TOKS = 512
VMEM_LIMIT = 30 * 1024 * 1024
REST_LIMIT = 36 * 1024 * 1024


def mm(a, b):
    return lax.dot_general(a, b, (((1,), (0,)), ((), ())), preferred_element_type=F32)


def mm_nt(a, b):
    return lax.dot_general(a, b, (((1,), (1,)), ((), ())), preferred_element_type=F32)


def mm_tn(a, b):
    return lax.dot_general(a, b, (((0,), (0,)), ((), ())), preferred_element_type=F32)


def near(*values):
    return tuple(pltpu.with_memory_space_constraint(v, pltpu.VMEM) for v in values)


def far(*values):
    return tuple(pltpu.with_memory_space_constraint(v, pltpu.HBM) for v in values)


def whole(*shape):
    return pl.BlockSpec(shape, lambda *_: (0,) * len(shape))


def rows_of(width, toks=TOKS):
    return pl.BlockSpec((toks, width), lambda i, *_: (i, 0))


def call(kernel, name, grid, in_specs, out_specs, out_shape, scratch, info, args, vmem=VMEM_LIMIT, aliases=()):
    return pl.pallas_call(
        kernel,
        grid_spec=pltpu.PrefetchScalarGridSpec(
            num_scalar_prefetch=1, grid=grid, in_specs=in_specs, out_specs=out_specs, scratch_shapes=scratch
        ),
        out_shape=out_shape,
        input_output_aliases=dict(aliases),
        compiler_params=pltpu.CompilerParams(vmem_limit_bytes=vmem),
        cost_estimate=pl.CostEstimate(flops=1000, bytes_accessed=1000, transcendentals=0),
        name=name,
    )(info, *args)


def unit_parts(rows):
    mean = jnp.mean(rows, axis=-1, keepdims=True)
    centered = rows - mean
    inv = lax.rsqrt(jnp.mean(centered * centered, axis=-1, keepdims=True) + NORM_EPS)
    return centered * inv, inv


def norm_back(incoming, unit, inv, gain):
    scaled = incoming * gain
    return inv * (
        scaled
        - jnp.mean(scaled, axis=-1, keepdims=True)
        - unit * jnp.mean(scaled * unit, axis=-1, keepdims=True)
    )


def gelu_pair(x):
    cdf = 0.5 * (1.0 + lax.erf(x * 0.7071067811865476))
    return x * cdf, cdf + x * jnp.exp(-0.5 * x * x) * 0.3989422804014327


def by_head(block):
    lane = lax.broadcasted_iota(jnp.int32, block.shape, 1)
    zero = jnp.zeros_like(block)
    first = lane < HEAD
    return jnp.concatenate([jnp.where(first, block, zero), jnp.where(first, zero, block)], axis=0)


def places(order, blocks):
    bits = blocks.bit_length() - 1
    table = []
    for place in range(blocks):
        owner = 0
        for step in range(bits):
            if place >> (bits - 1 - step) & 1:
                owner ^= order[step]
        table.append(owner)
    return table


def block_at(place, tables, core, own):
    first, second = tables[0][place], tables[1][place]
    if first == second:
        return own ^ first
    return own ^ jnp.where(core == 0, first, second)


def place_of(block, tables, core, own):
    wanted = own ^ block
    places_by_core = [[table.index(owner) for owner in range(len(table))] for table in tables]
    place = jnp.int32(0)
    for owner in range(len(tables[0])):
        first, second = places_by_core[0][owner], places_by_core[1][owner]
        place = jnp.where(wanted == owner, jnp.where(core == 0, first, second), place)
    return place


def permuted(dst_ref, acc_ref, chunk, tables, core, own, turned=0):
    blocks = len(tables[0])
    size = dst_ref.shape[0] // blocks
    for place in range(blocks):
        block = block_at(place, tables, core, own)
        rows = pl.ds(pl.multiple_of(block * size, size), size)
        to = pl.ds(pl.multiple_of(((place + turned * (blocks // 2)) & (blocks - 1)) * size, size), size)
        dst_ref[to, :] = acc_ref[chunk, rows, :].astype(dst_ref.dtype)


def attend_kernel(
    info_ref, tok_ref, g1_ref, c1_ref, wqkv_ref, wout_ref, g2_ref, c2_ref, seg_ref, step_ref, pad_ref,
    qkv_ref, prob_ref, mixed_ref, res_ref, second_ref,
):
    slots = seg_ref.shape[1]
    toks, width = tok_ref.shape
    rows = toks // slots
    at = pl.program_id(0)
    tokens = tok_ref[...].astype(F32)
    unit, _ = unit_parts(tokens)
    normed = (unit * g1_ref[...] + c1_ref[...]).astype(BF)
    qkv_ref[...] = mm(normed, wqkv_ref[...]).astype(BF)
    q_id = lax.broadcasted_iota(jnp.int32, (slots, slots), 0)
    k_id = lax.broadcasted_iota(jnp.int32, (slots, slots), 1)
    eye = q_id == k_id
    pairs = width // PAIR
    units = [(r, p) for r in range(rows) for p in range(pairs)]

    def part(r, p, which):
        return qkv_ref[r * slots : (r + 1) * slots, which * width + p * PAIR : which * width + (p + 1) * PAIR]

    masks = []
    for r in range(rows):
        here = pl.ds(at * rows + r, 1)
        seg = jnp.broadcast_to(seg_ref[here, :].astype(F32), (slots, slots))
        step = jnp.broadcast_to(step_ref[here, :].astype(F32), (slots, slots))
        live = jnp.broadcast_to(pad_ref[here, :].astype(F32), (slots, slots)).T == 0
        masks.append(((seg == seg.T) & (step.T <= step) & live) | eye)
    scores = [mm_nt(part(r, p, 1), by_head(part(r, p, 0) * HEAD ** (-0.5))) for r, p in units]
    probs = []
    for (r, p), score in zip(units, scores):
        halves = []
        for half in (score[:, :slots], score[:, slots:]):
            half = jnp.where(masks[r], half, -1e30)
            weight = jnp.exp(half - jnp.max(half, axis=0, keepdims=True))
            total = jnp.sum(weight, axis=0, keepdims=True)
            halves.append((weight * (1.0 / total)).astype(BF))
        probs.append(halves)
    for (r, p), halves in zip(units, probs):
        prob_ref[r, p] = jnp.concatenate(halves, axis=1)
        mixed = mm_tn(jnp.concatenate(halves, axis=0), by_head(part(r, p, 2)))
        mixed_ref[r * slots : (r + 1) * slots, p * PAIR : (p + 1) * PAIR] = mixed.astype(BF)
    residual = tokens + mm(mixed_ref[...], wout_ref[...])
    res_ref[...] = residual
    unit, _ = unit_parts(residual)
    second_ref[...] = (unit * g2_ref[...] + c2_ref[...]).astype(BF)


def attend(info, tokens, g1, c1, wqkv, wout, g2, c2, seg, step, pad):
    n, width = tokens.shape
    rows, slots = seg.shape
    per, pairs = TOKS // slots, width // PAIR
    return call(
        attend_kernel,
        "attend",
        (n // TOKS,),
        [rows_of(width), whole(1, width), whole(1, width), whole(*wqkv.shape), whole(*wout.shape)]
        + [whole(1, width)] * 2
        + [whole(rows, slots)] * 3,
        [
            rows_of(3 * width),
            pl.BlockSpec((per, pairs, slots, 2 * slots), lambda i, *_: (i, 0, 0, 0)),
            rows_of(width),
            rows_of(width),
            rows_of(width),
        ],
        [
            pltpu.HBM((n, 3 * width), BF),
            pltpu.HBM((rows, pairs, slots, 2 * slots), BF),
            pltpu.HBM((n, width), BF),
            pltpu.HBM((n, width), F32),
            pltpu.VMEM((n, width), BF),
        ],
        [],
        info,
        far(tokens, g1, c1) + (wqkv, wout) + far(g2, c2, seg, step, pad),
    )


def pack_kernel(info_ref, up_ref, bias_ref, down_ref, up_out, down_out):
    width = up_ref.shape[0]
    up_out[:width, :] = up_ref[...]
    units = up_ref.shape[1]
    bias = bias_ref[...].reshape(1, 2 * units)
    bias = jnp.where(info_ref[0] == 0, bias[:, :units], bias[:, units:])
    up_out[width:, :] = jnp.broadcast_to(bias, (TILE, units))
    down_out[...] = down_ref[...]


def pack(info, up, bias, down):
    width, units = up.shape[0], up.shape[1] // 2
    return call(
        pack_kernel,
        "pack",
        (1,),
        [
            pl.BlockSpec((width, units), lambda t, info: (0, info[0])),
            whole(2 * units),
            pl.BlockSpec((units, width), lambda t, info: (info[0], 0)),
        ],
        [whole(width + TILE, units), whole(units, width)],
        [jax.ShapeDtypeStruct((width + TILE, units), BF), jax.ShapeDtypeStruct((units, width), BF)],
        [],
        info,
        far(up, bias, down),
    )


def ffn_block(sec, dy, up, bias, down, acc_ref, bacc_ref):
    pre = mm(sec, up) + bias
    dhid = mm_nt(dy, down)
    hid, slope = gelu_pair(pre)
    hid = hid.astype(BF)
    dpre = (dhid * slope).astype(BF)
    grad_up = mm(sec.T, dpre)
    grad_down = mm(dy.T, hid)
    sums = jnp.sum(dpre.astype(F32), axis=0, keepdims=True)
    chunks, _, double = acc_ref.shape
    units = double // 2
    for i in range(chunks):
        cols = slice(i * units, (i + 1) * units)
        acc_ref[i, :, :units] += grad_up[:, cols]
        acc_ref[i, :, units:] += grad_down[:, cols]
        bacc_ref[i : i + 1, :] += sums[:, cols]
    return hid, dpre


def ffn_own_kernel(
    tables, mixing, info_ref, sec_ref, dy_ref, up_ref, bias_ref, down_ref, out_ref, dsec_ref, keep_ref, send_ref, bias_out,
    acc_ref,
):
    at, last = pl.program_id(0), pl.num_programs(0) - 1

    @pl.when(at == 0)
    def _():
        acc_ref[...] = jnp.zeros_like(acc_ref)
        bias_out[...] = jnp.zeros_like(bias_out)

    bias = bias_ref[...].astype(F32).reshape(1, up_ref.shape[1])
    hid, dpre = ffn_block(sec_ref[...], dy_ref[...], up_ref[...], bias, down_ref[...], acc_ref, bias_out)
    out_ref[...] = mm(hid, down_ref[...])
    dsec_ref[...] = mm_nt(dpre, up_ref[...])

    @pl.when(at == last)
    def _():
        core, own, other = info_ref[0], info_ref[1], info_ref[2]
        permuted(keep_ref, acc_ref, core, tables, core, own)
        permuted(send_ref, acc_ref, core ^ 1, tables, core ^ 1, other, core ^ 1 if mixing else 0)


def ffn_own(info, tables, mixing, second, dy, up, bias, down):
    n, width = second.shape
    units = up.shape[1] // 2
    return call(
        functools.partial(ffn_own_kernel, tables, mixing),
        "ffn_own",
        (n // TOKS,),
        [rows_of(width), rows_of(width), whole(*up.shape), whole(*bias.shape), whole(*down.shape)],
        [rows_of(width)] * 2 + [whole(width, 2 * units)] * 2 + [whole(2, units)],
        [pltpu.VMEM((n, width), F32)] * 2
        + [pltpu.HBM((width, 2 * units), BF)] * 2
        + [pltpu.HBM((2, units), F32)],
        [pltpu.VMEM((2, width, 2 * units), F32)],
        info,
        near(second) + far(dy) + (up,) + far(bias) + (down,),
    )


def ffn_rest_kernel(
    tables, count, mixing, info_ref, sec_in, dy_in, out_in, dsec_in, res_in, mixed_in, mine_ref, bdown_ref, g2_ref, wout_ref, *refs
):
    ups, downs = refs[:count], refs[count : 2 * count]
    block_out, gres_out, gmix_out, vec_ref, dwout_ref, bias_out = refs[2 * count : 2 * count + 6]
    grads, refs = refs[2 * count + 6 : 3 * count + 6 + mixing], refs[3 * count + 6 + mixing :]
    sec_ref, dy_ref, out_ref, dsec_ref, res_ref, mixed_ref, branch_ref, up_ref, bias_ref, down_ref, laid_ref, sems = refs
    n, width = sec_ref.shape
    units = down_ref.shape[0] // count
    core = info_ref[0]
    half = width // 2
    top, low = pl.ds(0, half), pl.ds(half, half)
    used = iter(range(sems.shape[0]))

    def move(*pairs):
        copies = [pltpu.make_async_copy(*pair, sems.at[next(used)]) for pair in pairs]
        for copy in copies:
            copy.start()
        return copies

    def arrived(copies):
        for copy in copies:
            copy.wait()

    def by_core(first, *sets):
        def each(act):
            for odd, pairs in enumerate(sets):

                @pl.when(core == odd)
                def _(pairs=pairs):
                    for i, pair in enumerate(pairs):
                        act(pltpu.make_async_copy(*pair, sems.at[first + i]))

        return lambda: each(lambda copy: copy.start()), lambda: each(lambda copy: copy.wait())

    cols = [pl.ds(i * units, units) for i in range(count)]
    first = move(
        (sec_in, sec_ref),
        *[(ups[i].at[pl.ds(0, width), :], up_ref.at[:, cols[i]]) for i in range(count)],
        *[(ups[i].at[pl.ds(width, TILE), :], bias_ref.at[:, cols[i]]) for i in range(count)],
    )
    second = move((dy_in, dy_ref), *[(downs[i], down_ref.at[cols[i], :]) for i in range(count)])
    third = move((out_in, out_ref), (dsec_in, dsec_ref), (res_in, res_ref), (mixed_in, mixed_ref))
    if mixing:
        keep_ref, send_ref, away_ref = grads
        own_start, own_wait = by_core(
            next(used),
            [(mine_ref, keep_ref)],
            [(mine_ref.at[top], keep_ref.at[low]), (mine_ref.at[low], send_ref.at[top])],
        )
        next(used)
        chunk_start, chunk_wait = by_core(
            next(used),
            [(laid_ref.at[0], send_ref)],
            [(laid_ref.at[0, top], keep_ref.at[top]), (laid_ref.at[0, low], send_ref.at[low])],
        )
        next(used)
        own_start()

    arrived(first)
    toks = n if count <= 2 else n // 2
    grad_up = grad_down = sums = None
    parts = []
    for t in range(n // toks):
        rows = slice(t * toks, (t + 1) * toks)
        sec = sec_ref[rows, :]
        every = up_ref.shape[1]
        parts_of = [slice(c * every // 2, (c + 1) * every // 2) for c in range(2)]
        pres = [mm(sec, up_ref[:, c]) + bias_ref[:, c].astype(F32)[:1] for c in parts_of]
        if t == 0:
            arrived(second)
        dy = dy_ref[rows, :]
        dhids = [mm_nt(dy, down_ref[c, :]) for c in parts_of]
        hids, dpres, grads_up, grads_down = [], [], [], []
        sec_t, dy_t = sec.T, dy.T
        for pre, dhid in zip(pres, dhids):
            hid, slope = gelu_pair(pre)
            hids.append(hid.astype(BF))
            dpres.append((dhid * slope).astype(BF))
            grads_up.append(mm(sec_t, dpres[-1]))
            grads_down.append(mm(dy_t, hids[-1]))
        hid, dpre = jnp.concatenate(hids, axis=1), jnp.concatenate(dpres, axis=1)
        more = (jnp.concatenate(grads_up, axis=1), jnp.concatenate(grads_down, axis=1), jnp.sum(dpre.astype(F32), axis=0, keepdims=True))
        if t:
            more = (grad_up + more[0], grad_down + more[1], sums + more[2])
        grad_up, grad_down, sums = more
        parts.append((hid, dpre))
    blocks = len(tables[0])
    size = width // blocks
    for i in range(count):
        at = slice(i * units, (i + 1) * units)
        bias_out[i : i + 1, :] = sums[:, at]
        for block in range(blocks):
            owner = core ^ (i % 2)
            place = place_of(block, tables, owner, info_ref[1 + i % 2])
            to = pl.ds(pl.multiple_of(place * size, size), size)
            rows = slice(block * size, (block + 1) * size)
            laid_ref[i, to, :units] = grad_up[rows, at].astype(BF)
            laid_ref[i, to, units:] = grad_down[rows, at].astype(BF)
    if mixing:
        chunk_start()
        gone = move((laid_ref.at[1], away_ref))
    else:
        gone = move(*[(laid_ref.at[i], grads[i]) for i in range(count)])

    arrived(third)
    step = min(TOKS // 2, toks)
    for t, (hid, dpre) in enumerate(parts):
        out_all, dsec_all = mm(hid, down_ref[...]), mm_nt(dpre, up_ref[...])
        for r in range(0, toks, step):
            rows = slice(t * toks + r, t * toks + r + step)
            span = pl.ds(rows.start, step)
            dy32 = dy_ref[rows, :].astype(F32)
            residual = res_ref[rows, :]
            dsec = dsec_all[r : r + step] + dsec_ref[rows, :]
            dy_ref[rows, :] = (residual + (out_all[r : r + step] + out_ref[rows, :] + bdown_ref[...])).astype(BF)
            unit, inv = unit_parts(residual)
            sums = [jnp.sum(v, axis=0, keepdims=True) for v in (dsec * unit, dsec, dy32)]
            for i, row in enumerate(sums):
                if rows.start:
                    vec_ref[i : i + 1, :] += row
                else:
                    vec_ref[i : i + 1, :] = row
            gres = dy32 + norm_back(dsec, unit, inv, g2_ref[...])
            out_ref[rows, :] = gres
            branch_ref[rows, :] = gres.astype(BF)
            gone += move((dy_ref.at[span, :], block_out.at[span, :]), (out_ref.at[span, :], gres_out.at[span, :]))
    vec_ref[3:, :] = jnp.zeros((vec_ref.shape[0] - 3, width), F32)
    sec_ref[...] = mm_nt(branch_ref[...], wout_ref[...]).astype(BF)
    gone += move((sec_ref, gmix_out))
    dwout_ref[...] = mm_tn(mixed_ref[...], branch_ref[...])
    arrived(gone)
    if mixing:
        own_wait()
        chunk_wait()


def ffn_rest(info, tables, mixing, second, dy, out_part, dsec_part, residual, mixed, bdown, g2, wout, mine, chunks):
    n, width = second.shape
    count = len(chunks)
    units = chunks[0][0].shape[1]
    anywhere = pl.BlockSpec(memory_space=pl.ANY)
    return call(
        functools.partial(ffn_rest_kernel, tables, count, mixing),
        "ffn_rest",
        (1,),
        [anywhere] * 7 + [whole(1, width)] * 2 + [whole(width, width)] + [anywhere] * (2 * count),
        [anywhere] * 3 + [whole(8, width), whole(width, width), whole(count, units)] + [anywhere] * (count + mixing),
        [
            jax.ShapeDtypeStruct((n, width), BF),
            pltpu.HBM((n, width), F32),
            pltpu.HBM((n, width), BF),
            pltpu.HBM((8, width), F32),
            pltpu.HBM((width, width), F32),
            pltpu.HBM((count, units), F32),
        ]
        + [jax.ShapeDtypeStruct((width, 2 * units), BF)] * (count + mixing),
        [
            pltpu.VMEM((n, width), BF),
            pltpu.VMEM((n, width), BF),
            pltpu.VMEM((n, width), F32),
            pltpu.VMEM((n, width), F32),
            pltpu.VMEM((n, width), F32),
            pltpu.VMEM((n, width), BF),
            pltpu.VMEM((n, width), BF),
            pltpu.VMEM((width, count * units), BF),
            pltpu.VMEM((TILE, count * units), BF),
            pltpu.VMEM((count * units, width), BF),
            pltpu.VMEM((count, width, 2 * units), BF),
            pltpu.SemaphoreType.DMA((24 + 4 * count,)),
        ],
        info,
        near(second)
        + far(dy)
        + near(out_part, dsec_part)
        + far(residual, mixed, mine, bdown, g2)
        + (wout,)
        + tuple(c[0] for c in chunks)
        + tuple(c[1] for c in chunks),
        REST_LIMIT if count <= 2 else 56 * 1024 * 1024,
    )


def join_kernel(info_ref, send_ref, got_ref, own_ref, out_ref):
    half = send_ref.shape[0] // 2
    out_ref[half:, :] = (send_ref[half:, :].astype(F32) + got_ref[half:, :].astype(F32)).astype(BF)

    @pl.when(info_ref[0] == 0)
    def _():
        out_ref[:half, :] = (send_ref[:half, :].astype(F32) + got_ref[:half, :].astype(F32)).astype(BF)

    @pl.when(info_ref[0] == 1)
    def _():
        out_ref[:half, :] = (send_ref[:half, :].astype(F32) + own_ref[:half, :].astype(F32)).astype(BF)


def split_kernel(info_ref, keep_ref, got_ref, own_ref, arrived_ref, keep_out, send_out):
    half = keep_ref.shape[0] // 2
    top, low = slice(0, half), slice(half, 2 * half)

    def total(*parts):
        value = parts[0].astype(F32)
        for part in parts[1:]:
            value += part.astype(F32)
        return value.astype(BF)

    @pl.when(info_ref[0] == 0)
    def _():
        keep_out[...] = total(keep_ref[top, :], own_ref[top, :], arrived_ref[top, :])
        send_out[...] = total(keep_ref[low, :], own_ref[low, :], arrived_ref[low, :])

    @pl.when(info_ref[0] == 1)
    def _():
        keep_out[...] = total(keep_ref[low, :], own_ref[low, :], arrived_ref[top, :])
        send_out[...] = total(keep_ref[top, :], got_ref[top, :], arrived_ref[low, :])


def direct(kernel, name, info, out_shape, args):
    return pl.pallas_call(
        kernel,
        in_specs=[pl.BlockSpec(memory_space=pltpu.SMEM)] + [pl.BlockSpec(memory_space=pltpu.VMEM)] * len(args),
        out_specs=jax.tree.map(lambda _: pl.BlockSpec(memory_space=pltpu.VMEM), out_shape),
        out_shape=out_shape,
        compiler_params=pltpu.CompilerParams(vmem_limit_bytes=VMEM_LIMIT),
        cost_estimate=pl.CostEstimate(flops=1000, bytes_accessed=1000, transcendentals=0),
        name=name,
    )(info, *args)


def join(info, send, got, own):
    return direct(join_kernel, "join", info, jax.ShapeDtypeStruct(send.shape, BF), (send, got, own))


def split(info, keep, got, own, arrived):
    shape = jax.ShapeDtypeStruct((keep.shape[0] // 2, keep.shape[1]), BF)
    return direct(split_kernel, "split", info, [shape, shape], (keep, got, own, arrived))


def attend_back_kernel(
    tables, info_ref, qkv_ref, prob_ref, gmix_ref, tok_ref, g1_ref, c1_ref, wqkv_ref, dwout_ref, vec_ref,
    *refs,
):
    *sums, grad_ref, dw_keep_ref, dw_send_ref, dqkv_ref, acc_ref, row_ref = refs
    at, last = pl.program_id(0), pl.num_programs(0) - 1
    toks, width = tok_ref.shape
    rows, pairs, slots, _ = prob_ref.shape

    @pl.when(at == 0)
    def _():
        acc_ref[:, : 3 * width] = jnp.zeros((width, 3 * width), F32)
        acc_ref[:, 3 * width : 4 * width] = dwout_ref[...]
        row_ref[...] = jnp.zeros_like(row_ref)
        row_ref[SUMS : SUMS + vec_ref.shape[0], :] = vec_ref[...]
        if sums:
            own_ref, rest_ref = sums
            first = SUMS + vec_ref.shape[0]
            for i in range(2):
                row_ref[pl.ds(first + 2 * info_ref[5] + i, 1), :] = own_ref[i : i + 1, :]
                row_ref[pl.ds(first + 2 * (info_ref[5] ^ 1) + (info_ref[0] ^ i), 1), :] = rest_ref[i : i + 1, :]

    scale = HEAD ** (-0.5)
    units = [(r, p) for r in range(rows) for p in range(pairs)]

    def place(r, p, which):
        return (slice(r * slots, (r + 1) * slots), slice(which * width + p * PAIR, which * width + (p + 1) * PAIR))

    grads = [gmix_ref[place(r, p, 0)] for r, p in units]
    by_grad = [by_head(g) for g in grads]
    dprobs = [mm_nt(qkv_ref[place(r, p, 2)], g) for (r, p), g in zip(units, by_grad)]
    for (r, p), g in zip(units, by_grad):
        dqkv_ref[place(r, p, 2)] = mm(prob_ref[r, p], g).astype(BF)
    dscores = []
    for (r, p), dprob in zip(units, dprobs):
        p32 = prob_ref[r, p].astype(F32)
        dscores.append((p32 * (dprob - jnp.sum(p32 * dprob, axis=0, keepdims=True))).astype(BF))
    for (r, p), ds in zip(units, dscores):
        q = qkv_ref[place(r, p, 0)]
        dqkv_ref[place(r, p, 1)] = mm(ds, by_head(q * scale)).astype(BF)
    for (r, p), ds in zip(units, dscores):
        k = qkv_ref[place(r, p, 1)]
        stacked = jnp.concatenate([ds[:, :slots], ds[:, slots:]], axis=0)
        dqkv_ref[place(r, p, 0)] = mm_tn(stacked, by_head(k * scale)).astype(BF)
    unit, _ = unit_parts(tok_ref[...].astype(F32))
    acc_ref[:, : 3 * width] += mm_tn(unit.astype(BF), dqkv_ref[...])
    grad_ref[...] = dqkv_ref[...]
    for i in range(3):
        part = dqkv_ref[:, i * width : (i + 1) * width].astype(F32)
        row_ref[i : i + 1, :] += jnp.sum(part, axis=0, keepdims=True)

    @pl.when(at == last)
    def _():
        core, own, other = info_ref[0], info_ref[3], info_ref[4]
        row_ref[5:6, :] = g1_ref[...]
        row_ref[6:7, :] = c1_ref[...]
        wide_row = jnp.concatenate([row_ref[i : i + 1, :] for i in range(3)], axis=1)
        step = width // 4
        for r in range(0, width, step):
            w = wqkv_ref[r : r + step, :].astype(F32)
            sums = acc_ref[r : r + step, : 3 * width]
            d_gain = jnp.sum(w * sums, axis=1, keepdims=True)
            d_bias = jnp.sum(w * wide_row, axis=1, keepdims=True)
            lane = lax.broadcasted_iota(jnp.int32, (step, LANES), 1)
            others = row_ref[:, r : r + step].T
            acc_ref[r : r + step, : 3 * width] = others[:, 5:6] * sums + others[:, 6:7] * wide_row
            acc_ref[r : r + step, 4 * width :] = jnp.where(lane == 3, d_gain, jnp.where(lane == 4, d_bias, others))
        half = width // 2
        size = width // len(tables[0])
        for place in range(len(tables[0])):
            dst = dw_keep_ref if place * size < half else dw_send_ref
            block = block_at(place, tables, core, own if place * size < half else other)
            rows_at = pl.ds(pl.multiple_of(block * size, size), size)
            to = place * size % half
            dst[to : to + size, :] = acc_ref[rows_at, :].astype(BF)


def attend_back(info, tables, qkv, prob, gmix, tokens, g1, c1, wqkv, dwout, *vecs):
    n, width = tokens.shape
    rows, pairs, slots, _ = prob.shape
    per = TOKS // slots
    return call(
        functools.partial(attend_back_kernel, tables),
        "attend_back",
        (n // TOKS,),
        [
            rows_of(3 * width),
            pl.BlockSpec((per, pairs, slots, 2 * slots), lambda i, *_: (i, 0, 0, 0)),
            rows_of(width),
            rows_of(width),
            whole(1, width),
            whole(1, width),
            whole(*wqkv.shape),
            whole(width, width),
        ]
        + [whole(*vec.shape) for vec in vecs],
        [rows_of(3 * width)] + [whole(width // 2, 4 * width + LANES)] * 2,
        [pltpu.VMEM((n, 3 * width), BF)] + [jax.ShapeDtypeStruct((width // 2, 4 * width + LANES), BF)] * 2,
        [
            pltpu.VMEM((TOKS, 3 * width), BF),
            pltpu.VMEM((width, 4 * width + LANES), F32),
            pltpu.VMEM((LANES, width), F32),
        ],
        info,
        far(qkv, prob, gmix, tokens, g1, c1, wqkv, dwout, *vecs),
    )


def first_back_kernel(info_ref, dqkv_ref, wqkv_ref, tok_ref, gres_ref, g1_ref, out_ref):
    dnormed = mm_nt(dqkv_ref[...], wqkv_ref[...])
    unit, inv = unit_parts(tok_ref[...].astype(F32))
    out_ref[...] = gres_ref[...] + norm_back(dnormed, unit, inv, g1_ref[...])


def first_back(info, dqkv, wqkv, tokens, gres, g1):
    n, width = tokens.shape
    return call(
        first_back_kernel,
        "first_back",
        (n // TOKS,),
        [rows_of(3 * width), whole(*wqkv.shape), rows_of(width), rows_of(width), whole(1, width)],
        rows_of(width),
        jax.ShapeDtypeStruct((n, width), F32),
        [],
        info,
        near(dqkv) + (wqkv,) + far(tokens, gres, g1),
    )


def ffn_end_kernel(tables, info_ref, keep_ref, other_ref, up_ref, down_ref, full_ref):
    core = info_ref[0]
    units = up_ref.shape[1]
    blocks = len(tables[0])
    size = keep_ref.shape[0] // blocks

    def lay(src_ref, whose, base):
        for place in range(blocks):
            block = block_at(place, tables, whose, base)
            rows = pl.ds(pl.multiple_of(block * size, size), size)
            part = src_ref[place * size : (place + 1) * size, :].astype(F32)
            up_ref[rows, :] = part[:, :units]
            full_ref[rows, :] = part[:, units:]
        down_ref[...] = full_ref[...].T

    @pl.when(pl.program_id(0) == 0)
    def _():
        lay(keep_ref, core, info_ref[1])

    @pl.when(pl.program_id(0) == 1)
    def _():
        lay(other_ref, core ^ 1, info_ref[2])


def ffn_end(info, tables, keep, other):
    width, double = keep.shape
    units = double // 2
    return call(
        functools.partial(ffn_end_kernel, tables),
        "ffn_end",
        (2,),
        [whole(width, double)] * 2,
        [
            pl.BlockSpec((width, units), lambda i, info: (0, info[0] ^ i)),
            pl.BlockSpec((units, width), lambda i, info: (info[0] ^ i, 0)),
        ],
        [jax.ShapeDtypeStruct((width, double), F32), jax.ShapeDtypeStruct((double, width), F32)],
        [pltpu.VMEM((width, units), F32)],
        info,
        (keep, other),
    )


def attend_end_kernel(tables, which, shares, info_ref, *refs):
    quarters, refs = refs[: 2 + 2 * which], refs[2 + 2 * which + 2 * which :]
    qkv_hbm, out_hbm, *refs = refs
    vec_refs, (qkv_ref, out_ref, *refs, sems) = refs[: 6 * which], refs[6 * which :]
    core = info_ref[0]
    width = out_ref.shape[1]
    blocks = len(tables[0])
    quarter = quarters[0].shape[0]
    size = 4 * quarter // blocks
    spots = []
    for place in range(blocks):
        row = place * size
        side, half = row // (2 * quarter), row // quarter % 2
        block = block_at(place, tables, core, info_ref[3 + side])
        at = row % quarter
        src = quarters[side + 2 * half * which] if half <= which else None
        spots.append((half, src, at, side * quarter + at, pl.multiple_of(block * size, size)))
    copies = []
    for half, src, at, row, to in spots:
        if half != which:
            continue
        here, there = pl.ds(row, size), pl.ds(to, size)
        for ref, hbm, cols in ((qkv_ref, qkv_hbm, slice(0, 3 * width)), (out_ref, out_hbm, slice(3 * width, 4 * width))):
            ref[row : row + size, :] = src[at : at + size, cols].astype(F32)
            copies.append(pltpu.make_async_copy(ref.at[here, :], hbm.at[there, :], sems.at[len(copies)]))
            copies[-1].start()
    if which:
        col_ref, row_ref = refs
        for half, src, at, _, to in spots:
            col_ref[pl.ds(to, size), :] = src[at : at + size, 4 * width :].astype(F32)
        vec = col_ref[...].T
        row_ref[...] = vec
        flat = lambda row: row.reshape(row.shape[1])
        for i, at in enumerate((3, 4, SUMS, SUMS + 1, SUMS + 2)):
            vec_refs[i][...] = flat(vec[at : at + 1, :])
        units = vec_refs[5].shape[0]
        if units >= width:
            first = SUMS + 8 + info_ref[5] * (units // width)
            for i in range(units // width):
                vec_refs[5][i * width : (i + 1) * width] = flat(row_ref[pl.ds(first + i, 1), :])
        else:
            row = row_ref[pl.ds(SUMS + 8 + info_ref[5] // shares, 1), :]
            share = row[:, :units]
            for i in range(1, shares):
                share = jnp.where(info_ref[5] % shares == i, row[:, i * units : (i + 1) * units], share)
            vec_refs[5][...] = flat(share)
    for copy in copies:
        copy.wait()


def attend_end(info, tables, quarters, width, units, written=()):
    rows = 4 * quarters[0].shape[0]
    which = 1 if written else 0
    anywhere = pl.BlockSpec(memory_space=pl.ANY)
    return call(
        functools.partial(attend_end_kernel, tables, which, max(1, width // units)),
        "attend_end",
        (1,),
        [whole(*quarters[0].shape)] * len(quarters) + [anywhere] * len(written),
        [anywhere] * 2 + ([whole(width)] * 5 + [whole(units)]) * which,
        [jax.ShapeDtypeStruct((rows, 3 * width), F32), jax.ShapeDtypeStruct((rows, width), F32)]
        + ([jax.ShapeDtypeStruct((width,), F32)] * 5 + [jax.ShapeDtypeStruct((units,), F32)]) * which,
        [pltpu.VMEM((rows // 2, 3 * width), F32), pltpu.VMEM((rows // 2, width), F32)]
        + [pltpu.VMEM((rows, LANES), F32), pltpu.VMEM((LANES, width), F32)] * which
        + [pltpu.SemaphoreType.DMA((len(tables[0]),))],
        info,
        (*quarters, *written),
        aliases=[(1 + len(quarters) + i, i) for i in range(len(written))],
    )


def local(
    wide, narrow, tokens_in, ln1_gain, ln1_bias, w_qkv, w_out, ln2_gain, ln2_bias, w_up, b_up, w_down, b_down, segment_ids,
    step_ids, pad_mask, cotangent,
):
    width = tokens_in.shape[1]
    units = w_up.shape[1] // 2
    core_mask = narrow
    narrow_masks = [1 << b for b in range(narrow.bit_length() - 1)]
    wide_masks = [narrow << b for b in range(1, wide.bit_length() - 1)]

    def swap(value, first, second=None):
        masks = (first, first if second is None else second)
        pairs = [(i, i ^ masks[i // narrow & 1]) for i in range(wide * narrow)]
        return lax.ppermute(value, AXES, pairs)

    def add(a, b):
        return (a.astype(F32) + b.astype(F32)).astype(a.dtype)

    def after(*values):
        return lax.optimization_barrier(values)

    def steps_of(halved, exchanged, gathered):
        pairs = lambda order: list(zip(*order))
        return (
            [("halve", *pair) for pair in pairs(halved)]
            + [("exchange", *pair) for pair in pairs(exchanged)]
            + [("gather", *pair) for pair in reversed(pairs(gathered))]
        )

    def start(value, step):
        kind, *masks = step
        if kind == "halve":
            half = value.shape[0] // 2
            return value[:half], swap(value[half:], *masks)
        return value, swap(value, *masks)

    def finish(kept, got, step):
        if step[0] == "gather":
            return jnp.concatenate([kept, got], axis=0)
        return add(kept, got) if step[0] in ("halve", "exchange") else (kept, got)

    wide_at, narrow_at = lax.axis_index("wide"), lax.axis_index("narrow")
    core = wide_at & 1
    flat = wide_at * narrow + narrow_at

    def named(owner, used):
        return sum((1 << b) for b, m in enumerate(used) if owner & m)

    def block_of(used):
        return sum(((flat & m) != 0).astype(jnp.int32) << b for b, m in enumerate(used))

    def split_at(pair, count):
        return tuple(o[:count] for o in pair), tuple(o[count:] for o in pair)

    def by_core(values):
        return jnp.where(core == 0, values[0], values[1]), jnp.where(core == 0, values[1], values[0])

    mixing = narrow == 2 and len(wide_masks) == 3
    if mixing:
        y, low, high = wide_masks
        ff_in, ff_rest, ff_out = ([y, low], [y, low]), ([high], [high]), ([low, y], [low, y])
        at_in, at_rest, at_out = ([y, 1, low], [low, y, 1]), ([high], [high]), ([y, 1, low], [low, 1, y])
        turns = "FAFAAFAFAAFFAA"
    else:
        ff_in, ff_rest = split_at((wide_masks, wide_masks), min(len(wide_masks) - 1, (width // TILE).bit_length() - 1))
        masks = narrow_masks + wide_masks
        at_in, at_rest = split_at((masks, masks), min(len(masks) - 1, (width // TILE // 2).bit_length() - 1))
        ff_out, at_out, turns = ff_in, at_in, ""
    ff_used = tuple(sorted(o) for o in ff_in)
    ff_in_tables, ff_out_tables = (
        tuple([named(owner, ff_used[c]) for owner in places(pair[c], 1 << len(ff_used[c]))] for c in range(2))
        for pair in (ff_in, ff_out)
    )
    at_used = tuple([core_mask] + sorted(o) for o in at_in)

    def at_tables(order):
        owners = [places(o, 1 << len(o)) for o in order]
        return tuple(
            [named(o, at_used[c]) for o in owners[c]] + [named(o ^ core_mask, at_used[1 - c]) for o in owners[1 - c]]
            for c in range(2)
        )

    ff_block = by_core([block_of(used) for used in ff_used])
    at_block = by_core([block_of(used) for used in at_used])
    info = jnp.stack([core, *ff_block, *at_block, narrow_at]).astype(jnp.int32)

    packed, tokens_in = after(pack(info, w_up, b_up, w_down), tokens_in)
    fetched = [packed]
    for mask in narrow_masks:
        fetched = fetched + [(swap(u, mask), swap(d, mask)) for u, d in fetched]

    row = lambda v: v[None].astype(F32)
    g1, c1, g2 = row(ln1_gain), row(ln1_bias), row(ln2_gain)
    qkv, prob, mixed, residual, second = attend(
        info, tokens_in, g1, c1, w_qkv, w_out, g2, row(ln2_bias), segment_ids, step_ids, pad_mask
    )
    out_part, dsec_part, own_keep, own_send, bias_own = ffn_own(
        info, ff_in_tables, mixing, second, cotangent, w_up, b_up, w_down
    )
    ups, downs = [u for u, _ in fetched[1:]], [d for _, d in fetched[1:]]
    own_send, ups = after(own_send, ups)
    away_ups = [swap(u, core_mask) for u in ups]
    away_downs = [swap(d, core_mask) for d in downs]
    chunks = [pair for here in zip(zip(ups, downs), zip(away_ups, away_downs)) for pair in here]
    rest = ffn_rest(
        info, ff_in_tables, mixing, second, cotangent, out_part, dsec_part, residual, mixed, row(b_down), g2, w_out, own_keep,
        chunks,
    )
    block_out, gres, gmix, vec, dwout, bias_rest = rest[:6]
    grads = rest[6:]

    if narrow == 2 and units == width:
        vecs = (vec, bias_own, bias_rest)
    else:
        b_rest = bias_rest.reshape(-1, 2, units)
        b_rest = jnp.where(core == 0, b_rest, jnp.flip(b_rest, axis=1))
        b_all = jnp.concatenate([bias_own[None], b_rest], axis=0)
        for bit in range(narrow.bit_length() - 1):
            flipped = jnp.flip(b_all.reshape(-1, 2, (1 << bit) * 2, units), axis=1).reshape(b_all.shape)
            b_all = jnp.where(narrow_at >> bit & 1, flipped, b_all)
        vecs = (jnp.concatenate([vec, b_all.reshape(-1, width)], axis=0),)

    if mixing:
        ff_keep, ff_send, away = grads
        got_own, got = swap(own_send, core_mask), swap(away, core_mask)
        ff_send = join(info, ff_send, got, got_own)
        gmix, ff_send = after(gmix, ff_send)
        ff_got = swap(ff_send, 1, y)
    else:
        held = [add(own_keep, swap(own_send, core_mask))] + [add(grads[2 * j], swap(grads[2 * j + 1], core_mask)) for j in range(narrow - 1)]
        gmix, held = after(gmix, held)
        for mask in reversed(narrow_masks):
            held = [add(held[j], swap(held[j + mask], mask)) for j in range(mask)]
        ff_keep = held[0]

    dqkv, keep, send = attend_back(info, at_tables(at_in), qkv, prob, gmix, tokens_in, g1, c1, w_qkv, dwout, *vecs)
    if mixing:
        send, ff_got = after(send, ff_got)
        ff_keep, ff_send = split(info, ff_keep, got, got_own, ff_got)
    keep = add(keep, swap(send, core_mask))
    grad_tokens = first_back(info, dqkv, w_qkv, tokens_in, gres, g1)
    steps = {
        "A": steps_of(at_in, at_rest, at_out)[:-1] + [("last", *steps_of(at_in, at_rest, at_out)[-1][1:]), ("core", core_mask)],
        "F": steps_of(ff_in, ff_rest, ff_out) + [("core", core_mask)],
    }
    if mixing:
        steps["F"] = [("halve", y, 1)] + steps["F"][1:]
        first = (ff_keep, swap(ff_send, y, 1))
    else:
        first = start(ff_keep, steps["F"][0])
    turns = turns or "".join(a + f for a, f in itertools.zip_longest("A" * len(steps["A"]), "F" * len(steps["F"]), fillvalue=""))
    under_way = {"A": start(keep, steps["A"][0]), "F": first}
    done, beside = (), (grad_tokens,)
    for turn in turns:
        other = "A" if turn == "F" else "F"
        kept, got = under_way.pop(turn)
        if other in under_way:
            other_kept, other_got = under_way[other]
            kept, other_kept, *beside = after(kept, other_kept, *beside)
            under_way[other] = other_kept, other_got
        else:
            kept, *beside = after(kept, *beside)
        if len(beside) == 1:
            (grad_tokens,), beside = beside, ()
        elif beside:
            (grad_w_up, grad_w_down), beside = beside, ()
        step, *steps[turn] = steps[turn]
        if step[0] == "last":
            written = attend_end(info, at_tables(at_out), (kept, crossed), width, 2 * units)
            got, written = after(got, written)
        value = finish(kept, got, step)
        if step[0] == "last":
            under_way[turn] = value, swap(got, core_mask)
        elif steps[turn]:
            under_way[turn] = start(value, steps[turn][0])
            if steps[turn][0][0] == "last":
                crossed = swap(value, core_mask)
        elif turn == "F":
            beside = ffn_end(info, ff_out_tables, *value)
        else:
            done = (value[0][0], crossed, value[0][1], value[1])
    grad_w_qkv, grad_w_out, d_gain1, d_bias1, d_gain2, d_bias2, d_bdown, grad_b_up = attend_end(
        info, at_tables(at_out), done, width, 2 * units, written
    )
    return (
        block_out, grad_tokens, d_gain1, d_bias1, grad_w_qkv, grad_w_out, d_gain2, d_bias2, grad_w_up, grad_b_up, grad_w_down,
        d_bdown,
    )


def solution(mesh):
    rows = P(("wide", "narrow"), None)
    in_specs = (
        rows, P(), P(), P(), P(), P(), P(), P(None, "narrow"), P("narrow"), P("narrow", None), P(), rows, rows, rows, rows,
    )
    out_specs = (
        rows, rows, P(), P(), P(), P(), P(), P(), P(None, "narrow"), P("narrow"), P("narrow", None), P(),
    )
    wide, narrow = mesh.shape["wide"], mesh.shape["narrow"]
    return jax.shard_map(
        functools.partial(local, wide, narrow), mesh=mesh, in_specs=in_specs, out_specs=out_specs, check_vma=False
    )
```

```python
import functools
import itertools

import jax
import jax.numpy as jnp
import numpy as np
from jax import lax
from jax.experimental import pallas as pl
from jax.experimental.pallas import tpu as pltpu
from jax.sharding import PartitionSpec as P

HEAD = 64
PAIR = 2 * HEAD
NORM_EPS = 1e-05
BF = jnp.bfloat16
F32 = jnp.float32
AXES = ("wide", "narrow")
LANES = 128
SUMS = 8
TILE = 16
TOKS = 512
VMEM_LIMIT = 30 * 1024 * 1024
REST_LIMIT = 36 * 1024 * 1024


def mm(a, b):
    return lax.dot_general(a, b, (((1,), (0,)), ((), ())), preferred_element_type=F32)


def mm_nt(a, b):
    return lax.dot_general(a, b, (((1,), (1,)), ((), ())), preferred_element_type=F32)


def mm_tn(a, b):
    return lax.dot_general(a, b, (((0,), (0,)), ((), ())), preferred_element_type=F32)


def near(*values):
    return tuple(pltpu.with_memory_space_constraint(v, pltpu.VMEM) for v in values)


def far(*values):
    return tuple(pltpu.with_memory_space_constraint(v, pltpu.HBM) for v in values)


def whole(*shape):
    return pl.BlockSpec(shape, lambda *_: (0,) * len(shape))


def rows_of(width, toks=TOKS):
    return pl.BlockSpec((toks, width), lambda i, *_: (i, 0))


def call(kernel, name, grid, in_specs, out_specs, out_shape, scratch, info, args, vmem=VMEM_LIMIT, aliases=()):
    return pl.pallas_call(
        kernel,
        grid_spec=pltpu.PrefetchScalarGridSpec(
            num_scalar_prefetch=1, grid=grid, in_specs=in_specs, out_specs=out_specs, scratch_shapes=scratch
        ),
        out_shape=out_shape,
        input_output_aliases=dict(aliases),
        compiler_params=pltpu.CompilerParams(vmem_limit_bytes=vmem),
        cost_estimate=pl.CostEstimate(flops=1000, bytes_accessed=1000, transcendentals=0),
        name=name,
    )(info, *args)


def unit_parts(rows):
    mean = jnp.mean(rows, axis=-1, keepdims=True)
    centered = rows - mean
    inv = lax.rsqrt(jnp.mean(centered * centered, axis=-1, keepdims=True) + NORM_EPS)
    return centered * inv, inv


def norm_back(incoming, unit, inv, gain):
    scaled = incoming * gain
    return inv * (
        scaled
        - jnp.mean(scaled, axis=-1, keepdims=True)
        - unit * jnp.mean(scaled * unit, axis=-1, keepdims=True)
    )


def gelu_pair(x):
    cdf = 0.5 * (1.0 + lax.erf(x * 0.7071067811865476))
    return x * cdf, cdf + x * jnp.exp(-0.5 * x * x) * 0.3989422804014327


def by_head(block):
    lane = lax.broadcasted_iota(jnp.int32, block.shape, 1)
    zero = jnp.zeros_like(block)
    first = lane < HEAD
    return jnp.concatenate([jnp.where(first, block, zero), jnp.where(first, zero, block)], axis=0)


def places(order, blocks):
    bits = blocks.bit_length() - 1
    table = []
    for place in range(blocks):
        owner = 0
        for step in range(bits):
            if place >> (bits - 1 - step) & 1:
                owner ^= order[step]
        table.append(owner)
    return table


def block_at(place, tables, core, own):
    first, second = tables[0][place], tables[1][place]
    if first == second:
        return own ^ first
    return own ^ jnp.where(core == 0, first, second)


def place_of(block, tables, core, own):
    wanted = own ^ block
    places_by_core = [[table.index(owner) for owner in range(len(table))] for table in tables]
    place = jnp.int32(0)
    for owner in range(len(tables[0])):
        first, second = places_by_core[0][owner], places_by_core[1][owner]
        place = jnp.where(wanted == owner, jnp.where(core == 0, first, second), place)
    return place


def permuted(dst_ref, acc_ref, chunk, tables, core, own, turned=0):
    blocks = len(tables[0])
    size = dst_ref.shape[0] // blocks
    for place in range(blocks):
        block = block_at(place, tables, core, own)
        rows = pl.ds(pl.multiple_of(block * size, size), size)
        to = pl.ds(pl.multiple_of(((place + turned * (blocks // 2)) & (blocks - 1)) * size, size), size)
        dst_ref[to, :] = acc_ref[chunk, rows, :].astype(dst_ref.dtype)


def attend_kernel(
    info_ref, tok_ref, g1_ref, c1_ref, wqkv_ref, wout_ref, g2_ref, c2_ref, seg_ref, step_ref, pad_ref,
    qkv_ref, prob_ref, mixed_ref, res_ref, second_ref,
):
    slots = seg_ref.shape[1]
    toks, width = tok_ref.shape
    rows = toks // slots
    at = pl.program_id(0)
    tokens = tok_ref[...].astype(F32)
    unit, _ = unit_parts(tokens)
    normed = (unit * g1_ref[...] + c1_ref[...]).astype(BF)
    qkv_ref[...] = mm(normed, wqkv_ref[...]).astype(BF)
    q_id = lax.broadcasted_iota(jnp.int32, (slots, slots), 0)
    k_id = lax.broadcasted_iota(jnp.int32, (slots, slots), 1)
    eye = q_id == k_id
    pairs = width // PAIR
    units = [(r, p) for r in range(rows) for p in range(pairs)]

    def part(r, p, which):
        return qkv_ref[r * slots : (r + 1) * slots, which * width + p * PAIR : which * width + (p + 1) * PAIR]

    masks = []
    for r in range(rows):
        here = pl.ds(at * rows + r, 1)
        seg = jnp.broadcast_to(seg_ref[here, :].astype(F32), (slots, slots))
        step = jnp.broadcast_to(step_ref[here, :].astype(F32), (slots, slots))
        live = jnp.broadcast_to(pad_ref[here, :].astype(F32), (slots, slots)).T == 0
        masks.append(((seg == seg.T) & (step.T <= step) & live) | eye)
    scores = [mm_nt(part(r, p, 1), by_head(part(r, p, 0) * HEAD ** (-0.5))) for r, p in units]
    probs = []
    for (r, p), score in zip(units, scores):
        halves = []
        for half in (score[:, :slots], score[:, slots:]):
            half = jnp.where(masks[r], half, -1e30)
            weight = jnp.exp(half - jnp.max(half, axis=0, keepdims=True))
            total = jnp.sum(weight, axis=0, keepdims=True)
            halves.append((weight * (1.0 / total)).astype(BF))
        probs.append(halves)
    for (r, p), halves in zip(units, probs):
        prob_ref[r, p] = jnp.concatenate(halves, axis=1)
        mixed = mm_tn(jnp.concatenate(halves, axis=0), by_head(part(r, p, 2)))
        mixed_ref[r * slots : (r + 1) * slots, p * PAIR : (p + 1) * PAIR] = mixed.astype(BF)
    residual = tokens + mm(mixed_ref[...], wout_ref[...])
    res_ref[...] = residual
    unit, _ = unit_parts(residual)
    second_ref[...] = (unit * g2_ref[...] + c2_ref[...]).astype(BF)


def attend(info, tokens, g1, c1, wqkv, wout, g2, c2, seg, step, pad):
    n, width = tokens.shape
    rows, slots = seg.shape
    per, pairs = TOKS // slots, width // PAIR
    return call(
        attend_kernel,
        "attend",
        (n // TOKS,),
        [rows_of(width), whole(1, width), whole(1, width), whole(*wqkv.shape), whole(*wout.shape)]
        + [whole(1, width)] * 2
        + [whole(rows, slots)] * 3,
        [
            rows_of(3 * width),
            pl.BlockSpec((per, pairs, slots, 2 * slots), lambda i, *_: (i, 0, 0, 0)),
            rows_of(width),
            rows_of(width),
            rows_of(width),
        ],
        [
            pltpu.HBM((n, 3 * width), BF),
            pltpu.HBM((rows, pairs, slots, 2 * slots), BF),
            pltpu.HBM((n, width), BF),
            pltpu.HBM((n, width), F32),
            pltpu.VMEM((n, width), BF),
        ],
        [],
        info,
        far(tokens, g1, c1) + (wqkv, wout) + far(g2, c2, seg, step, pad),
    )


def pack_kernel(info_ref, up_ref, bias_ref, down_ref, up_out, down_out):
    width = up_ref.shape[0]
    up_out[:width, :] = up_ref[...]
    units = up_ref.shape[1]
    bias = bias_ref[...].reshape(1, 2 * units)
    bias = jnp.where(info_ref[0] == 0, bias[:, :units], bias[:, units:])
    up_out[width:, :] = jnp.broadcast_to(bias, (TILE, units))
    down_out[...] = down_ref[...]


def pack(info, up, bias, down):
    width, units = up.shape[0], up.shape[1] // 2
    return call(
        pack_kernel,
        "pack",
        (1,),
        [
            pl.BlockSpec((width, units), lambda t, info: (0, info[0])),
            whole(2 * units),
            pl.BlockSpec((units, width), lambda t, info: (info[0], 0)),
        ],
        [whole(width + TILE, units), whole(units, width)],
        [jax.ShapeDtypeStruct((width + TILE, units), BF), jax.ShapeDtypeStruct((units, width), BF)],
        [],
        info,
        far(up, bias, down),
    )


def ffn_block(sec, dy, up, bias, down, acc_ref, bacc_ref):
    pre = mm(sec, up) + bias
    dhid = mm_nt(dy, down)
    hid, slope = gelu_pair(pre)
    hid = hid.astype(BF)
    dpre = (dhid * slope).astype(BF)
    grad_up = mm(sec.T, dpre)
    grad_down = mm(dy.T, hid)
    sums = jnp.sum(dpre.astype(F32), axis=0, keepdims=True)
    chunks, _, double = acc_ref.shape
    units = double // 2
    for i in range(chunks):
        cols = slice(i * units, (i + 1) * units)
        acc_ref[i, :, :units] += grad_up[:, cols]
        acc_ref[i, :, units:] += grad_down[:, cols]
        bacc_ref[i : i + 1, :] += sums[:, cols]
    return hid, dpre


def ffn_own_kernel(
    tables, mixing, info_ref, sec_ref, dy_ref, up_ref, bias_ref, down_ref, out_ref, dsec_ref, keep_ref, send_ref, bias_out,
    acc_ref,
):
    at, last = pl.program_id(0), pl.num_programs(0) - 1

    @pl.when(at == 0)
    def _():
        acc_ref[...] = jnp.zeros_like(acc_ref)
        bias_out[...] = jnp.zeros_like(bias_out)

    bias = bias_ref[...].astype(F32).reshape(1, up_ref.shape[1])
    hid, dpre = ffn_block(sec_ref[...], dy_ref[...], up_ref[...], bias, down_ref[...], acc_ref, bias_out)
    out_ref[...] = mm(hid, down_ref[...])
    dsec_ref[...] = mm_nt(dpre, up_ref[...])

    @pl.when(at == last)
    def _():
        core, own, other = info_ref[0], info_ref[1], info_ref[2]
        permuted(keep_ref, acc_ref, core, tables, core, own)
        permuted(send_ref, acc_ref, core ^ 1, tables, core ^ 1, other, core ^ 1 if mixing else 0)


def ffn_own(info, tables, mixing, second, dy, up, bias, down):
    n, width = second.shape
    units = up.shape[1] // 2
    return call(
        functools.partial(ffn_own_kernel, tables, mixing),
        "ffn_own",
        (n // TOKS,),
        [rows_of(width), rows_of(width), whole(*up.shape), whole(*bias.shape), whole(*down.shape)],
        [rows_of(width)] * 2 + [whole(width, 2 * units)] * 2 + [whole(2, units)],
        [pltpu.VMEM((n, width), F32)] * 2
        + [pltpu.HBM((width, 2 * units), BF)] * 2
        + [pltpu.HBM((2, units), F32)],
        [pltpu.VMEM((2, width, 2 * units), F32)],
        info,
        near(second) + far(dy) + (up,) + far(bias) + (down,),
    )


def ffn_rest_kernel(
    tables, count, mixing, info_ref, sec_in, dy_in, out_in, dsec_in, res_in, mixed_in, mine_ref, bdown_ref, g2_ref, wout_ref, *refs
):
    ups, downs = refs[:count], refs[count : 2 * count]
    block_out, gres_out, gmix_out, vec_ref, dwout_ref, bias_out = refs[2 * count : 2 * count + 6]
    grads, refs = refs[2 * count + 6 : 3 * count + 6 + mixing], refs[3 * count + 6 + mixing :]
    sec_ref, dy_ref, out_ref, dsec_ref, res_ref, mixed_ref, branch_ref, up_ref, bias_ref, down_ref, laid_ref, sems = refs
    n, width = sec_ref.shape
    units = down_ref.shape[0] // count
    core = info_ref[0]
    half = width // 2
    top, low = pl.ds(0, half), pl.ds(half, half)
    used = iter(range(sems.shape[0]))

    def move(*pairs):
        copies = [pltpu.make_async_copy(*pair, sems.at[next(used)]) for pair in pairs]
        for copy in copies:
            copy.start()
        return copies

    def arrived(copies):
        for copy in copies:
            copy.wait()

    def by_core(first, *sets):
        def each(act):
            for odd, pairs in enumerate(sets):

                @pl.when(core == odd)
                def _(pairs=pairs):
                    for i, pair in enumerate(pairs):
                        act(pltpu.make_async_copy(*pair, sems.at[first + i]))

        return lambda: each(lambda copy: copy.start()), lambda: each(lambda copy: copy.wait())

    cols = [pl.ds(i * units, units) for i in range(count)]
    first = move(
        (sec_in, sec_ref),
        *[(ups[i].at[pl.ds(0, width), :], up_ref.at[:, cols[i]]) for i in range(count)],
        *[(ups[i].at[pl.ds(width, TILE), :], bias_ref.at[:, cols[i]]) for i in range(count)],
    )
    second = move((dy_in, dy_ref), *[(downs[i], down_ref.at[cols[i], :]) for i in range(count)])
    third = move((out_in, out_ref), (dsec_in, dsec_ref), (res_in, res_ref), (mixed_in, mixed_ref))
    if mixing:
        keep_ref, send_ref, away_ref = grads
        own_start, own_wait = by_core(
            next(used),
            [(mine_ref, keep_ref)],
            [(mine_ref.at[top], keep_ref.at[low]), (mine_ref.at[low], send_ref.at[top])],
        )
        next(used)
        chunk_start, chunk_wait = by_core(
            next(used),
            [(laid_ref.at[0], send_ref)],
            [(laid_ref.at[0, top], keep_ref.at[top]), (laid_ref.at[0, low], send_ref.at[low])],
        )
        next(used)
        own_start()

    arrived(first)
    toks = n if count <= 2 else n // 2
    grad_up = grad_down = sums = None
    parts = []
    for t in range(n // toks):
        rows = slice(t * toks, (t + 1) * toks)
        sec = sec_ref[rows, :]
        every = up_ref.shape[1]
        parts_of = [slice(c * every // 2, (c + 1) * every // 2) for c in range(2)]
        pres = [mm(sec, up_ref[:, c]) + bias_ref[:, c].astype(F32)[:1] for c in parts_of]
        if t == 0:
            arrived(second)
        dy = dy_ref[rows, :]
        dhids = [mm_nt(dy, down_ref[c, :]) for c in parts_of]
        hids, dpres, grads_up, grads_down = [], [], [], []
        sec_t, dy_t = sec.T, dy.T
        for pre, dhid in zip(pres, dhids):
            hid, slope = gelu_pair(pre)
            hids.append(hid.astype(BF))
            dpres.append((dhid * slope).astype(BF))
            grads_up.append(mm(sec_t, dpres[-1]))
            grads_down.append(mm(dy_t, hids[-1]))
        hid, dpre = jnp.concatenate(hids, axis=1), jnp.concatenate(dpres, axis=1)
        more = (jnp.concatenate(grads_up, axis=1), jnp.concatenate(grads_down, axis=1), jnp.sum(dpre.astype(F32), axis=0, keepdims=True))
        if t:
            more = (grad_up + more[0], grad_down + more[1], sums + more[2])
        grad_up, grad_down, sums = more
        parts.append((hid, dpre))
    blocks = len(tables[0])
    size = width // blocks
    for i in range(count):
        at = slice(i * units, (i + 1) * units)
        bias_out[i : i + 1, :] = sums[:, at]
        for block in range(blocks):
            owner = core ^ (i % 2)
            place = place_of(block, tables, owner, info_ref[1 + i % 2])
            to = pl.ds(pl.multiple_of(place * size, size), size)
            rows = slice(block * size, (block + 1) * size)
            laid_ref[i, to, :units] = grad_up[rows, at].astype(BF)
            laid_ref[i, to, units:] = grad_down[rows, at].astype(BF)
    if mixing:
        chunk_start()
        gone = move((laid_ref.at[1], away_ref))
    else:
        gone = move(*[(laid_ref.at[i], grads[i]) for i in range(count)])

    arrived(third)
    step = min(TOKS // 2, toks)
    for t, (hid, dpre) in enumerate(parts):
        out_all, dsec_all = mm(hid, down_ref[...]), mm_nt(dpre, up_ref[...])
        for r in range(0, toks, step):
            rows = slice(t * toks + r, t * toks + r + step)
            span = pl.ds(rows.start, step)
            dy32 = dy_ref[rows, :].astype(F32)
            residual = res_ref[rows, :]
            dsec = dsec_all[r : r + step] + dsec_ref[rows, :]
            dy_ref[rows, :] = (residual + (out_all[r : r + step] + out_ref[rows, :] + bdown_ref[...])).astype(BF)
            unit, inv = unit_parts(residual)
            sums = [jnp.sum(v, axis=0, keepdims=True) for v in (dsec * unit, dsec, dy32)]
            for i, row in enumerate(sums):
                if rows.start:
                    vec_ref[i : i + 1, :] += row
                else:
                    vec_ref[i : i + 1, :] = row
            gres = dy32 + norm_back(dsec, unit, inv, g2_ref[...])
            out_ref[rows, :] = gres
            branch_ref[rows, :] = gres.astype(BF)
            gone += move((dy_ref.at[span, :], block_out.at[span, :]), (out_ref.at[span, :], gres_out.at[span, :]))
    vec_ref[3:, :] = jnp.zeros((vec_ref.shape[0] - 3, width), F32)
    sec_ref[...] = mm_nt(branch_ref[...], wout_ref[...]).astype(BF)
    gone += move((sec_ref, gmix_out))
    dwout_ref[...] = mm_tn(mixed_ref[...], branch_ref[...])
    arrived(gone)
    if mixing:
        own_wait()
        chunk_wait()


def ffn_rest(info, tables, mixing, second, dy, out_part, dsec_part, residual, mixed, bdown, g2, wout, mine, chunks):
    n, width = second.shape
    count = len(chunks)
    units = chunks[0][0].shape[1]
    anywhere = pl.BlockSpec(memory_space=pl.ANY)
    return call(
        functools.partial(ffn_rest_kernel, tables, count, mixing),
        "ffn_rest",
        (1,),
        [anywhere] * 7 + [whole(1, width)] * 2 + [whole(width, width)] + [anywhere] * (2 * count),
        [anywhere] * 3 + [whole(8, width), whole(width, width), whole(count, units)] + [anywhere] * (count + mixing),
        [
            jax.ShapeDtypeStruct((n, width), BF),
            pltpu.HBM((n, width), F32),
            pltpu.HBM((n, width), BF),
            pltpu.HBM((8, width), F32),
            pltpu.HBM((width, width), F32),
            pltpu.HBM((count, units), F32),
        ]
        + [jax.ShapeDtypeStruct((width, 2 * units), BF)] * (count + mixing),
        [
            pltpu.VMEM((n, width), BF),
            pltpu.VMEM((n, width), BF),
            pltpu.VMEM((n, width), F32),
            pltpu.VMEM((n, width), F32),
            pltpu.VMEM((n, width), F32),
            pltpu.VMEM((n, width), BF),
            pltpu.VMEM((n, width), BF),
            pltpu.VMEM((width, count * units), BF),
            pltpu.VMEM((TILE, count * units), BF),
            pltpu.VMEM((count * units, width), BF),
            pltpu.VMEM((count, width, 2 * units), BF),
            pltpu.SemaphoreType.DMA((24 + 4 * count,)),
        ],
        info,
        near(second)
        + far(dy)
        + near(out_part, dsec_part)
        + far(residual, mixed, mine, bdown, g2)
        + (wout,)
        + tuple(c[0] for c in chunks)
        + tuple(c[1] for c in chunks),
        REST_LIMIT if count <= 2 else 56 * 1024 * 1024,
    )


def join_kernel(info_ref, send_ref, got_ref, own_ref, out_ref):
    half = send_ref.shape[0] // 2
    out_ref[half:, :] = (send_ref[half:, :].astype(F32) + got_ref[half:, :].astype(F32)).astype(BF)

    @pl.when(info_ref[0] == 0)
    def _():
        out_ref[:half, :] = (send_ref[:half, :].astype(F32) + got_ref[:half, :].astype(F32)).astype(BF)

    @pl.when(info_ref[0] == 1)
    def _():
        out_ref[:half, :] = (send_ref[:half, :].astype(F32) + own_ref[:half, :].astype(F32)).astype(BF)


def split_kernel(info_ref, keep_ref, got_ref, own_ref, arrived_ref, keep_out, send_out):
    half = keep_ref.shape[0] // 2
    top, low = slice(0, half), slice(half, 2 * half)

    def total(*parts):
        value = parts[0].astype(F32)
        for part in parts[1:]:
            value += part.astype(F32)
        return value.astype(BF)

    @pl.when(info_ref[0] == 0)
    def _():
        keep_out[...] = total(keep_ref[top, :], own_ref[top, :], arrived_ref[top, :])
        send_out[...] = total(keep_ref[low, :], own_ref[low, :], arrived_ref[low, :])

    @pl.when(info_ref[0] == 1)
    def _():
        keep_out[...] = total(keep_ref[low, :], own_ref[low, :], arrived_ref[top, :])
        send_out[...] = total(keep_ref[top, :], got_ref[top, :], arrived_ref[low, :])


def direct(kernel, name, info, out_shape, args):
    return pl.pallas_call(
        kernel,
        in_specs=[pl.BlockSpec(memory_space=pltpu.SMEM)] + [pl.BlockSpec(memory_space=pltpu.VMEM)] * len(args),
        out_specs=jax.tree.map(lambda _: pl.BlockSpec(memory_space=pltpu.VMEM), out_shape),
        out_shape=out_shape,
        compiler_params=pltpu.CompilerParams(vmem_limit_bytes=VMEM_LIMIT),
        cost_estimate=pl.CostEstimate(flops=1000, bytes_accessed=1000, transcendentals=0),
        name=name,
    )(info, *args)


def join(info, send, got, own):
    return direct(join_kernel, "join", info, jax.ShapeDtypeStruct(send.shape, BF), (send, got, own))


def split(info, keep, got, own, arrived):
    shape = jax.ShapeDtypeStruct((keep.shape[0] // 2, keep.shape[1]), BF)
    return direct(split_kernel, "split", info, [shape, shape], (keep, got, own, arrived))


def attend_back_kernel(
    tables, info_ref, qkv_ref, prob_ref, gmix_ref, tok_ref, g1_ref, c1_ref, wqkv_ref, dwout_ref, vec_ref,
    *refs,
):
    *sums, grad_ref, dw_keep_ref, dw_send_ref, dqkv_ref, acc_ref, row_ref = refs
    at, last = pl.program_id(0), pl.num_programs(0) - 1
    toks, width = tok_ref.shape
    rows, pairs, slots, _ = prob_ref.shape

    @pl.when(at == 0)
    def _():
        acc_ref[:, : 3 * width] = jnp.zeros((width, 3 * width), F32)
        acc_ref[:, 3 * width : 4 * width] = dwout_ref[...]
        row_ref[...] = jnp.zeros_like(row_ref)
        row_ref[SUMS : SUMS + vec_ref.shape[0], :] = vec_ref[...]
        if sums:
            own_ref, rest_ref = sums
            first = SUMS + vec_ref.shape[0]
            for i in range(2):
                row_ref[pl.ds(first + 2 * info_ref[5] + i, 1), :] = own_ref[i : i + 1, :]
                row_ref[pl.ds(first + 2 * (info_ref[5] ^ 1) + (info_ref[0] ^ i), 1), :] = rest_ref[i : i + 1, :]

    scale = HEAD ** (-0.5)
    units = [(r, p) for r in range(rows) for p in range(pairs)]

    def place(r, p, which):
        return (slice(r * slots, (r + 1) * slots), slice(which * width + p * PAIR, which * width + (p + 1) * PAIR))

    grads = [gmix_ref[place(r, p, 0)] for r, p in units]
    by_grad = [by_head(g) for g in grads]
    dprobs = [mm_nt(qkv_ref[place(r, p, 2)], g) for (r, p), g in zip(units, by_grad)]
    for (r, p), g in zip(units, by_grad):
        dqkv_ref[place(r, p, 2)] = mm(prob_ref[r, p], g).astype(BF)
    dscores = []
    for (r, p), dprob in zip(units, dprobs):
        p32 = prob_ref[r, p].astype(F32)
        dscores.append((p32 * (dprob - jnp.sum(p32 * dprob, axis=0, keepdims=True))).astype(BF))
    for (r, p), ds in zip(units, dscores):
        q = qkv_ref[place(r, p, 0)]
        dqkv_ref[place(r, p, 1)] = mm(ds, by_head(q * scale)).astype(BF)
    for (r, p), ds in zip(units, dscores):
        k = qkv_ref[place(r, p, 1)]
        stacked = jnp.concatenate([ds[:, :slots], ds[:, slots:]], axis=0)
        dqkv_ref[place(r, p, 0)] = mm_tn(stacked, by_head(k * scale)).astype(BF)
    unit, _ = unit_parts(tok_ref[...].astype(F32))
    acc_ref[:, : 3 * width] += mm_tn(unit.astype(BF), dqkv_ref[...])
    grad_ref[...] = dqkv_ref[...]
    for i in range(3):
        part = dqkv_ref[:, i * width : (i + 1) * width].astype(F32)
        row_ref[i : i + 1, :] += jnp.sum(part, axis=0, keepdims=True)

    @pl.when(at == last)
    def _():
        core, own, other = info_ref[0], info_ref[3], info_ref[4]
        row_ref[5:6, :] = g1_ref[...]
        row_ref[6:7, :] = c1_ref[...]
        wide_row = jnp.concatenate([row_ref[i : i + 1, :] for i in range(3)], axis=1)
        step = width // 4
        for r in range(0, width, step):
            w = wqkv_ref[r : r + step, :].astype(F32)
            sums = acc_ref[r : r + step, : 3 * width]
            d_gain = jnp.sum(w * sums, axis=1, keepdims=True)
            d_bias = jnp.sum(w * wide_row, axis=1, keepdims=True)
            lane = lax.broadcasted_iota(jnp.int32, (step, LANES), 1)
            others = row_ref[:, r : r + step].T
            acc_ref[r : r + step, : 3 * width] = others[:, 5:6] * sums + others[:, 6:7] * wide_row
            acc_ref[r : r + step, 4 * width :] = jnp.where(lane == 3, d_gain, jnp.where(lane == 4, d_bias, others))
        half = width // 2
        size = width // len(tables[0])
        for place in range(len(tables[0])):
            dst = dw_keep_ref if place * size < half else dw_send_ref
            block = block_at(place, tables, core, own if place * size < half else other)
            rows_at = pl.ds(pl.multiple_of(block * size, size), size)
            to = place * size % half
            dst[to : to + size, :] = acc_ref[rows_at, :].astype(BF)


def attend_back(info, tables, qkv, prob, gmix, tokens, g1, c1, wqkv, dwout, *vecs):
    n, width = tokens.shape
    rows, pairs, slots, _ = prob.shape
    per = TOKS // slots
    return call(
        functools.partial(attend_back_kernel, tables),
        "attend_back",
        (n // TOKS,),
        [
            rows_of(3 * width),
            pl.BlockSpec((per, pairs, slots, 2 * slots), lambda i, *_: (i, 0, 0, 0)),
            rows_of(width),
            rows_of(width),
            whole(1, width),
            whole(1, width),
            whole(*wqkv.shape),
            whole(width, width),
        ]
        + [whole(*vec.shape) for vec in vecs],
        [rows_of(3 * width)] + [whole(width // 2, 4 * width + LANES)] * 2,
        [pltpu.VMEM((n, 3 * width), BF)] + [jax.ShapeDtypeStruct((width // 2, 4 * width + LANES), BF)] * 2,
        [
            pltpu.VMEM((TOKS, 3 * width), BF),
            pltpu.VMEM((width, 4 * width + LANES), F32),
            pltpu.VMEM((LANES, width), F32),
        ],
        info,
        far(qkv, prob, gmix, tokens, g1, c1, wqkv, dwout, *vecs),
    )


def first_back_kernel(info_ref, dqkv_ref, wqkv_ref, tok_ref, gres_ref, g1_ref, out_ref):
    dnormed = mm_nt(dqkv_ref[...], wqkv_ref[...])
    unit, inv = unit_parts(tok_ref[...].astype(F32))
    out_ref[...] = gres_ref[...] + norm_back(dnormed, unit, inv, g1_ref[...])


def first_back(info, dqkv, wqkv, tokens, gres, g1):
    n, width = tokens.shape
    return call(
        first_back_kernel,
        "first_back",
        (n // TOKS,),
        [rows_of(3 * width), whole(*wqkv.shape), rows_of(width), rows_of(width), whole(1, width)],
        rows_of(width),
        jax.ShapeDtypeStruct((n, width), F32),
        [],
        info,
        near(dqkv) + (wqkv,) + far(tokens, gres, g1),
    )


def ffn_end_kernel(tables, info_ref, keep_ref, other_ref, up_ref, down_ref, full_ref):
    core = info_ref[0]
    units = up_ref.shape[1]
    blocks = len(tables[0])
    size = keep_ref.shape[0] // blocks

    def lay(src_ref, whose, base):
        for place in range(blocks):
            block = block_at(place, tables, whose, base)
            rows = pl.ds(pl.multiple_of(block * size, size), size)
            part = src_ref[place * size : (place + 1) * size, :].astype(F32)
            up_ref[rows, :] = part[:, :units]
            full_ref[rows, :] = part[:, units:]
        down_ref[...] = full_ref[...].T

    @pl.when(pl.program_id(0) == 0)
    def _():
        lay(keep_ref, core, info_ref[1])

    @pl.when(pl.program_id(0) == 1)
    def _():
        lay(other_ref, core ^ 1, info_ref[2])


def ffn_end(info, tables, keep, other):
    width, double = keep.shape
    units = double // 2
    return call(
        functools.partial(ffn_end_kernel, tables),
        "ffn_end",
        (2,),
        [whole(width, double)] * 2,
        [
            pl.BlockSpec((width, units), lambda i, info: (0, info[0] ^ i)),
            pl.BlockSpec((units, width), lambda i, info: (info[0] ^ i, 0)),
        ],
        [jax.ShapeDtypeStruct((width, double), F32), jax.ShapeDtypeStruct((double, width), F32)],
        [pltpu.VMEM((width, units), F32)],
        info,
        (keep, other),
    )


def attend_end_kernel(tables, which, shares, info_ref, *refs):
    quarters, refs = refs[: 2 + 2 * which], refs[2 + 2 * which + 2 * which :]
    qkv_hbm, out_hbm, *refs = refs
    vec_refs, (qkv_ref, out_ref, *refs, sems) = refs[: 6 * which], refs[6 * which :]
    core = info_ref[0]
    width = out_ref.shape[1]
    blocks = len(tables[0])
    quarter = quarters[0].shape[0]
    size = 4 * quarter // blocks
    spots = []
    for place in range(blocks):
        row = place * size
        side, half = row // (2 * quarter), row // quarter % 2
        block = block_at(place, tables, core, info_ref[3 + side])
        at = row % quarter
        src = quarters[side + 2 * half * which] if half <= which else None
        spots.append((half, src, at, side * quarter + at, pl.multiple_of(block * size, size)))
    copies = []
    for half, src, at, row, to in spots:
        if half != which:
            continue
        here, there = pl.ds(row, size), pl.ds(to, size)
        for ref, hbm, cols in ((qkv_ref, qkv_hbm, slice(0, 3 * width)), (out_ref, out_hbm, slice(3 * width, 4 * width))):
            ref[row : row + size, :] = src[at : at + size, cols].astype(F32)
            copies.append(pltpu.make_async_copy(ref.at[here, :], hbm.at[there, :], sems.at[len(copies)]))
            copies[-1].start()
    if which:
        col_ref, row_ref = refs
        for half, src, at, _, to in spots:
            cols = slice(4 * width, None) if half else slice(None)
            col_ref[pl.ds(to, size), :] = src[at : at + size, cols].astype(F32)
        vec = col_ref[...].T
        row_ref[...] = vec
        flat = lambda row: row.reshape(row.shape[1])
        for i, at in enumerate((3, 4, SUMS, SUMS + 1, SUMS + 2)):
            vec_refs[i][...] = flat(vec[at : at + 1, :])
        units = vec_refs[5].shape[0]
        if units >= width:
            first = SUMS + 8 + info_ref[5] * (units // width)
            for i in range(units // width):
                vec_refs[5][i * width : (i + 1) * width] = flat(row_ref[pl.ds(first + i, 1), :])
        else:
            row = row_ref[pl.ds(SUMS + 8 + info_ref[5] // shares, 1), :]
            share = row[:, :units]
            for i in range(1, shares):
                share = jnp.where(info_ref[5] % shares == i, row[:, i * units : (i + 1) * units], share)
            vec_refs[5][...] = flat(share)
    for copy in copies:
        copy.wait()


def attend_end(info, tables, quarters, width, units, written=()):
    rows = 4 * quarters[0].shape[0]
    which = 1 if written else 0
    anywhere = pl.BlockSpec(memory_space=pl.ANY)
    return call(
        functools.partial(attend_end_kernel, tables, which, max(1, width // units)),
        "attend_end",
        (1,),
        [pl.BlockSpec((rows // 4, LANES), lambda *_: (0, 4 * width // LANES))] * (2 * which)
        + [whole(*quarters[0].shape)] * 2
        + [anywhere] * len(written),
        [anywhere] * 2 + ([whole(width)] * 5 + [whole(units)]) * which,
        [jax.ShapeDtypeStruct((rows, 3 * width), F32), jax.ShapeDtypeStruct((rows, width), F32)]
        + ([jax.ShapeDtypeStruct((width,), F32)] * 5 + [jax.ShapeDtypeStruct((units,), F32)]) * which,
        [pltpu.VMEM((rows // 2, 3 * width), F32), pltpu.VMEM((rows // 2, width), F32)]
        + [pltpu.VMEM((rows, LANES), F32), pltpu.VMEM((LANES, width), F32)] * which
        + [pltpu.SemaphoreType.DMA((len(tables[0]),))],
        info,
        (*quarters, *written),
        aliases=[(1 + len(quarters) + i, i) for i in range(len(written))],
    )


def local(
    wide, narrow, tokens_in, ln1_gain, ln1_bias, w_qkv, w_out, ln2_gain, ln2_bias, w_up, b_up, w_down, b_down, segment_ids,
    step_ids, pad_mask, cotangent,
):
    width = tokens_in.shape[1]
    units = w_up.shape[1] // 2
    core_mask = narrow
    narrow_masks = [1 << b for b in range(narrow.bit_length() - 1)]
    wide_masks = [narrow << b for b in range(1, wide.bit_length() - 1)]

    def swap(value, first, second=None):
        masks = (first, first if second is None else second)
        pairs = [(i, i ^ masks[i // narrow & 1]) for i in range(wide * narrow)]
        return lax.ppermute(value, AXES, pairs)

    def add(a, b):
        return (a.astype(F32) + b.astype(F32)).astype(a.dtype)

    def after(*values):
        return lax.optimization_barrier(values)

    def steps_of(halved, exchanged, gathered):
        pairs = lambda order: list(zip(*order))
        return (
            [("halve", *pair) for pair in pairs(halved)]
            + [("exchange", *pair) for pair in pairs(exchanged)]
            + [("gather", *pair) for pair in reversed(pairs(gathered))]
        )

    def start(value, step):
        kind, *masks = step
        if kind == "halve":
            half = value.shape[0] // 2
            return value[:half], swap(value[half:], *masks)
        return value, swap(value, *masks)

    def finish(kept, got, step):
        if step[0] == "gather":
            return jnp.concatenate([kept, got], axis=0)
        return add(kept, got) if step[0] in ("halve", "exchange") else (kept, got)

    wide_at, narrow_at = lax.axis_index("wide"), lax.axis_index("narrow")
    core = wide_at & 1
    flat = wide_at * narrow + narrow_at

    def named(owner, used):
        return sum((1 << b) for b, m in enumerate(used) if owner & m)

    def block_of(used):
        return sum(((flat & m) != 0).astype(jnp.int32) << b for b, m in enumerate(used))

    def split_at(pair, count):
        return tuple(o[:count] for o in pair), tuple(o[count:] for o in pair)

    def by_core(values):
        return jnp.where(core == 0, values[0], values[1]), jnp.where(core == 0, values[1], values[0])

    mixing = narrow == 2 and len(wide_masks) == 3
    if mixing:
        y, low, high = wide_masks
        ff_in, ff_rest, ff_out = ([y, low], [y, low]), ([high], [high]), ([low, y], [low, y])
        at_in, at_rest, at_out = ([y, 1, low], [low, y, 1]), ([high], [high]), ([y, 1, low], [low, 1, y])
        turns = "FAFAAFAFAAFFAA"
    else:
        ff_in, ff_rest = split_at((wide_masks, wide_masks), min(len(wide_masks) - 1, (width // TILE).bit_length() - 1))
        masks = narrow_masks + wide_masks
        at_in, at_rest = split_at((masks, masks), min(len(masks) - 1, (width // TILE // 2).bit_length() - 1))
        ff_out, at_out, turns = ff_in, at_in, ""
    ff_used = tuple(sorted(o) for o in ff_in)
    ff_in_tables, ff_out_tables = (
        tuple([named(owner, ff_used[c]) for owner in places(pair[c], 1 << len(ff_used[c]))] for c in range(2))
        for pair in (ff_in, ff_out)
    )
    at_used = tuple([core_mask] + sorted(o) for o in at_in)

    def at_tables(order):
        owners = [places(o, 1 << len(o)) for o in order]
        return tuple(
            [named(o, at_used[c]) for o in owners[c]] + [named(o ^ core_mask, at_used[1 - c]) for o in owners[1 - c]]
            for c in range(2)
        )

    ff_block = by_core([block_of(used) for used in ff_used])
    at_block = by_core([block_of(used) for used in at_used])
    info = jnp.stack([core, *ff_block, *at_block, narrow_at]).astype(jnp.int32)

    packed, tokens_in = after(pack(info, w_up, b_up, w_down), tokens_in)
    fetched = [packed]
    for mask in narrow_masks:
        fetched = fetched + [(swap(u, mask), swap(d, mask)) for u, d in fetched]

    row = lambda v: v[None].astype(F32)
    g1, c1, g2 = row(ln1_gain), row(ln1_bias), row(ln2_gain)
    qkv, prob, mixed, residual, second = attend(
        info, tokens_in, g1, c1, w_qkv, w_out, g2, row(ln2_bias), segment_ids, step_ids, pad_mask
    )
    out_part, dsec_part, own_keep, own_send, bias_own = ffn_own(
        info, ff_in_tables, mixing, second, cotangent, w_up, b_up, w_down
    )
    ups, downs = [u for u, _ in fetched[1:]], [d for _, d in fetched[1:]]
    own_send, ups = after(own_send, ups)
    away_ups = [swap(u, core_mask) for u in ups]
    away_downs = [swap(d, core_mask) for d in downs]
    chunks = [pair for here in zip(zip(ups, downs), zip(away_ups, away_downs)) for pair in here]
    rest = ffn_rest(
        info, ff_in_tables, mixing, second, cotangent, out_part, dsec_part, residual, mixed, row(b_down), g2, w_out, own_keep,
        chunks,
    )
    block_out, gres, gmix, vec, dwout, bias_rest = rest[:6]
    grads = rest[6:]

    if narrow == 2 and units == width:
        vecs = (vec, bias_own, bias_rest)
    else:
        b_rest = bias_rest.reshape(-1, 2, units)
        b_rest = jnp.where(core == 0, b_rest, jnp.flip(b_rest, axis=1))
        b_all = jnp.concatenate([bias_own[None], b_rest], axis=0)
        for bit in range(narrow.bit_length() - 1):
            flipped = jnp.flip(b_all.reshape(-1, 2, (1 << bit) * 2, units), axis=1).reshape(b_all.shape)
            b_all = jnp.where(narrow_at >> bit & 1, flipped, b_all)
        vecs = (jnp.concatenate([vec, b_all.reshape(-1, width)], axis=0),)

    if mixing:
        ff_keep, ff_send, away = grads
        got_own, got = swap(own_send, core_mask), swap(away, core_mask)
        ff_send = join(info, ff_send, got, got_own)
        gmix, ff_send = after(gmix, ff_send)
        ff_got = swap(ff_send, 1, y)
    else:
        held = [add(own_keep, swap(own_send, core_mask))] + [add(grads[2 * j], swap(grads[2 * j + 1], core_mask)) for j in range(narrow - 1)]
        gmix, held = after(gmix, held)
        for mask in reversed(narrow_masks):
            held = [add(held[j], swap(held[j + mask], mask)) for j in range(mask)]
        ff_keep = held[0]

    dqkv, keep, send = attend_back(info, at_tables(at_in), qkv, prob, gmix, tokens_in, g1, c1, w_qkv, dwout, *vecs)
    if mixing:
        send, ff_got = after(send, ff_got)
        ff_keep, ff_send = split(info, ff_keep, got, got_own, ff_got)
    keep = add(keep, swap(send, core_mask))
    grad_tokens = first_back(info, dqkv, w_qkv, tokens_in, gres, g1)
    steps = {
        "A": steps_of(at_in, at_rest, at_out)[:-1] + [("last", *steps_of(at_in, at_rest, at_out)[-1][1:]), ("core", core_mask)],
        "F": steps_of(ff_in, ff_rest, ff_out) + [("core", core_mask)],
    }
    if mixing:
        steps["F"] = [("halve", y, 1)] + steps["F"][1:]
        first = (ff_keep, swap(ff_send, y, 1))
    else:
        first = start(ff_keep, steps["F"][0])
    turns = turns or "".join(a + f for a, f in itertools.zip_longest("A" * len(steps["A"]), "F" * len(steps["F"]), fillvalue=""))
    under_way = {"A": start(keep, steps["A"][0]), "F": first}
    done, beside = (), ()
    for at_turn, turn in enumerate(turns):
        other = "A" if turn == "F" else "F"
        kept, got = under_way.pop(turn)
        if at_turn == 1:
            beside = (grad_tokens,)
        if other in under_way:
            other_kept, other_got = under_way[other]
            kept, other_kept, *beside = after(kept, other_kept, *beside)
            under_way[other] = other_kept, other_got
        else:
            kept, *beside = after(kept, *beside)
        if len(beside) == 1:
            (grad_tokens,), beside = beside, ()
        elif beside:
            (grad_w_up, grad_w_down), beside = beside, ()
        step, *steps[turn] = steps[turn]
        if step[0] == "last":
            written = attend_end(info, at_tables(at_out), (kept, crossed), width, 2 * units)
            got, written = after(got, written)
        value = finish(kept, got, step)
        if step[0] == "last":
            under_way[turn] = value, swap(got, core_mask)
        elif steps[turn]:
            under_way[turn] = start(value, steps[turn][0])
            if steps[turn][0][0] == "last":
                crossed = swap(value, core_mask)
        elif turn == "F":
            beside = ffn_end(info, ff_out_tables, *value)
        else:
            done = (value[0][0], crossed, value[0][1], value[1])
    grad_w_qkv, grad_w_out, d_gain1, d_bias1, d_gain2, d_bias2, d_bdown, grad_b_up = attend_end(
        info, at_tables(at_out), done, width, 2 * units, written
    )
    return (
        block_out, grad_tokens, d_gain1, d_bias1, grad_w_qkv, grad_w_out, d_gain2, d_bias2, grad_w_up, grad_b_up, grad_w_down,
        d_bdown,
    )


def solution(mesh):
    rows = P(("wide", "narrow"), None)
    in_specs = (
        rows, P(), P(), P(), P(), P(), P(), P(None, "narrow"), P("narrow"), P("narrow", None), P(), rows, rows, rows, rows,
    )
    out_specs = (
        rows, rows, P(), P(), P(), P(), P(), P(), P(None, "narrow"), P("narrow"), P("narrow", None), P(),
    )
    wide, narrow = mesh.shape["wide"], mesh.shape["narrow"]
    return jax.shard_map(
        functools.partial(local, wide, narrow), mesh=mesh, in_specs=in_specs, out_specs=out_specs, check_vma=False
    )
```

```python
import functools
import itertools

import jax
import jax.numpy as jnp
import numpy as np
from jax import lax
from jax.experimental import pallas as pl
from jax.experimental.pallas import tpu as pltpu
from jax.sharding import PartitionSpec as P

HEAD = 64
PAIR = 2 * HEAD
NORM_EPS = 1e-05
BF = jnp.bfloat16
F32 = jnp.float32
AXES = ("wide", "narrow")
LANES = 128
SUMS = 8
TILE = 16
TOKS = 512
VMEM_LIMIT = 30 * 1024 * 1024
REST_LIMIT = 36 * 1024 * 1024


def mm(a, b):
    return lax.dot_general(a, b, (((1,), (0,)), ((), ())), preferred_element_type=F32)


def mm_nt(a, b):
    return lax.dot_general(a, b, (((1,), (1,)), ((), ())), preferred_element_type=F32)


def mm_tn(a, b):
    return lax.dot_general(a, b, (((0,), (0,)), ((), ())), preferred_element_type=F32)


def near(*values):
    return tuple(pltpu.with_memory_space_constraint(v, pltpu.VMEM) for v in values)


def far(*values):
    return tuple(pltpu.with_memory_space_constraint(v, pltpu.HBM) for v in values)


def whole(*shape):
    return pl.BlockSpec(shape, lambda *_: (0,) * len(shape))


def rows_of(width, toks=TOKS):
    return pl.BlockSpec((toks, width), lambda i, *_: (i, 0))


def call(kernel, name, grid, in_specs, out_specs, out_shape, scratch, info, args, vmem=VMEM_LIMIT, aliases=()):
    return pl.pallas_call(
        kernel,
        grid_spec=pltpu.PrefetchScalarGridSpec(
            num_scalar_prefetch=1, grid=grid, in_specs=in_specs, out_specs=out_specs, scratch_shapes=scratch
        ),
        out_shape=out_shape,
        input_output_aliases=dict(aliases),
        compiler_params=pltpu.CompilerParams(vmem_limit_bytes=vmem),
        cost_estimate=pl.CostEstimate(flops=1000, bytes_accessed=1000, transcendentals=0),
        name=name,
    )(info, *args)


def unit_parts(rows):
    mean = jnp.mean(rows, axis=-1, keepdims=True)
    centered = rows - mean
    inv = lax.rsqrt(jnp.mean(centered * centered, axis=-1, keepdims=True) + NORM_EPS)
    return centered * inv, inv


def norm_back(incoming, unit, inv, gain):
    scaled = incoming * gain
    return inv * (
        scaled
        - jnp.mean(scaled, axis=-1, keepdims=True)
        - unit * jnp.mean(scaled * unit, axis=-1, keepdims=True)
    )


def gelu_pair(x):
    cdf = 0.5 * (1.0 + lax.erf(x * 0.7071067811865476))
    return x * cdf, cdf + x * jnp.exp(-0.5 * x * x) * 0.3989422804014327


def by_head(block):
    lane = lax.broadcasted_iota(jnp.int32, block.shape, 1)
    zero = jnp.zeros_like(block)
    first = lane < HEAD
    return jnp.concatenate([jnp.where(first, block, zero), jnp.where(first, zero, block)], axis=0)


def places(order, blocks):
    bits = blocks.bit_length() - 1
    table = []
    for place in range(blocks):
        owner = 0
        for step in range(bits):
            if place >> (bits - 1 - step) & 1:
                owner ^= order[step]
        table.append(owner)
    return table


def block_at(place, tables, core, own):
    first, second = tables[0][place], tables[1][place]
    if first == second:
        return own ^ first
    return own ^ jnp.where(core == 0, first, second)


def place_of(block, tables, core, own):
    wanted = own ^ block
    places_by_core = [[table.index(owner) for owner in range(len(table))] for table in tables]
    place = jnp.int32(0)
    for owner in range(len(tables[0])):
        first, second = places_by_core[0][owner], places_by_core[1][owner]
        place = jnp.where(wanted == owner, jnp.where(core == 0, first, second), place)
    return place


def permuted(dst_ref, acc_ref, chunk, tables, core, own, turned=0):
    blocks = len(tables[0])
    size = dst_ref.shape[0] // blocks
    for place in range(blocks):
        block = block_at(place, tables, core, own)
        rows = pl.ds(pl.multiple_of(block * size, size), size)
        to = pl.ds(pl.multiple_of(((place + turned * (blocks // 2)) & (blocks - 1)) * size, size), size)
        dst_ref[to, :] = acc_ref[chunk, rows, :].astype(dst_ref.dtype)


def attend_kernel(
    info_ref, tok_ref, g1_ref, c1_ref, wqkv_ref, wout_ref, g2_ref, c2_ref, seg_ref, step_ref, pad_ref,
    qkv_ref, prob_ref, mixed_ref, res_ref, second_ref,
):
    slots = seg_ref.shape[1]
    toks, width = tok_ref.shape
    rows = toks // slots
    at = pl.program_id(0)
    tokens = tok_ref[...].astype(F32)
    unit, _ = unit_parts(tokens)
    normed = (unit * g1_ref[...] + c1_ref[...]).astype(BF)
    qkv_ref[...] = mm(normed, wqkv_ref[...]).astype(BF)
    q_id = lax.broadcasted_iota(jnp.int32, (slots, slots), 0)
    k_id = lax.broadcasted_iota(jnp.int32, (slots, slots), 1)
    eye = q_id == k_id
    pairs = width // PAIR
    units = [(r, p) for r in range(rows) for p in range(pairs)]

    def part(r, p, which):
        return qkv_ref[r * slots : (r + 1) * slots, which * width + p * PAIR : which * width + (p + 1) * PAIR]

    masks = []
    for r in range(rows):
        here = pl.ds(at * rows + r, 1)
        seg = jnp.broadcast_to(seg_ref[here, :].astype(F32), (slots, slots))
        step = jnp.broadcast_to(step_ref[here, :].astype(F32), (slots, slots))
        live = jnp.broadcast_to(pad_ref[here, :].astype(F32), (slots, slots)).T == 0
        masks.append(((seg == seg.T) & (step.T <= step) & live) | eye)
    scores = [mm_nt(part(r, p, 1), by_head(part(r, p, 0) * HEAD ** (-0.5))) for r, p in units]
    probs = []
    for (r, p), score in zip(units, scores):
        halves = []
        for half in (score[:, :slots], score[:, slots:]):
            half = jnp.where(masks[r], half, -1e30)
            weight = jnp.exp(half - jnp.max(half, axis=0, keepdims=True))
            total = jnp.sum(weight, axis=0, keepdims=True)
            halves.append((weight * (1.0 / total)).astype(BF))
        probs.append(halves)
    for (r, p), halves in zip(units, probs):
        prob_ref[r, p] = jnp.concatenate(halves, axis=1)
        mixed = mm_tn(jnp.concatenate(halves, axis=0), by_head(part(r, p, 2)))
        mixed_ref[r * slots : (r + 1) * slots, p * PAIR : (p + 1) * PAIR] = mixed.astype(BF)
    residual = tokens + mm(mixed_ref[...], wout_ref[...])
    res_ref[...] = residual
    unit, _ = unit_parts(residual)
    second_ref[...] = (unit * g2_ref[...] + c2_ref[...]).astype(BF)


def attend(info, tokens, g1, c1, wqkv, wout, g2, c2, seg, step, pad):
    n, width = tokens.shape
    rows, slots = seg.shape
    per, pairs = TOKS // slots, width // PAIR
    return call(
        attend_kernel,
        "attend",
        (n // TOKS,),
        [rows_of(width), whole(1, width), whole(1, width), whole(*wqkv.shape), whole(*wout.shape)]
        + [whole(1, width)] * 2
        + [whole(rows, slots)] * 3,
        [
            rows_of(3 * width),
            pl.BlockSpec((per, pairs, slots, 2 * slots), lambda i, *_: (i, 0, 0, 0)),
            rows_of(width),
            rows_of(width),
            rows_of(width),
        ],
        [
            pltpu.HBM((n, 3 * width), BF),
            pltpu.HBM((rows, pairs, slots, 2 * slots), BF),
            pltpu.HBM((n, width), BF),
            pltpu.HBM((n, width), F32),
            pltpu.VMEM((n, width), BF),
        ],
        [],
        info,
        far(tokens, g1, c1) + (wqkv, wout) + far(g2, c2, seg, step, pad),
    )


def pack_kernel(info_ref, up_ref, bias_ref, down_ref, up_out, down_out):
    width = up_ref.shape[0]
    up_out[:width, :] = up_ref[...]
    units = up_ref.shape[1]
    bias = bias_ref[...].reshape(1, 2 * units)
    bias = jnp.where(info_ref[0] == 0, bias[:, :units], bias[:, units:])
    up_out[width:, :] = jnp.broadcast_to(bias, (TILE, units))
    down_out[...] = down_ref[...]


def pack(info, up, bias, down):
    width, units = up.shape[0], up.shape[1] // 2
    return call(
        pack_kernel,
        "pack",
        (1,),
        [
            pl.BlockSpec((width, units), lambda t, info: (0, info[0])),
            whole(2 * units),
            pl.BlockSpec((units, width), lambda t, info: (info[0], 0)),
        ],
        [whole(width + TILE, units), whole(units, width)],
        [jax.ShapeDtypeStruct((width + TILE, units), BF), jax.ShapeDtypeStruct((units, width), BF)],
        [],
        info,
        far(up, bias, down),
    )


def ffn_block(sec, dy, up, bias, down, acc_ref, bacc_ref):
    pre = mm(sec, up) + bias
    dhid = mm_nt(dy, down)
    hid, slope = gelu_pair(pre)
    hid = hid.astype(BF)
    dpre = (dhid * slope).astype(BF)
    grad_up = mm(sec.T, dpre)
    grad_down = mm(dy.T, hid)
    sums = jnp.sum(dpre.astype(F32), axis=0, keepdims=True)
    chunks, _, double = acc_ref.shape
    units = double // 2
    for i in range(chunks):
        cols = slice(i * units, (i + 1) * units)
        acc_ref[i, :, :units] += grad_up[:, cols]
        acc_ref[i, :, units:] += grad_down[:, cols]
        bacc_ref[i : i + 1, :] += sums[:, cols]
    return hid, dpre


def ffn_own_kernel(
    tables, mixing, info_ref, sec_ref, dy_ref, up_ref, bias_ref, down_ref, out_ref, dsec_ref, keep_ref, send_ref, bias_out,
    acc_ref,
):
    at, last = pl.program_id(0), pl.num_programs(0) - 1

    @pl.when(at == 0)
    def _():
        acc_ref[...] = jnp.zeros_like(acc_ref)
        bias_out[...] = jnp.zeros_like(bias_out)

    bias = bias_ref[...].astype(F32).reshape(1, up_ref.shape[1])
    hid, dpre = ffn_block(sec_ref[...], dy_ref[...], up_ref[...], bias, down_ref[...], acc_ref, bias_out)
    out_ref[...] = mm(hid, down_ref[...])
    dsec_ref[...] = mm_nt(dpre, up_ref[...])

    @pl.when(at == last)
    def _():
        core, own, other = info_ref[0], info_ref[1], info_ref[2]
        permuted(keep_ref, acc_ref, core, tables, core, own)
        permuted(send_ref, acc_ref, core ^ 1, tables, core ^ 1, other, core ^ 1 if mixing else 0)


def ffn_own(info, tables, mixing, second, dy, up, bias, down):
    n, width = second.shape
    units = up.shape[1] // 2
    return call(
        functools.partial(ffn_own_kernel, tables, mixing),
        "ffn_own",
        (n // TOKS,),
        [rows_of(width), rows_of(width), whole(*up.shape), whole(*bias.shape), whole(*down.shape)],
        [rows_of(width)] * 2 + [whole(width, 2 * units)] * 2 + [whole(2, units)],
        [pltpu.VMEM((n, width), F32)] * 2
        + [pltpu.HBM((width, 2 * units), BF)] * 2
        + [pltpu.HBM((2, units), F32)],
        [pltpu.VMEM((2, width, 2 * units), F32)],
        info,
        near(second) + far(dy) + (up,) + far(bias) + (down,),
    )


def ffn_rest_kernel(
    tables, count, mixing, info_ref, sec_in, dy_in, out_in, dsec_in, res_in, mine_ref, bdown_ref, g2_ref, wout_ref, *refs
):
    ups, downs = refs[:count], refs[count : 2 * count]
    block_out, gres_out, gmix_out, branch_out, vec_ref, bias_out = refs[2 * count : 2 * count + 6]
    grads, refs = refs[2 * count + 6 : 3 * count + 6 + mixing], refs[3 * count + 6 + mixing :]
    sec_ref, dy_ref, out_ref, dsec_ref, res_ref, branch_ref, up_ref, bias_ref, down_ref, laid_ref, sems = refs
    n, width = sec_ref.shape
    units = down_ref.shape[0] // count
    core = info_ref[0]
    half = width // 2
    top, low = pl.ds(0, half), pl.ds(half, half)
    used = iter(range(sems.shape[0]))

    def move(*pairs):
        copies = [pltpu.make_async_copy(*pair, sems.at[next(used)]) for pair in pairs]
        for copy in copies:
            copy.start()
        return copies

    def arrived(copies):
        for copy in copies:
            copy.wait()

    def by_core(first, *sets):
        def each(act):
            for odd, pairs in enumerate(sets):

                @pl.when(core == odd)
                def _(pairs=pairs):
                    for i, pair in enumerate(pairs):
                        act(pltpu.make_async_copy(*pair, sems.at[first + i]))

        return lambda: each(lambda copy: copy.start()), lambda: each(lambda copy: copy.wait())

    cols = [pl.ds(i * units, units) for i in range(count)]
    first = move(
        (sec_in, sec_ref),
        *[(ups[i].at[pl.ds(0, width), :], up_ref.at[:, cols[i]]) for i in range(count)],
        *[(ups[i].at[pl.ds(width, TILE), :], bias_ref.at[:, cols[i]]) for i in range(count)],
    )
    second = move((dy_in, dy_ref), *[(downs[i], down_ref.at[cols[i], :]) for i in range(count)])
    third = move((out_in, out_ref), (dsec_in, dsec_ref), (res_in, res_ref))
    if mixing:
        keep_ref, send_ref, away_ref = grads
        own_start, own_wait = by_core(
            next(used),
            [(mine_ref, keep_ref)],
            [(mine_ref.at[top], keep_ref.at[low]), (mine_ref.at[low], send_ref.at[top])],
        )
        next(used)
        chunk_start, chunk_wait = by_core(
            next(used),
            [(laid_ref.at[0], send_ref)],
            [(laid_ref.at[0, top], keep_ref.at[top]), (laid_ref.at[0, low], send_ref.at[low])],
        )
        next(used)
        own_start()

    arrived(first)
    toks = n if count <= 2 else n // 2
    grad_up = grad_down = sums = None
    parts = []
    for t in range(n // toks):
        rows = slice(t * toks, (t + 1) * toks)
        sec = sec_ref[rows, :]
        every = up_ref.shape[1]
        parts_of = [slice(c * every // 2, (c + 1) * every // 2) for c in range(2)]
        pres = [mm(sec, up_ref[:, c]) + bias_ref[:, c].astype(F32)[:1] for c in parts_of]
        if t == 0:
            arrived(second)
        dy = dy_ref[rows, :]
        dhids = [mm_nt(dy, down_ref[c, :]) for c in parts_of]
        hids, dpres, grads_up, grads_down = [], [], [], []
        sec_t, dy_t = sec.T, dy.T
        for pre, dhid in zip(pres, dhids):
            hid, slope = gelu_pair(pre)
            hids.append(hid.astype(BF))
            dpres.append((dhid * slope).astype(BF))
            grads_up.append(mm(sec_t, dpres[-1]))
            grads_down.append(mm(dy_t, hids[-1]))
        hid, dpre = jnp.concatenate(hids, axis=1), jnp.concatenate(dpres, axis=1)
        more = (jnp.concatenate(grads_up, axis=1), jnp.concatenate(grads_down, axis=1), jnp.sum(dpre.astype(F32), axis=0, keepdims=True))
        if t:
            more = (grad_up + more[0], grad_down + more[1], sums + more[2])
        grad_up, grad_down, sums = more
        parts.append((hid, dpre))
    blocks = len(tables[0])
    size = width // blocks
    for i in range(count):
        at = slice(i * units, (i + 1) * units)
        bias_out[i : i + 1, :] = sums[:, at]
        for block in range(blocks):
            owner = core ^ (i % 2)
            place = place_of(block, tables, owner, info_ref[1 + i % 2])
            to = pl.ds(pl.multiple_of(place * size, size), size)
            rows = slice(block * size, (block + 1) * size)
            laid_ref[i, to, :units] = grad_up[rows, at].astype(BF)
            laid_ref[i, to, units:] = grad_down[rows, at].astype(BF)
    if mixing:
        chunk_start()
        gone = move((laid_ref.at[1], away_ref))
    else:
        gone = move(*[(laid_ref.at[i], grads[i]) for i in range(count)])

    arrived(third)
    step = min(TOKS // 2, toks)
    for t, (hid, dpre) in enumerate(parts):
        out_all, dsec_all = mm(hid, down_ref[...]), mm_nt(dpre, up_ref[...])
        for r in range(0, toks, step):
            rows = slice(t * toks + r, t * toks + r + step)
            span = pl.ds(rows.start, step)
            dy32 = dy_ref[rows, :].astype(F32)
            residual = res_ref[rows, :]
            dsec = dsec_all[r : r + step] + dsec_ref[rows, :]
            dy_ref[rows, :] = (residual + (out_all[r : r + step] + out_ref[rows, :] + bdown_ref[...])).astype(BF)
            unit, inv = unit_parts(residual)
            sums = [jnp.sum(v, axis=0, keepdims=True) for v in (dsec * unit, dsec, dy32)]
            for i, row in enumerate(sums):
                if rows.start:
                    vec_ref[i : i + 1, :] += row
                else:
                    vec_ref[i : i + 1, :] = row
            gres = dy32 + norm_back(dsec, unit, inv, g2_ref[...])
            out_ref[rows, :] = gres
            branch_ref[rows, :] = gres.astype(BF)
            gone += move((dy_ref.at[span, :], block_out.at[span, :]), (out_ref.at[span, :], gres_out.at[span, :]))
    vec_ref[3:, :] = jnp.zeros((vec_ref.shape[0] - 3, width), F32)
    gone += move((branch_ref, branch_out))
    sec_ref[...] = mm_nt(branch_ref[...], wout_ref[...]).astype(BF)
    gone += move((sec_ref, gmix_out))
    arrived(gone)
    if mixing:
        own_wait()
        chunk_wait()


def ffn_rest(info, tables, mixing, second, dy, out_part, dsec_part, residual, bdown, g2, wout, mine, chunks):
    n, width = second.shape
    count = len(chunks)
    units = chunks[0][0].shape[1]
    anywhere = pl.BlockSpec(memory_space=pl.ANY)
    return call(
        functools.partial(ffn_rest_kernel, tables, count, mixing),
        "ffn_rest",
        (1,),
        [anywhere] * 6 + [whole(1, width)] * 2 + [whole(width, width)] + [anywhere] * (2 * count),
        [anywhere] * 4 + [whole(8, width), whole(count, units)] + [anywhere] * (count + mixing),
        [
            jax.ShapeDtypeStruct((n, width), BF),
            pltpu.HBM((n, width), F32),
            pltpu.HBM((n, width), BF),
            pltpu.HBM((n, width), BF),
            pltpu.HBM((8, width), F32),
            pltpu.HBM((count, units), F32),
        ]
        + [jax.ShapeDtypeStruct((width, 2 * units), BF)] * (count + mixing),
        [
            pltpu.VMEM((n, width), BF),
            pltpu.VMEM((n, width), BF),
            pltpu.VMEM((n, width), F32),
            pltpu.VMEM((n, width), F32),
            pltpu.VMEM((n, width), F32),
            pltpu.VMEM((n, width), BF),
            pltpu.VMEM((width, count * units), BF),
            pltpu.VMEM((TILE, count * units), BF),
            pltpu.VMEM((count * units, width), BF),
            pltpu.VMEM((count, width, 2 * units), BF),
            pltpu.SemaphoreType.DMA((24 + 4 * count,)),
        ],
        info,
        near(second)
        + far(dy)
        + near(out_part, dsec_part)
        + far(residual, mine, bdown, g2)
        + (wout,)
        + tuple(c[0] for c in chunks)
        + tuple(c[1] for c in chunks),
        REST_LIMIT if count <= 2 else 56 * 1024 * 1024,
    )


def join_kernel(info_ref, send_ref, got_ref, own_ref, out_ref):
    half = send_ref.shape[0] // 2
    out_ref[half:, :] = (send_ref[half:, :].astype(F32) + got_ref[half:, :].astype(F32)).astype(BF)

    @pl.when(info_ref[0] == 0)
    def _():
        out_ref[:half, :] = (send_ref[:half, :].astype(F32) + got_ref[:half, :].astype(F32)).astype(BF)

    @pl.when(info_ref[0] == 1)
    def _():
        out_ref[:half, :] = (send_ref[:half, :].astype(F32) + own_ref[:half, :].astype(F32)).astype(BF)


def split_kernel(info_ref, keep_ref, got_ref, own_ref, arrived_ref, keep_out, send_out):
    half = keep_ref.shape[0] // 2
    top, low = slice(0, half), slice(half, 2 * half)

    def total(*parts):
        value = parts[0].astype(F32)
        for part in parts[1:]:
            value += part.astype(F32)
        return value.astype(BF)

    @pl.when(info_ref[0] == 0)
    def _():
        keep_out[...] = total(keep_ref[top, :], own_ref[top, :], arrived_ref[top, :])
        send_out[...] = total(keep_ref[low, :], own_ref[low, :], arrived_ref[low, :])

    @pl.when(info_ref[0] == 1)
    def _():
        keep_out[...] = total(keep_ref[low, :], own_ref[low, :], arrived_ref[top, :])
        send_out[...] = total(keep_ref[top, :], got_ref[top, :], arrived_ref[low, :])


def direct(kernel, name, info, out_shape, args):
    return pl.pallas_call(
        kernel,
        in_specs=[pl.BlockSpec(memory_space=pltpu.SMEM)] + [pl.BlockSpec(memory_space=pltpu.VMEM)] * len(args),
        out_specs=jax.tree.map(lambda _: pl.BlockSpec(memory_space=pltpu.VMEM), out_shape),
        out_shape=out_shape,
        compiler_params=pltpu.CompilerParams(vmem_limit_bytes=VMEM_LIMIT),
        cost_estimate=pl.CostEstimate(flops=1000, bytes_accessed=1000, transcendentals=0),
        name=name,
    )(info, *args)


def join(info, send, got, own):
    return direct(join_kernel, "join", info, jax.ShapeDtypeStruct(send.shape, BF), (send, got, own))


def split(info, keep, got, own, arrived):
    shape = jax.ShapeDtypeStruct((keep.shape[0] // 2, keep.shape[1]), BF)
    return direct(split_kernel, "split", info, [shape, shape], (keep, got, own, arrived))


def attend_back_kernel(
    tables, info_ref, qkv_ref, prob_ref, gmix_ref, tok_ref, mixed_ref, branch_ref, g1_ref, c1_ref, wqkv_ref, vec_ref,
    *refs,
):
    *sums, grad_ref, dw_keep_ref, dw_send_ref, dqkv_ref, acc_ref, row_ref = refs
    at, last = pl.program_id(0), pl.num_programs(0) - 1
    toks, width = tok_ref.shape
    rows, pairs, slots, _ = prob_ref.shape

    @pl.when(at == 0)
    def _():
        acc_ref[:, : 4 * width] = jnp.zeros((width, 4 * width), F32)
        row_ref[...] = jnp.zeros_like(row_ref)
        row_ref[SUMS : SUMS + vec_ref.shape[0], :] = vec_ref[...]
        if sums:
            own_ref, rest_ref = sums
            first = SUMS + vec_ref.shape[0]
            for i in range(2):
                row_ref[pl.ds(first + 2 * info_ref[5] + i, 1), :] = own_ref[i : i + 1, :]
                row_ref[pl.ds(first + 2 * (info_ref[5] ^ 1) + (info_ref[0] ^ i), 1), :] = rest_ref[i : i + 1, :]

    scale = HEAD ** (-0.5)
    units = [(r, p) for r in range(rows) for p in range(pairs)]

    def place(r, p, which):
        return (slice(r * slots, (r + 1) * slots), slice(which * width + p * PAIR, which * width + (p + 1) * PAIR))

    grads = [gmix_ref[place(r, p, 0)] for r, p in units]
    by_grad = [by_head(g) for g in grads]
    dprobs = [mm_nt(qkv_ref[place(r, p, 2)], g) for (r, p), g in zip(units, by_grad)]
    for (r, p), g in zip(units, by_grad):
        dqkv_ref[place(r, p, 2)] = mm(prob_ref[r, p], g).astype(BF)
    dscores = []
    for (r, p), dprob in zip(units, dprobs):
        p32 = prob_ref[r, p].astype(F32)
        dscores.append((p32 * (dprob - jnp.sum(p32 * dprob, axis=0, keepdims=True))).astype(BF))
    for (r, p), ds in zip(units, dscores):
        q = qkv_ref[place(r, p, 0)]
        dqkv_ref[place(r, p, 1)] = mm(ds, by_head(q * scale)).astype(BF)
    for (r, p), ds in zip(units, dscores):
        k = qkv_ref[place(r, p, 1)]
        stacked = jnp.concatenate([ds[:, :slots], ds[:, slots:]], axis=0)
        dqkv_ref[place(r, p, 0)] = mm_tn(stacked, by_head(k * scale)).astype(BF)
    unit, _ = unit_parts(tok_ref[...].astype(F32))
    acc_ref[:, : 3 * width] += mm_tn(unit.astype(BF), dqkv_ref[...])
    acc_ref[:, 3 * width : 4 * width] += mm_tn(mixed_ref[...], branch_ref[...])
    grad_ref[...] = dqkv_ref[...]
    for i in range(3):
        part = dqkv_ref[:, i * width : (i + 1) * width].astype(F32)
        row_ref[i : i + 1, :] += jnp.sum(part, axis=0, keepdims=True)

    @pl.when(at == last)
    def _():
        core, own, other = info_ref[0], info_ref[3], info_ref[4]
        row_ref[5:6, :] = g1_ref[...]
        row_ref[6:7, :] = c1_ref[...]
        wide_row = jnp.concatenate([row_ref[i : i + 1, :] for i in range(3)], axis=1)
        step = width // 4
        for r in range(0, width, step):
            w = wqkv_ref[r : r + step, :].astype(F32)
            sums = acc_ref[r : r + step, : 3 * width]
            d_gain = jnp.sum(w * sums, axis=1, keepdims=True)
            d_bias = jnp.sum(w * wide_row, axis=1, keepdims=True)
            lane = lax.broadcasted_iota(jnp.int32, (step, LANES), 1)
            others = row_ref[:, r : r + step].T
            acc_ref[r : r + step, : 3 * width] = others[:, 5:6] * sums + others[:, 6:7] * wide_row
            acc_ref[r : r + step, 4 * width :] = jnp.where(lane == 3, d_gain, jnp.where(lane == 4, d_bias, others))
        half = width // 2
        size = width // len(tables[0])
        for place in range(len(tables[0])):
            dst = dw_keep_ref if place * size < half else dw_send_ref
            block = block_at(place, tables, core, own if place * size < half else other)
            rows_at = pl.ds(pl.multiple_of(block * size, size), size)
            to = place * size % half
            dst[to : to + size, :] = acc_ref[rows_at, :].astype(BF)


def attend_back(info, tables, qkv, prob, gmix, tokens, mixed, branch, g1, c1, wqkv, *vecs):
    n, width = tokens.shape
    rows, pairs, slots, _ = prob.shape
    per = TOKS // slots
    return call(
        functools.partial(attend_back_kernel, tables),
        "attend_back",
        (n // TOKS,),
        [
            rows_of(3 * width),
            pl.BlockSpec((per, pairs, slots, 2 * slots), lambda i, *_: (i, 0, 0, 0)),
            rows_of(width),
            rows_of(width),
            rows_of(width),
            rows_of(width),
            whole(1, width),
            whole(1, width),
            whole(*wqkv.shape),
        ]
        + [whole(*vec.shape) for vec in vecs],
        [rows_of(3 * width)] + [whole(width // 2, 4 * width + LANES)] * 2,
        [pltpu.VMEM((n, 3 * width), BF)] + [jax.ShapeDtypeStruct((width // 2, 4 * width + LANES), BF)] * 2,
        [
            pltpu.VMEM((TOKS, 3 * width), BF),
            pltpu.VMEM((width, 4 * width + LANES), F32),
            pltpu.VMEM((LANES, width), F32),
        ],
        info,
        far(qkv, prob, gmix, tokens, mixed, branch, g1, c1, wqkv, *vecs),
    )


def first_back_kernel(info_ref, dqkv_ref, wqkv_ref, tok_ref, gres_ref, g1_ref, out_ref):
    dnormed = mm_nt(dqkv_ref[...], wqkv_ref[...])
    unit, inv = unit_parts(tok_ref[...].astype(F32))
    out_ref[...] = gres_ref[...] + norm_back(dnormed, unit, inv, g1_ref[...])


def first_back(info, dqkv, wqkv, tokens, gres, g1):
    n, width = tokens.shape
    return call(
        first_back_kernel,
        "first_back",
        (n // TOKS,),
        [rows_of(3 * width), whole(*wqkv.shape), rows_of(width), rows_of(width), whole(1, width)],
        rows_of(width),
        jax.ShapeDtypeStruct((n, width), F32),
        [],
        info,
        near(dqkv) + (wqkv,) + far(tokens, gres, g1),
    )


def ffn_end_kernel(tables, info_ref, keep_ref, other_ref, up_ref, down_ref, full_ref):
    core = info_ref[0]
    units = up_ref.shape[1]
    blocks = len(tables[0])
    size = keep_ref.shape[0] // blocks

    def lay(src_ref, whose, base):
        for place in range(blocks):
            block = block_at(place, tables, whose, base)
            rows = pl.ds(pl.multiple_of(block * size, size), size)
            part = src_ref[place * size : (place + 1) * size, :].astype(F32)
            up_ref[rows, :] = part[:, :units]
            full_ref[rows, :] = part[:, units:]
        down_ref[...] = full_ref[...].T

    @pl.when(pl.program_id(0) == 0)
    def _():
        lay(keep_ref, core, info_ref[1])

    @pl.when(pl.program_id(0) == 1)
    def _():
        lay(other_ref, core ^ 1, info_ref[2])


def ffn_end(info, tables, keep, other):
    width, double = keep.shape
    units = double // 2
    return call(
        functools.partial(ffn_end_kernel, tables),
        "ffn_end",
        (2,),
        [whole(width, double)] * 2,
        [
            pl.BlockSpec((width, units), lambda i, info: (0, info[0] ^ i)),
            pl.BlockSpec((units, width), lambda i, info: (info[0] ^ i, 0)),
        ],
        [jax.ShapeDtypeStruct((width, double), F32), jax.ShapeDtypeStruct((double, width), F32)],
        [pltpu.VMEM((width, units), F32)],
        info,
        (keep, other),
    )


def attend_end_kernel(tables, which, shares, info_ref, *refs):
    quarters, refs = refs[: 2 + 2 * which], refs[2 + 2 * which + 2 * which :]
    qkv_hbm, out_hbm, *refs = refs
    vec_refs, (qkv_ref, out_ref, *refs, sems) = refs[: 6 * which], refs[6 * which :]
    core = info_ref[0]
    width = out_ref.shape[1]
    blocks = len(tables[0])
    quarter = quarters[0].shape[0]
    size = 4 * quarter // blocks
    spots = []
    for place in range(blocks):
        row = place * size
        side, half = row // (2 * quarter), row // quarter % 2
        block = block_at(place, tables, core, info_ref[3 + side])
        at = row % quarter
        src = quarters[side + 2 * half * which] if half <= which else None
        spots.append((half, src, at, side * quarter + at, pl.multiple_of(block * size, size)))
    copies = []
    for half, src, at, row, to in spots:
        if half != which:
            continue
        here, there = pl.ds(row, size), pl.ds(to, size)
        for ref, hbm, cols in ((qkv_ref, qkv_hbm, slice(0, 3 * width)), (out_ref, out_hbm, slice(3 * width, 4 * width))):
            ref[row : row + size, :] = src[at : at + size, cols].astype(F32)
            copies.append(pltpu.make_async_copy(ref.at[here, :], hbm.at[there, :], sems.at[len(copies)]))
            copies[-1].start()
    if which:
        col_ref, row_ref = refs
        for half, src, at, _, to in spots:
            col_ref[pl.ds(to, size), :] = src[at : at + size, 4 * width :].astype(F32)
        vec = col_ref[...].T
        row_ref[...] = vec
        flat = lambda row: row.reshape(row.shape[1])
        for i, at in enumerate((3, 4, SUMS, SUMS + 1, SUMS + 2)):
            vec_refs[i][...] = flat(vec[at : at + 1, :])
        units = vec_refs[5].shape[0]
        if units >= width:
            first = SUMS + 8 + info_ref[5] * (units // width)
            for i in range(units // width):
                vec_refs[5][i * width : (i + 1) * width] = flat(row_ref[pl.ds(first + i, 1), :])
        else:
            row = row_ref[pl.ds(SUMS + 8 + info_ref[5] // shares, 1), :]
            share = row[:, :units]
            for i in range(1, shares):
                share = jnp.where(info_ref[5] % shares == i, row[:, i * units : (i + 1) * units], share)
            vec_refs[5][...] = flat(share)
    for copy in copies:
        copy.wait()


def attend_end(info, tables, quarters, width, units, written=()):
    rows = 4 * quarters[0].shape[0]
    which = 1 if written else 0
    anywhere = pl.BlockSpec(memory_space=pl.ANY)
    return call(
        functools.partial(attend_end_kernel, tables, which, max(1, width // units)),
        "attend_end",
        (1,),
        [whole(*quarters[0].shape)] * len(quarters) + [anywhere] * len(written),
        [anywhere] * 2 + ([whole(width)] * 5 + [whole(units)]) * which,
        [jax.ShapeDtypeStruct((rows, 3 * width), F32), jax.ShapeDtypeStruct((rows, width), F32)]
        + ([jax.ShapeDtypeStruct((width,), F32)] * 5 + [jax.ShapeDtypeStruct((units,), F32)]) * which,
        [pltpu.VMEM((rows // 2, 3 * width), F32), pltpu.VMEM((rows // 2, width), F32)]
        + [pltpu.VMEM((rows, LANES), F32), pltpu.VMEM((LANES, width), F32)] * which
        + [pltpu.SemaphoreType.DMA((len(tables[0]),))],
        info,
        (*quarters, *written),
        aliases=[(1 + len(quarters) + i, i) for i in range(len(written))],
    )


def local(
    wide, narrow, tokens_in, ln1_gain, ln1_bias, w_qkv, w_out, ln2_gain, ln2_bias, w_up, b_up, w_down, b_down, segment_ids,
    step_ids, pad_mask, cotangent,
):
    width = tokens_in.shape[1]
    units = w_up.shape[1] // 2
    core_mask = narrow
    narrow_masks = [1 << b for b in range(narrow.bit_length() - 1)]
    wide_masks = [narrow << b for b in range(1, wide.bit_length() - 1)]

    def swap(value, first, second=None):
        masks = (first, first if second is None else second)
        pairs = [(i, i ^ masks[i // narrow & 1]) for i in range(wide * narrow)]
        return lax.ppermute(value, AXES, pairs)

    def add(a, b):
        return (a.astype(F32) + b.astype(F32)).astype(a.dtype)

    def after(*values):
        return lax.optimization_barrier(values)

    def steps_of(halved, exchanged, gathered):
        pairs = lambda order: list(zip(*order))
        return (
            [("halve", *pair) for pair in pairs(halved)]
            + [("exchange", *pair) for pair in pairs(exchanged)]
            + [("gather", *pair) for pair in reversed(pairs(gathered))]
        )

    def start(value, step):
        kind, *masks = step
        if kind == "halve":
            half = value.shape[0] // 2
            return value[:half], swap(value[half:], *masks)
        return value, swap(value, *masks)

    def finish(kept, got, step):
        if step[0] == "gather":
            return jnp.concatenate([kept, got], axis=0)
        return add(kept, got) if step[0] in ("halve", "exchange") else (kept, got)

    wide_at, narrow_at = lax.axis_index("wide"), lax.axis_index("narrow")
    core = wide_at & 1
    flat = wide_at * narrow + narrow_at

    def named(owner, used):
        return sum((1 << b) for b, m in enumerate(used) if owner & m)

    def block_of(used):
        return sum(((flat & m) != 0).astype(jnp.int32) << b for b, m in enumerate(used))

    def split_at(pair, count):
        return tuple(o[:count] for o in pair), tuple(o[count:] for o in pair)

    def by_core(values):
        return jnp.where(core == 0, values[0], values[1]), jnp.where(core == 0, values[1], values[0])

    mixing = narrow == 2 and len(wide_masks) == 3
    if mixing:
        y, low, high = wide_masks
        ff_in, ff_rest, ff_out = ([y, low], [y, low]), ([high], [high]), ([low, y], [low, y])
        at_in, at_rest, at_out = ([y, 1, low], [low, y, 1]), ([high], [high]), ([y, 1, low], [low, 1, y])
        turns = "FAFAAFAFAAFFAA"
    else:
        ff_in, ff_rest = split_at((wide_masks, wide_masks), min(len(wide_masks) - 1, (width // TILE).bit_length() - 1))
        masks = narrow_masks + wide_masks
        at_in, at_rest = split_at((masks, masks), min(len(masks) - 1, (width // TILE // 2).bit_length() - 1))
        ff_out, at_out, turns = ff_in, at_in, ""
    ff_used = tuple(sorted(o) for o in ff_in)
    ff_in_tables, ff_out_tables = (
        tuple([named(owner, ff_used[c]) for owner in places(pair[c], 1 << len(ff_used[c]))] for c in range(2))
        for pair in (ff_in, ff_out)
    )
    at_used = tuple([core_mask] + sorted(o) for o in at_in)

    def at_tables(order):
        owners = [places(o, 1 << len(o)) for o in order]
        return tuple(
            [named(o, at_used[c]) for o in owners[c]] + [named(o ^ core_mask, at_used[1 - c]) for o in owners[1 - c]]
            for c in range(2)
        )

    ff_block = by_core([block_of(used) for used in ff_used])
    at_block = by_core([block_of(used) for used in at_used])
    info = jnp.stack([core, *ff_block, *at_block, narrow_at]).astype(jnp.int32)

    packed, tokens_in = after(pack(info, w_up, b_up, w_down), tokens_in)
    fetched = [packed]
    for mask in narrow_masks:
        fetched = fetched + [(swap(u, mask), swap(d, mask)) for u, d in fetched]

    row = lambda v: v[None].astype(F32)
    g1, c1, g2 = row(ln1_gain), row(ln1_bias), row(ln2_gain)
    qkv, prob, mixed, residual, second = attend(
        info, tokens_in, g1, c1, w_qkv, w_out, g2, row(ln2_bias), segment_ids, step_ids, pad_mask
    )
    out_part, dsec_part, own_keep, own_send, bias_own = ffn_own(
        info, ff_in_tables, mixing, second, cotangent, w_up, b_up, w_down
    )
    ups, downs = [u for u, _ in fetched[1:]], [d for _, d in fetched[1:]]
    own_send, ups = after(own_send, ups)
    away_ups = [swap(u, core_mask) for u in ups]
    away_downs = [swap(d, core_mask) for d in downs]
    chunks = [pair for here in zip(zip(ups, downs), zip(away_ups, away_downs)) for pair in here]
    rest = ffn_rest(
        info, ff_in_tables, mixing, second, cotangent, out_part, dsec_part, residual, row(b_down), g2, w_out, own_keep,
        chunks,
    )
    block_out, gres, gmix, branch, vec, bias_rest = rest[:6]
    grads = rest[6:]

    if narrow == 2 and units == width:
        vecs = (vec, bias_own, bias_rest)
    else:
        b_rest = bias_rest.reshape(-1, 2, units)
        b_rest = jnp.where(core == 0, b_rest, jnp.flip(b_rest, axis=1))
        b_all = jnp.concatenate([bias_own[None], b_rest], axis=0)
        for bit in range(narrow.bit_length() - 1):
            flipped = jnp.flip(b_all.reshape(-1, 2, (1 << bit) * 2, units), axis=1).reshape(b_all.shape)
            b_all = jnp.where(narrow_at >> bit & 1, flipped, b_all)
        vecs = (jnp.concatenate([vec, b_all.reshape(-1, width)], axis=0),)

    if mixing:
        ff_keep, ff_send, away = grads
        got_own, got = swap(own_send, core_mask), swap(away, core_mask)
        ff_send = join(info, ff_send, got, got_own)
        gmix, ff_send = after(gmix, ff_send)
        ff_got = swap(ff_send, 1, y)
    else:
        held = [add(own_keep, swap(own_send, core_mask))] + [add(grads[2 * j], swap(grads[2 * j + 1], core_mask)) for j in range(narrow - 1)]
        gmix, held = after(gmix, held)
        for mask in reversed(narrow_masks):
            held = [add(held[j], swap(held[j + mask], mask)) for j in range(mask)]
        ff_keep = held[0]

    dqkv, keep, send = attend_back(info, at_tables(at_in), qkv, prob, gmix, tokens_in, mixed, branch, g1, c1, w_qkv, *vecs)
    if mixing:
        send, ff_got = after(send, ff_got)
        ff_keep, ff_send = split(info, ff_keep, got, got_own, ff_got)
    keep = add(keep, swap(send, core_mask))
    grad_tokens = first_back(info, dqkv, w_qkv, tokens_in, gres, g1)
    steps = {
        "A": steps_of(at_in, at_rest, at_out)[:-1] + [("last", *steps_of(at_in, at_rest, at_out)[-1][1:]), ("core", core_mask)],
        "F": steps_of(ff_in, ff_rest, ff_out) + [("core", core_mask)],
    }
    if mixing:
        steps["F"] = [("halve", y, 1)] + steps["F"][1:]
        first = (ff_keep, swap(ff_send, y, 1))
    else:
        first = start(ff_keep, steps["F"][0])
    turns = turns or "".join(a + f for a, f in itertools.zip_longest("A" * len(steps["A"]), "F" * len(steps["F"]), fillvalue=""))
    under_way = {"A": start(keep, steps["A"][0]), "F": first}
    done, beside = (), (grad_tokens,)
    for turn in turns:
        other = "A" if turn == "F" else "F"
        kept, got = under_way.pop(turn)
        if other in under_way:
            other_kept, other_got = under_way[other]
            kept, other_kept, *beside = after(kept, other_kept, *beside)
            under_way[other] = other_kept, other_got
        else:
            kept, *beside = after(kept, *beside)
        if len(beside) == 1:
            (grad_tokens,), beside = beside, ()
        elif beside:
            (grad_w_up, grad_w_down), beside = beside, ()
        step, *steps[turn] = steps[turn]
        if step[0] == "last":
            written = attend_end(info, at_tables(at_out), (kept, crossed), width, 2 * units)
            got, written = after(got, written)
        value = finish(kept, got, step)
        if step[0] == "last":
            under_way[turn] = value, swap(got, core_mask)
        elif steps[turn]:
            under_way[turn] = start(value, steps[turn][0])
            if steps[turn][0][0] == "last":
                crossed = swap(value, core_mask)
        elif turn == "F":
            beside = ffn_end(info, ff_out_tables, *value)
        else:
            done = (value[0][0], crossed, value[0][1], value[1])
    grad_w_qkv, grad_w_out, d_gain1, d_bias1, d_gain2, d_bias2, d_bdown, grad_b_up = attend_end(
        info, at_tables(at_out), done, width, 2 * units, written
    )
    return (
        block_out, grad_tokens, d_gain1, d_bias1, grad_w_qkv, grad_w_out, d_gain2, d_bias2, grad_w_up, grad_b_up, grad_w_down,
        d_bdown,
    )


def solution(mesh):
    rows = P(("wide", "narrow"), None)
    in_specs = (
        rows, P(), P(), P(), P(), P(), P(), P(None, "narrow"), P("narrow"), P("narrow", None), P(), rows, rows, rows, rows,
    )
    out_specs = (
        rows, rows, P(), P(), P(), P(), P(), P(), P(None, "narrow"), P("narrow"), P("narrow", None), P(),
    )
    wide, narrow = mesh.shape["wide"], mesh.shape["narrow"]
    return jax.shard_map(
        functools.partial(local, wide, narrow), mesh=mesh, in_specs=in_specs, out_specs=out_specs, check_vma=False
    )
```

```python
import functools
import itertools

import jax
import jax.numpy as jnp
import numpy as np
from jax import lax
from jax.experimental import pallas as pl
from jax.experimental.pallas import tpu as pltpu
from jax.sharding import PartitionSpec as P

HEAD = 64
PAIR = 2 * HEAD
NORM_EPS = 1e-05
BF = jnp.bfloat16
F32 = jnp.float32
AXES = ("wide", "narrow")
LANES = 128
SUMS = 8
TILE = 16
TOKS = 512
VMEM_LIMIT = 30 * 1024 * 1024
REST_LIMIT = 36 * 1024 * 1024


def mm(a, b):
    return lax.dot_general(a, b, (((1,), (0,)), ((), ())), preferred_element_type=F32)


def mm_nt(a, b):
    return lax.dot_general(a, b, (((1,), (1,)), ((), ())), preferred_element_type=F32)


def mm_tn(a, b):
    return lax.dot_general(a, b, (((0,), (0,)), ((), ())), preferred_element_type=F32)


def near(*values):
    return tuple(pltpu.with_memory_space_constraint(v, pltpu.VMEM) for v in values)


def far(*values):
    return tuple(pltpu.with_memory_space_constraint(v, pltpu.HBM) for v in values)


def whole(*shape):
    return pl.BlockSpec(shape, lambda *_: (0,) * len(shape))


def rows_of(width, toks=TOKS):
    return pl.BlockSpec((toks, width), lambda i, *_: (i, 0))


def call(kernel, name, grid, in_specs, out_specs, out_shape, scratch, info, args, vmem=VMEM_LIMIT, aliases=()):
    return pl.pallas_call(
        kernel,
        grid_spec=pltpu.PrefetchScalarGridSpec(
            num_scalar_prefetch=1, grid=grid, in_specs=in_specs, out_specs=out_specs, scratch_shapes=scratch
        ),
        out_shape=out_shape,
        input_output_aliases=dict(aliases),
        compiler_params=pltpu.CompilerParams(vmem_limit_bytes=vmem),
        cost_estimate=pl.CostEstimate(flops=1000, bytes_accessed=1000, transcendentals=0),
        name=name,
    )(info, *args)


def unit_parts(rows):
    mean = jnp.mean(rows, axis=-1, keepdims=True)
    centered = rows - mean
    inv = lax.rsqrt(jnp.mean(centered * centered, axis=-1, keepdims=True) + NORM_EPS)
    return centered * inv, inv


def norm_back(incoming, unit, inv, gain):
    scaled = incoming * gain
    return inv * (
        scaled
        - jnp.mean(scaled, axis=-1, keepdims=True)
        - unit * jnp.mean(scaled * unit, axis=-1, keepdims=True)
    )


def gelu_pair(x):
    cdf = 0.5 * (1.0 + lax.erf(x * 0.7071067811865476))
    return x * cdf, cdf + x * jnp.exp(-0.5 * x * x) * 0.3989422804014327


def by_head(block):
    lane = lax.broadcasted_iota(jnp.int32, block.shape, 1)
    zero = jnp.zeros_like(block)
    first = lane < HEAD
    return jnp.concatenate([jnp.where(first, block, zero), jnp.where(first, zero, block)], axis=0)


def places(order, blocks):
    bits = blocks.bit_length() - 1
    table = []
    for place in range(blocks):
        owner = 0
        for step in range(bits):
            if place >> (bits - 1 - step) & 1:
                owner ^= order[step]
        table.append(owner)
    return table


def block_at(place, tables, core, own):
    first, second = tables[0][place], tables[1][place]
    if first == second:
        return own ^ first
    return own ^ jnp.where(core == 0, first, second)


def place_of(block, tables, core, own):
    wanted = own ^ block
    places_by_core = [[table.index(owner) for owner in range(len(table))] for table in tables]
    place = jnp.int32(0)
    for owner in range(len(tables[0])):
        first, second = places_by_core[0][owner], places_by_core[1][owner]
        place = jnp.where(wanted == owner, jnp.where(core == 0, first, second), place)
    return place


def permuted(dst_ref, acc_ref, chunk, tables, core, own, turned=0):
    blocks = len(tables[0])
    size = dst_ref.shape[0] // blocks
    for place in range(blocks):
        block = block_at(place, tables, core, own)
        rows = pl.ds(pl.multiple_of(block * size, size), size)
        to = pl.ds(pl.multiple_of(((place + turned * (blocks // 2)) & (blocks - 1)) * size, size), size)
        dst_ref[to, :] = acc_ref[chunk, rows, :].astype(dst_ref.dtype)


def attend_kernel(
    info_ref, tok_ref, g1_ref, c1_ref, wqkv_ref, wout_ref, g2_ref, c2_ref, seg_ref, step_ref, pad_ref,
    qkv_ref, prob_ref, mixed_ref, res_ref, second_ref,
):
    slots = seg_ref.shape[1]
    toks, width = tok_ref.shape
    rows = toks // slots
    at = pl.program_id(0)
    tokens = tok_ref[...].astype(F32)
    unit, _ = unit_parts(tokens)
    normed = (unit * g1_ref[...] + c1_ref[...]).astype(BF)
    qkv_ref[...] = mm(normed, wqkv_ref[...]).astype(BF)
    q_id = lax.broadcasted_iota(jnp.int32, (slots, slots), 0)
    k_id = lax.broadcasted_iota(jnp.int32, (slots, slots), 1)
    eye = q_id == k_id
    pairs = width // PAIR
    units = [(r, p) for r in range(rows) for p in range(pairs)]

    def part(r, p, which):
        return qkv_ref[r * slots : (r + 1) * slots, which * width + p * PAIR : which * width + (p + 1) * PAIR]

    masks = []
    for r in range(rows):
        here = pl.ds(at * rows + r, 1)
        seg = jnp.broadcast_to(seg_ref[here, :].astype(F32), (slots, slots))
        step = jnp.broadcast_to(step_ref[here, :].astype(F32), (slots, slots))
        live = jnp.broadcast_to(pad_ref[here, :].astype(F32), (slots, slots)).T == 0
        masks.append(((seg == seg.T) & (step.T <= step) & live) | eye)
    scores = [mm_nt(part(r, p, 1), by_head(part(r, p, 0) * HEAD ** (-0.5))) for r, p in units]
    probs = []
    for (r, p), score in zip(units, scores):
        halves = []
        for half in (score[:, :slots], score[:, slots:]):
            half = jnp.where(masks[r], half, -1e30)
            weight = jnp.exp(half - jnp.max(half, axis=0, keepdims=True))
            total = jnp.sum(weight, axis=0, keepdims=True)
            halves.append((weight * (1.0 / total)).astype(BF))
        probs.append(halves)
    for (r, p), halves in zip(units, probs):
        prob_ref[r, p] = jnp.concatenate(halves, axis=1)
        mixed = mm_tn(jnp.concatenate(halves, axis=0), by_head(part(r, p, 2)))
        mixed_ref[r * slots : (r + 1) * slots, p * PAIR : (p + 1) * PAIR] = mixed.astype(BF)
    residual = tokens + mm(mixed_ref[...], wout_ref[...])
    res_ref[...] = residual
    unit, _ = unit_parts(residual)
    second_ref[...] = (unit * g2_ref[...] + c2_ref[...]).astype(BF)


def attend(info, tokens, g1, c1, wqkv, wout, g2, c2, seg, step, pad):
    n, width = tokens.shape
    rows, slots = seg.shape
    per, pairs = TOKS // slots, width // PAIR
    return call(
        attend_kernel,
        "attend",
        (n // TOKS,),
        [rows_of(width), whole(1, width), whole(1, width), whole(*wqkv.shape), whole(*wout.shape)]
        + [whole(1, width)] * 2
        + [whole(rows, slots)] * 3,
        [
            rows_of(3 * width),
            pl.BlockSpec((per, pairs, slots, 2 * slots), lambda i, *_: (i, 0, 0, 0)),
            rows_of(width),
            rows_of(width),
            rows_of(width),
        ],
        [
            pltpu.HBM((n, 3 * width), BF),
            pltpu.HBM((rows, pairs, slots, 2 * slots), BF),
            pltpu.HBM((n, width), BF),
            pltpu.HBM((n, width), F32),
            pltpu.VMEM((n, width), BF),
        ],
        [],
        info,
        far(tokens, g1, c1) + (wqkv, wout) + far(g2, c2, seg, step, pad),
    )


def pack_kernel(info_ref, up_ref, bias_ref, down_ref, up_out, down_out):
    width = up_ref.shape[0]
    up_out[:width, :] = up_ref[...]
    units = up_ref.shape[1]
    bias = bias_ref[...].reshape(1, 2 * units)
    bias = jnp.where(info_ref[0] == 0, bias[:, :units], bias[:, units:])
    up_out[width:, :] = jnp.broadcast_to(bias, (TILE, units))
    down_out[...] = down_ref[...]


def pack(info, up, bias, down):
    width, units = up.shape[0], up.shape[1] // 2
    return call(
        pack_kernel,
        "pack",
        (1,),
        [
            pl.BlockSpec((width, units), lambda t, info: (0, info[0])),
            whole(2 * units),
            pl.BlockSpec((units, width), lambda t, info: (info[0], 0)),
        ],
        [whole(width + TILE, units), whole(units, width)],
        [jax.ShapeDtypeStruct((width + TILE, units), BF), jax.ShapeDtypeStruct((units, width), BF)],
        [],
        info,
        far(up, bias, down),
    )


def ffn_block(sec, dy, up, bias, down, acc_ref, bacc_ref):
    pre = mm(sec, up) + bias
    dhid = mm_nt(dy, down)
    hid, slope = gelu_pair(pre)
    hid = hid.astype(BF)
    dpre = (dhid * slope).astype(BF)
    grad_up = mm(sec.T, dpre)
    grad_down = mm(dy.T, hid)
    sums = jnp.sum(dpre.astype(F32), axis=0, keepdims=True)
    chunks, _, double = acc_ref.shape
    units = double // 2
    for i in range(chunks):
        cols = slice(i * units, (i + 1) * units)
        acc_ref[i, :, :units] += grad_up[:, cols]
        acc_ref[i, :, units:] += grad_down[:, cols]
        bacc_ref[i : i + 1, :] += sums[:, cols]
    return hid, dpre


def ffn_own_kernel(
    tables, mixing, info_ref, sec_ref, dy_ref, up_ref, bias_ref, down_ref, out_ref, dsec_ref, keep_ref, send_ref, bias_out,
    acc_ref,
):
    at, last = pl.program_id(0), pl.num_programs(0) - 1

    @pl.when(at == 0)
    def _():
        acc_ref[...] = jnp.zeros_like(acc_ref)
        bias_out[...] = jnp.zeros_like(bias_out)

    bias = bias_ref[...].astype(F32).reshape(1, up_ref.shape[1])
    hid, dpre = ffn_block(sec_ref[...], dy_ref[...], up_ref[...], bias, down_ref[...], acc_ref, bias_out)
    out_ref[...] = mm(hid, down_ref[...])
    dsec_ref[...] = mm_nt(dpre, up_ref[...])

    @pl.when(at == last)
    def _():
        core, own, other = info_ref[0], info_ref[1], info_ref[2]
        permuted(keep_ref, acc_ref, core, tables, core, own)
        permuted(send_ref, acc_ref, core ^ 1, tables, core ^ 1, other, core ^ 1 if mixing else 0)


def ffn_own(info, tables, mixing, second, dy, up, bias, down):
    n, width = second.shape
    units = up.shape[1] // 2
    return call(
        functools.partial(ffn_own_kernel, tables, mixing),
        "ffn_own",
        (n // TOKS,),
        [rows_of(width), rows_of(width), whole(*up.shape), whole(*bias.shape), whole(*down.shape)],
        [rows_of(width)] * 2 + [whole(width, 2 * units)] * 2 + [whole(2, units)],
        [pltpu.VMEM((n, width), F32)] * 2
        + [pltpu.HBM((width, 2 * units), BF)] * 2
        + [pltpu.HBM((2, units), F32)],
        [pltpu.VMEM((2, width, 2 * units), F32)],
        info,
        near(second) + far(dy) + (up,) + far(bias) + (down,),
    )


def ffn_rest_kernel(
    tables, count, mixing, info_ref, sec_in, dy_in, out_in, dsec_in, res_in, mine_ref, bdown_ref, g2_ref, wout_ref, *refs
):
    ups, downs = refs[:count], refs[count : 2 * count]
    block_out, gres_out, gmix_out, branch_out, vec_ref, bias_out = refs[2 * count : 2 * count + 6]
    grads, refs = refs[2 * count + 6 : 3 * count + 6 + mixing], refs[3 * count + 6 + mixing :]
    sec_ref, dy_ref, out_ref, dsec_ref, res_ref, branch_ref, up_ref, bias_ref, down_ref, laid_ref, sems = refs
    n, width = sec_ref.shape
    units = down_ref.shape[0] // count
    core = info_ref[0]
    half = width // 2
    top, low = pl.ds(0, half), pl.ds(half, half)
    used = iter(range(sems.shape[0]))

    def move(*pairs):
        copies = [pltpu.make_async_copy(*pair, sems.at[next(used)]) for pair in pairs]
        for copy in copies:
            copy.start()
        return copies

    def arrived(copies):
        for copy in copies:
            copy.wait()

    def by_core(first, *sets):
        def each(act):
            for odd, pairs in enumerate(sets):

                @pl.when(core == odd)
                def _(pairs=pairs):
                    for i, pair in enumerate(pairs):
                        act(pltpu.make_async_copy(*pair, sems.at[first + i]))

        return lambda: each(lambda copy: copy.start()), lambda: each(lambda copy: copy.wait())

    cols = [pl.ds(i * units, units) for i in range(count)]
    first = move(
        (sec_in, sec_ref),
        *[(ups[i].at[pl.ds(0, width), :], up_ref.at[:, cols[i]]) for i in range(count)],
        *[(ups[i].at[pl.ds(width, TILE), :], bias_ref.at[:, cols[i]]) for i in range(count)],
    )
    second = move((dy_in, dy_ref), *[(downs[i], down_ref.at[cols[i], :]) for i in range(count)])
    third = move((out_in, out_ref), (dsec_in, dsec_ref), (res_in, res_ref))
    if mixing:
        keep_ref, send_ref, away_ref = grads
        own_start, own_wait = by_core(
            next(used),
            [(mine_ref, keep_ref)],
            [(mine_ref.at[top], keep_ref.at[low]), (mine_ref.at[low], send_ref.at[top])],
        )
        next(used)
        chunk_start, chunk_wait = by_core(
            next(used),
            [(laid_ref.at[0], send_ref)],
            [(laid_ref.at[0, top], keep_ref.at[top]), (laid_ref.at[0, low], send_ref.at[low])],
        )
        next(used)
        own_start()

    arrived(first)
    toks = n if count <= 2 else n // 2
    grad_up = grad_down = sums = None
    parts = []
    for t in range(n // toks):
        rows = slice(t * toks, (t + 1) * toks)
        sec = sec_ref[rows, :]
        every = up_ref.shape[1]
        parts_of = [slice(c * every // 2, (c + 1) * every // 2) for c in range(2)]
        pres = [mm(sec, up_ref[:, c]) + bias_ref[:, c].astype(F32)[:1] for c in parts_of]
        if t == 0:
            arrived(second)
        dy = dy_ref[rows, :]
        dhids = [mm_nt(dy, down_ref[c, :]) for c in parts_of]
        hids, dpres, grads_up, grads_down = [], [], [], []
        sec_t, dy_t = sec.T, dy.T
        for pre, dhid in zip(pres, dhids):
            hid, slope = gelu_pair(pre)
            hids.append(hid.astype(BF))
            dpres.append((dhid * slope).astype(BF))
            grads_up.append(mm(sec_t, dpres[-1]))
            grads_down.append(mm(dy_t, hids[-1]))
        hid, dpre = jnp.concatenate(hids, axis=1), jnp.concatenate(dpres, axis=1)
        more = (jnp.concatenate(grads_up, axis=1), jnp.concatenate(grads_down, axis=1), jnp.sum(dpre.astype(F32), axis=0, keepdims=True))
        if t:
            more = (grad_up + more[0], grad_down + more[1], sums + more[2])
        grad_up, grad_down, sums = more
        parts.append((hid, dpre))
    blocks = len(tables[0])
    size = width // blocks
    for i in range(count):
        at = slice(i * units, (i + 1) * units)
        bias_out[i : i + 1, :] = sums[:, at]
        for block in range(blocks):
            owner = core ^ (i % 2)
            place = place_of(block, tables, owner, info_ref[1 + i % 2])
            to = pl.ds(pl.multiple_of(place * size, size), size)
            rows = slice(block * size, (block + 1) * size)
            laid_ref[i, to, :units] = grad_up[rows, at].astype(BF)
            laid_ref[i, to, units:] = grad_down[rows, at].astype(BF)
    if mixing:
        chunk_start()
        gone = move((laid_ref.at[1], away_ref))
    else:
        gone = move(*[(laid_ref.at[i], grads[i]) for i in range(count)])

    arrived(third)
    step = min(64, toks)
    for t, (hid, dpre) in enumerate(parts):
        out_all, dsec_all = mm(hid, down_ref[...]), mm_nt(dpre, up_ref[...])
        for r in range(0, toks, step):
            rows = slice(t * toks + r, t * toks + r + step)
            span = pl.ds(rows.start, step)
            dy32 = dy_ref[rows, :].astype(F32)
            residual = res_ref[rows, :]
            dsec = dsec_all[r : r + step] + dsec_ref[rows, :]
            dy_ref[rows, :] = (residual + (out_all[r : r + step] + out_ref[rows, :] + bdown_ref[...])).astype(BF)
            unit, inv = unit_parts(residual)
            sums = [jnp.sum(v, axis=0, keepdims=True) for v in (dsec * unit, dsec, dy32)]
            for i, row in enumerate(sums):
                if rows.start:
                    vec_ref[i : i + 1, :] += row
                else:
                    vec_ref[i : i + 1, :] = row
            gres = dy32 + norm_back(dsec, unit, inv, g2_ref[...])
            out_ref[rows, :] = gres
            branch_ref[rows, :] = gres.astype(BF)
            gone += move((dy_ref.at[span, :], block_out.at[span, :]), (out_ref.at[span, :], gres_out.at[span, :]))
    vec_ref[3:, :] = jnp.zeros((vec_ref.shape[0] - 3, width), F32)
    gone += move((branch_ref, branch_out))
    sec_ref[...] = mm_nt(branch_ref[...], wout_ref[...]).astype(BF)
    gone += move((sec_ref, gmix_out))
    arrived(gone)
    if mixing:
        own_wait()
        chunk_wait()


def ffn_rest(info, tables, mixing, second, dy, out_part, dsec_part, residual, bdown, g2, wout, mine, chunks):
    n, width = second.shape
    count = len(chunks)
    units = chunks[0][0].shape[1]
    anywhere = pl.BlockSpec(memory_space=pl.ANY)
    return call(
        functools.partial(ffn_rest_kernel, tables, count, mixing),
        "ffn_rest",
        (1,),
        [anywhere] * 6 + [whole(1, width)] * 2 + [whole(width, width)] + [anywhere] * (2 * count),
        [anywhere] * 4 + [whole(8, width), whole(count, units)] + [anywhere] * (count + mixing),
        [
            jax.ShapeDtypeStruct((n, width), BF),
            pltpu.HBM((n, width), F32),
            pltpu.HBM((n, width), BF),
            pltpu.HBM((n, width), BF),
            pltpu.HBM((8, width), F32),
            pltpu.HBM((count, units), F32),
        ]
        + [jax.ShapeDtypeStruct((width, 2 * units), BF)] * (count + mixing),
        [
            pltpu.VMEM((n, width), BF),
            pltpu.VMEM((n, width), BF),
            pltpu.VMEM((n, width), F32),
            pltpu.VMEM((n, width), F32),
            pltpu.VMEM((n, width), F32),
            pltpu.VMEM((n, width), BF),
            pltpu.VMEM((width, count * units), BF),
            pltpu.VMEM((TILE, count * units), BF),
            pltpu.VMEM((count * units, width), BF),
            pltpu.VMEM((count, width, 2 * units), BF),
            pltpu.SemaphoreType.DMA((24 + 4 * count + n // 32,)),
        ],
        info,
        near(second)
        + far(dy)
        + near(out_part, dsec_part)
        + far(residual, mine, bdown, g2)
        + (wout,)
        + tuple(c[0] for c in chunks)
        + tuple(c[1] for c in chunks),
        REST_LIMIT if count <= 2 else 56 * 1024 * 1024,
    )


def join_kernel(info_ref, send_ref, got_ref, own_ref, out_ref):
    half = send_ref.shape[0] // 2
    out_ref[half:, :] = (send_ref[half:, :].astype(F32) + got_ref[half:, :].astype(F32)).astype(BF)

    @pl.when(info_ref[0] == 0)
    def _():
        out_ref[:half, :] = (send_ref[:half, :].astype(F32) + got_ref[:half, :].astype(F32)).astype(BF)

    @pl.when(info_ref[0] == 1)
    def _():
        out_ref[:half, :] = (send_ref[:half, :].astype(F32) + own_ref[:half, :].astype(F32)).astype(BF)


def split_kernel(info_ref, keep_ref, got_ref, own_ref, arrived_ref, keep_out, send_out):
    half = keep_ref.shape[0] // 2
    top, low = slice(0, half), slice(half, 2 * half)

    def total(*parts):
        value = parts[0].astype(F32)
        for part in parts[1:]:
            value += part.astype(F32)
        return value.astype(BF)

    @pl.when(info_ref[0] == 0)
    def _():
        keep_out[...] = total(keep_ref[top, :], own_ref[top, :], arrived_ref[top, :])
        send_out[...] = total(keep_ref[low, :], own_ref[low, :], arrived_ref[low, :])

    @pl.when(info_ref[0] == 1)
    def _():
        keep_out[...] = total(keep_ref[low, :], own_ref[low, :], arrived_ref[top, :])
        send_out[...] = total(keep_ref[top, :], got_ref[top, :], arrived_ref[low, :])


def direct(kernel, name, info, out_shape, args):
    return pl.pallas_call(
        kernel,
        in_specs=[pl.BlockSpec(memory_space=pltpu.SMEM)] + [pl.BlockSpec(memory_space=pltpu.VMEM)] * len(args),
        out_specs=jax.tree.map(lambda _: pl.BlockSpec(memory_space=pltpu.VMEM), out_shape),
        out_shape=out_shape,
        compiler_params=pltpu.CompilerParams(vmem_limit_bytes=VMEM_LIMIT),
        cost_estimate=pl.CostEstimate(flops=1000, bytes_accessed=1000, transcendentals=0),
        name=name,
    )(info, *args)


def join(info, send, got, own):
    return direct(join_kernel, "join", info, jax.ShapeDtypeStruct(send.shape, BF), (send, got, own))


def split(info, keep, got, own, arrived):
    shape = jax.ShapeDtypeStruct((keep.shape[0] // 2, keep.shape[1]), BF)
    return direct(split_kernel, "split", info, [shape, shape], (keep, got, own, arrived))


def attend_back_kernel(
    tables, info_ref, qkv_ref, prob_ref, gmix_ref, tok_ref, mixed_ref, branch_ref, g1_ref, c1_ref, wqkv_ref, vec_ref,
    *refs,
):
    *sums, grad_ref, dw_keep_ref, dw_send_ref, dqkv_ref, acc_ref, row_ref = refs
    at, last = pl.program_id(0), pl.num_programs(0) - 1
    toks, width = tok_ref.shape
    rows, pairs, slots, _ = prob_ref.shape

    @pl.when(at == 0)
    def _():
        acc_ref[:, : 4 * width] = jnp.zeros((width, 4 * width), F32)
        row_ref[...] = jnp.zeros_like(row_ref)
        row_ref[SUMS : SUMS + vec_ref.shape[0], :] = vec_ref[...]
        if sums:
            own_ref, rest_ref = sums
            first = SUMS + vec_ref.shape[0]
            for i in range(2):
                row_ref[pl.ds(first + 2 * info_ref[5] + i, 1), :] = own_ref[i : i + 1, :]
                row_ref[pl.ds(first + 2 * (info_ref[5] ^ 1) + (info_ref[0] ^ i), 1), :] = rest_ref[i : i + 1, :]

    scale = HEAD ** (-0.5)
    units = [(r, p) for r in range(rows) for p in range(pairs)]

    def place(r, p, which):
        return (slice(r * slots, (r + 1) * slots), slice(which * width + p * PAIR, which * width + (p + 1) * PAIR))

    grads = [gmix_ref[place(r, p, 0)] for r, p in units]
    by_grad = [by_head(g) for g in grads]
    dprobs = [mm_nt(qkv_ref[place(r, p, 2)], g) for (r, p), g in zip(units, by_grad)]
    for (r, p), g in zip(units, by_grad):
        dqkv_ref[place(r, p, 2)] = mm(prob_ref[r, p], g).astype(BF)
    dscores = []
    for (r, p), dprob in zip(units, dprobs):
        p32 = prob_ref[r, p].astype(F32)
        dscores.append((p32 * (dprob - jnp.sum(p32 * dprob, axis=0, keepdims=True))).astype(BF))
    for (r, p), ds in zip(units, dscores):
        q = qkv_ref[place(r, p, 0)]
        dqkv_ref[place(r, p, 1)] = mm(ds, by_head(q * scale)).astype(BF)
    for (r, p), ds in zip(units, dscores):
        k = qkv_ref[place(r, p, 1)]
        stacked = jnp.concatenate([ds[:, :slots], ds[:, slots:]], axis=0)
        dqkv_ref[place(r, p, 0)] = mm_tn(stacked, by_head(k * scale)).astype(BF)
    unit, _ = unit_parts(tok_ref[...].astype(F32))
    acc_ref[:, : 3 * width] += mm_tn(unit.astype(BF), dqkv_ref[...])
    acc_ref[:, 3 * width : 4 * width] += mm_tn(mixed_ref[...], branch_ref[...])
    grad_ref[...] = dqkv_ref[...]
    for i in range(3):
        part = dqkv_ref[:, i * width : (i + 1) * width].astype(F32)
        row_ref[i : i + 1, :] += jnp.sum(part, axis=0, keepdims=True)

    @pl.when(at == last)
    def _():
        core, own, other = info_ref[0], info_ref[3], info_ref[4]
        row_ref[5:6, :] = g1_ref[...]
        row_ref[6:7, :] = c1_ref[...]
        wide_row = jnp.concatenate([row_ref[i : i + 1, :] for i in range(3)], axis=1)
        step = width // 4
        for r in range(0, width, step):
            w = wqkv_ref[r : r + step, :].astype(F32)
            sums = acc_ref[r : r + step, : 3 * width]
            d_gain = jnp.sum(w * sums, axis=1, keepdims=True)
            d_bias = jnp.sum(w * wide_row, axis=1, keepdims=True)
            lane = lax.broadcasted_iota(jnp.int32, (step, LANES), 1)
            others = row_ref[:, r : r + step].T
            acc_ref[r : r + step, : 3 * width] = others[:, 5:6] * sums + others[:, 6:7] * wide_row
            acc_ref[r : r + step, 4 * width :] = jnp.where(lane == 3, d_gain, jnp.where(lane == 4, d_bias, others))
        half = width // 2
        size = width // len(tables[0])
        for place in range(len(tables[0])):
            dst = dw_keep_ref if place * size < half else dw_send_ref
            block = block_at(place, tables, core, own if place * size < half else other)
            rows_at = pl.ds(pl.multiple_of(block * size, size), size)
            to = place * size % half
            dst[to : to + size, :] = acc_ref[rows_at, :].astype(BF)


def attend_back(info, tables, qkv, prob, gmix, tokens, mixed, branch, g1, c1, wqkv, *vecs):
    n, width = tokens.shape
    rows, pairs, slots, _ = prob.shape
    per = TOKS // slots
    return call(
        functools.partial(attend_back_kernel, tables),
        "attend_back",
        (n // TOKS,),
        [
            rows_of(3 * width),
            pl.BlockSpec((per, pairs, slots, 2 * slots), lambda i, *_: (i, 0, 0, 0)),
            rows_of(width),
            rows_of(width),
            rows_of(width),
            rows_of(width),
            whole(1, width),
            whole(1, width),
            whole(*wqkv.shape),
        ]
        + [whole(*vec.shape) for vec in vecs],
        [rows_of(3 * width)] + [whole(width // 2, 4 * width + LANES)] * 2,
        [pltpu.VMEM((n, 3 * width), BF)] + [jax.ShapeDtypeStruct((width // 2, 4 * width + LANES), BF)] * 2,
        [
            pltpu.VMEM((TOKS, 3 * width), BF),
            pltpu.VMEM((width, 4 * width + LANES), F32),
            pltpu.VMEM((LANES, width), F32),
        ],
        info,
        far(qkv, prob, gmix, tokens, mixed, branch, g1, c1, wqkv, *vecs),
    )


def first_back_kernel(info_ref, dqkv_ref, wqkv_ref, tok_ref, gres_ref, g1_ref, out_ref):
    dnormed = mm_nt(dqkv_ref[...], wqkv_ref[...])
    unit, inv = unit_parts(tok_ref[...].astype(F32))
    out_ref[...] = gres_ref[...] + norm_back(dnormed, unit, inv, g1_ref[...])


def first_back(info, dqkv, wqkv, tokens, gres, g1):
    n, width = tokens.shape
    return call(
        first_back_kernel,
        "first_back",
        (n // TOKS,),
        [rows_of(3 * width), whole(*wqkv.shape), rows_of(width), rows_of(width), whole(1, width)],
        rows_of(width),
        jax.ShapeDtypeStruct((n, width), F32),
        [],
        info,
        near(dqkv) + (wqkv,) + far(tokens, gres, g1),
    )


def ffn_end_kernel(tables, info_ref, keep_ref, other_ref, up_ref, down_ref, full_ref):
    core = info_ref[0]
    units = up_ref.shape[1]
    blocks = len(tables[0])
    size = keep_ref.shape[0] // blocks

    def lay(src_ref, whose, base):
        for place in range(blocks):
            block = block_at(place, tables, whose, base)
            rows = pl.ds(pl.multiple_of(block * size, size), size)
            part = src_ref[place * size : (place + 1) * size, :].astype(F32)
            up_ref[rows, :] = part[:, :units]
            full_ref[rows, :] = part[:, units:]
        down_ref[...] = full_ref[...].T

    @pl.when(pl.program_id(0) == 0)
    def _():
        lay(keep_ref, core, info_ref[1])

    @pl.when(pl.program_id(0) == 1)
    def _():
        lay(other_ref, core ^ 1, info_ref[2])


def ffn_end(info, tables, keep, other):
    width, double = keep.shape
    units = double // 2
    return call(
        functools.partial(ffn_end_kernel, tables),
        "ffn_end",
        (2,),
        [whole(width, double)] * 2,
        [
            pl.BlockSpec((width, units), lambda i, info: (0, info[0] ^ i)),
            pl.BlockSpec((units, width), lambda i, info: (info[0] ^ i, 0)),
        ],
        [jax.ShapeDtypeStruct((width, double), F32), jax.ShapeDtypeStruct((double, width), F32)],
        [pltpu.VMEM((width, units), F32)],
        info,
        (keep, other),
    )


def attend_end_kernel(tables, which, shares, info_ref, *refs):
    quarters, refs = refs[: 2 + 2 * which], refs[2 + 2 * which + 2 * which :]
    qkv_hbm, out_hbm, *refs = refs
    vec_refs, (qkv_ref, out_ref, *refs, sems) = refs[: 6 * which], refs[6 * which :]
    core = info_ref[0]
    width = out_ref.shape[1]
    blocks = len(tables[0])
    quarter = quarters[0].shape[0]
    size = 4 * quarter // blocks
    spots = []
    for place in range(blocks):
        row = place * size
        side, half = row // (2 * quarter), row // quarter % 2
        block = block_at(place, tables, core, info_ref[3 + side])
        at = row % quarter
        src = quarters[side + 2 * half * which] if half <= which else None
        spots.append((half, src, at, side * quarter + at, pl.multiple_of(block * size, size)))
    copies = []
    for half, src, at, row, to in spots:
        if half != which:
            continue
        here, there = pl.ds(row, size), pl.ds(to, size)
        for ref, hbm, cols in ((qkv_ref, qkv_hbm, slice(0, 3 * width)), (out_ref, out_hbm, slice(3 * width, 4 * width))):
            ref[row : row + size, :] = src[at : at + size, cols].astype(F32)
            copies.append(pltpu.make_async_copy(ref.at[here, :], hbm.at[there, :], sems.at[len(copies)]))
            copies[-1].start()
    if which:
        col_ref, row_ref = refs
        for half, src, at, _, to in spots:
            col_ref[pl.ds(to, size), :] = src[at : at + size, 4 * width :].astype(F32)
        vec = col_ref[...].T
        row_ref[...] = vec
        flat = lambda row: row.reshape(row.shape[1])
        for i, at in enumerate((3, 4, SUMS, SUMS + 1, SUMS + 2)):
            vec_refs[i][...] = flat(vec[at : at + 1, :])
        units = vec_refs[5].shape[0]
        if units >= width:
            first = SUMS + 8 + info_ref[5] * (units // width)
            for i in range(units // width):
                vec_refs[5][i * width : (i + 1) * width] = flat(row_ref[pl.ds(first + i, 1), :])
        else:
            row = row_ref[pl.ds(SUMS + 8 + info_ref[5] // shares, 1), :]
            share = row[:, :units]
            for i in range(1, shares):
                share = jnp.where(info_ref[5] % shares == i, row[:, i * units : (i + 1) * units], share)
            vec_refs[5][...] = flat(share)
    for copy in copies:
        copy.wait()


def attend_end(info, tables, quarters, width, units, written=()):
    rows = 4 * quarters[0].shape[0]
    which = 1 if written else 0
    anywhere = pl.BlockSpec(memory_space=pl.ANY)
    return call(
        functools.partial(attend_end_kernel, tables, which, max(1, width // units)),
        "attend_end",
        (1,),
        [whole(*quarters[0].shape)] * len(quarters) + [anywhere] * len(written),
        [anywhere] * 2 + ([whole(width)] * 5 + [whole(units)]) * which,
        [jax.ShapeDtypeStruct((rows, 3 * width), F32), jax.ShapeDtypeStruct((rows, width), F32)]
        + ([jax.ShapeDtypeStruct((width,), F32)] * 5 + [jax.ShapeDtypeStruct((units,), F32)]) * which,
        [pltpu.VMEM((rows // 2, 3 * width), F32), pltpu.VMEM((rows // 2, width), F32)]
        + [pltpu.VMEM((rows, LANES), F32), pltpu.VMEM((LANES, width), F32)] * which
        + [pltpu.SemaphoreType.DMA((len(tables[0]),))],
        info,
        (*quarters, *written),
        aliases=[(1 + len(quarters) + i, i) for i in range(len(written))],
    )


def local(
    wide, narrow, tokens_in, ln1_gain, ln1_bias, w_qkv, w_out, ln2_gain, ln2_bias, w_up, b_up, w_down, b_down, segment_ids,
    step_ids, pad_mask, cotangent,
):
    width = tokens_in.shape[1]
    units = w_up.shape[1] // 2
    core_mask = narrow
    narrow_masks = [1 << b for b in range(narrow.bit_length() - 1)]
    wide_masks = [narrow << b for b in range(1, wide.bit_length() - 1)]

    def swap(value, first, second=None):
        masks = (first, first if second is None else second)
        pairs = [(i, i ^ masks[i // narrow & 1]) for i in range(wide * narrow)]
        return lax.ppermute(value, AXES, pairs)

    def add(a, b):
        return (a.astype(F32) + b.astype(F32)).astype(a.dtype)

    def after(*values):
        return lax.optimization_barrier(values)

    def steps_of(halved, exchanged, gathered):
        pairs = lambda order: list(zip(*order))
        return (
            [("halve", *pair) for pair in pairs(halved)]
            + [("exchange", *pair) for pair in pairs(exchanged)]
            + [("gather", *pair) for pair in reversed(pairs(gathered))]
        )

    def start(value, step):
        kind, *masks = step
        if kind == "halve":
            half = value.shape[0] // 2
            return value[:half], swap(value[half:], *masks)
        return value, swap(value, *masks)

    def finish(kept, got, step):
        if step[0] == "gather":
            return jnp.concatenate([kept, got], axis=0)
        return add(kept, got) if step[0] in ("halve", "exchange") else (kept, got)

    wide_at, narrow_at = lax.axis_index("wide"), lax.axis_index("narrow")
    core = wide_at & 1
    flat = wide_at * narrow + narrow_at

    def named(owner, used):
        return sum((1 << b) for b, m in enumerate(used) if owner & m)

    def block_of(used):
        return sum(((flat & m) != 0).astype(jnp.int32) << b for b, m in enumerate(used))

    def split_at(pair, count):
        return tuple(o[:count] for o in pair), tuple(o[count:] for o in pair)

    def by_core(values):
        return jnp.where(core == 0, values[0], values[1]), jnp.where(core == 0, values[1], values[0])

    mixing = narrow == 2 and len(wide_masks) == 3
    if mixing:
        y, low, high = wide_masks
        ff_in, ff_rest, ff_out = ([y, low], [y, low]), ([high], [high]), ([low, y], [low, y])
        at_in, at_rest, at_out = ([y, 1, low], [low, y, 1]), ([high], [high]), ([y, 1, low], [low, 1, y])
        turns = "FAFAAFAFAAFFAA"
    else:
        ff_in, ff_rest = split_at((wide_masks, wide_masks), min(len(wide_masks) - 1, (width // TILE).bit_length() - 1))
        masks = narrow_masks + wide_masks
        at_in, at_rest = split_at((masks, masks), min(len(masks) - 1, (width // TILE // 2).bit_length() - 1))
        ff_out, at_out, turns = ff_in, at_in, ""
    ff_used = tuple(sorted(o) for o in ff_in)
    ff_in_tables, ff_out_tables = (
        tuple([named(owner, ff_used[c]) for owner in places(pair[c], 1 << len(ff_used[c]))] for c in range(2))
        for pair in (ff_in, ff_out)
    )
    at_used = tuple([core_mask] + sorted(o) for o in at_in)

    def at_tables(order):
        owners = [places(o, 1 << len(o)) for o in order]
        return tuple(
            [named(o, at_used[c]) for o in owners[c]] + [named(o ^ core_mask, at_used[1 - c]) for o in owners[1 - c]]
            for c in range(2)
        )

    ff_block = by_core([block_of(used) for used in ff_used])
    at_block = by_core([block_of(used) for used in at_used])
    info = jnp.stack([core, *ff_block, *at_block, narrow_at]).astype(jnp.int32)

    packed, tokens_in = after(pack(info, w_up, b_up, w_down), tokens_in)
    fetched = [packed]
    for mask in narrow_masks:
        fetched = fetched + [(swap(u, mask), swap(d, mask)) for u, d in fetched]

    row = lambda v: v[None].astype(F32)
    g1, c1, g2 = row(ln1_gain), row(ln1_bias), row(ln2_gain)
    qkv, prob, mixed, residual, second = attend(
        info, tokens_in, g1, c1, w_qkv, w_out, g2, row(ln2_bias), segment_ids, step_ids, pad_mask
    )
    out_part, dsec_part, own_keep, own_send, bias_own = ffn_own(
        info, ff_in_tables, mixing, second, cotangent, w_up, b_up, w_down
    )
    ups, downs = [u for u, _ in fetched[1:]], [d for _, d in fetched[1:]]
    own_send, ups = after(own_send, ups)
    away_ups = [swap(u, core_mask) for u in ups]
    away_downs = [swap(d, core_mask) for d in downs]
    chunks = [pair for here in zip(zip(ups, downs), zip(away_ups, away_downs)) for pair in here]
    rest = ffn_rest(
        info, ff_in_tables, mixing, second, cotangent, out_part, dsec_part, residual, row(b_down), g2, w_out, own_keep,
        chunks,
    )
    block_out, gres, gmix, branch, vec, bias_rest = rest[:6]
    grads = rest[6:]

    if narrow == 2 and units == width:
        vecs = (vec, bias_own, bias_rest)
    else:
        b_rest = bias_rest.reshape(-1, 2, units)
        b_rest = jnp.where(core == 0, b_rest, jnp.flip(b_rest, axis=1))
        b_all = jnp.concatenate([bias_own[None], b_rest], axis=0)
        for bit in range(narrow.bit_length() - 1):
            flipped = jnp.flip(b_all.reshape(-1, 2, (1 << bit) * 2, units), axis=1).reshape(b_all.shape)
            b_all = jnp.where(narrow_at >> bit & 1, flipped, b_all)
        vecs = (jnp.concatenate([vec, b_all.reshape(-1, width)], axis=0),)

    if mixing:
        ff_keep, ff_send, away = grads
        got_own, got = swap(own_send, core_mask), swap(away, core_mask)
        ff_send = join(info, ff_send, got, got_own)
        gmix, ff_send = after(gmix, ff_send)
        ff_got = swap(ff_send, 1, y)
    else:
        held = [add(own_keep, swap(own_send, core_mask))] + [add(grads[2 * j], swap(grads[2 * j + 1], core_mask)) for j in range(narrow - 1)]
        gmix, held = after(gmix, held)
        for mask in reversed(narrow_masks):
            held = [add(held[j], swap(held[j + mask], mask)) for j in range(mask)]
        ff_keep = held[0]

    dqkv, keep, send = attend_back(info, at_tables(at_in), qkv, prob, gmix, tokens_in, mixed, branch, g1, c1, w_qkv, *vecs)
    if mixing:
        send, ff_got = after(send, ff_got)
        ff_keep, ff_send = split(info, ff_keep, got, got_own, ff_got)
    keep = add(keep, swap(send, core_mask))
    grad_tokens = first_back(info, dqkv, w_qkv, tokens_in, gres, g1)
    steps = {
        "A": steps_of(at_in, at_rest, at_out)[:-1] + [("last", *steps_of(at_in, at_rest, at_out)[-1][1:]), ("core", core_mask)],
        "F": steps_of(ff_in, ff_rest, ff_out) + [("core", core_mask)],
    }
    if mixing:
        steps["F"] = [("halve", y, 1)] + steps["F"][1:]
        first = (ff_keep, swap(ff_send, y, 1))
    else:
        first = start(ff_keep, steps["F"][0])
    turns = turns or "".join(a + f for a, f in itertools.zip_longest("A" * len(steps["A"]), "F" * len(steps["F"]), fillvalue=""))
    under_way = {"A": start(keep, steps["A"][0]), "F": first}
    done, beside = (), (grad_tokens,)
    for turn in turns:
        other = "A" if turn == "F" else "F"
        kept, got = under_way.pop(turn)
        if other in under_way:
            other_kept, other_got = under_way[other]
            kept, other_kept, *beside = after(kept, other_kept, *beside)
            under_way[other] = other_kept, other_got
        else:
            kept, *beside = after(kept, *beside)
        if len(beside) == 1:
            (grad_tokens,), beside = beside, ()
        elif beside:
            (grad_w_up, grad_w_down), beside = beside, ()
        step, *steps[turn] = steps[turn]
        if step[0] == "last":
            written = attend_end(info, at_tables(at_out), (kept, crossed), width, 2 * units)
            got, written = after(got, written)
        value = finish(kept, got, step)
        if step[0] == "last":
            under_way[turn] = value, swap(got, core_mask)
        elif steps[turn]:
            under_way[turn] = start(value, steps[turn][0])
            if steps[turn][0][0] == "last":
                crossed = swap(value, core_mask)
        elif turn == "F":
            beside = ffn_end(info, ff_out_tables, *value)
        else:
            done = (value[0][0], crossed, value[0][1], value[1])
    grad_w_qkv, grad_w_out, d_gain1, d_bias1, d_gain2, d_bias2, d_bdown, grad_b_up = attend_end(
        info, at_tables(at_out), done, width, 2 * units, written
    )
    return (
        block_out, grad_tokens, d_gain1, d_bias1, grad_w_qkv, grad_w_out, d_gain2, d_bias2, grad_w_up, grad_b_up, grad_w_down,
        d_bdown,
    )


def solution(mesh):
    rows = P(("wide", "narrow"), None)
    in_specs = (
        rows, P(), P(), P(), P(), P(), P(), P(None, "narrow"), P("narrow"), P("narrow", None), P(), rows, rows, rows, rows,
    )
    out_specs = (
        rows, rows, P(), P(), P(), P(), P(), P(), P(None, "narrow"), P("narrow"), P("narrow", None), P(),
    )
    wide, narrow = mesh.shape["wide"], mesh.shape["narrow"]
    return jax.shard_map(
        functools.partial(local, wide, narrow), mesh=mesh, in_specs=in_specs, out_specs=out_specs, check_vma=False
    )
```
